32 devices in a mesh: tx: 4 (over z), ty: 2 (over x), mode: 4 (over y, core).
Axes of the slice: x: 2, y: 2, z: 4, core: 2. Of those that a mesh axis runs over, the one named last changes fastest.
Arguments:
- object_field: float32 [2, 512, 512], P(None, 'tx', 'ty'), may hold values from -5 to 5
- probe: float32 [2, 8, 256, 256], P(None, 'mode'), may hold values from -1.5 to 1.5
- amplitudes: bfloat16 [4, 2, 2, 256, 256], P('tx', 'ty'), may hold values from 0.29882812 to 2.5
- centers: int32 [4, 2, 2, 2], P('tx', 'ty'), may hold values from 0 to 255, as said below
- live: int32 [4, 2], P('tx', 'ty'), may hold values from 1 to 2, as said below
Outputs:
- updated: float32 [2, 512, 512], P(None, 'tx', 'ty')
The draws below stay inside these ranges and needn't reach their ends.
Inputs may be any that keep to these rules, and one draw needn't show every extreme that they name: `centers`: the first component is under 128, the second under 256; some live slot sits at offsets (127, 255) and some at (0, 0). A tile's positions fill its slots 0 to live - 1; some tile has all 2 slots live and some only one.
All inputs are finite; a program needn't handle non-finite values.
Results may differ from the reference program's by a relative error of at most 0.006.
Values may be sent and summed in bfloat16 or wider, within the bound.
No kernel may reach another device: no remote copies, remote signals or barrier semaphores. Data moves between devices by JAX's collectives and lax.ppermute only.
A program may use at most 64 MiB of HBM per device.

```python
import math
import jax
import jax.numpy as jnp
from jax import lax

W = 256
MODES = 8
SLOTS = 2
TR = 128
TC = 256
NTR = 4
NTC = 2
NX = 512
NY = 512


def draw_centers(key, part):
    key_spots = jax.random.fold_in(key, 11)
    key_high = jax.random.fold_in(key, 12)
    key_low = jax.random.fold_in(key, 13)
    limits = jnp.array([TR, TC], dtype=jnp.int32)
    spots = jax.random.randint(key_spots, (NTR * NTC, SLOTS, 2), 0, limits)
    high_tile = jax.random.randint(key_high, (), 0, NTR * NTC)
    low_tile = (high_tile + 1 + jax.random.randint(key_low, (), 0, NTR * NTC - 1)) % (NTR * NTC)
    spots = spots.at[high_tile, 0].set(limits - 1)
    spots = spots.at[low_tile, 0].set(jnp.zeros((2,), jnp.int32))
    return spots.reshape(NTR, NTC, SLOTS, 2)


def draw_live(key, part):
    key_base = jax.random.fold_in(key, 21)
    key_full = jax.random.fold_in(key, 22)
    key_most = jax.random.fold_in(key, 23)
    key_least = jax.random.fold_in(key, 24)
    tiles = NTR * NTC
    base = 1 + jax.random.randint(key_base, (tiles,), 0, max(1, SLOTS // 2))
    crowded = jax.random.randint(key_full, (tiles,), 0, 8) == 0
    counts = jnp.where(crowded, SLOTS, base).astype(jnp.int32)
    most_tile = jax.random.randint(key_most, (), 0, tiles)
    least_tile = (most_tile + 1 + jax.random.randint(key_least, (), 0, tiles - 1)) % tiles
    counts = counts.at[most_tile].set(SLOTS)
    counts = counts.at[least_tile].set(1)
    return counts.reshape(NTR, NTC)


def steps_of(key, shape, shards, least, largest):
    gain, own = 1.0, jax.random.fold_in(key, 6)
    for axis_at, shards_of in shards:
        heights = jnp.exp(jax.random.uniform(jax.random.fold_in(own, axis_at), (shards_of,), jnp.float32, least / len(shards), largest / len(shards)))
        gain = gain * jnp.repeat(heights, shape[axis_at] // shards_of).reshape([-1 if axis == axis_at else 1 for axis in range(len(shape))])
    return gain


def noise(rng, dims, spread, reach, cuts=(), held_as=jnp.bfloat16):
    result = spread * jax.random.normal(rng, dims, jnp.float32)
    if cuts:
        result = result * steps_of(rng, dims, cuts, -0.22, 0.18)
    return jnp.clip(result, -reach, reach).astype(held_as)


def setup_inputs(seed: int = 0) -> dict:
    arg_keys = jax.random.split(jax.random.key(seed), 6)
    return {
        "object_field": noise(arg_keys[0], (2, NX, NY), 0.7, 5.0, ((1, 4), (2, 2)), jnp.float32),
        "probe": noise(arg_keys[1], (2, MODES, W, W), 0.25, 1.5, ((1, 4),), jnp.float32),
        "amplitudes": jnp.clip(0.29882812 + 2.2011719 * jax.random.uniform(arg_keys[2], (NTR, NTC, SLOTS, W, W), jnp.float32) ** steps_of(arg_keys[2], (NTR, NTC, SLOTS, W, W), ((0, 4), (1, 2)), -0.2, 0.2), 0.29882812, 2.5).astype(jnp.bfloat16),
        "centers": draw_centers(jax.random.fold_in(arg_keys[5], 71), 0),
        "live": draw_live(jax.random.fold_in(arg_keys[5], 71), 0),
    }


power_floor = 0.01
regularizer = 0.1

def dft_tables(pattern_side):
    index_line = jnp.arange(pattern_side, dtype=jnp.int32)
    product_table = index_line[:, None] * index_line[None, :] % pattern_side
    angle_table = product_table.astype(jnp.float32) * (2.0 * math.pi / pattern_side)
    scaling = 1.0 / math.sqrt(pattern_side)
    table_real = (jnp.cos(angle_table) * scaling).astype(jnp.bfloat16)
    table_imaginary = (-jnp.sin(angle_table) * scaling).astype(jnp.bfloat16)
    return (table_real, table_imaginary)

def left_mult(matrix, signal):
    return jnp.einsum('uv,kvw->kuw', matrix.astype(jnp.float32), signal.astype(jnp.float32))

def right_mult(signal, matrix):
    return jnp.einsum('kuv,vw->kuw', signal.astype(jnp.float32), matrix.astype(jnp.float32))

def left_apply(matrix_real, matrix_imaginary, signal_real, signal_imaginary):
    return (left_mult(matrix_real, signal_real) - left_mult(matrix_imaginary, signal_imaginary), left_mult(matrix_real, signal_imaginary) + left_mult(matrix_imaginary, signal_real))

def right_apply(matrix_real, matrix_imaginary, signal_real, signal_imaginary):
    return (right_mult(signal_real, matrix_real) - right_mult(signal_imaginary, matrix_imaginary), right_mult(signal_real, matrix_imaginary) + right_mult(signal_imaginary, matrix_real))

def slot_gradient(patch, amplitude, probe_real, probe_imaginary, table_real, table_imaginary):
    patch_real = patch[0].astype(jnp.float32)
    patch_imaginary = patch[1].astype(jnp.float32)
    exit_real = (probe_real * patch_real - probe_imaginary * patch_imaginary).astype(jnp.bfloat16)
    exit_imaginary = (probe_real * patch_imaginary + probe_imaginary * patch_real).astype(jnp.bfloat16)
    half_real, half_imaginary = left_apply(table_real, table_imaginary, exit_real, exit_imaginary)
    far_real, far_imaginary = right_apply(table_real, table_imaginary, half_real.astype(jnp.bfloat16), half_imaginary.astype(jnp.bfloat16))
    power = lax.optimization_barrier(jnp.sum(far_real * far_real + far_imaginary * far_imaginary, axis=0))
    factor = amplitude.astype(jnp.float32) / jnp.sqrt(power + power_floor)
    fixed_real = (far_real * factor).astype(jnp.bfloat16)
    fixed_imaginary = (far_imaginary * factor).astype(jnp.bfloat16)
    back_half_real, back_half_imaginary = left_apply(table_real, -table_imaginary, fixed_real, fixed_imaginary)
    back_real, back_imaginary = right_apply(table_real, -table_imaginary, back_half_real.astype(jnp.bfloat16), back_half_imaginary.astype(jnp.bfloat16))
    diff_real = back_real - exit_real.astype(jnp.float32)
    diff_imaginary = back_imaginary - exit_imaginary.astype(jnp.float32)
    grad_real = lax.optimization_barrier(jnp.sum(probe_real * diff_real + probe_imaginary * diff_imaginary, axis=0))
    grad_imaginary = lax.optimization_barrier(jnp.sum(probe_real * diff_imaginary - probe_imaginary * diff_real, axis=0))
    return (grad_real, grad_imaginary)

def reference(object_field, probe, amplitudes, centers, live):
    half_width = W // 2
    table_real, table_imaginary = dft_tables(W)
    object_low = object_field.astype(jnp.bfloat16)
    padded = jnp.pad(object_low, ((0, 0), (half_width, half_width), (half_width, half_width)))
    probe_real = probe[0]
    probe_imaginary = probe[1]
    probe_power = lax.optimization_barrier(jnp.sum(probe_real * probe_real + probe_imaginary * probe_imaginary, axis=0))
    total_items = NTR * NTC * SLOTS
    item_index = jnp.arange(total_items, dtype=jnp.int32)
    tile_index = item_index // SLOTS
    slot_index = item_index % SLOTS
    tile_row = tile_index // NTC
    tile_col = tile_index % NTC
    flat_centers = centers.reshape(total_items, 2).astype(jnp.int32)
    flat_live = live.reshape(NTR * NTC).astype(jnp.int32)
    live_flag = slot_index < flat_live[tile_index]
    row_start = (tile_row * TR + flat_centers[:, 0]).astype(jnp.int32)
    col_start = (tile_col * TC + flat_centers[:, 1]).astype(jnp.int32)
    flat_amplitudes = amplitudes.reshape(total_items, W, W)
    anchor = jnp.zeros((), jnp.int32)
    summed = jnp.zeros((3, NX + W, NY + W), jnp.float32)

    def advance(summed, record):
        row_at, col_at, amplitude, flag = record

        def work(summed):
            patch = lax.dynamic_slice(padded, (anchor, row_at, col_at), (2, W, W))
            grad_real, grad_imaginary = slot_gradient(patch, amplitude, probe_real, probe_imaginary, table_real, table_imaginary)
            block = jnp.stack([grad_real, grad_imaginary, probe_power])
            current = lax.dynamic_slice(summed, (anchor, row_at, col_at), (3, W, W))
            return lax.dynamic_update_slice(summed, current + block, (anchor, row_at, col_at))
        return (lax.cond(flag, work, lambda keep: keep, summed), None)
    summed, _ = lax.scan(advance, summed, (row_start, col_start, flat_amplitudes, live_flag))
    inner = summed[:, half_width:half_width + NX, half_width:half_width + NY]
    return object_field + inner[:2] / (inner[2] + regularizer)
```

```python
import functools
import math

import jax
import jax.numpy as jnp
import numpy as np
from jax import lax
from jax.experimental import pallas as pl
from jax.experimental.pallas import tpu as pltpu
from jax.sharding import PartitionSpec as P

power_floor = 0.01
regularizer = 0.1
nowhere = -(1 << 20)


def dft_matrices(side):
    line = np.arange(side, dtype=np.int32)
    angle = (line[:, None] * line[None, :] % side).astype(np.float32) * np.float32(
        2.0 * math.pi / side
    )
    scaling = np.float32(1.0 / math.sqrt(side))
    real = (np.cos(angle) * scaling).astype(jnp.bfloat16)
    imag = (-np.sin(angle) * scaling).astype(jnp.bfloat16)
    direct = np.block([[real, -imag], [imag, real]])
    swapped = np.block([[real, imag], [-imag, real]])
    return direct, swapped


def dot(left, right):
    return jnp.dot(left, right, preferred_element_type=jnp.float32)


def iota(shape, dim):
    return lax.broadcasted_iota(jnp.int32, shape, dim)


def column_coordinate(at, tile_cols, half, sides, x_index, x_count):
    own = at + half
    if sides == 1:
        side = at - tile_cols + jnp.where(x_index == 0, half + tile_cols, 0)
        return jnp.where(at < tile_cols, own, side)
    left = jnp.where(x_index > 0, at - tile_cols, nowhere)
    right = jnp.where(x_index < x_count - 1, at, nowhere)
    return jnp.where(at < tile_cols, own, jnp.where(at < tile_cols + half, left, right))


def wave_kernel(
    sides,
    slots,
    z_count,
    x_count,
    place_ref,
    *refs,
):
    n_pieces = 3 + 3 * sides
    pieces = refs[:n_pieces]
    groups = refs[n_pieces : n_pieces + 4]
    amplitude_ref, direct_ref, swapped_ref = refs[n_pieces + 4 : n_pieces + 7]
    outs = refs[n_pieces + 7 : n_pieces + 7 + n_pieces + 1]
    ext_ref, exit_ref, far_ref, grad_ref = refs[n_pieces + 7 + n_pieces + 1 :]
    row_at, col_at, is_live = place_ref[0], place_ref[1], place_ref[2]
    z_index, x_index, parity = place_ref[3], place_ref[4], place_ref[5]
    own_ref, rows_a, rows_b = pieces[:3]
    tile_rows, tile_cols = own_ref.shape[1:]
    side = groups[0].shape[2]
    half = side // 2
    ext_rows = tile_rows + side
    ext_cols = tile_cols + sides * half
    a_at = pl.multiple_of(jnp.where(parity == 0, 0, half + tile_rows), half)
    b_at = pl.multiple_of(jnp.where(parity == 0, half + tile_rows, 0), half)

    for channel in range(2):
        base = channel * ext_rows
        own_rows = pl.ds(base + half, tile_rows)
        ext_ref[own_rows, :tile_cols] = own_ref[channel]
        ext_ref[pl.ds(base + a_at, half), :tile_cols] = rows_a[channel]
        ext_ref[pl.ds(base + b_at, half), :tile_cols] = rows_b[channel]
        for index in range(sides):
            level, corner_a, corner_b = pieces[3 + 3 * index : 6 + 3 * index]
            columns = slice(tile_cols + index * half, tile_cols + (index + 1) * half)
            ext_ref[own_rows, columns] = level[channel]
            ext_ref[pl.ds(base + a_at, half), columns] = corner_a[channel]
            ext_ref[pl.ds(base + b_at, half), columns] = corner_b[channel]

    def column_of(at):
        return column_coordinate(at, tile_cols, half, sides, x_index, x_count)

    def row_of(at):
        first = jnp.where(z_index > 0, 0, half)
        last = jnp.where(z_index < z_count - 1, ext_rows, half + tile_rows)
        return jnp.where((at >= first) & (at < last), at, nowhere)

    pick_cols = (
        column_of(iota((ext_cols, side), 0)) == iota((ext_cols, side), 1) + col_at
    ).astype(jnp.bfloat16)
    pick_rows = (row_of(iota((side, ext_rows), 1)) == iota((side, ext_rows), 0) + row_at).astype(
        jnp.bfloat16
    )
    narrow = dot(ext_ref[...], pick_cols).astype(jnp.bfloat16)
    patch_real = dot(pick_rows, narrow[:ext_rows])
    patch_imag = dot(pick_rows, narrow[ext_rows:])

    direct = direct_ref[...]
    swapped = swapped_ref[...]
    modes = groups[0].shape[1]

    def wide(tall):
        return jnp.concatenate([tall[:side], tall[side:]], axis=1)

    def tall(wide):
        return jnp.concatenate([wide[:, :side], wide[:, side:]], axis=0)

    def forward(group, slot):
        power = jnp.zeros((side, side), jnp.float32)
        weight = jnp.zeros((side, side), jnp.float32)
        for k in range(modes):
            real = group[0, k].astype(jnp.float32)
            imag = group[1, k].astype(jnp.float32)
            exit_wave = jnp.concatenate(
                [
                    (real * patch_real - imag * patch_imag).astype(jnp.bfloat16),
                    (real * patch_imag + imag * patch_real).astype(jnp.bfloat16),
                ],
                axis=0,
            )
            exit_ref[slot + k] = exit_wave
            half_wave = dot(direct, exit_wave).astype(jnp.bfloat16)
            far = dot(wide(half_wave), swapped)
            far_ref[slot + k] = far
            power = power + (far[:, :side] * far[:, :side] + far[:, side:] * far[:, side:])
            weight = weight + (real * real + imag * imag)
        return power, weight

    sums = [forward(group, index * modes) for index, group in enumerate(groups)]
    power = (sums[0][0] + sums[1][0]) + (sums[2][0] + sums[3][0])
    weight = (sums[0][1] + sums[1][1]) + (sums[2][1] + sums[3][1])
    outs[-1][...] = weight.astype(jnp.bfloat16)
    factor = amplitude_ref[0].astype(jnp.float32) / jnp.sqrt(power + power_floor)
    factor = jnp.concatenate([factor, factor], axis=1)

    def backward(group, slot):
        grad_real = jnp.zeros((side, side), jnp.float32)
        grad_imag = jnp.zeros((side, side), jnp.float32)
        for k in range(modes):
            fixed = (far_ref[slot + k] * factor).astype(jnp.bfloat16)
            back_half = dot(swapped, tall(fixed)).astype(jnp.bfloat16)
            back = dot(wide(back_half), direct)
            exit_wave = exit_ref[slot + k].astype(jnp.float32)
            real = group[0, k].astype(jnp.float32)
            imag = group[1, k].astype(jnp.float32)
            diff_real = back[:, :side] - exit_wave[:side]
            diff_imag = back[:, side:] - exit_wave[side:]
            grad_real = grad_real + (real * diff_real + imag * diff_imag)
            grad_imag = grad_imag + (real * diff_imag - imag * diff_real)
        return grad_real, grad_imag

    grads = [backward(group, index * modes) for index, group in enumerate(groups)]
    put_cols = (
        (column_of(iota((side, ext_cols), 1)) == iota((side, ext_cols), 0) + col_at)
        & (is_live > 0)
    ).astype(jnp.bfloat16)
    put_rows = (iota((ext_rows, side), 0) == iota((ext_rows, side), 1) + row_at).astype(
        jnp.bfloat16
    )
    for channel in range(2):
        gradient = (grads[0][channel] + grads[1][channel]) + (grads[2][channel] + grads[3][channel])
        placed = dot(put_rows, gradient.astype(jnp.bfloat16)).astype(jnp.bfloat16)
        grad_ref[...] = dot(placed, put_cols).astype(jnp.bfloat16)
        outs[0][channel] = grad_ref[half : half + tile_rows, :tile_cols]
        outs[1][channel] = grad_ref[pl.ds(b_at, half), :tile_cols]
        outs[2][channel] = grad_ref[pl.ds(a_at, half), :tile_cols]
        for index in range(sides):
            columns = slice(tile_cols + index * half, tile_cols + (index + 1) * half)
            outs[3 + 3 * index][channel] = grad_ref[half : half + tile_rows, columns]
            outs[4 + 3 * index][channel] = grad_ref[pl.ds(b_at, half), columns]
            outs[5 + 3 * index][channel] = grad_ref[pl.ds(a_at, half), columns]


def weight_kernel(slots, z_count, x_count, place_ref, table_ref, weight_ref, out_ref):
    tile_rows, tile_cols = out_ref.shape
    side = weight_ref.shape[0]
    half = side // 2
    z_index, x_index = place_ref[3], place_ref[4]
    x_tiles = (
        [(x, x - x_index) for x in range(x_count)]
        if x_count <= 3
        else [(x_index + step, step) for step in (-1, 0, 1)]
    )
    weight = weight_ref[...]
    total = jnp.zeros((tile_rows, tile_cols), jnp.float32)
    for z_step in (-1, 0, 1):
        z_tile = z_index + z_step
        z_held = jnp.clip(z_tile, 0, z_count - 1)
        for x_tile, x_step in x_tiles:
            x_held = jnp.clip(x_tile, 0, x_count - 1)
            inside = (z_held == z_tile) & (x_held == x_tile)
            record = z_held * x_count + x_held
            for slot in range(slots):
                shown = inside & (slot < table_ref[record, 2 * slots])
                row = table_ref[record, 2 * slot] + z_step * tile_rows - half
                col = table_ref[record, 2 * slot + 1] + x_step * tile_cols - half
                row = jnp.where(shown, row, nowhere)
                put_rows = (
                    iota((tile_rows, side), 0) == iota((tile_rows, side), 1) + row
                ).astype(jnp.bfloat16)
                put_cols = (
                    iota((side, tile_cols), 1) == iota((side, tile_cols), 0) + col
                ).astype(jnp.bfloat16)
                placed = dot(put_rows, weight).astype(jnp.bfloat16)
                total = total + dot(placed, put_cols)
    out_ref[...] = total


def sum_kernel(sides, z_count, x_count, place_ref, *refs):
    pieces, out_ref = refs[:-1], refs[-1]
    own_ref, rows_a, rows_b = pieces[:3]
    tile_cols = own_ref.shape[2]
    half = pieces[3].shape[2]
    z_index, x_index, parity = place_ref[3], place_ref[4], place_ref[5]
    below = z_index > 0
    above = z_index < z_count - 1
    a_on = jnp.where(parity == 0, below, above)
    b_on = jnp.where(parity == 0, above, below)

    def gate(on, ref, channel):
        return jnp.where(on, ref[channel].astype(jnp.float32), 0.0)

    for channel in range(2):
        total = own_ref[channel].astype(jnp.float32)
        total = total + gate(a_on, rows_a, channel) + gate(b_on, rows_b, channel)
        first = jnp.zeros((total.shape[0], half), jnp.float32)
        last = first
        for index in range(sides):
            level, corner_a, corner_b = pieces[3 + 3 * index : 6 + 3 * index]
            edge = level[channel].astype(jnp.float32)
            edge = edge + gate(a_on, corner_a, channel) + gate(b_on, corner_b, channel)
            if sides == 1:
                first = jnp.where(x_index == 1, edge, 0.0)
                last = jnp.where(x_index == 0, edge, 0.0)
            elif index == 0:
                last = jnp.where(x_index < x_count - 1, edge, 0.0)
            else:
                first = jnp.where(x_index > 0, edge, 0.0)
        zero = jnp.zeros((total.shape[0], tile_cols - 2 * half), jnp.float32)
        parts = [first, zero, last] if tile_cols > 2 * half else [first, last]
        total = total + jnp.concatenate(parts, axis=1)
        out_ref[channel] = total.astype(jnp.bfloat16)


def smem():
    return pl.BlockSpec(memory_space=pltpu.SMEM)


def vmem():
    return pl.BlockSpec(memory_space=pltpu.VMEM)


def on_device(object_field, probe, amplitudes, centers, live):
    side = probe.shape[2]
    half = side // 2
    _, tile_rows, tile_cols = object_field.shape
    slots = centers.shape[2]
    z_count = lax.axis_size("tx")
    x_count = lax.axis_size("ty")
    m_count = lax.axis_size("mode")
    if tile_rows != half or slots != 2 or m_count != 4 or x_count < 2:
        raise ValueError("unsupported sizes")
    z_index = lax.axis_index("tx")
    x_index = lax.axis_index("ty")
    member = lax.axis_index("mode")
    parity = member % 2
    sides = 1 if x_count == 2 else 2
    axes = ("tx", "ty", "mode")

    def zigzag(flip, x_step):
        def moved(z, m):
            down = (m % 2 == 0) != flip
            if down:
                return (z + 1, m) if z < z_count - 1 else (z, m ^ 1)
            return (z - 1, m) if z > 0 else (z, m ^ 1)

        pairs = []
        for z in range(z_count):
            for x in range(x_count):
                for m in range(m_count):
                    z_to, m_to = moved(z, m)
                    x_to = (x + x_step) % x_count
                    pairs.append(
                        (
                            (z * x_count + x) * m_count + m,
                            (z_to * x_count + x_to) * m_count + m_to,
                        )
                    )
        return pairs

    def level(step):
        return [(x, (x + step) % x_count) for x in range(x_count)]

    def exchange(array, flip):
        return lax.ppermute(array, "mode", [(m, m ^ flip) for m in range(m_count)])

    probe_low = probe.astype(jnp.bfloat16)
    probe_y = exchange(probe_low, 2)
    probe_core = exchange(probe_low, 1)
    object_low = object_field.astype(jnp.bfloat16)
    x_steps = [1] if sides == 1 else [1, -1]
    if sides == 1:
        edges = [
            lax.dynamic_slice_in_dim(object_low, (tile_cols - half) * (1 - x_index), half, axis=2)
        ]
    else:
        edges = [object_low[:, :, tile_cols - half :], object_low[:, :, :half]]
    pieces = [object_low]
    pieces += [lax.ppermute(object_low, axes, zigzag(flip, 0)) for flip in (False, True)]
    for step, edge in zip(x_steps, edges):
        pieces.append(lax.ppermute(edge, "ty", level(step)))
        pieces += [lax.ppermute(edge, axes, zigzag(flip, step)) for flip in (False, True)]
    probe_diagonal = exchange(probe_y, 1)

    slot = parity
    place = jnp.stack(
        [
            centers[0, 0, slot, 0],
            centers[0, 0, slot, 1],
            (slot < live[0, 0]).astype(jnp.int32),
            z_index,
            x_index,
            parity,
        ]
    )
    record = jnp.concatenate([centers.reshape(1, 2 * slots), live.reshape(1, 1)], axis=1)
    table = lax.all_gather(record, ("tx", "ty"), axis=0, tiled=True)
    amplitude = lax.dynamic_slice_in_dim(amplitudes[0, 0], slot, 1, axis=0)
    direct, swapped = dft_matrices(side)
    ext_rows = tile_rows + side
    ext_cols = tile_cols + sides * half
    n_pieces = len(pieces)
    results = pl.pallas_call(
        functools.partial(wave_kernel, sides, slots, z_count, x_count),
        out_shape=[jax.ShapeDtypeStruct(piece.shape, jnp.bfloat16) for piece in pieces]
        + [jax.ShapeDtypeStruct((side, side), jnp.bfloat16)],
        in_specs=[smem()] + [vmem()] * (n_pieces + 7),
        out_specs=[vmem()] * (n_pieces + 1),
        scratch_shapes=[
            pltpu.VMEM((2 * ext_rows, ext_cols), jnp.bfloat16),
            pltpu.VMEM((4 * probe.shape[1], 2 * side, side), jnp.bfloat16),
            pltpu.VMEM((4 * probe.shape[1], side, 2 * side), jnp.float32),
            pltpu.VMEM((ext_rows, ext_cols), jnp.bfloat16),
        ],
        compiler_params=pltpu.CompilerParams(vmem_limit_bytes=48 * 1024 * 1024),
        name="waves",
    )(
        place,
        *pieces,
        probe_low,
        probe_core,
        probe_y,
        probe_diagonal,
        amplitude,
        jnp.asarray(direct),
        jnp.asarray(swapped),
    )
    weight = pl.pallas_call(
        functools.partial(weight_kernel, slots, z_count, x_count),
        out_shape=jax.ShapeDtypeStruct((tile_rows, tile_cols), jnp.float32),
        in_specs=[smem(), smem(), vmem()],
        out_specs=vmem(),
        name="weights",
    )(place, table, results[-1])
    received = [results[0]]
    received += [
        lax.ppermute(results[1 + index], axes, zigzag(flip, 0))
        for index, flip in enumerate((False, True))
    ]
    for index, step in enumerate(x_steps):
        back_step = -step
        received.append(lax.ppermute(results[3 + 3 * index], "ty", level(back_step)))
        received += [
            lax.ppermute(results[4 + 3 * index + turn], axes, zigzag(flip, back_step))
            for turn, flip in enumerate((False, True))
        ]
    summed = pl.pallas_call(
        functools.partial(sum_kernel, sides, z_count, x_count),
        out_shape=jax.ShapeDtypeStruct(object_field.shape, jnp.bfloat16),
        in_specs=[smem()] + [vmem()] * n_pieces,
        out_specs=vmem(),
        name="sums",
    )(place, *received)
    other = exchange(summed, 1)
    gradient = summed.astype(jnp.float32) + other.astype(jnp.float32)
    return object_field + gradient / (weight + regularizer)


def solution(mesh):
    return jax.shard_map(
        on_device,
        mesh=mesh,
        in_specs=(
            P(None, "tx", "ty"),
            P(None, "mode", None, None),
            P("tx", "ty", None, None, None),
            P("tx", "ty", None, None),
            P("tx", "ty"),
        ),
        out_specs=P(None, "tx", "ty"),
        check_vma=False,
    )
```

```python
import functools
import math

import jax
import jax.numpy as jnp
import numpy as np
from jax import lax
from jax.experimental import pallas as pl
from jax.experimental.pallas import tpu as pltpu
from jax.sharding import PartitionSpec as P

power_floor = 0.01
regularizer = 0.1
nowhere = -(1 << 20)
record_rows = 16
vmem_bytes = 40 * 1024 * 1024


def dft_matrices(side):
    line = np.arange(side, dtype=np.int32)
    angle = (line[:, None] * line[None, :] % side).astype(np.float32) * np.float32(
        2.0 * math.pi / side
    )
    scaling = np.float32(1.0 / math.sqrt(side))
    real = (np.cos(angle) * scaling).astype(jnp.bfloat16)
    imag = (-np.sin(angle) * scaling).astype(jnp.bfloat16)
    direct = np.block([[real, -imag], [imag, real]])
    swapped = np.block([[real, imag], [-imag, real]])
    return direct, swapped


def dot(left, right):
    return jnp.dot(left, right, preferred_element_type=jnp.float32)


def iota(shape, dim):
    return lax.broadcasted_iota(jnp.int32, shape, dim)


def column_coordinate(at, tile_cols, half, sides, x_index, x_count):
    own = at + half
    if sides == 1:
        side = at - tile_cols + jnp.where(x_index == 0, half + tile_cols, 0)
        return jnp.where(at < tile_cols, own, side)
    left = jnp.where(x_index > 0, at - tile_cols, nowhere)
    right = jnp.where(x_index < x_count - 1, at, nowhere)
    return jnp.where(at < tile_cols, own, jnp.where(at < tile_cols + half, left, right))


def wide(tall):
    side = tall.shape[0] // 2
    return jnp.concatenate([tall[:side], tall[side:]], axis=1)


def tall(wide):
    side = wide.shape[1] // 2
    return jnp.concatenate([wide[:, :side], wide[:, side:]], axis=0)


def here():
    return (lax.axis_index("tx"), lax.axis_index("ty"), lax.axis_index("mode") % 2)


def pack_kernel(sides, slots, centers_ref, live_ref, object_ref, *outs):
    _, tile_rows, tile_cols = object_ref.shape
    half = outs[1].shape[1]
    _, x_index, _ = here()
    record = jnp.zeros((record_rows, tile_cols), jnp.float32)
    line = iota((record_rows, tile_cols), 0)
    for slot in range(slots):
        for axis in range(2):
            value = centers_ref[0, 0, slot, axis].astype(jnp.float32)
            record = jnp.where(line == 2 * slot + axis, value, record)
    record = jnp.where(line == 2 * slots, live_ref[0, 0].astype(jnp.float32), record)
    record = record.astype(jnp.bfloat16)
    first, last = slice(0, half), slice(tile_cols - half, tile_cols)
    for channel in range(2):
        rows = slice(channel * tile_rows, (channel + 1) * tile_rows)
        values = object_ref[channel].astype(jnp.bfloat16)
        outs[0][rows] = values
        if sides == 1:
            outs[1][rows] = jnp.where(x_index == 0, values[:, last], values[:, first])
        else:
            outs[1][rows] = values[:, last]
            outs[2][rows] = values[:, first]
    rows = slice(2 * tile_rows, 2 * tile_rows + record_rows)
    outs[0][rows] = record
    for out in outs[1:]:
        out[rows] = record[:, :half]


def row_starts(half, tile_rows, parity):
    low, high = 0, half + tile_rows
    return (
        pl.multiple_of(jnp.where(parity == 0, low, high), half),
        pl.multiple_of(jnp.where(parity == 0, high, low), half),
    )


def patch_of(sides, z_count, x_count, tile_rows, side, centers_ref, pieces, ext_ref):
    z_index, x_index, parity = here()
    row_at = centers_ref[0, 0, parity, 0]
    col_at = centers_ref[0, 0, parity, 1]
    half = side // 2
    tile_cols = pieces[0].shape[1]
    ext_rows = tile_rows + side
    ext_cols = tile_cols + sides * half
    a_at, b_at = row_starts(half, tile_rows, parity)
    for channel in range(2):
        base = channel * ext_rows
        rows = slice(channel * tile_rows, (channel + 1) * tile_rows)
        for index in range(1 + sides):
            columns = (
                slice(0, tile_cols)
                if index == 0
                else slice(tile_cols + (index - 1) * half, tile_cols + index * half)
            )
            level, turn_a, turn_b = pieces[3 * index : 3 * index + 3]
            ext_ref[pl.ds(base + half, tile_rows), columns] = level[rows]
            ext_ref[pl.ds(base + a_at, half), columns] = turn_a[rows]
            ext_ref[pl.ds(base + b_at, half), columns] = turn_b[rows]
    at = iota((ext_cols, side), 0)
    column = column_coordinate(at, tile_cols, half, sides, x_index, x_count)
    pick_cols = (column == iota((ext_cols, side), 1) + col_at).astype(jnp.bfloat16)
    at = iota((side, ext_rows), 1)
    first = jnp.where(z_index > 0, 0, half)
    last = jnp.where(z_index < z_count - 1, ext_rows, half + tile_rows)
    row = jnp.where((at >= first) & (at < last), at, nowhere)
    pick_rows = (row == iota((side, ext_rows), 0) + row_at).astype(jnp.bfloat16)
    narrow = dot(ext_ref[...], pick_cols).astype(jnp.bfloat16)
    return dot(pick_rows, narrow[:ext_rows]), dot(pick_rows, narrow[ext_rows:])


def forward(groups, patch, direct, swapped, far_ref, exit_ref, at):
    patch_real, patch_imag = patch
    side = patch_real.shape[0]
    sums = []
    for group in groups:
        modes = group.shape[1]
        power = jnp.zeros((side, side), jnp.float32)
        weight = jnp.zeros((side, side), jnp.float32)
        halves = []
        for k in range(modes):
            real = group[0, k].astype(jnp.float32)
            imag = group[1, k].astype(jnp.float32)
            exit_wave = jnp.concatenate(
                [
                    (real * patch_real - imag * patch_imag).astype(jnp.bfloat16),
                    (real * patch_imag + imag * patch_real).astype(jnp.bfloat16),
                ],
                axis=0,
            )
            exit_ref[at + k] = exit_wave
            halves.append(wide(dot(direct, exit_wave).astype(jnp.bfloat16)))
            weight = weight + (real * real + imag * imag)
        far_both = dot(jnp.concatenate(halves, axis=0), swapped)
        for k in range(modes):
            far = far_both[k * side : (k + 1) * side]
            far_ref[at + k] = far
            power = power + (far[:, :side] * far[:, :side] + far[:, side:] * far[:, side:])
        sums.append((power, weight))
        at += modes
    return sums


def backward(groups, factor, direct, swapped, far_ref, exit_ref):
    side = factor.shape[0]
    grads = []
    at = 0
    for group in groups:
        modes = group.shape[1]
        grad_real = jnp.zeros((side, side), jnp.float32)
        grad_imag = jnp.zeros((side, side), jnp.float32)
        halves = []
        for k in range(modes):
            fixed = (far_ref[at + k] * factor).astype(jnp.bfloat16)
            halves.append(wide(dot(swapped, tall(fixed)).astype(jnp.bfloat16)))
        back_both = dot(jnp.concatenate(halves, axis=0), direct)
        for k in range(modes):
            back = back_both[k * side : (k + 1) * side]
            exit_wave = exit_ref[at + k].astype(jnp.float32)
            real = group[0, k].astype(jnp.float32)
            imag = group[1, k].astype(jnp.float32)
            diff_real = back[:, :side] - exit_wave[:side]
            diff_imag = back[:, side:] - exit_wave[side:]
            grad_real = grad_real + (real * diff_real + imag * diff_imag)
            grad_imag = grad_imag + (real * diff_imag - imag * diff_real)
        grads.append((grad_real, grad_imag))
        at += modes
    return grads


def near_kernel(sides, z_count, x_count, tile_rows, centers_ref, *refs):
    n_pieces = 3 + 3 * sides
    pieces = refs[:n_pieces]
    own, core, direct, swapped = refs[n_pieces : n_pieces + 4]
    patch_ref, far_ref, exit_ref, sum_ref, ext_ref = refs[n_pieces + 4 :]
    side = own.shape[2]
    patch = patch_of(sides, z_count, x_count, tile_rows, side, centers_ref, pieces, ext_ref)
    patch_ref[0], patch_ref[1] = patch
    sums = forward((own, core), patch, direct[...], swapped[...], far_ref, exit_ref, 0)
    sum_ref[0] = sums[0][0] + sums[1][0]
    sum_ref[1] = sums[0][1] + sums[1][1]


def far_kernel(patch_ref, group, direct, swapped, far_ref, exit_ref, sum_ref):
    patch = (patch_ref[0], patch_ref[1])
    ((power, weight),) = forward((group,), patch, direct[...], swapped[...], far_ref, exit_ref, 0)
    sum_ref[0] = power
    sum_ref[1] = weight


def back_kernel(sides, x_count, tile_rows, tile_cols, centers_ref, live_ref, *refs):
    n_pieces = 3 + 3 * sides
    amplitude_ref, patch_ref, own, core, over, last, direct_ref, swapped_ref = refs[:8]
    near_far, near_exit, near_sum, over_far, over_exit, over_sum = refs[8:14]
    outs = refs[14 : 14 + n_pieces + 1]
    last_far, last_exit, grad_ref = refs[14 + n_pieces + 1 :]
    side = own.shape[2]
    half = side // 2
    modes = own.shape[1]
    ext_rows = tile_rows + side
    ext_cols = tile_cols + sides * half
    _, x_index, parity = here()
    row_at = centers_ref[0, 0, parity, 0]
    col_at = centers_ref[0, 0, parity, 1]
    is_live = parity < live_ref[0, 0]
    direct = direct_ref[...]
    swapped = swapped_ref[...]
    patch = (patch_ref[0], patch_ref[1])
    ((power, weight),) = forward((last,), patch, direct, swapped, last_far, last_exit, 0)
    power = near_sum[0] + (over_sum[0] + power)
    weight = near_sum[1] + (over_sum[1] + weight)
    outs[-1][...] = weight.astype(jnp.bfloat16)
    amplitude = amplitude_ref[0, 0, parity].astype(jnp.float32)
    factor = amplitude / jnp.sqrt(power + power_floor)
    factor = jnp.concatenate([factor, factor], axis=1)
    near = backward((own, core), factor, direct, swapped, near_far, near_exit)
    (beyond,) = backward((over,), factor, direct, swapped, over_far, over_exit)
    (final,) = backward((last,), factor, direct, swapped, last_far, last_exit)
    at = iota((side, ext_cols), 1)
    column = column_coordinate(at, tile_cols, half, sides, x_index, x_count)
    put_cols = ((column == iota((side, ext_cols), 0) + col_at) & is_live).astype(jnp.bfloat16)
    put_rows = (iota((ext_rows, side), 0) == iota((ext_rows, side), 1) + row_at).astype(
        jnp.bfloat16
    )
    a_at, b_at = row_starts(half, tile_rows, parity)
    for channel in range(2):
        gradient = (near[0][channel] + near[1][channel]) + (beyond[channel] + final[channel])
        placed = dot(put_rows, gradient.astype(jnp.bfloat16)).astype(jnp.bfloat16)
        grad_ref[...] = dot(placed, put_cols).astype(jnp.bfloat16)
        for index in range(1 + sides):
            columns = (
                slice(0, tile_cols)
                if index == 0
                else slice(tile_cols + (index - 1) * half, tile_cols + index * half)
            )
            outs[3 * index][channel] = grad_ref[half : half + tile_rows, columns]
            outs[3 * index + 1][channel] = grad_ref[pl.ds(b_at, half), columns]
            outs[3 * index + 2][channel] = grad_ref[pl.ds(a_at, half), columns]


def weight_kernel(sides, slots, z_count, x_count, weight_ref, *refs):
    pieces, out_ref = refs[:-1], refs[-1]
    tile_rows, tile_cols = out_ref.shape
    side = weight_ref.shape[0]
    half = side // 2
    z_index, x_index, parity = here()
    z_step_a = jnp.where(parity == 0, -1, 1)
    if sides == 1:
        x_steps = [0, jnp.where(x_index == 0, 1, -1)]
        x_shown = [True, True]
    else:
        x_steps = [0, -1, 1]
        x_shown = [True, x_index > 0, x_index < x_count - 1]
    weight = weight_ref[...]
    total = jnp.zeros((tile_rows, tile_cols), jnp.float32)
    for index, x_step in enumerate(x_steps):
        turns = []
        for turn, z_step in enumerate((0, z_step_a, -z_step_a)):
            part = jnp.zeros((tile_rows, tile_cols), jnp.float32)
            z_tile = z_index + z_step
            shown = (z_tile >= 0) & (z_tile < z_count) & x_shown[index]
            record = pieces[3 * index + turn][2 * tile_rows :].astype(jnp.float32)
            record = record.astype(jnp.int32)
            if record.shape[1] < side:
                record = jnp.concatenate([record] * (side // record.shape[1]), axis=1)
            count = record[2 * slots : 2 * slots + 1, :side]
            for slot in range(slots):
                row = record[2 * slot : 2 * slot + 1, :side] + (z_step * tile_rows - half)
                col = record[2 * slot + 1 : 2 * slot + 2, :side] + (x_step * tile_cols - half)
                row = jnp.where((count > slot) & shown, row, nowhere)
                put_rows = (
                    iota((tile_rows, side), 0) == iota((tile_rows, side), 1) + row
                ).astype(jnp.bfloat16)
                put_cols = (
                    iota((side, tile_cols), 1) == iota((side, tile_cols), 0) + col[:, :1]
                ).astype(jnp.bfloat16)
                placed = dot(put_rows, weight).astype(jnp.bfloat16)
                part = part + dot(placed, put_cols)
            turns.append(part)
        total = total + (turns[0] + (turns[1] + turns[2]))
    out_ref[...] = total


def sum_kernel(sides, z_count, x_count, *refs):
    pieces, out_ref = refs[:-1], refs[-1]
    own_ref, rows_a, rows_b = pieces[:3]
    tile_cols = own_ref.shape[2]
    half = pieces[3].shape[2]
    z_index, x_index, parity = here()
    below = z_index > 0
    above = z_index < z_count - 1
    a_on = jnp.where(parity == 0, below, above)
    b_on = jnp.where(parity == 0, above, below)

    def gate(on, ref, channel):
        return jnp.where(on, ref[channel].astype(jnp.float32), 0.0)

    for channel in range(2):
        total = own_ref[channel].astype(jnp.float32)
        total = total + gate(a_on, rows_a, channel) + gate(b_on, rows_b, channel)
        first = jnp.zeros((total.shape[0], half), jnp.float32)
        last = first
        for index in range(sides):
            level, corner_a, corner_b = pieces[3 + 3 * index : 6 + 3 * index]
            edge = level[channel].astype(jnp.float32)
            edge = edge + gate(a_on, corner_a, channel) + gate(b_on, corner_b, channel)
            if sides == 1:
                first = jnp.where(x_index == 1, edge, 0.0)
                last = jnp.where(x_index == 0, edge, 0.0)
            elif index == 0:
                last = jnp.where(x_index < x_count - 1, edge, 0.0)
            else:
                first = jnp.where(x_index > 0, edge, 0.0)
        zero = jnp.zeros((total.shape[0], tile_cols - 2 * half), jnp.float32)
        parts = [first, zero, last] if tile_cols > 2 * half else [first, last]
        total = total + jnp.concatenate(parts, axis=1)
        out_ref[channel] = total.astype(jnp.bfloat16)


def smem():
    return pl.BlockSpec(memory_space=pltpu.SMEM)


def vmem():
    return pl.BlockSpec(memory_space=pltpu.VMEM)


def on_device(object_field, probe, amplitudes, centers, live):
    side = probe.shape[2]
    half = side // 2
    _, tile_rows, tile_cols = object_field.shape
    slots = centers.shape[2]
    z_count = lax.axis_size("tx")
    x_count = lax.axis_size("ty")
    m_count = lax.axis_size("mode")
    if tile_rows != half or slots != 2 or m_count != 4 or x_count < 2:
        raise ValueError("unsupported sizes")
    sides = 1 if x_count == 2 else 2
    axes = ("tx", "ty", "mode")

    def zigzag(flip, x_step):
        def moved(z, m):
            down = (m % 2 == 0) != flip
            if down:
                return (z + 1, m) if z < z_count - 1 else (z, m ^ 1)
            return (z - 1, m) if z > 0 else (z, m ^ 1)

        pairs = []
        for z in range(z_count):
            for x in range(x_count):
                for m in range(m_count):
                    z_to, m_to = moved(z, m)
                    x_to = (x + x_step) % x_count
                    pairs.append(
                        (
                            (z * x_count + x) * m_count + m,
                            (z_to * x_count + x_to) * m_count + m_to,
                        )
                    )
        return pairs

    def level(step):
        return [(x, (x + step) % x_count) for x in range(x_count)]

    def exchange(array, flip):
        return lax.ppermute(array, "mode", [(m, m ^ flip) for m in range(m_count)])

    probe_low = probe.astype(jnp.bfloat16)
    probe_y = exchange(probe_low, 2)
    probe_core = exchange(probe_low, 1)
    packed_rows = 2 * tile_rows + record_rows
    packed = pl.pallas_call(
        functools.partial(pack_kernel, sides, slots),
        out_shape=[jax.ShapeDtypeStruct((packed_rows, tile_cols), jnp.bfloat16)]
        + [jax.ShapeDtypeStruct((packed_rows, half), jnp.bfloat16)] * sides,
        in_specs=[smem(), smem(), vmem()],
        out_specs=[vmem()] * (1 + sides),
        name="pack",
    )(centers, live, object_field)
    x_steps = [1] if sides == 1 else [1, -1]
    pieces = [packed[0]]
    pieces += [lax.ppermute(packed[0], axes, zigzag(flip, 0)) for flip in (False, True)]
    for step, edge in zip(x_steps, packed[1:]):
        pieces.append(lax.ppermute(edge, "ty", level(step)))
        pieces += [lax.ppermute(edge, axes, zigzag(flip, step)) for flip in (False, True)]
    probe_y, probe_core, *pieces = lax.optimization_barrier((probe_y, probe_core, *pieces))
    probe_diagonal = exchange(probe_y, 1)

    n_pieces = len(pieces)
    modes = probe.shape[1]
    ext_rows = tile_rows + side
    ext_cols = tile_cols + sides * half
    direct, swapped = (jnp.asarray(matrix) for matrix in dft_matrices(side))

    def waves(count):
        return [
            jax.ShapeDtypeStruct((count, side, 2 * side), jnp.float32),
            jax.ShapeDtypeStruct((count, 2 * side, side), jnp.bfloat16),
            jax.ShapeDtypeStruct((2, side, side), jnp.float32),
        ]

    patch, *near = pl.pallas_call(
        functools.partial(near_kernel, sides, z_count, x_count, tile_rows),
        out_shape=[jax.ShapeDtypeStruct((2, side, side), jnp.float32)] + waves(2 * modes),
        in_specs=[smem()] + [vmem()] * (n_pieces + 4),
        out_specs=[vmem()] * 4,
        scratch_shapes=[pltpu.VMEM((2 * ext_rows, ext_cols), jnp.bfloat16)],
        compiler_params=pltpu.CompilerParams(vmem_limit_bytes=vmem_bytes),
        name="near",
    )(centers, *pieces, probe_low, probe_core, direct, swapped)
    over = pl.pallas_call(
        far_kernel,
        out_shape=waves(modes),
        in_specs=[vmem()] * 4,
        out_specs=[vmem()] * 3,
        compiler_params=pltpu.CompilerParams(vmem_limit_bytes=vmem_bytes),
        name="over",
    )(patch, probe_y, direct, swapped)
    shapes = [(2, tile_rows, tile_cols)] + [(2, half, tile_cols)] * 2
    shapes += ([(2, tile_rows, half)] + [(2, half, half)] * 2) * sides
    results = pl.pallas_call(
        functools.partial(back_kernel, sides, x_count, tile_rows, tile_cols),
        out_shape=[jax.ShapeDtypeStruct(shape, jnp.bfloat16) for shape in shapes]
        + [jax.ShapeDtypeStruct((side, side), jnp.bfloat16)],
        in_specs=[smem(), smem()] + [vmem()] * 14,
        out_specs=[vmem()] * (n_pieces + 1),
        scratch_shapes=[
            pltpu.VMEM((modes, side, 2 * side), jnp.float32),
            pltpu.VMEM((modes, 2 * side, side), jnp.bfloat16),
            pltpu.VMEM((ext_rows, ext_cols), jnp.bfloat16),
        ],
        compiler_params=pltpu.CompilerParams(vmem_limit_bytes=vmem_bytes),
        name="back",
    )(
        centers,
        live,
        amplitudes,
        patch,
        probe_low,
        probe_core,
        probe_y,
        probe_diagonal,
        direct,
        swapped,
        *near,
        *over,
    )
    weight = pl.pallas_call(
        functools.partial(weight_kernel, sides, slots, z_count, x_count),
        out_shape=jax.ShapeDtypeStruct((tile_rows, tile_cols), jnp.float32),
        in_specs=[vmem()] * (n_pieces + 1),
        out_specs=vmem(),
        name="weights",
    )(results[-1], *pieces)
    received = [results[0]]
    received += [
        lax.ppermute(results[1 + index], axes, zigzag(flip, 0))
        for index, flip in enumerate((False, True))
    ]
    for index, step in enumerate(x_steps):
        back_step = -step
        received.append(lax.ppermute(results[3 + 3 * index], "ty", level(back_step)))
        received += [
            lax.ppermute(results[4 + 3 * index + turn], axes, zigzag(flip, back_step))
            for turn, flip in enumerate((False, True))
        ]
    summed = pl.pallas_call(
        functools.partial(sum_kernel, sides, z_count, x_count),
        out_shape=jax.ShapeDtypeStruct(object_field.shape, jnp.bfloat16),
        in_specs=[vmem()] * n_pieces,
        out_specs=vmem(),
        name="sums",
    )(*received)
    other = exchange(summed, 1)
    gradient = summed.astype(jnp.float32) + other.astype(jnp.float32)
    return object_field + gradient / (weight + regularizer)


def solution(mesh):
    return jax.shard_map(
        on_device,
        mesh=mesh,
        in_specs=(
            P(None, "tx", "ty"),
            P(None, "mode", None, None),
            P("tx", "ty", None, None, None),
            P("tx", "ty", None, None),
            P("tx", "ty"),
        ),
        out_specs=P(None, "tx", "ty"),
        check_vma=False,
    )
```

```python
import functools
import math

import jax
import jax.numpy as jnp
import numpy as np
from jax import lax
from jax.experimental import pallas as pl
from jax.experimental.pallas import tpu as pltpu
from jax.sharding import PartitionSpec as P

power_floor = 0.01
regularizer = 0.1
nowhere = -(1 << 20)
record_rows = 16
wave_bytes = 32 * 1024 * 1024
small_bytes = 8 * 1024 * 1024


def dft_matrices(side):
    line = np.arange(side, dtype=np.int32)
    angle = (line[:, None] * line[None, :] % side).astype(np.float32) * np.float32(
        2.0 * math.pi / side
    )
    scaling = np.float32(1.0 / math.sqrt(side))
    real = (np.cos(angle) * scaling).astype(jnp.bfloat16)
    imag = (-np.sin(angle) * scaling).astype(jnp.bfloat16)
    direct = np.block([[real, -imag], [imag, real]])
    swapped = np.block([[real, imag], [-imag, real]])
    return direct, swapped


def dot(left, right):
    return jnp.dot(left, right, preferred_element_type=jnp.float32)


def iota(shape, dim):
    return lax.broadcasted_iota(jnp.int32, shape, dim)


def column_coordinate(at, tile_cols, half, sides, x_index, x_count):
    own = at + half
    if sides == 1:
        side = at - tile_cols + jnp.where(x_index == 0, half + tile_cols, 0)
        return jnp.where(at < tile_cols, own, side)
    left = jnp.where(x_index > 0, at - tile_cols, nowhere)
    right = jnp.where(x_index < x_count - 1, at, nowhere)
    return jnp.where(at < tile_cols, own, jnp.where(at < tile_cols + half, left, right))


def wide(tall):
    side = tall.shape[0] // 2
    return jnp.concatenate([tall[:side], tall[side:]], axis=1)


def tall(wide):
    side = wide.shape[1] // 2
    return jnp.concatenate([wide[:, :side], wide[:, side:]], axis=0)


def here():
    return (lax.axis_index("tx"), lax.axis_index("ty"), lax.axis_index("mode") % 2)


def pack_kernel(sides, slots, centers_ref, live_ref, object_ref, *outs):
    _, tile_rows, tile_cols = object_ref.shape
    half = outs[1].shape[1]
    _, x_index, _ = here()
    record = jnp.zeros((record_rows, tile_cols), jnp.float32)
    line = iota((record_rows, tile_cols), 0)
    for slot in range(slots):
        for axis in range(2):
            value = centers_ref[0, 0, slot, axis].astype(jnp.float32)
            record = jnp.where(line == 2 * slot + axis, value, record)
    record = jnp.where(line == 2 * slots, live_ref[0, 0].astype(jnp.float32), record)
    record = record.astype(jnp.bfloat16)
    first, last = slice(0, half), slice(tile_cols - half, tile_cols)
    for channel in range(2):
        rows = slice(channel * tile_rows, (channel + 1) * tile_rows)
        values = object_ref[channel].astype(jnp.bfloat16)
        outs[0][rows] = values
        if sides == 1:
            outs[1][rows] = jnp.where(x_index == 0, values[:, last], values[:, first])
        else:
            outs[1][rows] = values[:, last]
            outs[2][rows] = values[:, first]
    rows = slice(2 * tile_rows, 2 * tile_rows + record_rows)
    outs[0][rows] = record
    for out in outs[1:]:
        out[rows] = record[:, :half]


def row_starts(half, tile_rows, parity):
    low, high = 0, half + tile_rows
    return (
        pl.multiple_of(jnp.where(parity == 0, low, high), half),
        pl.multiple_of(jnp.where(parity == 0, high, low), half),
    )


def patch_of(sides, z_count, x_count, tile_rows, side, centers_ref, pieces, ext_ref):
    z_index, x_index, parity = here()
    row_at = centers_ref[0, 0, parity, 0]
    col_at = centers_ref[0, 0, parity, 1]
    half = side // 2
    tile_cols = pieces[0].shape[1]
    ext_rows = tile_rows + side
    ext_cols = tile_cols + sides * half
    a_at, b_at = row_starts(half, tile_rows, parity)
    for channel in range(2):
        base = channel * ext_rows
        rows = slice(channel * tile_rows, (channel + 1) * tile_rows)
        for index in range(1 + sides):
            columns = (
                slice(0, tile_cols)
                if index == 0
                else slice(tile_cols + (index - 1) * half, tile_cols + index * half)
            )
            level, turn_a, turn_b = pieces[3 * index : 3 * index + 3]
            ext_ref[pl.ds(base + half, tile_rows), columns] = level[rows]
            ext_ref[pl.ds(base + a_at, half), columns] = turn_a[rows]
            ext_ref[pl.ds(base + b_at, half), columns] = turn_b[rows]
    at = iota((ext_cols, side), 0)
    column = column_coordinate(at, tile_cols, half, sides, x_index, x_count)
    pick_cols = (column == iota((ext_cols, side), 1) + col_at).astype(jnp.bfloat16)
    at = iota((side, ext_rows), 1)
    first = jnp.where(z_index > 0, 0, half)
    last = jnp.where(z_index < z_count - 1, ext_rows, half + tile_rows)
    row = jnp.where((at >= first) & (at < last), at, nowhere)
    pick_rows = (row == iota((side, ext_rows), 0) + row_at).astype(jnp.bfloat16)
    narrow = dot(ext_ref[...], pick_cols).astype(jnp.bfloat16)
    return dot(pick_rows, narrow[:ext_rows]), dot(pick_rows, narrow[ext_rows:])


def forward(groups, patch, direct, swapped, far_ref, exit_ref, at):
    patch_real, patch_imag = patch
    side = patch_real.shape[0]
    sums = []
    for group in groups:
        modes = group.shape[1]
        power = jnp.zeros((side, side), jnp.float32)
        weight = jnp.zeros((side, side), jnp.float32)
        halves = []
        for k in range(modes):
            real = group[0, k].astype(jnp.float32)
            imag = group[1, k].astype(jnp.float32)
            exit_wave = jnp.concatenate(
                [
                    (real * patch_real - imag * patch_imag).astype(jnp.bfloat16),
                    (real * patch_imag + imag * patch_real).astype(jnp.bfloat16),
                ],
                axis=0,
            )
            exit_ref[at + k] = exit_wave
            halves.append(wide(dot(direct, exit_wave).astype(jnp.bfloat16)))
            weight = weight + (real * real + imag * imag)
        far_both = dot(jnp.concatenate(halves, axis=0), swapped)
        for k in range(modes):
            far = far_both[k * side : (k + 1) * side]
            far_ref[at + k] = far
            power = power + (far[:, :side] * far[:, :side] + far[:, side:] * far[:, side:])
        sums.append((power, weight))
        at += modes
    return sums


def backward(groups, factor, direct, swapped, far_ref, exit_ref):
    side = factor.shape[0]
    grads = []
    at = 0
    for group in groups:
        modes = group.shape[1]
        grad_real = jnp.zeros((side, side), jnp.float32)
        grad_imag = jnp.zeros((side, side), jnp.float32)
        halves = []
        for k in range(modes):
            fixed = (far_ref[at + k] * factor).astype(jnp.bfloat16)
            halves.append(wide(dot(swapped, tall(fixed)).astype(jnp.bfloat16)))
        back_both = dot(jnp.concatenate(halves, axis=0), direct)
        for k in range(modes):
            back = back_both[k * side : (k + 1) * side]
            exit_wave = exit_ref[at + k].astype(jnp.float32)
            real = group[0, k].astype(jnp.float32)
            imag = group[1, k].astype(jnp.float32)
            diff_real = back[:, :side] - exit_wave[:side]
            diff_imag = back[:, side:] - exit_wave[side:]
            grad_real = grad_real + (real * diff_real + imag * diff_imag)
            grad_imag = grad_imag + (real * diff_imag - imag * diff_real)
        grads.append((grad_real, grad_imag))
        at += modes
    return grads


def near_kernel(sides, z_count, x_count, tile_rows, centers_ref, *refs):
    n_pieces = 3 + 3 * sides
    pieces = refs[:n_pieces]
    own, core, direct, swapped = refs[n_pieces : n_pieces + 4]
    patch_ref, far_ref, exit_ref, sum_ref, ext_ref = refs[n_pieces + 4 :]
    side = own.shape[2]
    patch = patch_of(sides, z_count, x_count, tile_rows, side, centers_ref, pieces, ext_ref)
    patch_ref[0], patch_ref[1] = patch
    sums = forward((own, core), patch, direct[...], swapped[...], far_ref, exit_ref, 0)
    sum_ref[0] = sums[0][0] + sums[1][0]
    sum_ref[1] = sums[0][1] + sums[1][1]


def far_kernel(patch_ref, group, direct, swapped, far_ref, exit_ref, sum_ref):
    patch = (patch_ref[0], patch_ref[1])
    ((power, weight),) = forward((group,), patch, direct[...], swapped[...], far_ref, exit_ref, 0)
    sum_ref[0] = power
    sum_ref[1] = weight


def back_kernel(sides, x_count, tile_rows, tile_cols, centers_ref, live_ref, *refs):
    n_pieces = 3 + 3 * sides
    amplitude_ref, patch_ref, own, core, over, last, direct_ref, swapped_ref = refs[:8]
    near_far, near_exit, near_sum, over_far, over_exit, over_sum = refs[8:14]
    outs = refs[14 : 14 + n_pieces + 1]
    last_far, last_exit, grad_ref = refs[14 + n_pieces + 1 :]
    side = own.shape[2]
    half = side // 2
    modes = own.shape[1]
    ext_rows = tile_rows + side
    ext_cols = tile_cols + sides * half
    _, x_index, parity = here()
    row_at = centers_ref[0, 0, parity, 0]
    col_at = centers_ref[0, 0, parity, 1]
    is_live = parity < live_ref[0, 0]
    direct = direct_ref[...]
    swapped = swapped_ref[...]
    patch = (patch_ref[0], patch_ref[1])
    ((power, weight),) = forward((last,), patch, direct, swapped, last_far, last_exit, 0)
    power = near_sum[0] + (over_sum[0] + power)
    weight = near_sum[1] + (over_sum[1] + weight)
    outs[-1][...] = weight.astype(jnp.bfloat16)
    amplitude = amplitude_ref[0, 0, parity].astype(jnp.float32)
    factor = amplitude / jnp.sqrt(power + power_floor)
    factor = jnp.concatenate([factor, factor], axis=1)
    near = backward((own, core), factor, direct, swapped, near_far, near_exit)
    (beyond,) = backward((over,), factor, direct, swapped, over_far, over_exit)
    (final,) = backward((last,), factor, direct, swapped, last_far, last_exit)
    at = iota((side, ext_cols), 1)
    column = column_coordinate(at, tile_cols, half, sides, x_index, x_count)
    put_cols = ((column == iota((side, ext_cols), 0) + col_at) & is_live).astype(jnp.bfloat16)
    put_rows = (iota((ext_rows, side), 0) == iota((ext_rows, side), 1) + row_at).astype(
        jnp.bfloat16
    )
    a_at, b_at = row_starts(half, tile_rows, parity)
    for channel in range(2):
        gradient = (near[0][channel] + near[1][channel]) + (beyond[channel] + final[channel])
        placed = dot(put_rows, gradient.astype(jnp.bfloat16)).astype(jnp.bfloat16)
        grad_ref[...] = dot(placed, put_cols).astype(jnp.bfloat16)
        for index in range(1 + sides):
            columns = (
                slice(0, tile_cols)
                if index == 0
                else slice(tile_cols + (index - 1) * half, tile_cols + index * half)
            )
            outs[3 * index][channel] = grad_ref[half : half + tile_rows, columns]
            outs[3 * index + 1][channel] = grad_ref[pl.ds(b_at, half), columns]
            outs[3 * index + 2][channel] = grad_ref[pl.ds(a_at, half), columns]


def weight_kernel(sides, slots, z_count, x_count, weight_ref, *refs):
    pieces, out_ref = refs[:-1], refs[-1]
    tile_rows, tile_cols = out_ref.shape
    side = weight_ref.shape[0]
    half = side // 2
    z_index, x_index, parity = here()
    z_step_a = jnp.where(parity == 0, -1, 1)
    if sides == 1:
        x_steps = [0, jnp.where(x_index == 0, 1, -1)]
        x_shown = [True, True]
    else:
        x_steps = [0, -1, 1]
        x_shown = [True, x_index > 0, x_index < x_count - 1]
    weight = weight_ref[...]
    total = jnp.zeros((tile_rows, tile_cols), jnp.float32)
    for index, x_step in enumerate(x_steps):
        turns = []
        for turn, z_step in enumerate((0, z_step_a, -z_step_a)):
            part = jnp.zeros((tile_rows, tile_cols), jnp.float32)
            z_tile = z_index + z_step
            shown = (z_tile >= 0) & (z_tile < z_count) & x_shown[index]
            record = pieces[3 * index + turn][2 * tile_rows :].astype(jnp.float32)
            record = record.astype(jnp.int32)
            if record.shape[1] < side:
                record = jnp.concatenate([record] * (side // record.shape[1]), axis=1)
            count = record[2 * slots : 2 * slots + 1, :side]
            for slot in range(slots):
                row = record[2 * slot : 2 * slot + 1, :side] + (z_step * tile_rows - half)
                col = record[2 * slot + 1 : 2 * slot + 2, :side] + (x_step * tile_cols - half)
                row = jnp.where((count > slot) & shown, row, nowhere)
                put_rows = (
                    iota((tile_rows, side), 0) == iota((tile_rows, side), 1) + row
                ).astype(jnp.bfloat16)
                put_cols = (
                    iota((side, tile_cols), 1) == iota((side, tile_cols), 0) + col[:, :1]
                ).astype(jnp.bfloat16)
                placed = dot(put_rows, weight).astype(jnp.bfloat16)
                part = part + dot(placed, put_cols)
            turns.append(part)
        total = total + (turns[0] + (turns[1] + turns[2]))
    out_ref[...] = total + regularizer


def sum_kernel(sides, z_count, x_count, *refs):
    pieces, out_ref = refs[:-1], refs[-1]
    own_ref, rows_a, rows_b = pieces[:3]
    tile_cols = own_ref.shape[2]
    half = pieces[3].shape[2]
    z_index, x_index, parity = here()
    below = z_index > 0
    above = z_index < z_count - 1
    a_on = jnp.where(parity == 0, below, above)
    b_on = jnp.where(parity == 0, above, below)

    def gate(on, ref, channel):
        return jnp.where(on, ref[channel].astype(jnp.float32), 0.0)

    for channel in range(2):
        total = own_ref[channel].astype(jnp.float32)
        total = total + gate(a_on, rows_a, channel) + gate(b_on, rows_b, channel)
        first = jnp.zeros((total.shape[0], half), jnp.float32)
        last = first
        for index in range(sides):
            level, corner_a, corner_b = pieces[3 + 3 * index : 6 + 3 * index]
            edge = level[channel].astype(jnp.float32)
            edge = edge + gate(a_on, corner_a, channel) + gate(b_on, corner_b, channel)
            if sides == 1:
                first = jnp.where(x_index == 1, edge, 0.0)
                last = jnp.where(x_index == 0, edge, 0.0)
            elif index == 0:
                last = jnp.where(x_index < x_count - 1, edge, 0.0)
            else:
                first = jnp.where(x_index > 0, edge, 0.0)
        zero = jnp.zeros((total.shape[0], tile_cols - 2 * half), jnp.float32)
        parts = [first, zero, last] if tile_cols > 2 * half else [first, last]
        total = total + jnp.concatenate(parts, axis=1)
        out_ref[channel] = total.astype(jnp.bfloat16)


def update_kernel(object_ref, own_ref, other_ref, weight_ref, out_ref):
    for channel in range(2):
        gradient = own_ref[channel].astype(jnp.float32) + other_ref[channel].astype(jnp.float32)
        out_ref[channel] = object_ref[channel] + gradient / weight_ref[...]


def smem():
    return pl.BlockSpec(memory_space=pltpu.SMEM)


def vmem():
    return pl.BlockSpec(memory_space=pltpu.VMEM)


def on_device(object_field, probe, amplitudes, centers, live):
    side = probe.shape[2]
    half = side // 2
    _, tile_rows, tile_cols = object_field.shape
    slots = centers.shape[2]
    z_count = lax.axis_size("tx")
    x_count = lax.axis_size("ty")
    m_count = lax.axis_size("mode")
    if tile_rows != half or slots != 2 or m_count != 4 or x_count < 2:
        raise ValueError("unsupported sizes")
    sides = 1 if x_count == 2 else 2
    axes = ("tx", "ty", "mode")

    def zigzag(flip, x_step):
        def moved(z, m):
            down = (m % 2 == 0) != flip
            if down:
                return (z + 1, m) if z < z_count - 1 else (z, m ^ 1)
            return (z - 1, m) if z > 0 else (z, m ^ 1)

        pairs = []
        for z in range(z_count):
            for x in range(x_count):
                for m in range(m_count):
                    z_to, m_to = moved(z, m)
                    x_to = (x + x_step) % x_count
                    pairs.append(
                        (
                            (z * x_count + x) * m_count + m,
                            (z_to * x_count + x_to) * m_count + m_to,
                        )
                    )
        return pairs

    def level(step):
        return [(x, (x + step) % x_count) for x in range(x_count)]

    def exchange(array, flip):
        return lax.ppermute(array, "mode", [(m, m ^ flip) for m in range(m_count)])

    probe_low = probe.astype(jnp.bfloat16)
    probe_y = exchange(probe_low, 2)
    probe_core = exchange(probe_low, 1)
    packed_rows = 2 * tile_rows + record_rows
    packed = pl.pallas_call(
        functools.partial(pack_kernel, sides, slots),
        out_shape=[jax.ShapeDtypeStruct((packed_rows, tile_cols), jnp.bfloat16)]
        + [jax.ShapeDtypeStruct((packed_rows, half), jnp.bfloat16)] * sides,
        in_specs=[smem(), smem(), vmem()],
        out_specs=[vmem()] * (1 + sides),
        compiler_params=pltpu.CompilerParams(vmem_limit_bytes=small_bytes),
        name="pack",
    )(centers, live, object_field)
    probe_core, *packed = lax.optimization_barrier((probe_core, *packed))
    x_steps = [1] if sides == 1 else [1, -1]
    pieces = [packed[0]]
    pieces += [lax.ppermute(packed[0], axes, zigzag(flip, 0)) for flip in (False, True)]
    for step, edge in zip(x_steps, packed[1:]):
        pieces.append(lax.ppermute(edge, "ty", level(step)))
        pieces += [lax.ppermute(edge, axes, zigzag(flip, step)) for flip in (False, True)]

    n_pieces = len(pieces)
    modes = probe.shape[1]
    ext_rows = tile_rows + side
    ext_cols = tile_cols + sides * half
    direct, swapped = (jnp.asarray(matrix) for matrix in dft_matrices(side))

    def waves(count):
        return [
            jax.ShapeDtypeStruct((count, side, 2 * side), jnp.float32),
            jax.ShapeDtypeStruct((count, 2 * side, side), jnp.bfloat16),
            jax.ShapeDtypeStruct((2, side, side), jnp.float32),
        ]

    patch, *near = pl.pallas_call(
        functools.partial(near_kernel, sides, z_count, x_count, tile_rows),
        out_shape=[jax.ShapeDtypeStruct((2, side, side), jnp.float32)] + waves(2 * modes),
        in_specs=[smem()] + [vmem()] * (n_pieces + 4),
        out_specs=[vmem()] * 4,
        scratch_shapes=[pltpu.VMEM((2 * ext_rows, ext_cols), jnp.bfloat16)],
        compiler_params=pltpu.CompilerParams(vmem_limit_bytes=wave_bytes),
        name="near",
    )(centers, *pieces, probe_low, probe_core, direct, swapped)
    probe_y, patch = lax.optimization_barrier((probe_y, patch))
    probe_diagonal = exchange(probe_y, 1)
    over = pl.pallas_call(
        far_kernel,
        out_shape=waves(modes),
        in_specs=[vmem()] * 4,
        out_specs=[vmem()] * 3,
        compiler_params=pltpu.CompilerParams(vmem_limit_bytes=wave_bytes),
        name="over",
    )(patch, probe_y, direct, swapped)
    shapes = [(2, tile_rows, tile_cols)] + [(2, half, tile_cols)] * 2
    shapes += ([(2, tile_rows, half)] + [(2, half, half)] * 2) * sides
    results = pl.pallas_call(
        functools.partial(back_kernel, sides, x_count, tile_rows, tile_cols),
        out_shape=[jax.ShapeDtypeStruct(shape, jnp.bfloat16) for shape in shapes]
        + [jax.ShapeDtypeStruct((side, side), jnp.bfloat16)],
        in_specs=[smem(), smem()] + [vmem()] * 14,
        out_specs=[vmem()] * (n_pieces + 1),
        scratch_shapes=[
            pltpu.VMEM((modes, side, 2 * side), jnp.float32),
            pltpu.VMEM((modes, 2 * side, side), jnp.bfloat16),
            pltpu.VMEM((ext_rows, ext_cols), jnp.bfloat16),
        ],
        compiler_params=pltpu.CompilerParams(vmem_limit_bytes=wave_bytes),
        name="back",
    )(
        centers,
        live,
        amplitudes,
        patch,
        probe_low,
        probe_core,
        probe_y,
        probe_diagonal,
        direct,
        swapped,
        *near,
        *over,
    )
    weight = pl.pallas_call(
        functools.partial(weight_kernel, sides, slots, z_count, x_count),
        out_shape=jax.ShapeDtypeStruct((tile_rows, tile_cols), jnp.float32),
        in_specs=[vmem()] * (n_pieces + 1),
        out_specs=vmem(),
        compiler_params=pltpu.CompilerParams(vmem_limit_bytes=small_bytes),
        name="weights",
    )(results[-1], *pieces)
    received = [results[0]]
    received += [
        lax.ppermute(results[1 + index], axes, zigzag(flip, 0))
        for index, flip in enumerate((False, True))
    ]
    for index, step in enumerate(x_steps):
        back_step = -step
        received.append(lax.ppermute(results[3 + 3 * index], "ty", level(back_step)))
        received += [
            lax.ppermute(results[4 + 3 * index + turn], axes, zigzag(flip, back_step))
            for turn, flip in enumerate((False, True))
        ]
    weight, *received = lax.optimization_barrier((weight, *received))
    summed = pl.pallas_call(
        functools.partial(sum_kernel, sides, z_count, x_count),
        out_shape=jax.ShapeDtypeStruct(object_field.shape, jnp.bfloat16),
        in_specs=[vmem()] * n_pieces,
        out_specs=vmem(),
        compiler_params=pltpu.CompilerParams(vmem_limit_bytes=small_bytes),
        name="sums",
    )(*received)
    other = exchange(summed, 1)
    return pl.pallas_call(
        update_kernel,
        out_shape=jax.ShapeDtypeStruct(object_field.shape, jnp.float32),
        in_specs=[vmem()] * 4,
        out_specs=vmem(),
        compiler_params=pltpu.CompilerParams(vmem_limit_bytes=small_bytes),
        name="update",
    )(object_field, summed, other, weight)


def solution(mesh):
    return jax.shard_map(
        on_device,
        mesh=mesh,
        in_specs=(
            P(None, "tx", "ty"),
            P(None, "mode", None, None),
            P("tx", "ty", None, None, None),
            P("tx", "ty", None, None),
            P("tx", "ty"),
        ),
        out_specs=P(None, "tx", "ty"),
        check_vma=False,
    )
```

```python
import functools
import math

import jax
import jax.numpy as jnp
import numpy as np
from jax import lax
from jax.experimental import pallas as pl
from jax.experimental.pallas import tpu as pltpu
from jax.sharding import PartitionSpec as P

power_floor = 0.01
regularizer = 0.1
nowhere = -(1 << 20)
record_rows = 16
wave_bytes = 32 * 1024 * 1024
small_bytes = 8 * 1024 * 1024


def dft_matrices(side):
    line = np.arange(side, dtype=np.int32)
    angle = (line[:, None] * line[None, :] % side).astype(np.float32) * np.float32(
        2.0 * math.pi / side
    )
    scaling = np.float32(1.0 / math.sqrt(side))
    real = (np.cos(angle) * scaling).astype(jnp.bfloat16)
    imag = (-np.sin(angle) * scaling).astype(jnp.bfloat16)
    direct = np.block([[real, -imag], [imag, real]])
    swapped = np.block([[real, imag], [-imag, real]])
    return direct, swapped


def dot(left, right):
    return jnp.dot(left, right, preferred_element_type=jnp.float32)


def iota(shape, dim):
    return lax.broadcasted_iota(jnp.int32, shape, dim)


def column_coordinate(at, tile_cols, half, sides, x_index, x_count):
    own = at + half
    if sides == 1:
        side = at - tile_cols + jnp.where(x_index == 0, half + tile_cols, 0)
        return jnp.where(at < tile_cols, own, side)
    left = jnp.where(x_index > 0, at - tile_cols, nowhere)
    right = jnp.where(x_index < x_count - 1, at, nowhere)
    return jnp.where(at < tile_cols, own, jnp.where(at < tile_cols + half, left, right))


def wide(tall):
    side = tall.shape[0] // 2
    return jnp.concatenate([tall[:side], tall[side:]], axis=1)


def tall(wide):
    side = wide.shape[1] // 2
    return jnp.concatenate([wide[:, :side], wide[:, side:]], axis=0)


def here():
    return (lax.axis_index("tx"), lax.axis_index("ty"), lax.axis_index("mode") % 2)


def start_kernel(sides, object_hbm, probe_hbm, low_ref, packed_ref, *rest):
    edges = rest[:sides]
    object_ref, probe_ref, sems = rest[sides:]
    copies = [
        pltpu.make_async_copy(source, target, sems.at[index])
        for index, (source, target) in enumerate(
            ((probe_hbm, probe_ref), (object_hbm, object_ref))
        )
    ]
    for copy in copies:
        copy.start()
    tile_cols = object_ref.shape[2]
    half = edges[0].shape[2]
    _, x_index, _ = here()
    copies[0].wait()
    low_ref[...] = probe_ref[...].astype(jnp.bfloat16)
    copies[1].wait()
    first, last = slice(0, half), slice(tile_cols - half, tile_cols)
    for channel in range(2):
        values = object_ref[channel].astype(jnp.bfloat16)
        packed_ref[channel] = values
        if sides == 1:
            edges[0][channel] = jnp.where(x_index == 0, values[:, last], values[:, first])
        else:
            edges[0][channel] = values[:, last]
            edges[1][channel] = values[:, first]


def record_kernel(slots, centers_ref, live_ref, out_ref):
    record = jnp.zeros(out_ref.shape, jnp.float32)
    line = iota(out_ref.shape, 0)
    for slot in range(slots):
        for axis in range(2):
            value = centers_ref[0, 0, slot, axis].astype(jnp.float32)
            record = jnp.where(line == 2 * slot + axis, value, record)
    record = jnp.where(line == 2 * slots, live_ref[0, 0].astype(jnp.float32), record)
    out_ref[...] = record.astype(jnp.bfloat16)


def positions(record_ref, slots):
    _, _, parity = here()
    record = record_ref[:, :128].astype(jnp.float32).astype(jnp.int32)[:, :1]

    def of_slot(axis):
        value = record[axis : axis + 1]
        for slot in range(1, slots):
            value = jnp.where(parity == slot, record[2 * slot + axis : 2 * slot + axis + 1], value)
        return value

    return of_slot(0), of_slot(1), record[2 * slots : 2 * slots + 1] > parity


def row_starts(half, tile_rows, parity):
    low, high = 0, half + tile_rows
    return (
        pl.multiple_of(jnp.where(parity == 0, low, high), half),
        pl.multiple_of(jnp.where(parity == 0, high, low), half),
    )


def patch_of(sides, slots, z_count, x_count, side, record_ref, pieces, ext_ref):
    z_index, x_index, parity = here()
    row_at, col_at, _ = positions(record_ref, slots)
    half = side // 2
    _, tile_rows, tile_cols = pieces[0].shape
    ext_rows = tile_rows + side
    ext_cols = tile_cols + sides * half
    a_at, b_at = row_starts(half, tile_rows, parity)
    for channel in range(2):
        base = channel * ext_rows
        for index in range(1 + sides):
            columns = (
                slice(0, tile_cols)
                if index == 0
                else slice(tile_cols + (index - 1) * half, tile_cols + index * half)
            )
            level, turn_a, turn_b = pieces[3 * index : 3 * index + 3]
            ext_ref[pl.ds(base + half, tile_rows), columns] = level[channel]
            ext_ref[pl.ds(base + a_at, half), columns] = turn_a[channel]
            ext_ref[pl.ds(base + b_at, half), columns] = turn_b[channel]
    at = iota((ext_cols, side), 0)
    column = column_coordinate(at, tile_cols, half, sides, x_index, x_count)
    pick_cols = (column == iota((ext_cols, side), 1) + col_at).astype(jnp.bfloat16)
    at = iota((side, ext_rows), 1)
    first = jnp.where(z_index > 0, 0, half)
    last = jnp.where(z_index < z_count - 1, ext_rows, half + tile_rows)
    row = jnp.where((at >= first) & (at < last), at, nowhere)
    pick_rows = (row == iota((side, ext_rows), 0) + row_at).astype(jnp.bfloat16)
    narrow = dot(ext_ref[...], pick_cols).astype(jnp.bfloat16)
    return dot(pick_rows, narrow[:ext_rows]), dot(pick_rows, narrow[ext_rows:])


def forward(groups, patch, direct, swapped, far_ref, exit_ref, at):
    patch_real, patch_imag = patch
    side = patch_real.shape[0]
    sums = []
    for group in groups:
        modes = group.shape[1]
        power = jnp.zeros((side, side), jnp.float32)
        weight = jnp.zeros((side, side), jnp.float32)
        halves = []
        for k in range(modes):
            real = group[0, k].astype(jnp.float32)
            imag = group[1, k].astype(jnp.float32)
            exit_wave = jnp.concatenate(
                [
                    (real * patch_real - imag * patch_imag).astype(jnp.bfloat16),
                    (real * patch_imag + imag * patch_real).astype(jnp.bfloat16),
                ],
                axis=0,
            )
            exit_ref[at + k] = exit_wave
            halves.append(wide(dot(direct, exit_wave).astype(jnp.bfloat16)))
            weight = weight + (real * real + imag * imag)
        far_both = dot(jnp.concatenate(halves, axis=0), swapped)
        for k in range(modes):
            far = far_both[k * side : (k + 1) * side]
            far_ref[at + k] = far
            power = power + (far[:, :side] * far[:, :side] + far[:, side:] * far[:, side:])
        sums.append((power, weight))
        at += modes
    return sums


def backward(groups, factor, direct, swapped, far_ref, exit_ref):
    side = factor.shape[0]
    grads = []
    at = 0
    for group in groups:
        modes = group.shape[1]
        grad_real = jnp.zeros((side, side), jnp.float32)
        grad_imag = jnp.zeros((side, side), jnp.float32)
        halves = []
        for k in range(modes):
            fixed = (far_ref[at + k] * factor).astype(jnp.bfloat16)
            halves.append(wide(dot(swapped, tall(fixed)).astype(jnp.bfloat16)))
        back_both = dot(jnp.concatenate(halves, axis=0), direct)
        for k in range(modes):
            back = back_both[k * side : (k + 1) * side]
            exit_wave = exit_ref[at + k].astype(jnp.float32)
            real = group[0, k].astype(jnp.float32)
            imag = group[1, k].astype(jnp.float32)
            diff_real = back[:, :side] - exit_wave[:side]
            diff_imag = back[:, side:] - exit_wave[side:]
            grad_real = grad_real + (real * diff_real + imag * diff_imag)
            grad_imag = grad_imag + (real * diff_imag - imag * diff_real)
        grads.append((grad_real, grad_imag))
        at += modes
    return grads


def near_kernel(sides, slots, z_count, x_count, record_ref, *refs):
    n_pieces = 3 + 3 * sides
    pieces = refs[:n_pieces]
    own, core, direct, swapped = refs[n_pieces : n_pieces + 4]
    patch_ref, far_ref, exit_ref, sum_ref, ext_ref = refs[n_pieces + 4 :]
    side = own.shape[2]
    patch = patch_of(sides, slots, z_count, x_count, side, record_ref, pieces, ext_ref)
    patch_ref[0], patch_ref[1] = patch
    sums = forward((own, core), patch, direct[...], swapped[...], far_ref, exit_ref, 0)
    sum_ref[0] = sums[0][0] + sums[1][0]
    sum_ref[1] = sums[0][1] + sums[1][1]


def far_kernel(patch_ref, group, direct, swapped, far_ref, exit_ref, sum_ref):
    patch = (patch_ref[0], patch_ref[1])
    ((power, weight),) = forward((group,), patch, direct[...], swapped[...], far_ref, exit_ref, 0)
    sum_ref[0] = power
    sum_ref[1] = weight


def back_kernel(sides, slots, x_count, tile_rows, tile_cols, record_ref, *refs):
    n_pieces = 3 + 3 * sides
    amplitude_ref, patch_ref, own, core, over, last, direct_ref, swapped_ref = refs[:8]
    near_far, near_exit, near_sum, over_far, over_exit, over_sum = refs[8:14]
    outs = refs[14 : 14 + n_pieces + 1]
    last_far, last_exit, grad_ref = refs[14 + n_pieces + 1 :]
    side = own.shape[2]
    half = side // 2
    modes = own.shape[1]
    ext_rows = tile_rows + side
    ext_cols = tile_cols + sides * half
    _, x_index, parity = here()
    row_at, col_at, is_live = positions(record_ref, slots)
    direct = direct_ref[...]
    swapped = swapped_ref[...]
    patch = (patch_ref[0], patch_ref[1])
    ((power, weight),) = forward((last,), patch, direct, swapped, last_far, last_exit, 0)
    power = near_sum[0] + (over_sum[0] + power)
    weight = near_sum[1] + (over_sum[1] + weight)
    outs[-1][...] = weight.astype(jnp.bfloat16)
    amplitude = amplitude_ref[0, 0, parity].astype(jnp.float32)
    factor = amplitude / jnp.sqrt(power + power_floor)
    factor = jnp.concatenate([factor, factor], axis=1)
    near = backward((own, core), factor, direct, swapped, near_far, near_exit)
    (beyond,) = backward((over,), factor, direct, swapped, over_far, over_exit)
    (final,) = backward((last,), factor, direct, swapped, last_far, last_exit)
    at = iota((side, ext_cols), 1)
    column = column_coordinate(at, tile_cols, half, sides, x_index, x_count)
    put_cols = ((column == iota((side, ext_cols), 0) + col_at) & is_live).astype(jnp.bfloat16)
    put_rows = (iota((ext_rows, side), 0) == iota((ext_rows, side), 1) + row_at).astype(
        jnp.bfloat16
    )
    a_at, b_at = row_starts(half, tile_rows, parity)
    for channel in range(2):
        gradient = (near[0][channel] + near[1][channel]) + (beyond[channel] + final[channel])
        placed = dot(put_rows, gradient.astype(jnp.bfloat16)).astype(jnp.bfloat16)
        grad_ref[...] = dot(placed, put_cols).astype(jnp.bfloat16)
        rows = slice(channel * half, (channel + 1) * half)
        for index in range(1 + sides):
            columns = (
                slice(0, tile_cols)
                if index == 0
                else slice(tile_cols + (index - 1) * half, tile_cols + index * half)
            )
            outs[3 * index][rows] = grad_ref[half : half + tile_rows, columns]
            outs[3 * index + 1][rows] = grad_ref[pl.ds(b_at, half), columns]
            outs[3 * index + 2][rows] = grad_ref[pl.ds(a_at, half), columns]
    for out in outs[:n_pieces]:
        out[2 * half :] = record_ref[:, : out.shape[1]]


def weight_kernel(sides, slots, z_count, x_count, weight_ref, *refs):
    pieces, out_ref = refs[:-1], refs[-1]
    tile_rows, tile_cols = out_ref.shape
    side = weight_ref.shape[0]
    half = side // 2
    z_index, x_index, parity = here()
    z_step_a = jnp.where(parity == 0, -1, 1)
    if sides == 1:
        x_steps = [0, jnp.where(x_index == 0, 1, -1)]
        x_shown = [True, True]
    else:
        x_steps = [0, 1, -1]
        x_shown = [True, x_index < x_count - 1, x_index > 0]
    weight = weight_ref[...]
    total = jnp.zeros((tile_rows, tile_cols), jnp.float32)
    for index, x_step in enumerate(x_steps):
        turns = []
        for turn, z_step in enumerate((0, z_step_a, -z_step_a)):
            part = jnp.zeros((tile_rows, tile_cols), jnp.float32)
            z_tile = z_index + z_step
            shown = (z_tile >= 0) & (z_tile < z_count) & x_shown[index]
            record = pieces[3 * index + turn][2 * half :].astype(jnp.float32)
            record = record.astype(jnp.int32)
            if record.shape[1] < side:
                record = jnp.concatenate([record] * (side // record.shape[1]), axis=1)
            count = record[2 * slots : 2 * slots + 1, :side]
            for slot in range(slots):
                row = record[2 * slot : 2 * slot + 1, :side] + (z_step * tile_rows - half)
                col = record[2 * slot + 1 : 2 * slot + 2, :side] + (x_step * tile_cols - half)
                row = jnp.where((count > slot) & shown, row, nowhere)
                put_rows = (
                    iota((tile_rows, side), 0) == iota((tile_rows, side), 1) + row
                ).astype(jnp.bfloat16)
                put_cols = (
                    iota((side, tile_cols), 1) == iota((side, tile_cols), 0) + col[:, :1]
                ).astype(jnp.bfloat16)
                placed = dot(put_rows, weight).astype(jnp.bfloat16)
                part = part + dot(placed, put_cols)
            turns.append(part)
        total = total + (turns[0] + (turns[1] + turns[2]))
    out_ref[...] = total + regularizer


def sum_kernel(sides, z_count, x_count, *refs):
    pieces, out_ref = refs[:-1], refs[-1]
    own_ref, rows_a, rows_b = pieces[:3]
    _, tile_rows, tile_cols = out_ref.shape
    half = pieces[3].shape[1]
    z_index, x_index, parity = here()
    below = z_index > 0
    above = z_index < z_count - 1
    a_on = jnp.where(parity == 0, below, above)
    b_on = jnp.where(parity == 0, above, below)

    for channel in range(2):
        rows = slice(channel * tile_rows, (channel + 1) * tile_rows)

        def gate(on, ref, rows=rows):
            return jnp.where(on, ref[rows].astype(jnp.float32), 0.0)

        total = own_ref[rows].astype(jnp.float32)
        total = total + gate(a_on, rows_a) + gate(b_on, rows_b)
        first = jnp.zeros((tile_rows, half), jnp.float32)
        last = first
        for index in range(sides):
            level, corner_a, corner_b = pieces[3 + 3 * index : 6 + 3 * index]
            edge = level[rows].astype(jnp.float32)
            edge = edge + gate(a_on, corner_a) + gate(b_on, corner_b)
            if sides == 1:
                first = jnp.where(x_index == 1, edge, 0.0)
                last = jnp.where(x_index == 0, edge, 0.0)
            elif index == 0:
                last = jnp.where(x_index < x_count - 1, edge, 0.0)
            else:
                first = jnp.where(x_index > 0, edge, 0.0)
        zero = jnp.zeros((tile_rows, tile_cols - 2 * half), jnp.float32)
        parts = [first, zero, last] if tile_cols > 2 * half else [first, last]
        total = total + jnp.concatenate(parts, axis=1)
        out_ref[channel] = total.astype(jnp.bfloat16)


def update_kernel(object_ref, own_ref, other_ref, weight_ref, out_ref):
    for channel in range(2):
        gradient = own_ref[channel].astype(jnp.float32) + other_ref[channel].astype(jnp.float32)
        out_ref[channel] = object_ref[channel] + gradient / weight_ref[...]


def in_hbm(array):
    return pltpu.with_memory_space_constraint(array, pltpu.HBM)


def smem():
    return pl.BlockSpec(memory_space=pltpu.SMEM)


def hbm():
    return pl.BlockSpec(memory_space=pltpu.HBM)


def vmem():
    return pl.BlockSpec(memory_space=pltpu.VMEM)


def on_device(object_field, probe, amplitudes, centers, live):
    side = probe.shape[2]
    half = side // 2
    _, tile_rows, tile_cols = object_field.shape
    slots = centers.shape[2]
    z_count = lax.axis_size("tx")
    x_count = lax.axis_size("ty")
    m_count = lax.axis_size("mode")
    if tile_rows != half or slots != 2 or m_count != 4 or x_count < 2:
        raise ValueError("unsupported sizes")
    sides = 1 if x_count == 2 else 2
    axes = ("tx", "ty", "mode")

    def zigzag(flip, x_step):
        def moved(z, m):
            down = (m % 2 == 0) != flip
            if down:
                return (z + 1, m) if z < z_count - 1 else (z, m ^ 1)
            return (z - 1, m) if z > 0 else (z, m ^ 1)

        pairs = []
        for z in range(z_count):
            for x in range(x_count):
                for m in range(m_count):
                    z_to, m_to = moved(z, m)
                    x_to = (x + x_step) % x_count
                    pairs.append(
                        (
                            (z * x_count + x) * m_count + m,
                            (z_to * x_count + x_to) * m_count + m_to,
                        )
                    )
        return pairs

    def level(step):
        return [(x, (x + step) % x_count) for x in range(x_count)]

    def exchange(array, flip):
        return lax.ppermute(array, "mode", [(m, m ^ flip) for m in range(m_count)])

    probe_low, *packed = pl.pallas_call(
        functools.partial(start_kernel, sides),
        out_shape=[
            jax.ShapeDtypeStruct(probe.shape, jnp.bfloat16),
            jax.ShapeDtypeStruct(object_field.shape, jnp.bfloat16),
        ]
        + [jax.ShapeDtypeStruct((2, tile_rows, half), jnp.bfloat16)] * sides,
        in_specs=[hbm()] * 2,
        out_specs=[vmem()] * (2 + sides),
        scratch_shapes=[
            pltpu.VMEM(object_field.shape, jnp.float32),
            pltpu.VMEM(probe.shape, jnp.float32),
            pltpu.SemaphoreType.DMA((2,)),
        ],
        compiler_params=pltpu.CompilerParams(vmem_limit_bytes=small_bytes),
        name="start",
    )(in_hbm(object_field), in_hbm(probe))
    probe_y = exchange(probe_low, 2)
    probe_core = exchange(probe_low, 1)
    probe_core, *packed = lax.optimization_barrier((probe_core, *packed))
    x_steps = [1] if sides == 1 else [1, -1]
    pieces = [packed[0]]
    pieces += [lax.ppermute(packed[0], axes, zigzag(flip, 0)) for flip in (False, True)]
    for step, edge in zip(x_steps, packed[1:]):
        pieces.append(lax.ppermute(edge, "ty", level(step)))
        pieces += [lax.ppermute(edge, axes, zigzag(flip, step)) for flip in (False, True)]

    centers, live, pieces[3] = lax.optimization_barrier((centers, live, pieces[3]))
    record = pl.pallas_call(
        functools.partial(record_kernel, slots),
        out_shape=jax.ShapeDtypeStruct((record_rows, tile_cols), jnp.bfloat16),
        in_specs=[smem(), smem()],
        out_specs=vmem(),
        compiler_params=pltpu.CompilerParams(vmem_limit_bytes=small_bytes),
        name="record",
    )(centers, live)
    n_pieces = len(pieces)
    modes = probe.shape[1]
    ext_rows = tile_rows + side
    ext_cols = tile_cols + sides * half
    direct, swapped = (jnp.asarray(matrix) for matrix in dft_matrices(side))

    def waves(count):
        return [
            jax.ShapeDtypeStruct((count, side, 2 * side), jnp.float32),
            jax.ShapeDtypeStruct((count, 2 * side, side), jnp.bfloat16),
            jax.ShapeDtypeStruct((2, side, side), jnp.float32),
        ]

    patch, *near = pl.pallas_call(
        functools.partial(near_kernel, sides, slots, z_count, x_count),
        out_shape=[jax.ShapeDtypeStruct((2, side, side), jnp.float32)] + waves(2 * modes),
        in_specs=[vmem()] * (n_pieces + 5),
        out_specs=[vmem()] * 4,
        scratch_shapes=[pltpu.VMEM((2 * ext_rows, ext_cols), jnp.bfloat16)],
        compiler_params=pltpu.CompilerParams(vmem_limit_bytes=wave_bytes),
        name="near",
    )(record, *pieces, probe_low, probe_core, direct, swapped)
    probe_y, patch = lax.optimization_barrier((probe_y, patch))
    probe_diagonal = exchange(probe_y, 1)
    over = pl.pallas_call(
        far_kernel,
        out_shape=waves(modes),
        in_specs=[vmem()] * 4,
        out_specs=[vmem()] * 3,
        compiler_params=pltpu.CompilerParams(vmem_limit_bytes=wave_bytes),
        name="over",
    )(patch, probe_y, direct, swapped)
    shapes = [(2 * half + record_rows, tile_cols)] * 3
    shapes += [(2 * half + record_rows, half)] * (3 * sides)
    results = pl.pallas_call(
        functools.partial(back_kernel, sides, slots, x_count, tile_rows, tile_cols),
        out_shape=[jax.ShapeDtypeStruct(shape, jnp.bfloat16) for shape in shapes]
        + [jax.ShapeDtypeStruct((side, side), jnp.bfloat16)],
        in_specs=[vmem()] * 15,
        out_specs=[vmem()] * (n_pieces + 1),
        scratch_shapes=[
            pltpu.VMEM((modes, side, 2 * side), jnp.float32),
            pltpu.VMEM((modes, 2 * side, side), jnp.bfloat16),
            pltpu.VMEM((ext_rows, ext_cols), jnp.bfloat16),
        ],
        compiler_params=pltpu.CompilerParams(vmem_limit_bytes=wave_bytes),
        name="back",
    )(
        record,
        amplitudes,
        patch,
        probe_low,
        probe_core,
        probe_y,
        probe_diagonal,
        direct,
        swapped,
        *near,
        *over,
    )
    received = [results[0]]
    received += [
        lax.ppermute(results[1 + index], axes, zigzag(flip, 0))
        for index, flip in enumerate((False, True))
    ]
    for index, step in enumerate(x_steps):
        back_step = -step
        received.append(lax.ppermute(results[3 + 3 * index], "ty", level(back_step)))
        received += [
            lax.ppermute(results[4 + 3 * index + turn], axes, zigzag(flip, back_step))
            for turn, flip in enumerate((False, True))
        ]
    summed = pl.pallas_call(
        functools.partial(sum_kernel, sides, z_count, x_count),
        out_shape=jax.ShapeDtypeStruct(object_field.shape, jnp.bfloat16),
        in_specs=[vmem()] * n_pieces,
        out_specs=vmem(),
        compiler_params=pltpu.CompilerParams(vmem_limit_bytes=small_bytes),
        name="sums",
    )(*received)
    weight = pl.pallas_call(
        functools.partial(weight_kernel, sides, slots, z_count, x_count),
        out_shape=jax.ShapeDtypeStruct((tile_rows, tile_cols), jnp.float32),
        in_specs=[vmem()] * (n_pieces + 1),
        out_specs=vmem(),
        compiler_params=pltpu.CompilerParams(vmem_limit_bytes=small_bytes),
        name="weights",
    )(results[-1], *received)
    other = exchange(summed, 1)
    return pl.pallas_call(
        update_kernel,
        out_shape=jax.ShapeDtypeStruct(object_field.shape, jnp.float32),
        in_specs=[vmem()] * 4,
        out_specs=vmem(),
        compiler_params=pltpu.CompilerParams(vmem_limit_bytes=small_bytes),
        name="update",
    )(object_field, summed, other, weight)


def solution(mesh):
    return jax.shard_map(
        on_device,
        mesh=mesh,
        in_specs=(
            P(None, "tx", "ty"),
            P(None, "mode", None, None),
            P("tx", "ty", None, None, None),
            P("tx", "ty", None, None),
            P("tx", "ty"),
        ),
        out_specs=P(None, "tx", "ty"),
        check_vma=False,
    )
```

```python
import functools
import math

import jax
import jax.numpy as jnp
import numpy as np
from jax import lax
from jax.experimental import pallas as pl
from jax.experimental.pallas import tpu as pltpu
from jax.sharding import PartitionSpec as P

power_floor = 0.01
regularizer = 0.1
nowhere = -(1 << 20)
record_rows = 16
wave_bytes = 32 * 1024 * 1024
small_bytes = 8 * 1024 * 1024


def dft_matrices(side):
    line = np.arange(side, dtype=np.int32)
    angle = (line[:, None] * line[None, :] % side).astype(np.float32) * np.float32(
        2.0 * math.pi / side
    )
    scaling = np.float32(1.0 / math.sqrt(side))
    real = (np.cos(angle) * scaling).astype(jnp.bfloat16)
    imag = (-np.sin(angle) * scaling).astype(jnp.bfloat16)
    direct = np.block([[real, -imag], [imag, real]])
    swapped = np.block([[real, imag], [-imag, real]])
    return direct, swapped


def dot(left, right):
    return jnp.dot(left, right, preferred_element_type=jnp.float32)


def iota(shape, dim):
    return lax.broadcasted_iota(jnp.int32, shape, dim)


def column_coordinate(at, tile_cols, half, sides, x_index, x_count):
    own = at + half
    if sides == 1:
        side = at - tile_cols + jnp.where(x_index == 0, half + tile_cols, 0)
        return jnp.where(at < tile_cols, own, side)
    left = jnp.where(x_index > 0, at - tile_cols, nowhere)
    right = jnp.where(x_index < x_count - 1, at, nowhere)
    return jnp.where(at < tile_cols, own, jnp.where(at < tile_cols + half, left, right))


def sent_order(sides):
    corners = [at for index in range(sides) for at in (4 + 3 * index, 5 + 3 * index)]
    return [0] + corners + [1, 2] + [3 + 3 * index for index in range(sides)]


def in_sent_order(pieces):
    return [pieces[at] for at in sent_order(len(pieces) // 3 - 1)]


def from_sent_order(pieces):
    order = sent_order(len(pieces) // 3 - 1)
    return [pieces[order.index(at)] for at in range(len(pieces))]


def wide(tall):
    side = tall.shape[0] // 2
    return jnp.concatenate([tall[:side], tall[side:]], axis=1)


def tall(wide):
    side = wide.shape[1] // 2
    return jnp.concatenate([wide[:, :side], wide[:, side:]], axis=0)


def here():
    return (lax.axis_index("tx"), lax.axis_index("ty"), lax.axis_index("mode") % 2)


def start_kernel(sides, object_hbm, probe_hbm, low_ref, packed_ref, *rest):
    edges = rest[:sides]
    object_ref, probe_ref, sems = rest[sides:]
    copies = [
        pltpu.make_async_copy(source, target, sems.at[index])
        for index, (source, target) in enumerate(
            ((probe_hbm, probe_ref), (object_hbm, object_ref))
        )
    ]
    for copy in copies:
        copy.start()
    tile_cols = object_ref.shape[2]
    half = edges[0].shape[2]
    _, x_index, _ = here()
    copies[0].wait()
    low_ref[...] = probe_ref[...].astype(jnp.bfloat16)
    copies[1].wait()
    first, last = slice(0, half), slice(tile_cols - half, tile_cols)
    for channel in range(2):
        values = object_ref[channel].astype(jnp.bfloat16)
        packed_ref[channel] = values
        if sides == 1:
            edges[0][channel] = jnp.where(x_index == 0, values[:, last], values[:, first])
        else:
            edges[0][channel] = values[:, last]
            edges[1][channel] = values[:, first]


def record_kernel(
    slots, centers_ref, live_ref, direct_hbm, swapped_hbm, out_ref, direct_ref, swapped_ref, sems
):
    copies = [
        pltpu.make_async_copy(direct_hbm, direct_ref, sems.at[0]),
        pltpu.make_async_copy(swapped_hbm, swapped_ref, sems.at[1]),
    ]
    for copy in copies:
        copy.start()
    record = jnp.zeros(out_ref.shape, jnp.float32)
    line = iota(out_ref.shape, 0)
    for slot in range(slots):
        for axis in range(2):
            value = centers_ref[0, 0, slot, axis].astype(jnp.float32)
            record = jnp.where(line == 2 * slot + axis, value, record)
    record = jnp.where(line == 2 * slots, live_ref[0, 0].astype(jnp.float32), record)
    out_ref[...] = record.astype(jnp.bfloat16)
    for copy in copies:
        copy.wait()


def positions(record_ref, slots):
    _, _, parity = here()
    record = record_ref[:, :128].astype(jnp.float32).astype(jnp.int32)[:, :1]

    def of_slot(axis):
        value = record[axis : axis + 1]
        for slot in range(1, slots):
            value = jnp.where(parity == slot, record[2 * slot + axis : 2 * slot + axis + 1], value)
        return value

    return of_slot(0), of_slot(1), record[2 * slots : 2 * slots + 1] > parity


def row_starts(half, tile_rows, parity):
    low, high = 0, half + tile_rows
    return (
        pl.multiple_of(jnp.where(parity == 0, low, high), half),
        pl.multiple_of(jnp.where(parity == 0, high, low), half),
    )


def patch_of(sides, slots, z_count, x_count, side, record_ref, pieces, ext_ref):
    z_index, x_index, parity = here()
    row_at, col_at, _ = positions(record_ref, slots)
    half = side // 2
    _, tile_rows, tile_cols = pieces[0].shape
    ext_rows = tile_rows + side
    ext_cols = tile_cols + sides * half
    a_at, b_at = row_starts(half, tile_rows, parity)
    for channel in range(2):
        base = channel * ext_rows
        for index in range(1 + sides):
            columns = (
                slice(0, tile_cols)
                if index == 0
                else slice(tile_cols + (index - 1) * half, tile_cols + index * half)
            )
            level, turn_a, turn_b = pieces[3 * index : 3 * index + 3]
            ext_ref[pl.ds(base + half, tile_rows), columns] = level[channel]
            ext_ref[pl.ds(base + a_at, half), columns] = turn_a[channel]
            ext_ref[pl.ds(base + b_at, half), columns] = turn_b[channel]
    at = iota((ext_cols, side), 0)
    column = column_coordinate(at, tile_cols, half, sides, x_index, x_count)
    pick_cols = (column == iota((ext_cols, side), 1) + col_at).astype(jnp.bfloat16)
    at = iota((side, ext_rows), 1)
    first = jnp.where(z_index > 0, 0, half)
    last = jnp.where(z_index < z_count - 1, ext_rows, half + tile_rows)
    row = jnp.where((at >= first) & (at < last), at, nowhere)
    pick_rows = (row == iota((side, ext_rows), 0) + row_at).astype(jnp.bfloat16)
    narrow = dot(ext_ref[...], pick_cols).astype(jnp.bfloat16)
    return dot(pick_rows, narrow[:ext_rows]), dot(pick_rows, narrow[ext_rows:])


def forward(groups, patch, direct, swapped, far_ref, exit_ref, at):
    patch_real, patch_imag = patch
    side = patch_real.shape[0]
    sums = []
    for group in groups:
        modes = group.shape[1]
        power = jnp.zeros((side, side), jnp.float32)
        weight = jnp.zeros((side, side), jnp.float32)
        halves = []
        for k in range(modes):
            real = group[0, k].astype(jnp.float32)
            imag = group[1, k].astype(jnp.float32)
            exit_wave = jnp.concatenate(
                [
                    (real * patch_real - imag * patch_imag).astype(jnp.bfloat16),
                    (real * patch_imag + imag * patch_real).astype(jnp.bfloat16),
                ],
                axis=0,
            )
            exit_ref[at + k] = exit_wave
            halves.append(wide(dot(direct, exit_wave).astype(jnp.bfloat16)))
            weight = weight + (real * real + imag * imag)
        far_both = dot(jnp.concatenate(halves, axis=0), swapped)
        for k in range(modes):
            far = far_both[k * side : (k + 1) * side]
            far_ref[at + k] = far
            power = power + (far[:, :side] * far[:, :side] + far[:, side:] * far[:, side:])
        sums.append((power, weight))
        at += modes
    return sums


def backward(groups, factor, direct, swapped, far_ref, exit_ref):
    side = factor.shape[0]
    grads = []
    at = 0
    for group in groups:
        modes = group.shape[1]
        grad_real = jnp.zeros((side, side), jnp.float32)
        grad_imag = jnp.zeros((side, side), jnp.float32)
        halves = []
        for k in range(modes):
            fixed = (far_ref[at + k] * factor).astype(jnp.bfloat16)
            halves.append(wide(dot(swapped, tall(fixed)).astype(jnp.bfloat16)))
        back_both = dot(jnp.concatenate(halves, axis=0), direct)
        for k in range(modes):
            back = back_both[k * side : (k + 1) * side]
            exit_wave = exit_ref[at + k].astype(jnp.float32)
            real = group[0, k].astype(jnp.float32)
            imag = group[1, k].astype(jnp.float32)
            diff_real = back[:, :side] - exit_wave[:side]
            diff_imag = back[:, side:] - exit_wave[side:]
            grad_real = grad_real + (real * diff_real + imag * diff_imag)
            grad_imag = grad_imag + (real * diff_imag - imag * diff_real)
        grads.append((grad_real, grad_imag))
        at += modes
    return grads


def near_kernel(sides, slots, z_count, x_count, record_ref, *refs):
    n_pieces = 3 + 3 * sides
    pieces = from_sent_order(refs[:n_pieces])
    own, core, direct, swapped = refs[n_pieces : n_pieces + 4]
    patch_ref, far_ref, exit_ref, sum_ref, ext_ref = refs[n_pieces + 4 :]
    side = own.shape[2]
    patch = patch_of(sides, slots, z_count, x_count, side, record_ref, pieces, ext_ref)
    patch_ref[0], patch_ref[1] = patch
    sums = forward((own, core), patch, direct[...], swapped[...], far_ref, exit_ref, 0)
    sum_ref[0] = sums[0][0] + sums[1][0]
    sum_ref[1] = sums[0][1] + sums[1][1]


def far_kernel(patch_ref, group, direct, swapped, far_ref, exit_ref, sum_ref):
    patch = (patch_ref[0], patch_ref[1])
    ((power, weight),) = forward((group,), patch, direct[...], swapped[...], far_ref, exit_ref, 0)
    sum_ref[0] = power
    sum_ref[1] = weight


def back_kernel(sides, slots, x_count, tile_rows, tile_cols, record_ref, *refs):
    n_pieces = 3 + 3 * sides
    amplitude_ref, patch_ref, own, core, over, last, direct_ref, swapped_ref = refs[:8]
    near_far, near_exit, near_sum, over_far, over_exit, over_sum = refs[8:14]
    outs = refs[14 : 14 + n_pieces + 1]
    last_far, last_exit, grad_ref = refs[14 + n_pieces + 1 :]
    side = own.shape[2]
    half = side // 2
    modes = own.shape[1]
    ext_rows = tile_rows + side
    ext_cols = tile_cols + sides * half
    _, x_index, parity = here()
    row_at, col_at, is_live = positions(record_ref, slots)
    direct = direct_ref[...]
    swapped = swapped_ref[...]
    patch = (patch_ref[0], patch_ref[1])
    ((power, weight),) = forward((last,), patch, direct, swapped, last_far, last_exit, 0)
    power = near_sum[0] + (over_sum[0] + power)
    weight = near_sum[1] + (over_sum[1] + weight)
    outs[-1][...] = weight.astype(jnp.bfloat16)
    amplitude = amplitude_ref[0, 0, parity].astype(jnp.float32)
    factor = amplitude / jnp.sqrt(power + power_floor)
    factor = jnp.concatenate([factor, factor], axis=1)
    near = backward((own, core), factor, direct, swapped, near_far, near_exit)
    (beyond,) = backward((over,), factor, direct, swapped, over_far, over_exit)
    (final,) = backward((last,), factor, direct, swapped, last_far, last_exit)
    at = iota((side, ext_cols), 1)
    column = column_coordinate(at, tile_cols, half, sides, x_index, x_count)
    put_cols = ((column == iota((side, ext_cols), 0) + col_at) & is_live).astype(jnp.bfloat16)
    put_rows = (iota((ext_rows, side), 0) == iota((ext_rows, side), 1) + row_at).astype(
        jnp.bfloat16
    )
    a_at, b_at = row_starts(half, tile_rows, parity)
    for channel in range(2):
        gradient = (near[0][channel] + near[1][channel]) + (beyond[channel] + final[channel])
        placed = dot(put_rows, gradient.astype(jnp.bfloat16)).astype(jnp.bfloat16)
        grad_ref[...] = dot(placed, put_cols).astype(jnp.bfloat16)
        rows = slice(channel * half, (channel + 1) * half)
        for index in range(1 + sides):
            columns = (
                slice(0, tile_cols)
                if index == 0
                else slice(tile_cols + (index - 1) * half, tile_cols + index * half)
            )
            outs[3 * index][rows] = grad_ref[half : half + tile_rows, columns]
            outs[3 * index + 1][rows] = grad_ref[pl.ds(b_at, half), columns]
            outs[3 * index + 2][rows] = grad_ref[pl.ds(a_at, half), columns]
    for out in outs[:n_pieces]:
        out[2 * half :] = record_ref[:, : out.shape[1]]


def weight_kernel(sides, slots, z_count, x_count, weight_ref, *refs):
    pieces, out_ref = from_sent_order(refs[:-1]), refs[-1]
    tile_rows, tile_cols = out_ref.shape
    side = weight_ref.shape[0]
    half = side // 2
    z_index, x_index, parity = here()
    z_step_a = jnp.where(parity == 0, -1, 1)
    if sides == 1:
        x_steps = [0, jnp.where(x_index == 0, 1, -1)]
        x_shown = [True, True]
    else:
        x_steps = [0, 1, -1]
        x_shown = [True, x_index < x_count - 1, x_index > 0]
    weight = weight_ref[...]
    total = jnp.zeros((tile_rows, tile_cols), jnp.float32)
    for index, x_step in enumerate(x_steps):
        turns = []
        for turn, z_step in enumerate((0, z_step_a, -z_step_a)):
            part = jnp.zeros((tile_rows, tile_cols), jnp.float32)
            z_tile = z_index + z_step
            shown = (z_tile >= 0) & (z_tile < z_count) & x_shown[index]
            record = pieces[3 * index + turn][2 * half :].astype(jnp.float32)
            record = record.astype(jnp.int32)
            if record.shape[1] < side:
                record = jnp.concatenate([record] * (side // record.shape[1]), axis=1)
            count = record[2 * slots : 2 * slots + 1, :side]
            for slot in range(slots):
                row = record[2 * slot : 2 * slot + 1, :side] + (z_step * tile_rows - half)
                col = record[2 * slot + 1 : 2 * slot + 2, :side] + (x_step * tile_cols - half)
                row = jnp.where((count > slot) & shown, row, nowhere)
                put_rows = (
                    iota((tile_rows, side), 0) == iota((tile_rows, side), 1) + row
                ).astype(jnp.bfloat16)
                put_cols = (
                    iota((side, tile_cols), 1) == iota((side, tile_cols), 0) + col[:, :1]
                ).astype(jnp.bfloat16)
                placed = dot(put_rows, weight).astype(jnp.bfloat16)
                part = part + dot(placed, put_cols)
            turns.append(part)
        total = total + (turns[0] + (turns[1] + turns[2]))
    out_ref[...] = total + regularizer


def sum_kernel(sides, z_count, x_count, *refs):
    pieces, out_ref = from_sent_order(refs[:-1]), refs[-1]
    own_ref, rows_a, rows_b = pieces[:3]
    _, tile_rows, tile_cols = out_ref.shape
    half = pieces[3].shape[1]
    z_index, x_index, parity = here()
    below = z_index > 0
    above = z_index < z_count - 1
    a_on = jnp.where(parity == 0, below, above)
    b_on = jnp.where(parity == 0, above, below)

    for channel in range(2):
        rows = slice(channel * tile_rows, (channel + 1) * tile_rows)

        def gate(on, ref, rows=rows):
            return jnp.where(on, ref[rows].astype(jnp.float32), 0.0)

        total = own_ref[rows].astype(jnp.float32)
        total = total + gate(a_on, rows_a) + gate(b_on, rows_b)
        first = jnp.zeros((tile_rows, half), jnp.float32)
        last = first
        for index in range(sides):
            level, corner_a, corner_b = pieces[3 + 3 * index : 6 + 3 * index]
            edge = level[rows].astype(jnp.float32)
            edge = edge + gate(a_on, corner_a) + gate(b_on, corner_b)
            if sides == 1:
                first = jnp.where(x_index == 1, edge, 0.0)
                last = jnp.where(x_index == 0, edge, 0.0)
            elif index == 0:
                last = jnp.where(x_index < x_count - 1, edge, 0.0)
            else:
                first = jnp.where(x_index > 0, edge, 0.0)
        zero = jnp.zeros((tile_rows, tile_cols - 2 * half), jnp.float32)
        parts = [first, zero, last] if tile_cols > 2 * half else [first, last]
        total = total + jnp.concatenate(parts, axis=1)
        out_ref[channel] = total.astype(jnp.bfloat16)


def update_kernel(object_ref, own_ref, other_ref, weight_ref, out_ref):
    for channel in range(2):
        gradient = own_ref[channel].astype(jnp.float32) + other_ref[channel].astype(jnp.float32)
        out_ref[channel] = object_ref[channel] + gradient / weight_ref[...]


def in_hbm(array):
    return pltpu.with_memory_space_constraint(array, pltpu.HBM)


def smem():
    return pl.BlockSpec(memory_space=pltpu.SMEM)


def hbm():
    return pl.BlockSpec(memory_space=pltpu.HBM)


def vmem():
    return pl.BlockSpec(memory_space=pltpu.VMEM)


def on_device(object_field, probe, amplitudes, centers, live):
    side = probe.shape[2]
    half = side // 2
    _, tile_rows, tile_cols = object_field.shape
    slots = centers.shape[2]
    z_count = lax.axis_size("tx")
    x_count = lax.axis_size("ty")
    m_count = lax.axis_size("mode")
    if tile_rows != half or slots != 2 or m_count != 4 or x_count < 2:
        raise ValueError("unsupported sizes")
    sides = 1 if x_count == 2 else 2
    axes = ("tx", "ty", "mode")

    def zigzag(x_step, flip=False):
        def moved(z, m):
            down = (m % 2 == 0) != flip
            if down:
                return (z + 1, m) if z < z_count - 1 else (z, m ^ 1)
            return (z - 1, m) if z > 0 else (z, m ^ 1)

        pairs = []
        for z in range(z_count):
            for x in range(x_count):
                for m in range(m_count):
                    z_to, m_to = moved(z, m)
                    x_to = (x + x_step) % x_count
                    pairs.append(
                        (
                            (z * x_count + x) * m_count + m,
                            (z_to * x_count + x_to) * m_count + m_to,
                        )
                    )
        return pairs

    def level(step):
        return [(x, (x + step) % x_count) for x in range(x_count)]

    def exchange(array, flip):
        return lax.ppermute(array, "mode", [(m, m ^ flip) for m in range(m_count)])

    probe_low, *packed = pl.pallas_call(
        functools.partial(start_kernel, sides),
        out_shape=[
            jax.ShapeDtypeStruct(probe.shape, jnp.bfloat16),
            jax.ShapeDtypeStruct(object_field.shape, jnp.bfloat16),
        ]
        + [jax.ShapeDtypeStruct((2, tile_rows, half), jnp.bfloat16)] * sides,
        in_specs=[hbm()] * 2,
        out_specs=[vmem()] * (2 + sides),
        scratch_shapes=[
            pltpu.VMEM(object_field.shape, jnp.float32),
            pltpu.VMEM(probe.shape, jnp.float32),
            pltpu.SemaphoreType.DMA((2,)),
        ],
        compiler_params=pltpu.CompilerParams(vmem_limit_bytes=small_bytes),
        name="start",
    )(in_hbm(object_field), in_hbm(probe))
    probe_y = exchange(probe_low, 2)
    probe_core = exchange(probe_low, 1)
    probe_core, *packed = lax.optimization_barrier((probe_core, *packed))
    x_steps = [1] if sides == 1 else [1, -1]
    moved = [lax.ppermute(packed[0], axes, zigzag(0))]
    levels = []
    for step, edge in zip(x_steps, packed[1:]):
        moved.append(lax.ppermute(edge, axes, zigzag(step)))
        levels.append(lax.ppermute(edge, "ty", level(step)))
    pieces = [packed[0], moved[0], exchange(moved[0], 1)]
    for here_level, corner in zip(levels, moved[1:]):
        pieces += [here_level, corner, exchange(corner, 1)]
    tables = [in_hbm(jnp.asarray(matrix)) for matrix in dft_matrices(side)]
    centers, live, pieces[3] = lax.optimization_barrier((centers, live, pieces[3]))
    record, direct, swapped = pl.pallas_call(
        functools.partial(record_kernel, slots),
        out_shape=[jax.ShapeDtypeStruct((record_rows, tile_cols), jnp.bfloat16)]
        + [jax.ShapeDtypeStruct((2 * side, 2 * side), jnp.bfloat16)] * 2,
        in_specs=[smem(), smem(), hbm(), hbm()],
        out_specs=[vmem()] * 3,
        scratch_shapes=[pltpu.SemaphoreType.DMA((2,))],
        compiler_params=pltpu.CompilerParams(vmem_limit_bytes=small_bytes),
        name="record",
    )(centers, live, *tables)
    n_pieces = len(pieces)
    modes = probe.shape[1]
    ext_rows = tile_rows + side
    ext_cols = tile_cols + sides * half
    def waves(count):
        return [
            jax.ShapeDtypeStruct((count, side, 2 * side), jnp.float32),
            jax.ShapeDtypeStruct((count, 2 * side, side), jnp.bfloat16),
            jax.ShapeDtypeStruct((2, side, side), jnp.float32),
        ]

    patch, *near = pl.pallas_call(
        functools.partial(near_kernel, sides, slots, z_count, x_count),
        out_shape=[jax.ShapeDtypeStruct((2, side, side), jnp.float32)] + waves(2 * modes),
        in_specs=[vmem()] * (n_pieces + 5),
        out_specs=[vmem()] * 4,
        scratch_shapes=[pltpu.VMEM((2 * ext_rows, ext_cols), jnp.bfloat16)],
        compiler_params=pltpu.CompilerParams(vmem_limit_bytes=wave_bytes),
        name="near",
    )(record, *in_sent_order(pieces), probe_low, probe_core, direct, swapped)
    probe_y, patch = lax.optimization_barrier((probe_y, patch))
    probe_diagonal = exchange(probe_y, 1)
    over = pl.pallas_call(
        far_kernel,
        out_shape=waves(modes),
        in_specs=[vmem()] * 4,
        out_specs=[vmem()] * 3,
        compiler_params=pltpu.CompilerParams(vmem_limit_bytes=wave_bytes),
        name="over",
    )(patch, probe_y, direct, swapped)
    shapes = [(2 * half + record_rows, tile_cols)] * 3
    shapes += [(2 * half + record_rows, half)] * (3 * sides)
    results = pl.pallas_call(
        functools.partial(back_kernel, sides, slots, x_count, tile_rows, tile_cols),
        out_shape=[jax.ShapeDtypeStruct(shape, jnp.bfloat16) for shape in shapes]
        + [jax.ShapeDtypeStruct((side, side), jnp.bfloat16)],
        in_specs=[vmem()] * 15,
        out_specs=[vmem()] * (n_pieces + 1),
        scratch_shapes=[
            pltpu.VMEM((modes, side, 2 * side), jnp.float32),
            pltpu.VMEM((modes, 2 * side, side), jnp.bfloat16),
            pltpu.VMEM((ext_rows, ext_cols), jnp.bfloat16),
        ],
        compiler_params=pltpu.CompilerParams(vmem_limit_bytes=wave_bytes),
        name="back",
    )(
        record,
        amplitudes,
        patch,
        probe_low,
        probe_core,
        probe_y,
        probe_diagonal,
        direct,
        swapped,
        *near,
        *over,
    )
    received = [results[0]] + [None] * (n_pieces - 1)
    for index, step in enumerate(x_steps):
        at = 3 + 3 * index
        for turn, flip in enumerate((False, True)):
            received[at + 1 + turn] = lax.ppermute(results[at + 1 + turn], axes, zigzag(-step, flip))
    for turn, flip in enumerate((False, True)):
        received[1 + turn] = lax.ppermute(results[1 + turn], axes, zigzag(0, flip))
    for index, step in enumerate(x_steps):
        received[3 + 3 * index] = lax.ppermute(results[3 + 3 * index], "ty", level(-step))
    summed = pl.pallas_call(
        functools.partial(sum_kernel, sides, z_count, x_count),
        out_shape=jax.ShapeDtypeStruct(object_field.shape, jnp.bfloat16),
        in_specs=[vmem()] * n_pieces,
        out_specs=vmem(),
        compiler_params=pltpu.CompilerParams(vmem_limit_bytes=small_bytes),
        name="sums",
    )(*in_sent_order(received))
    weight = pl.pallas_call(
        functools.partial(weight_kernel, sides, slots, z_count, x_count),
        out_shape=jax.ShapeDtypeStruct((tile_rows, tile_cols), jnp.float32),
        in_specs=[vmem()] * (n_pieces + 1),
        out_specs=vmem(),
        compiler_params=pltpu.CompilerParams(vmem_limit_bytes=small_bytes),
        name="weights",
    )(results[-1], *in_sent_order(received))
    other = exchange(summed, 1)
    return pl.pallas_call(
        update_kernel,
        out_shape=jax.ShapeDtypeStruct(object_field.shape, jnp.float32),
        in_specs=[vmem()] * 4,
        out_specs=vmem(),
        compiler_params=pltpu.CompilerParams(vmem_limit_bytes=small_bytes),
        name="update",
    )(object_field, summed, other, weight)


def solution(mesh):
    return jax.shard_map(
        on_device,
        mesh=mesh,
        in_specs=(
            P(None, "tx", "ty"),
            P(None, "mode", None, None),
            P("tx", "ty", None, None, None),
            P("tx", "ty", None, None),
            P("tx", "ty"),
        ),
        out_specs=P(None, "tx", "ty"),
        check_vma=False,
    )
```

```python
import functools
import math

import jax
import jax.numpy as jnp
import numpy as np
from jax import lax
from jax.experimental import pallas as pl
from jax.experimental.pallas import tpu as pltpu
from jax.sharding import PartitionSpec as P

power_floor = 0.01
regularizer = 0.1
nowhere = -(1 << 20)
record_rows = 16
wave_bytes = 32 * 1024 * 1024
small_bytes = 8 * 1024 * 1024


def dft_matrices(side):
    line = np.arange(side, dtype=np.int32)
    angle = (line[:, None] * line[None, :] % side).astype(np.float32) * np.float32(
        2.0 * math.pi / side
    )
    scaling = np.float32(1.0 / math.sqrt(side))
    real = (np.cos(angle) * scaling).astype(jnp.bfloat16)
    imag = (-np.sin(angle) * scaling).astype(jnp.bfloat16)
    direct = np.block([[real, -imag], [imag, real]])
    swapped = np.block([[real, imag], [-imag, real]])
    return direct, swapped


def dot(left, right):
    return jnp.dot(left, right, preferred_element_type=jnp.float32)


def iota(shape, dim):
    return lax.broadcasted_iota(jnp.int32, shape, dim)


def column_coordinate(at, tile_cols, half, sides, x_index, x_count):
    own = at + half
    if sides == 1:
        side = at - tile_cols + jnp.where(x_index == 0, half + tile_cols, 0)
        return jnp.where(at < tile_cols, own, side)
    left = jnp.where(x_index > 0, at - tile_cols, nowhere)
    right = jnp.where(x_index < x_count - 1, at, nowhere)
    return jnp.where(at < tile_cols, own, jnp.where(at < tile_cols + half, left, right))


def sent_order(sides):
    corners = [at for index in range(sides) for at in (4 + 3 * index, 5 + 3 * index)]
    return [0] + corners + [1, 2] + [3 + 3 * index for index in range(sides)]


def in_sent_order(pieces):
    return [pieces[at] for at in sent_order(len(pieces) // 3 - 1)]


def from_sent_order(pieces):
    order = sent_order(len(pieces) // 3 - 1)
    return [pieces[order.index(at)] for at in range(len(pieces))]


def wide(tall):
    side = tall.shape[0] // 2
    return jnp.concatenate([tall[:side], tall[side:]], axis=1)


def tall(wide):
    side = wide.shape[1] // 2
    return jnp.concatenate([wide[:, :side], wide[:, side:]], axis=0)


def here():
    return (lax.axis_index("tx"), lax.axis_index("ty"), lax.axis_index("mode") % 2)


def start_kernel(sides, object_hbm, probe_hbm, low_ref, packed_ref, *rest):
    edges = rest[:sides]
    object_ref, probe_ref, sems = rest[sides:]
    copies = [
        pltpu.make_async_copy(source, target, sems.at[index])
        for index, (source, target) in enumerate(
            ((probe_hbm, probe_ref), (object_hbm, object_ref))
        )
    ]
    for copy in copies:
        copy.start()
    tile_cols = object_ref.shape[2]
    half = edges[0].shape[2]
    _, x_index, _ = here()
    copies[0].wait()
    low_ref[...] = probe_ref[...].astype(jnp.bfloat16)
    copies[1].wait()
    first, last = slice(0, half), slice(tile_cols - half, tile_cols)
    for channel in range(2):
        values = object_ref[channel].astype(jnp.bfloat16)
        packed_ref[channel] = values
        if sides == 1:
            edges[0][channel] = jnp.where(x_index == 0, values[:, last], values[:, first])
        else:
            edges[0][channel] = values[:, last]
            edges[1][channel] = values[:, first]


def record_kernel(
    slots, centers_ref, live_ref, direct_hbm, swapped_hbm, out_ref, direct_ref, swapped_ref, sems
):
    copies = [
        pltpu.make_async_copy(direct_hbm, direct_ref, sems.at[0]),
        pltpu.make_async_copy(swapped_hbm, swapped_ref, sems.at[1]),
    ]
    for copy in copies:
        copy.start()
    record = jnp.zeros(out_ref.shape, jnp.float32)
    line = iota(out_ref.shape, 0)
    for slot in range(slots):
        for axis in range(2):
            value = centers_ref[0, 0, slot, axis].astype(jnp.float32)
            record = jnp.where(line == 2 * slot + axis, value, record)
    record = jnp.where(line == 2 * slots, live_ref[0, 0].astype(jnp.float32), record)
    out_ref[...] = record.astype(jnp.bfloat16)
    for copy in copies:
        copy.wait()


def positions(record_ref, slots):
    _, _, parity = here()
    record = record_ref[:, :128].astype(jnp.float32).astype(jnp.int32)[:, :1]

    def of_slot(axis):
        value = record[axis : axis + 1]
        for slot in range(1, slots):
            value = jnp.where(parity == slot, record[2 * slot + axis : 2 * slot + axis + 1], value)
        return value

    return of_slot(0), of_slot(1), record[2 * slots : 2 * slots + 1] > parity


def row_starts(half, tile_rows, parity):
    low, high = 0, half + tile_rows
    return (
        pl.multiple_of(jnp.where(parity == 0, low, high), half),
        pl.multiple_of(jnp.where(parity == 0, high, low), half),
    )


def patch_of(sides, slots, z_count, x_count, side, record_ref, pieces, ext_ref):
    z_index, x_index, parity = here()
    row_at, col_at, _ = positions(record_ref, slots)
    half = side // 2
    _, tile_rows, tile_cols = pieces[0].shape
    ext_rows = tile_rows + side
    ext_cols = tile_cols + sides * half
    a_at, b_at = row_starts(half, tile_rows, parity)
    for channel in range(2):
        base = channel * ext_rows
        for index in range(1 + sides):
            columns = (
                slice(0, tile_cols)
                if index == 0
                else slice(tile_cols + (index - 1) * half, tile_cols + index * half)
            )
            level, turn_a, turn_b = pieces[3 * index : 3 * index + 3]
            ext_ref[pl.ds(base + half, tile_rows), columns] = level[channel]
            ext_ref[pl.ds(base + a_at, half), columns] = turn_a[channel]
            ext_ref[pl.ds(base + b_at, half), columns] = turn_b[channel]
    at = iota((ext_cols, side), 0)
    column = column_coordinate(at, tile_cols, half, sides, x_index, x_count)
    pick_cols = (column == iota((ext_cols, side), 1) + col_at).astype(jnp.bfloat16)
    at = iota((side, ext_rows), 1)
    first = jnp.where(z_index > 0, 0, half)
    last = jnp.where(z_index < z_count - 1, ext_rows, half + tile_rows)
    row = jnp.where((at >= first) & (at < last), at, nowhere)
    pick_rows = (row == iota((side, ext_rows), 0) + row_at).astype(jnp.bfloat16)
    narrow = dot(ext_ref[...], pick_cols).astype(jnp.bfloat16)
    return dot(pick_rows, narrow[:ext_rows]), dot(pick_rows, narrow[ext_rows:])


def forward(groups, patch, direct, swapped, far_ref, exit_ref, at):
    patch_real, patch_imag = patch
    side = patch_real.shape[0]
    sums = []
    for group in groups:
        modes = group.shape[1]
        power = jnp.zeros((side, side), jnp.float32)
        weight = jnp.zeros((side, side), jnp.float32)
        halves = []
        for k in range(modes):
            real = group[0, k].astype(jnp.float32)
            imag = group[1, k].astype(jnp.float32)
            exit_wave = jnp.concatenate(
                [
                    (real * patch_real - imag * patch_imag).astype(jnp.bfloat16),
                    (real * patch_imag + imag * patch_real).astype(jnp.bfloat16),
                ],
                axis=0,
            )
            exit_ref[at + k] = exit_wave
            halves.append(wide(dot(direct, exit_wave).astype(jnp.bfloat16)))
            weight = weight + (real * real + imag * imag)
        far_both = dot(jnp.concatenate(halves, axis=0), swapped)
        for k in range(modes):
            far = far_both[k * side : (k + 1) * side]
            far_ref[at + k] = far
            power = power + (far[:, :side] * far[:, :side] + far[:, side:] * far[:, side:])
        sums.append((power, weight))
        at += modes
    return sums


def backward(groups, factor, direct, swapped, far_ref, exit_ref):
    side = factor.shape[0]
    grads = []
    at = 0
    for group in groups:
        modes = group.shape[1]
        grad_real = jnp.zeros((side, side), jnp.float32)
        grad_imag = jnp.zeros((side, side), jnp.float32)
        halves = []
        for k in range(modes):
            fixed = (far_ref[at + k] * factor).astype(jnp.bfloat16)
            halves.append(wide(dot(swapped, tall(fixed)).astype(jnp.bfloat16)))
        back_both = dot(jnp.concatenate(halves, axis=0), direct)
        for k in range(modes):
            back = back_both[k * side : (k + 1) * side]
            exit_wave = exit_ref[at + k].astype(jnp.float32)
            real = group[0, k].astype(jnp.float32)
            imag = group[1, k].astype(jnp.float32)
            diff_real = back[:, :side] - exit_wave[:side]
            diff_imag = back[:, side:] - exit_wave[side:]
            grad_real = grad_real + (real * diff_real + imag * diff_imag)
            grad_imag = grad_imag + (real * diff_imag - imag * diff_real)
        grads.append((grad_real, grad_imag))
        at += modes
    return grads


def near_kernel(sides, slots, z_count, x_count, record_ref, *refs):
    n_pieces = 3 + 3 * sides
    pieces = from_sent_order(refs[:n_pieces])
    own, core, direct, swapped = refs[n_pieces : n_pieces + 4]
    patch_ref, far_ref, exit_ref, sum_ref, ext_ref = refs[n_pieces + 4 :]
    side = own.shape[2]
    patch = patch_of(sides, slots, z_count, x_count, side, record_ref, pieces, ext_ref)
    patch_ref[0], patch_ref[1] = patch
    sums = forward((own, core), patch, direct[...], swapped[...], far_ref, exit_ref, 0)
    sum_ref[0] = sums[0][0] + sums[1][0]
    sum_ref[1] = sums[0][1] + sums[1][1]


def far_kernel(patch_ref, group, direct, swapped, far_ref, exit_ref, sum_ref):
    patch = (patch_ref[0], patch_ref[1])
    ((power, weight),) = forward((group,), patch, direct[...], swapped[...], far_ref, exit_ref, 0)
    sum_ref[0] = power
    sum_ref[1] = weight


def back_kernel(sides, slots, x_count, tile_rows, tile_cols, record_ref, *refs):
    n_pieces = 3 + 3 * sides
    amplitude_ref, patch_ref, own, core, over, last, direct_ref, swapped_ref = refs[:8]
    near_far, near_exit, near_sum, over_far, over_exit, over_sum = refs[8:14]
    outs = refs[14 : 14 + n_pieces + 1]
    last_far, last_exit, grad_ref = refs[14 + n_pieces + 1 :]
    side = own.shape[2]
    half = side // 2
    modes = own.shape[1]
    ext_rows = tile_rows + side
    ext_cols = tile_cols + sides * half
    _, x_index, parity = here()
    row_at, col_at, is_live = positions(record_ref, slots)
    direct = direct_ref[...]
    swapped = swapped_ref[...]
    patch = (patch_ref[0], patch_ref[1])
    ((power, weight),) = forward((last,), patch, direct, swapped, last_far, last_exit, 0)
    power = near_sum[0] + (over_sum[0] + power)
    weight = near_sum[1] + (over_sum[1] + weight)
    outs[-1][...] = weight.astype(jnp.bfloat16)
    amplitude = amplitude_ref[0, 0, parity].astype(jnp.float32)
    factor = amplitude / jnp.sqrt(power + power_floor)
    factor = jnp.concatenate([factor, factor], axis=1)
    near = backward((own, core), factor, direct, swapped, near_far, near_exit)
    (beyond,) = backward((over,), factor, direct, swapped, over_far, over_exit)
    (final,) = backward((last,), factor, direct, swapped, last_far, last_exit)
    at = iota((side, ext_cols), 1)
    column = column_coordinate(at, tile_cols, half, sides, x_index, x_count)
    put_cols = ((column == iota((side, ext_cols), 0) + col_at) & is_live).astype(jnp.bfloat16)
    put_rows = (iota((ext_rows, side), 0) == iota((ext_rows, side), 1) + row_at).astype(
        jnp.bfloat16
    )
    a_at, b_at = row_starts(half, tile_rows, parity)
    for channel in range(2):
        gradient = (near[0][channel] + near[1][channel]) + (beyond[channel] + final[channel])
        placed = dot(put_rows, gradient.astype(jnp.bfloat16)).astype(jnp.bfloat16)
        grad_ref[...] = dot(placed, put_cols).astype(jnp.bfloat16)
        rows = slice(channel * half, (channel + 1) * half)
        for index in range(1 + sides):
            columns = (
                slice(0, tile_cols)
                if index == 0
                else slice(tile_cols + (index - 1) * half, tile_cols + index * half)
            )
            outs[3 * index][rows] = grad_ref[half : half + tile_rows, columns]
            outs[3 * index + 1][rows] = grad_ref[pl.ds(b_at, half), columns]
            outs[3 * index + 2][rows] = grad_ref[pl.ds(a_at, half), columns]
    for out in outs[:n_pieces]:
        out[2 * half :] = record_ref[:, : out.shape[1]]


def weight_kernel(sides, slots, z_count, x_count, weight_ref, *refs):
    pieces, out_ref = from_sent_order(refs[:-1]), refs[-1]
    tile_rows, tile_cols = out_ref.shape
    side = weight_ref.shape[0]
    half = side // 2
    z_index, x_index, parity = here()
    z_step_a = jnp.where(parity == 0, -1, 1)
    if sides == 1:
        x_steps = [0, jnp.where(x_index == 0, 1, -1)]
        x_shown = [True, True]
    else:
        x_steps = [0, 1, -1]
        x_shown = [True, x_index < x_count - 1, x_index > 0]
    weight = weight_ref[...]
    total = jnp.zeros((tile_rows, tile_cols), jnp.float32)
    for index, x_step in enumerate(x_steps):
        turns = []
        for turn, z_step in enumerate((0, z_step_a, -z_step_a)):
            part = jnp.zeros((tile_rows, tile_cols), jnp.float32)
            z_tile = z_index + z_step
            shown = (z_tile >= 0) & (z_tile < z_count) & x_shown[index]
            record = pieces[3 * index + turn][2 * half :].astype(jnp.float32)
            record = record.astype(jnp.int32)
            if record.shape[1] < side:
                record = jnp.concatenate([record] * (side // record.shape[1]), axis=1)
            count = record[2 * slots : 2 * slots + 1, :side]
            for slot in range(slots):
                row = record[2 * slot : 2 * slot + 1, :side] + (z_step * tile_rows - half)
                col = record[2 * slot + 1 : 2 * slot + 2, :side] + (x_step * tile_cols - half)
                row = jnp.where((count > slot) & shown, row, nowhere)
                put_rows = (
                    iota((tile_rows, side), 0) == iota((tile_rows, side), 1) + row
                ).astype(jnp.bfloat16)
                put_cols = (
                    iota((side, tile_cols), 1) == iota((side, tile_cols), 0) + col[:, :1]
                ).astype(jnp.bfloat16)
                placed = dot(put_rows, weight).astype(jnp.bfloat16)
                part = part + dot(placed, put_cols)
            turns.append(part)
        total = total + (turns[0] + (turns[1] + turns[2]))
    out_ref[...] = total + regularizer


def sum_kernel(sides, z_count, x_count, *refs):
    pieces, out_ref = from_sent_order(refs[:-1]), refs[-1]
    own_ref, rows_a, rows_b = pieces[:3]
    _, tile_rows, tile_cols = out_ref.shape
    half = pieces[3].shape[1]
    z_index, x_index, parity = here()
    below = z_index > 0
    above = z_index < z_count - 1
    a_on = jnp.where(parity == 0, below, above)
    b_on = jnp.where(parity == 0, above, below)

    for channel in range(2):
        rows = slice(channel * tile_rows, (channel + 1) * tile_rows)

        def gate(on, ref, rows=rows):
            return jnp.where(on, ref[rows].astype(jnp.float32), 0.0)

        total = own_ref[rows].astype(jnp.float32)
        total = total + gate(a_on, rows_a) + gate(b_on, rows_b)
        first = jnp.zeros((tile_rows, half), jnp.float32)
        last = first
        for index in range(sides):
            level, corner_a, corner_b = pieces[3 + 3 * index : 6 + 3 * index]
            edge = level[rows].astype(jnp.float32)
            edge = edge + gate(a_on, corner_a) + gate(b_on, corner_b)
            if sides == 1:
                first = jnp.where(x_index == 1, edge, 0.0)
                last = jnp.where(x_index == 0, edge, 0.0)
            elif index == 0:
                last = jnp.where(x_index < x_count - 1, edge, 0.0)
            else:
                first = jnp.where(x_index > 0, edge, 0.0)
        zero = jnp.zeros((tile_rows, tile_cols - 2 * half), jnp.float32)
        parts = [first, zero, last] if tile_cols > 2 * half else [first, last]
        total = total + jnp.concatenate(parts, axis=1)
        out_ref[channel] = total.astype(jnp.bfloat16)


def update_kernel(object_ref, own_ref, other_ref, weight_ref, out_ref):
    for channel in range(2):
        gradient = own_ref[channel].astype(jnp.float32) + other_ref[channel].astype(jnp.float32)
        out_ref[channel] = object_ref[channel] + gradient / weight_ref[...]


def in_hbm(array):
    return pltpu.with_memory_space_constraint(array, pltpu.HBM)


def smem():
    return pl.BlockSpec(memory_space=pltpu.SMEM)


def hbm():
    return pl.BlockSpec(memory_space=pltpu.HBM)


def vmem():
    return pl.BlockSpec(memory_space=pltpu.VMEM)


def on_device(object_field, probe, amplitudes, centers, live):
    side = probe.shape[2]
    half = side // 2
    _, tile_rows, tile_cols = object_field.shape
    slots = centers.shape[2]
    z_count = lax.axis_size("tx")
    x_count = lax.axis_size("ty")
    m_count = lax.axis_size("mode")
    if tile_rows != half or slots != 2 or m_count != 4 or x_count < 2:
        raise ValueError("unsupported sizes")
    sides = 1 if x_count == 2 else 2
    axes = ("tx", "ty", "mode")

    def zigzag(x_step, flip=False):
        def moved(z, m):
            down = (m % 2 == 0) != flip
            if down:
                return (z + 1, m) if z < z_count - 1 else (z, m ^ 1)
            return (z - 1, m) if z > 0 else (z, m ^ 1)

        pairs = []
        for z in range(z_count):
            for x in range(x_count):
                for m in range(m_count):
                    z_to, m_to = moved(z, m)
                    x_to = (x + x_step) % x_count
                    pairs.append(
                        (
                            (z * x_count + x) * m_count + m,
                            (z_to * x_count + x_to) * m_count + m_to,
                        )
                    )
        return pairs

    def level(step):
        return [(x, (x + step) % x_count) for x in range(x_count)]

    def exchange(array, flip):
        return lax.ppermute(array, "mode", [(m, m ^ flip) for m in range(m_count)])

    probe_low, *packed = pl.pallas_call(
        functools.partial(start_kernel, sides),
        out_shape=[
            jax.ShapeDtypeStruct(probe.shape, jnp.bfloat16),
            jax.ShapeDtypeStruct(object_field.shape, jnp.bfloat16),
        ]
        + [jax.ShapeDtypeStruct((2, tile_rows, half), jnp.bfloat16)] * sides,
        in_specs=[hbm()] * 2,
        out_specs=[vmem()] * (2 + sides),
        scratch_shapes=[
            pltpu.VMEM(object_field.shape, jnp.float32),
            pltpu.VMEM(probe.shape, jnp.float32),
            pltpu.SemaphoreType.DMA((2,)),
        ],
        compiler_params=pltpu.CompilerParams(vmem_limit_bytes=small_bytes),
        name="start",
    )(in_hbm(object_field), in_hbm(probe))
    probe_y = exchange(probe_low, 2)
    probe_core = exchange(probe_low, 1)
    probe_core, *packed = lax.optimization_barrier((probe_core, *packed))
    x_steps = [1] if sides == 1 else [1, -1]
    moved = [lax.ppermute(packed[0], axes, zigzag(0))]
    levels = []
    for step, edge in zip(x_steps, packed[1:]):
        moved.append(lax.ppermute(edge, axes, zigzag(step)))
        levels.append(lax.ppermute(edge, "ty", level(step)))
    pieces = [packed[0], moved[0], exchange(moved[0], 1)]
    for here_level, corner in zip(levels, moved[1:]):
        pieces += [here_level, corner, exchange(corner, 1)]
    tables = [in_hbm(jnp.asarray(matrix)) for matrix in dft_matrices(side)]
    centers, live, moved[0] = lax.optimization_barrier((centers, live, moved[0]))
    record, direct, swapped = pl.pallas_call(
        functools.partial(record_kernel, slots),
        out_shape=[jax.ShapeDtypeStruct((record_rows, tile_cols), jnp.bfloat16)]
        + [jax.ShapeDtypeStruct((2 * side, 2 * side), jnp.bfloat16)] * 2,
        in_specs=[smem(), smem(), hbm(), hbm()],
        out_specs=[vmem()] * 3,
        scratch_shapes=[pltpu.SemaphoreType.DMA((2,))],
        compiler_params=pltpu.CompilerParams(vmem_limit_bytes=small_bytes),
        name="record",
    )(centers, live, *tables)
    n_pieces = len(pieces)
    modes = probe.shape[1]
    ext_rows = tile_rows + side
    ext_cols = tile_cols + sides * half
    def waves(count):
        return [
            jax.ShapeDtypeStruct((count, side, 2 * side), jnp.float32),
            jax.ShapeDtypeStruct((count, 2 * side, side), jnp.bfloat16),
            jax.ShapeDtypeStruct((2, side, side), jnp.float32),
        ]

    patch, *near = pl.pallas_call(
        functools.partial(near_kernel, sides, slots, z_count, x_count),
        out_shape=[jax.ShapeDtypeStruct((2, side, side), jnp.float32)] + waves(2 * modes),
        in_specs=[vmem()] * (n_pieces + 5),
        out_specs=[vmem()] * 4,
        scratch_shapes=[pltpu.VMEM((2 * ext_rows, ext_cols), jnp.bfloat16)],
        compiler_params=pltpu.CompilerParams(vmem_limit_bytes=wave_bytes),
        name="near",
    )(record, *in_sent_order(pieces), probe_low, probe_core, direct, swapped)
    probe_y, patch = lax.optimization_barrier((probe_y, patch))
    probe_diagonal = exchange(probe_y, 1)
    over = pl.pallas_call(
        far_kernel,
        out_shape=waves(modes),
        in_specs=[vmem()] * 4,
        out_specs=[vmem()] * 3,
        compiler_params=pltpu.CompilerParams(vmem_limit_bytes=wave_bytes),
        name="over",
    )(patch, probe_y, direct, swapped)
    shapes = [(2 * half + record_rows, tile_cols)] * 3
    shapes += [(2 * half + record_rows, half)] * (3 * sides)
    results = pl.pallas_call(
        functools.partial(back_kernel, sides, slots, x_count, tile_rows, tile_cols),
        out_shape=[jax.ShapeDtypeStruct(shape, jnp.bfloat16) for shape in shapes]
        + [jax.ShapeDtypeStruct((side, side), jnp.bfloat16)],
        in_specs=[vmem()] * 15,
        out_specs=[vmem()] * (n_pieces + 1),
        scratch_shapes=[
            pltpu.VMEM((modes, side, 2 * side), jnp.float32),
            pltpu.VMEM((modes, 2 * side, side), jnp.bfloat16),
            pltpu.VMEM((ext_rows, ext_cols), jnp.bfloat16),
        ],
        compiler_params=pltpu.CompilerParams(vmem_limit_bytes=wave_bytes),
        name="back",
    )(
        record,
        amplitudes,
        patch,
        probe_low,
        probe_core,
        probe_y,
        probe_diagonal,
        direct,
        swapped,
        *near,
        *over,
    )
    received = [results[0]] + [None] * (n_pieces - 1)
    for index, step in enumerate(x_steps):
        at = 3 + 3 * index
        for turn, flip in enumerate((False, True)):
            received[at + 1 + turn] = lax.ppermute(results[at + 1 + turn], axes, zigzag(-step, flip))
    for turn, flip in enumerate((False, True)):
        received[1 + turn] = lax.ppermute(results[1 + turn], axes, zigzag(0, flip))
    for index, step in enumerate(x_steps):
        received[3 + 3 * index] = lax.ppermute(results[3 + 3 * index], "ty", level(-step))
    summed = pl.pallas_call(
        functools.partial(sum_kernel, sides, z_count, x_count),
        out_shape=jax.ShapeDtypeStruct(object_field.shape, jnp.bfloat16),
        in_specs=[vmem()] * n_pieces,
        out_specs=vmem(),
        compiler_params=pltpu.CompilerParams(vmem_limit_bytes=small_bytes),
        name="sums",
    )(*in_sent_order(received))
    weight = pl.pallas_call(
        functools.partial(weight_kernel, sides, slots, z_count, x_count),
        out_shape=jax.ShapeDtypeStruct((tile_rows, tile_cols), jnp.float32),
        in_specs=[vmem()] * (n_pieces + 1),
        out_specs=vmem(),
        compiler_params=pltpu.CompilerParams(vmem_limit_bytes=small_bytes),
        name="weights",
    )(results[-1], *in_sent_order(received))
    other = exchange(summed, 1)
    return pl.pallas_call(
        update_kernel,
        out_shape=jax.ShapeDtypeStruct(object_field.shape, jnp.float32),
        in_specs=[vmem()] * 4,
        out_specs=vmem(),
        compiler_params=pltpu.CompilerParams(vmem_limit_bytes=small_bytes),
        name="update",
    )(object_field, summed, other, weight)


def solution(mesh):
    return jax.shard_map(
        on_device,
        mesh=mesh,
        in_specs=(
            P(None, "tx", "ty"),
            P(None, "mode", None, None),
            P("tx", "ty", None, None, None),
            P("tx", "ty", None, None),
            P("tx", "ty"),
        ),
        out_specs=P(None, "tx", "ty"),
        check_vma=False,
    )
```

```python
import functools
import math

import jax
import jax.numpy as jnp
import numpy as np
from jax import lax
from jax.experimental import pallas as pl
from jax.experimental.pallas import tpu as pltpu
from jax.sharding import PartitionSpec as P

power_floor = 0.01
regularizer = 0.1
nowhere = -(1 << 20)
record_rows = 16
wave_bytes = 32 * 1024 * 1024
small_bytes = 8 * 1024 * 1024


def dft_matrices(side):
    line = np.arange(side, dtype=np.int32)
    angle = (line[:, None] * line[None, :] % side).astype(np.float32) * np.float32(
        2.0 * math.pi / side
    )
    scaling = np.float32(1.0 / math.sqrt(side))
    real = (np.cos(angle) * scaling).astype(jnp.bfloat16)
    imag = (-np.sin(angle) * scaling).astype(jnp.bfloat16)
    direct = np.block([[real, -imag], [imag, real]])
    swapped = np.block([[real, imag], [-imag, real]])
    return direct, swapped


def dot(left, right):
    return jnp.dot(left, right, preferred_element_type=jnp.float32)


def iota(shape, dim):
    return lax.broadcasted_iota(jnp.int32, shape, dim)


def column_coordinate(at, tile_cols, half, sides, x_index, x_count):
    own = at + half
    if sides == 1:
        side = at - tile_cols + jnp.where(x_index == 0, half + tile_cols, 0)
        return jnp.where(at < tile_cols, own, side)
    left = jnp.where(x_index > 0, at - tile_cols, nowhere)
    right = jnp.where(x_index < x_count - 1, at, nowhere)
    return jnp.where(at < tile_cols, own, jnp.where(at < tile_cols + half, left, right))


def sent_order(sides):
    corners = [at for index in range(sides) for at in (4 + 3 * index, 5 + 3 * index)]
    return [0] + corners + [1, 2] + [3 + 3 * index for index in range(sides)]


def in_sent_order(pieces):
    return [pieces[at] for at in sent_order(len(pieces) // 3 - 1)]


def from_sent_order(pieces):
    order = sent_order(len(pieces) // 3 - 1)
    return [pieces[order.index(at)] for at in range(len(pieces))]


def wide(tall):
    side = tall.shape[0] // 2
    return jnp.concatenate([tall[:side], tall[side:]], axis=1)


def tall(wide):
    side = wide.shape[1] // 2
    return jnp.concatenate([wide[:, :side], wide[:, side:]], axis=0)


def here():
    return (lax.axis_index("tx"), lax.axis_index("ty"), lax.axis_index("mode") % 2)


def start_kernel(sides, object_hbm, probe_hbm, low_ref, shared_ref, rest_ref, packed_ref, *rest):
    edges = rest[:sides]
    object_ref, probe_ref, sems = rest[sides:]
    copies = [
        pltpu.make_async_copy(source, target, sems.at[index])
        for index, (source, target) in enumerate(
            ((probe_hbm, probe_ref), (object_hbm, object_ref))
        )
    ]
    for copy in copies:
        copy.start()
    tile_cols = object_ref.shape[2]
    half = edges[0].shape[2]
    _, x_index, _ = here()
    copies[0].wait()
    low_ref[...] = probe_ref[...].astype(jnp.bfloat16)
    shared_ref[...] = jnp.where(x_index % 2 == 0, low_ref[0, 0], low_ref[1, 0])
    rest_ref[...] = low_ref[:, 1:]
    copies[1].wait()
    first, last = slice(0, half), slice(tile_cols - half, tile_cols)
    for channel in range(2):
        values = object_ref[channel].astype(jnp.bfloat16)
        packed_ref[channel] = values
        if sides == 1:
            edges[0][channel] = jnp.where(x_index == 0, values[:, last], values[:, first])
        else:
            edges[0][channel] = values[:, last]
            edges[1][channel] = values[:, first]


def record_kernel(
    slots, centers_ref, live_ref, direct_hbm, swapped_hbm, out_ref, direct_ref, swapped_ref, sems
):
    copies = [
        pltpu.make_async_copy(direct_hbm, direct_ref, sems.at[0]),
        pltpu.make_async_copy(swapped_hbm, swapped_ref, sems.at[1]),
    ]
    for copy in copies:
        copy.start()
    record = jnp.zeros(out_ref.shape, jnp.float32)
    line = iota(out_ref.shape, 0)
    for slot in range(slots):
        for axis in range(2):
            value = centers_ref[0, 0, slot, axis].astype(jnp.float32)
            record = jnp.where(line == 2 * slot + axis, value, record)
    record = jnp.where(line == 2 * slots, live_ref[0, 0].astype(jnp.float32), record)
    out_ref[...] = record.astype(jnp.bfloat16)
    for copy in copies:
        copy.wait()


def positions(record_ref, slots):
    _, _, parity = here()
    record = record_ref[:, :128].astype(jnp.float32).astype(jnp.int32)[:, :1]

    def of_slot(axis):
        value = record[axis : axis + 1]
        for slot in range(1, slots):
            value = jnp.where(parity == slot, record[2 * slot + axis : 2 * slot + axis + 1], value)
        return value

    return of_slot(0), of_slot(1), record[2 * slots : 2 * slots + 1] > parity


def row_starts(half, tile_rows, parity):
    low, high = 0, half + tile_rows
    return (
        pl.multiple_of(jnp.where(parity == 0, low, high), half),
        pl.multiple_of(jnp.where(parity == 0, high, low), half),
    )


def patch_of(sides, slots, z_count, x_count, side, record_ref, pieces, ext_ref):
    z_index, x_index, parity = here()
    row_at, col_at, _ = positions(record_ref, slots)
    half = side // 2
    _, tile_rows, tile_cols = pieces[0].shape
    ext_rows = tile_rows + side
    ext_cols = tile_cols + sides * half
    a_at, b_at = row_starts(half, tile_rows, parity)
    for channel in range(2):
        base = channel * ext_rows
        for index in range(1 + sides):
            columns = (
                slice(0, tile_cols)
                if index == 0
                else slice(tile_cols + (index - 1) * half, tile_cols + index * half)
            )
            level, turn_a, turn_b = pieces[3 * index : 3 * index + 3]
            ext_ref[pl.ds(base + half, tile_rows), columns] = level[channel]
            ext_ref[pl.ds(base + a_at, half), columns] = turn_a[channel]
            ext_ref[pl.ds(base + b_at, half), columns] = turn_b[channel]
    at = iota((ext_cols, side), 0)
    column = column_coordinate(at, tile_cols, half, sides, x_index, x_count)
    pick_cols = (column == iota((ext_cols, side), 1) + col_at).astype(jnp.bfloat16)
    at = iota((side, ext_rows), 1)
    first = jnp.where(z_index > 0, 0, half)
    last = jnp.where(z_index < z_count - 1, ext_rows, half + tile_rows)
    row = jnp.where((at >= first) & (at < last), at, nowhere)
    pick_rows = (row == iota((side, ext_rows), 0) + row_at).astype(jnp.bfloat16)
    narrow = dot(ext_ref[...], pick_cols).astype(jnp.bfloat16)
    return dot(pick_rows, narrow[:ext_rows]), dot(pick_rows, narrow[ext_rows:])


def modes_of(group):
    def reader(k):
        return lambda: (group[0, k].astype(jnp.float32), group[1, k].astype(jnp.float32))

    return [reader(k) for k in range(group.shape[1])]


def shared_mode(over_y, over_x):
    def read():
        _, x_index, _ = here()
        even = x_index % 2 == 0
        over_y_values = over_y[...].astype(jnp.float32)
        over_x_values = over_x[...].astype(jnp.float32)
        return (
            jnp.where(even, over_y_values, over_x_values),
            jnp.where(even, over_x_values, over_y_values),
        )

    return read


def forward(modes, patch, direct, swapped, far_ref, exit_ref, at):
    patch_real, patch_imag = patch
    side = patch_real.shape[0]
    power = jnp.zeros((side, side), jnp.float32)
    weight = jnp.zeros((side, side), jnp.float32)
    halves = []
    for k, mode in enumerate(modes):
        real, imag = mode()
        exit_wave = jnp.concatenate(
            [
                (real * patch_real - imag * patch_imag).astype(jnp.bfloat16),
                (real * patch_imag + imag * patch_real).astype(jnp.bfloat16),
            ],
            axis=0,
        )
        exit_ref[at + k] = exit_wave
        halves.append(wide(dot(direct, exit_wave).astype(jnp.bfloat16)))
        weight = weight + (real * real + imag * imag)
    far_all = dot(jnp.concatenate(halves, axis=0), swapped)
    for k in range(len(modes)):
        far = far_all[k * side : (k + 1) * side]
        far_ref[at + k] = far
        power = power + (far[:, :side] * far[:, :side] + far[:, side:] * far[:, side:])
    return power, weight


def backward(modes, factor, direct, swapped, far_ref, exit_ref, at):
    side = factor.shape[0]
    grad_real = jnp.zeros((side, side), jnp.float32)
    grad_imag = jnp.zeros((side, side), jnp.float32)
    halves = []
    for k in range(len(modes)):
        fixed = (far_ref[at + k] * factor).astype(jnp.bfloat16)
        halves.append(wide(dot(swapped, tall(fixed)).astype(jnp.bfloat16)))
    back_all = dot(jnp.concatenate(halves, axis=0), direct)
    for k, mode in enumerate(modes):
        back = back_all[k * side : (k + 1) * side]
        exit_wave = exit_ref[at + k].astype(jnp.float32)
        real, imag = mode()
        diff_real = back[:, :side] - exit_wave[:side]
        diff_imag = back[:, side:] - exit_wave[side:]
        grad_real = grad_real + (real * diff_real + imag * diff_imag)
        grad_imag = grad_imag + (real * diff_imag - imag * diff_real)
    return grad_real, grad_imag


def near_kernel(sides, slots, z_count, x_count, record_ref, *refs):
    n_pieces = 3 + 3 * sides
    pieces = from_sent_order(refs[:n_pieces])
    own, core, direct, swapped = refs[n_pieces : n_pieces + 4]
    patch_ref, far_ref, exit_ref, sum_ref, ext_ref = refs[n_pieces + 4 :]
    side = own.shape[2]
    patch = patch_of(sides, slots, z_count, x_count, side, record_ref, pieces, ext_ref)
    patch_ref[0], patch_ref[1] = patch
    tables = (direct[...], swapped[...], far_ref, exit_ref)
    first = forward(modes_of(own), patch, *tables, 0)
    second = forward(modes_of(core), patch, *tables, own.shape[1])
    sum_ref[0] = first[0] + second[0]
    sum_ref[1] = first[1] + second[1]


def over_kernel(patch_ref, over_y, over_x, rest, direct, swapped, far_ref, exit_ref, sum_ref):
    patch = (patch_ref[0], patch_ref[1])
    modes = [shared_mode(over_y, over_x)] + modes_of(rest)
    sum_ref[0], sum_ref[1] = forward(
        modes, patch, direct[...], swapped[...], far_ref, exit_ref, 0
    )


def back_kernel(sides, slots, x_count, tile_rows, tile_cols, record_ref, *refs):
    n_pieces = 3 + 3 * sides
    amplitude_ref, patch_ref, own, core = refs[:4]
    over_modes = [shared_mode(*refs[4:6])] + modes_of(refs[6])
    last_modes = [shared_mode(*refs[7:9])] + modes_of(refs[9])
    direct_ref, swapped_ref = refs[10:12]
    near_far, near_exit, near_sum, over_far, over_exit, over_sum = refs[12:18]
    outs = refs[18 : 18 + n_pieces + 1]
    last_far, last_exit, grad_ref = refs[18 + n_pieces + 1 :]
    side = own.shape[2]
    half = side // 2
    modes = own.shape[1]
    ext_rows = tile_rows + side
    ext_cols = tile_cols + sides * half
    _, x_index, parity = here()
    row_at, col_at, is_live = positions(record_ref, slots)
    direct = direct_ref[...]
    swapped = swapped_ref[...]
    patch = (patch_ref[0], patch_ref[1])
    power, weight = forward(last_modes, patch, direct, swapped, last_far, last_exit, 0)
    power = near_sum[0] + (over_sum[0] + power)
    weight = near_sum[1] + (over_sum[1] + weight)
    outs[-1][...] = weight.astype(jnp.bfloat16)
    amplitude = amplitude_ref[0, 0, parity].astype(jnp.float32)
    factor = amplitude / jnp.sqrt(power + power_floor)
    factor = jnp.concatenate([factor, factor], axis=1)
    tables = (factor, direct, swapped)
    grads = [
        backward(modes_of(own), *tables, near_far, near_exit, 0),
        backward(modes_of(core), *tables, near_far, near_exit, modes),
        backward(over_modes, *tables, over_far, over_exit, 0),
        backward(last_modes, *tables, last_far, last_exit, 0),
    ]
    at = iota((side, ext_cols), 1)
    column = column_coordinate(at, tile_cols, half, sides, x_index, x_count)
    put_cols = ((column == iota((side, ext_cols), 0) + col_at) & is_live).astype(jnp.bfloat16)
    put_rows = (iota((ext_rows, side), 0) == iota((ext_rows, side), 1) + row_at).astype(
        jnp.bfloat16
    )
    a_at, b_at = row_starts(half, tile_rows, parity)
    for channel in range(2):
        gradient = (grads[0][channel] + grads[1][channel]) + (grads[2][channel] + grads[3][channel])
        placed = dot(put_rows, gradient.astype(jnp.bfloat16)).astype(jnp.bfloat16)
        grad_ref[...] = dot(placed, put_cols).astype(jnp.bfloat16)
        rows = slice(channel * half, (channel + 1) * half)
        for index in range(1 + sides):
            columns = (
                slice(0, tile_cols)
                if index == 0
                else slice(tile_cols + (index - 1) * half, tile_cols + index * half)
            )
            outs[3 * index][rows] = grad_ref[half : half + tile_rows, columns]
            outs[3 * index + 1][rows] = grad_ref[pl.ds(b_at, half), columns]
            outs[3 * index + 2][rows] = grad_ref[pl.ds(a_at, half), columns]
    for out in outs[:n_pieces]:
        out[2 * half :] = record_ref[:, : out.shape[1]]


def weight_kernel(sides, slots, z_count, x_count, weight_ref, *refs):
    pieces, out_ref = from_sent_order(refs[:-1]), refs[-1]
    tile_rows, tile_cols = out_ref.shape
    side = weight_ref.shape[0]
    half = side // 2
    z_index, x_index, parity = here()
    z_step_a = jnp.where(parity == 0, -1, 1)
    if sides == 1:
        x_steps = [0, jnp.where(x_index == 0, 1, -1)]
        x_shown = [True, True]
    else:
        x_steps = [0, 1, -1]
        x_shown = [True, x_index < x_count - 1, x_index > 0]
    weight = weight_ref[...]
    total = jnp.zeros((tile_rows, tile_cols), jnp.float32)
    for index, x_step in enumerate(x_steps):
        turns = []
        for turn, z_step in enumerate((0, z_step_a, -z_step_a)):
            part = jnp.zeros((tile_rows, tile_cols), jnp.float32)
            z_tile = z_index + z_step
            shown = (z_tile >= 0) & (z_tile < z_count) & x_shown[index]
            record = pieces[3 * index + turn][2 * half :].astype(jnp.float32)
            record = record.astype(jnp.int32)
            if record.shape[1] < side:
                record = jnp.concatenate([record] * (side // record.shape[1]), axis=1)
            count = record[2 * slots : 2 * slots + 1, :side]
            for slot in range(slots):
                row = record[2 * slot : 2 * slot + 1, :side] + (z_step * tile_rows - half)
                col = record[2 * slot + 1 : 2 * slot + 2, :side] + (x_step * tile_cols - half)
                row = jnp.where((count > slot) & shown, row, nowhere)
                put_rows = (
                    iota((tile_rows, side), 0) == iota((tile_rows, side), 1) + row
                ).astype(jnp.bfloat16)
                put_cols = (
                    iota((side, tile_cols), 1) == iota((side, tile_cols), 0) + col[:, :1]
                ).astype(jnp.bfloat16)
                placed = dot(put_rows, weight).astype(jnp.bfloat16)
                part = part + dot(placed, put_cols)
            turns.append(part)
        total = total + (turns[0] + (turns[1] + turns[2]))
    out_ref[...] = total + regularizer


def sum_kernel(sides, z_count, x_count, *refs):
    pieces, out_ref = from_sent_order(refs[:-1]), refs[-1]
    own_ref, rows_a, rows_b = pieces[:3]
    _, tile_rows, tile_cols = out_ref.shape
    half = pieces[3].shape[1]
    z_index, x_index, parity = here()
    below = z_index > 0
    above = z_index < z_count - 1
    a_on = jnp.where(parity == 0, below, above)
    b_on = jnp.where(parity == 0, above, below)

    for channel in range(2):
        rows = slice(channel * tile_rows, (channel + 1) * tile_rows)

        def gate(on, ref, rows=rows):
            return jnp.where(on, ref[rows].astype(jnp.float32), 0.0)

        total = own_ref[rows].astype(jnp.float32)
        total = total + gate(a_on, rows_a) + gate(b_on, rows_b)
        first = jnp.zeros((tile_rows, half), jnp.float32)
        last = first
        for index in range(sides):
            level, corner_a, corner_b = pieces[3 + 3 * index : 6 + 3 * index]
            edge = level[rows].astype(jnp.float32)
            edge = edge + gate(a_on, corner_a) + gate(b_on, corner_b)
            if sides == 1:
                first = jnp.where(x_index == 1, edge, 0.0)
                last = jnp.where(x_index == 0, edge, 0.0)
            elif index == 0:
                last = jnp.where(x_index < x_count - 1, edge, 0.0)
            else:
                first = jnp.where(x_index > 0, edge, 0.0)
        zero = jnp.zeros((tile_rows, tile_cols - 2 * half), jnp.float32)
        parts = [first, zero, last] if tile_cols > 2 * half else [first, last]
        total = total + jnp.concatenate(parts, axis=1)
        out_ref[channel] = total.astype(jnp.bfloat16)


def update_kernel(object_ref, own_ref, other_ref, weight_ref, out_ref):
    for channel in range(2):
        gradient = own_ref[channel].astype(jnp.float32) + other_ref[channel].astype(jnp.float32)
        out_ref[channel] = object_ref[channel] + gradient / weight_ref[...]


def in_hbm(array):
    return pltpu.with_memory_space_constraint(array, pltpu.HBM)


def smem():
    return pl.BlockSpec(memory_space=pltpu.SMEM)


def hbm():
    return pl.BlockSpec(memory_space=pltpu.HBM)


def vmem():
    return pl.BlockSpec(memory_space=pltpu.VMEM)


def on_device(object_field, probe, amplitudes, centers, live):
    side = probe.shape[2]
    half = side // 2
    _, tile_rows, tile_cols = object_field.shape
    slots = centers.shape[2]
    z_count = lax.axis_size("tx")
    x_count = lax.axis_size("ty")
    m_count = lax.axis_size("mode")
    modes = probe.shape[1]
    if tile_rows != half or slots != 2 or m_count != 4 or x_count % 2 or modes < 2:
        raise ValueError("unsupported sizes")
    sides = 1 if x_count == 2 else 2
    axes = ("tx", "ty", "mode")

    def zigzag(x_step, flip=False):
        def moved(z, m):
            down = (m % 2 == 0) != flip
            if down:
                return (z + 1, m) if z < z_count - 1 else (z, m ^ 1)
            return (z - 1, m) if z > 0 else (z, m ^ 1)

        pairs = []
        for z in range(z_count):
            for x in range(x_count):
                for m in range(m_count):
                    z_to, m_to = moved(z, m)
                    x_to = (x + x_step) % x_count
                    pairs.append(
                        (
                            (z * x_count + x) * m_count + m,
                            (z_to * x_count + x_to) * m_count + m_to,
                        )
                    )
        return pairs

    def level(step):
        return [(x, (x + step) % x_count) for x in range(x_count)]

    def exchange(array, flip):
        return lax.ppermute(array, "mode", [(m, m ^ flip) for m in range(m_count)])

    probe_low, shared, rest, *packed = pl.pallas_call(
        functools.partial(start_kernel, sides),
        out_shape=[
            jax.ShapeDtypeStruct(probe.shape, jnp.bfloat16),
            jax.ShapeDtypeStruct((side, side), jnp.bfloat16),
            jax.ShapeDtypeStruct((2, modes - 1, side, side), jnp.bfloat16),
            jax.ShapeDtypeStruct(object_field.shape, jnp.bfloat16),
        ]
        + [jax.ShapeDtypeStruct((2, tile_rows, half), jnp.bfloat16)] * sides,
        in_specs=[hbm()] * 2,
        out_specs=[vmem()] * (4 + sides),
        scratch_shapes=[
            pltpu.VMEM(object_field.shape, jnp.float32),
            pltpu.VMEM(probe.shape, jnp.float32),
            pltpu.SemaphoreType.DMA((2,)),
        ],
        compiler_params=pltpu.CompilerParams(vmem_limit_bytes=small_bytes),
        name="start",
    )(in_hbm(object_field), in_hbm(probe))
    over_y = exchange(shared, 2)
    probe_core = exchange(probe_low, 1)
    probe_core, rest = lax.optimization_barrier((probe_core, rest))
    rest = exchange(rest, 2)
    over_x = lax.ppermute(over_y, "ty", [(x, x ^ 1) for x in range(x_count)])
    x_steps = [1] if sides == 1 else [1, -1]
    moved = [lax.ppermute(packed[0], axes, zigzag(0))]
    levels = []
    for step, edge in zip(x_steps, packed[1:]):
        moved.append(lax.ppermute(edge, axes, zigzag(step)))
        levels.append(lax.ppermute(edge, "ty", level(step)))
    pieces = [packed[0], moved[0], exchange(moved[0], 1)]
    for here_level, corner in zip(levels, moved[1:]):
        pieces += [here_level, corner, exchange(corner, 1)]
    tables = [in_hbm(jnp.asarray(matrix)) for matrix in dft_matrices(side)]
    centers, live, moved[0] = lax.optimization_barrier((centers, live, moved[0]))
    record, direct, swapped = pl.pallas_call(
        functools.partial(record_kernel, slots),
        out_shape=[jax.ShapeDtypeStruct((record_rows, tile_cols), jnp.bfloat16)]
        + [jax.ShapeDtypeStruct((2 * side, 2 * side), jnp.bfloat16)] * 2,
        in_specs=[smem(), smem(), hbm(), hbm()],
        out_specs=[vmem()] * 3,
        scratch_shapes=[pltpu.SemaphoreType.DMA((2,))],
        compiler_params=pltpu.CompilerParams(vmem_limit_bytes=small_bytes),
        name="record",
    )(centers, live, *tables)
    n_pieces = len(pieces)
    ext_rows = tile_rows + side
    ext_cols = tile_cols + sides * half

    def waves(count):
        return [
            jax.ShapeDtypeStruct((count, side, 2 * side), jnp.float32),
            jax.ShapeDtypeStruct((count, 2 * side, side), jnp.bfloat16),
            jax.ShapeDtypeStruct((2, side, side), jnp.float32),
        ]

    patch, *near = pl.pallas_call(
        functools.partial(near_kernel, sides, slots, z_count, x_count),
        out_shape=[jax.ShapeDtypeStruct((2, side, side), jnp.float32)] + waves(2 * modes),
        in_specs=[vmem()] * (n_pieces + 5),
        out_specs=[vmem()] * 4,
        scratch_shapes=[pltpu.VMEM((2 * ext_rows, ext_cols), jnp.bfloat16)],
        compiler_params=pltpu.CompilerParams(vmem_limit_bytes=wave_bytes),
        name="near",
    )(record, *in_sent_order(pieces), probe_low, probe_core, direct, swapped)
    over_x, rest, patch = lax.optimization_barrier((over_x, rest, patch))
    over_group = (over_y, over_x, rest)
    last_group = [exchange(part, 1) for part in over_group]
    over = pl.pallas_call(
        over_kernel,
        out_shape=waves(modes),
        in_specs=[vmem()] * 6,
        out_specs=[vmem()] * 3,
        compiler_params=pltpu.CompilerParams(vmem_limit_bytes=wave_bytes),
        name="over",
    )(patch, *over_group, direct, swapped)
    shapes = [(2 * half + record_rows, tile_cols)] * 3
    shapes += [(2 * half + record_rows, half)] * (3 * sides)
    results = pl.pallas_call(
        functools.partial(back_kernel, sides, slots, x_count, tile_rows, tile_cols),
        out_shape=[jax.ShapeDtypeStruct(shape, jnp.bfloat16) for shape in shapes]
        + [jax.ShapeDtypeStruct((side, side), jnp.bfloat16)],
        in_specs=[vmem()] * 19,
        out_specs=[vmem()] * (n_pieces + 1),
        scratch_shapes=[
            pltpu.VMEM((modes, side, 2 * side), jnp.float32),
            pltpu.VMEM((modes, 2 * side, side), jnp.bfloat16),
            pltpu.VMEM((ext_rows, ext_cols), jnp.bfloat16),
        ],
        compiler_params=pltpu.CompilerParams(vmem_limit_bytes=wave_bytes),
        name="back",
    )(
        record,
        amplitudes,
        patch,
        probe_low,
        probe_core,
        *over_group,
        *last_group,
        direct,
        swapped,
        *near,
        *over,
    )
    received = [results[0]] + [None] * (n_pieces - 1)
    for index, step in enumerate(x_steps):
        at = 3 + 3 * index
        for turn, flip in enumerate((False, True)):
            received[at + 1 + turn] = lax.ppermute(results[at + 1 + turn], axes, zigzag(-step, flip))
    for turn, flip in enumerate((False, True)):
        received[1 + turn] = lax.ppermute(results[1 + turn], axes, zigzag(0, flip))
    for index, step in enumerate(x_steps):
        received[3 + 3 * index] = lax.ppermute(results[3 + 3 * index], "ty", level(-step))
    summed = pl.pallas_call(
        functools.partial(sum_kernel, sides, z_count, x_count),
        out_shape=jax.ShapeDtypeStruct(object_field.shape, jnp.bfloat16),
        in_specs=[vmem()] * n_pieces,
        out_specs=vmem(),
        compiler_params=pltpu.CompilerParams(vmem_limit_bytes=small_bytes),
        name="sums",
    )(*in_sent_order(received))
    weight = pl.pallas_call(
        functools.partial(weight_kernel, sides, slots, z_count, x_count),
        out_shape=jax.ShapeDtypeStruct((tile_rows, tile_cols), jnp.float32),
        in_specs=[vmem()] * (n_pieces + 1),
        out_specs=vmem(),
        compiler_params=pltpu.CompilerParams(vmem_limit_bytes=small_bytes),
        name="weights",
    )(results[-1], *in_sent_order(received))
    other = exchange(summed, 1)
    return pl.pallas_call(
        update_kernel,
        out_shape=jax.ShapeDtypeStruct(object_field.shape, jnp.float32),
        in_specs=[vmem()] * 4,
        out_specs=vmem(),
        compiler_params=pltpu.CompilerParams(vmem_limit_bytes=small_bytes),
        name="update",
    )(object_field, summed, other, weight)


def solution(mesh):
    return jax.shard_map(
        on_device,
        mesh=mesh,
        in_specs=(
            P(None, "tx", "ty"),
            P(None, "mode", None, None),
            P("tx", "ty", None, None, None),
            P("tx", "ty", None, None),
            P("tx", "ty"),
        ),
        out_specs=P(None, "tx", "ty"),
        check_vma=False,
    )
```

```python
import functools
import math

import jax
import jax.numpy as jnp
import numpy as np
from jax import lax
from jax.experimental import pallas as pl
from jax.experimental.pallas import tpu as pltpu
from jax.sharding import PartitionSpec as P

power_floor = 0.01
regularizer = 0.1
nowhere = -(1 << 20)
record_rows = 16
wave_bytes = 32 * 1024 * 1024
small_bytes = 8 * 1024 * 1024


def dft_matrices(side):
    line = np.arange(side, dtype=np.int32)
    angle = (line[:, None] * line[None, :] % side).astype(np.float32) * np.float32(
        2.0 * math.pi / side
    )
    scaling = np.float32(1.0 / math.sqrt(side))
    real = (np.cos(angle) * scaling).astype(jnp.bfloat16)
    imag = (-np.sin(angle) * scaling).astype(jnp.bfloat16)
    direct = np.block([[real, -imag], [imag, real]])
    swapped = np.block([[real, imag], [-imag, real]])
    return direct, swapped


def dot(left, right):
    return jnp.dot(left, right, preferred_element_type=jnp.float32)


def iota(shape, dim):
    return lax.broadcasted_iota(jnp.int32, shape, dim)


def column_coordinate(at, tile_cols, half, sides, x_index, x_count):
    own = at + half
    if sides == 1:
        side = at - tile_cols + jnp.where(x_index == 0, half + tile_cols, 0)
        return jnp.where(at < tile_cols, own, side)
    left = jnp.where(x_index > 0, at - tile_cols, nowhere)
    right = jnp.where(x_index < x_count - 1, at, nowhere)
    return jnp.where(at < tile_cols, own, jnp.where(at < tile_cols + half, left, right))


def sent_order(sides):
    corners = [at for index in range(sides) for at in (4 + 3 * index, 5 + 3 * index)]
    return [0] + corners + [1, 2] + [3 + 3 * index for index in range(sides)]


def in_sent_order(pieces):
    return [pieces[at] for at in sent_order(len(pieces) // 3 - 1)]


def from_sent_order(pieces):
    order = sent_order(len(pieces) // 3 - 1)
    return [pieces[order.index(at)] for at in range(len(pieces))]


def wide(tall):
    side = tall.shape[0] // 2
    return jnp.concatenate([tall[:side], tall[side:]], axis=1)


def tall(wide):
    side = wide.shape[1] // 2
    return jnp.concatenate([wide[:, :side], wide[:, side:]], axis=0)


def here():
    return (lax.axis_index("tx"), lax.axis_index("ty"), lax.axis_index("mode") % 2)


def start_kernel(
    sides,
    slots,
    object_hbm,
    probe_hbm,
    centers_hbm,
    direct_hbm,
    swapped_hbm,
    low_ref,
    shared_ref,
    rest_ref,
    record_ref,
    direct_ref,
    swapped_ref,
    packed_ref,
    *refs,
):
    edges = refs[:sides]
    object_ref, probe_ref, centers_ref, sems = refs[sides:]
    copies = [
        pltpu.make_async_copy(source, target, sems.at[index])
        for index, (source, target) in enumerate(
            (
                (probe_hbm, probe_ref),
                (object_hbm, object_ref),
                (centers_hbm, centers_ref),
                (direct_hbm, direct_ref),
                (swapped_hbm, swapped_ref),
            )
        )
    ]
    for copy in copies:
        copy.start()
    tile_cols = object_ref.shape[2]
    half = edges[0].shape[2]
    _, x_index, _ = here()
    copies[0].wait()
    low_ref[...] = probe_ref[...].astype(jnp.bfloat16)
    shared_ref[...] = jnp.where(x_index % 2 == 0, low_ref[0, 0], low_ref[1, 0])
    rest_ref[...] = low_ref[:, 1:]
    copies[1].wait()
    first, last = slice(0, half), slice(tile_cols - half, tile_cols)
    for channel in range(2):
        values = object_ref[channel].astype(jnp.bfloat16)
        packed_ref[channel] = values
        if sides == 1:
            edges[0][channel] = jnp.where(x_index == 0, values[:, last], values[:, first])
        else:
            edges[0][channel] = values[:, last]
            edges[1][channel] = values[:, first]
    copies[2].wait()
    record = jnp.zeros(record_ref.shape, jnp.float32)
    line = iota(record_ref.shape, 0)
    for slot in range(slots):
        for axis in range(2):
            value = centers_ref[0, 0, slot, axis].astype(jnp.float32)
            record = jnp.where(line == 2 * slot + axis, value, record)
    record_ref[...] = record.astype(jnp.bfloat16)
    copies[3].wait()
    copies[4].wait()


def live_kernel(slots, record_ref, live_ref, out_ref):
    line = iota(record_ref.shape, 0)
    record = record_ref[...].astype(jnp.float32)
    record = jnp.where(line == 2 * slots, live_ref[0, 0].astype(jnp.float32), record)
    out_ref[...] = record.astype(jnp.bfloat16)


def positions(record_ref, slots):
    _, _, parity = here()
    record = record_ref[:, :128].astype(jnp.float32).astype(jnp.int32)[:, :1]

    def of_slot(axis):
        value = record[axis : axis + 1]
        for slot in range(1, slots):
            value = jnp.where(parity == slot, record[2 * slot + axis : 2 * slot + axis + 1], value)
        return value

    return of_slot(0), of_slot(1), record[2 * slots : 2 * slots + 1] > parity


def row_starts(half, tile_rows, parity):
    low, high = 0, half + tile_rows
    return (
        pl.multiple_of(jnp.where(parity == 0, low, high), half),
        pl.multiple_of(jnp.where(parity == 0, high, low), half),
    )


def patch_of(sides, slots, z_count, x_count, side, record_ref, pieces, ext_ref):
    z_index, x_index, parity = here()
    row_at, col_at, _ = positions(record_ref, slots)
    half = side // 2
    _, tile_rows, tile_cols = pieces[0].shape
    ext_rows = tile_rows + side
    ext_cols = tile_cols + sides * half
    a_at, b_at = row_starts(half, tile_rows, parity)
    for channel in range(2):
        base = channel * ext_rows
        for index in range(1 + sides):
            columns = (
                slice(0, tile_cols)
                if index == 0
                else slice(tile_cols + (index - 1) * half, tile_cols + index * half)
            )
            level, turn_a, turn_b = pieces[3 * index : 3 * index + 3]
            ext_ref[pl.ds(base + half, tile_rows), columns] = level[channel]
            ext_ref[pl.ds(base + a_at, half), columns] = turn_a[channel]
            ext_ref[pl.ds(base + b_at, half), columns] = turn_b[channel]
    at = iota((ext_cols, side), 0)
    column = column_coordinate(at, tile_cols, half, sides, x_index, x_count)
    pick_cols = (column == iota((ext_cols, side), 1) + col_at).astype(jnp.bfloat16)
    at = iota((side, ext_rows), 1)
    first = jnp.where(z_index > 0, 0, half)
    last = jnp.where(z_index < z_count - 1, ext_rows, half + tile_rows)
    row = jnp.where((at >= first) & (at < last), at, nowhere)
    pick_rows = (row == iota((side, ext_rows), 0) + row_at).astype(jnp.bfloat16)
    narrow = dot(ext_ref[...], pick_cols).astype(jnp.bfloat16)
    return dot(pick_rows, narrow[:ext_rows]), dot(pick_rows, narrow[ext_rows:])


def modes_of(group):
    def reader(k):
        return lambda: (group[0, k].astype(jnp.float32), group[1, k].astype(jnp.float32))

    return [reader(k) for k in range(group.shape[1])]


def shared_mode(over_y, over_x):
    def read():
        _, x_index, _ = here()
        even = x_index % 2 == 0
        over_y_values = over_y[...].astype(jnp.float32)
        over_x_values = over_x[...].astype(jnp.float32)
        return (
            jnp.where(even, over_y_values, over_x_values),
            jnp.where(even, over_x_values, over_y_values),
        )

    return read


def forward(modes, patch, direct, swapped, far_ref, exit_ref, at):
    patch_real, patch_imag = patch
    side = patch_real.shape[0]
    power = jnp.zeros((side, side), jnp.float32)
    weight = jnp.zeros((side, side), jnp.float32)
    halves = []
    for k, mode in enumerate(modes):
        real, imag = mode()
        exit_wave = jnp.concatenate(
            [
                (real * patch_real - imag * patch_imag).astype(jnp.bfloat16),
                (real * patch_imag + imag * patch_real).astype(jnp.bfloat16),
            ],
            axis=0,
        )
        exit_ref[at + k] = exit_wave
        halves.append(wide(dot(direct, exit_wave).astype(jnp.bfloat16)))
        weight = weight + (real * real + imag * imag)
    far_all = dot(jnp.concatenate(halves, axis=0), swapped)
    for k in range(len(modes)):
        far = far_all[k * side : (k + 1) * side]
        far_ref[at + k] = far
        power = power + (far[:, :side] * far[:, :side] + far[:, side:] * far[:, side:])
    return power, weight


def backward(modes, factor, direct, swapped, far_ref, exit_ref, at):
    side = factor.shape[0]
    grad_real = jnp.zeros((side, side), jnp.float32)
    grad_imag = jnp.zeros((side, side), jnp.float32)
    halves = []
    for k in range(len(modes)):
        fixed = (far_ref[at + k] * factor).astype(jnp.bfloat16)
        halves.append(wide(dot(swapped, tall(fixed)).astype(jnp.bfloat16)))
    back_all = dot(jnp.concatenate(halves, axis=0), direct)
    for k, mode in enumerate(modes):
        back = back_all[k * side : (k + 1) * side]
        exit_wave = exit_ref[at + k].astype(jnp.float32)
        real, imag = mode()
        diff_real = back[:, :side] - exit_wave[:side]
        diff_imag = back[:, side:] - exit_wave[side:]
        grad_real = grad_real + (real * diff_real + imag * diff_imag)
        grad_imag = grad_imag + (real * diff_imag - imag * diff_real)
    return grad_real, grad_imag


def near_kernel(sides, slots, z_count, x_count, record_ref, *refs):
    n_pieces = 3 + 3 * sides
    pieces = from_sent_order(refs[:n_pieces])
    own, core, direct, swapped = refs[n_pieces : n_pieces + 4]
    patch_ref, far_ref, exit_ref, sum_ref, ext_ref = refs[n_pieces + 4 :]
    side = own.shape[2]
    patch = patch_of(sides, slots, z_count, x_count, side, record_ref, pieces, ext_ref)
    patch_ref[0], patch_ref[1] = patch
    tables = (direct[...], swapped[...], far_ref, exit_ref)
    first = forward(modes_of(own), patch, *tables, 0)
    second = forward(modes_of(core), patch, *tables, own.shape[1])
    sum_ref[0] = first[0] + second[0]
    sum_ref[1] = first[1] + second[1]


def over_kernel(patch_ref, over_y, over_x, rest, direct, swapped, far_ref, exit_ref, sum_ref):
    patch = (patch_ref[0], patch_ref[1])
    modes = [shared_mode(over_y, over_x)] + modes_of(rest)
    sum_ref[0], sum_ref[1] = forward(
        modes, patch, direct[...], swapped[...], far_ref, exit_ref, 0
    )


def back_kernel(sides, slots, x_count, tile_rows, tile_cols, record_ref, *refs):
    n_pieces = 3 + 3 * sides
    amplitude_ref, patch_ref, own, core = refs[:4]
    over_modes = [shared_mode(*refs[4:6])] + modes_of(refs[6])
    last_modes = [shared_mode(*refs[7:9])] + modes_of(refs[9])
    direct_ref, swapped_ref = refs[10:12]
    near_far, near_exit, near_sum, over_far, over_exit, over_sum = refs[12:18]
    outs = refs[18 : 18 + n_pieces + 1]
    last_far, last_exit, grad_ref = refs[18 + n_pieces + 1 :]
    side = own.shape[2]
    half = side // 2
    modes = own.shape[1]
    ext_rows = tile_rows + side
    ext_cols = tile_cols + sides * half
    _, x_index, parity = here()
    row_at, col_at, is_live = positions(record_ref, slots)
    direct = direct_ref[...]
    swapped = swapped_ref[...]
    patch = (patch_ref[0], patch_ref[1])
    power, weight = forward(last_modes, patch, direct, swapped, last_far, last_exit, 0)
    power = near_sum[0] + (over_sum[0] + power)
    weight = near_sum[1] + (over_sum[1] + weight)
    outs[-1][...] = weight.astype(jnp.bfloat16)
    amplitude = amplitude_ref[0, 0, parity].astype(jnp.float32)
    factor = amplitude / jnp.sqrt(power + power_floor)
    factor = jnp.concatenate([factor, factor], axis=1)
    tables = (factor, direct, swapped)
    grads = [
        backward(modes_of(own), *tables, near_far, near_exit, 0),
        backward(modes_of(core), *tables, near_far, near_exit, modes),
        backward(over_modes, *tables, over_far, over_exit, 0),
        backward(last_modes, *tables, last_far, last_exit, 0),
    ]
    at = iota((side, ext_cols), 1)
    column = column_coordinate(at, tile_cols, half, sides, x_index, x_count)
    put_cols = ((column == iota((side, ext_cols), 0) + col_at) & is_live).astype(jnp.bfloat16)
    put_rows = (iota((ext_rows, side), 0) == iota((ext_rows, side), 1) + row_at).astype(
        jnp.bfloat16
    )
    a_at, b_at = row_starts(half, tile_rows, parity)
    for channel in range(2):
        gradient = (grads[0][channel] + grads[1][channel]) + (grads[2][channel] + grads[3][channel])
        placed = dot(put_rows, gradient.astype(jnp.bfloat16)).astype(jnp.bfloat16)
        grad_ref[...] = dot(placed, put_cols).astype(jnp.bfloat16)
        rows = slice(channel * half, (channel + 1) * half)
        for index in range(1 + sides):
            columns = (
                slice(0, tile_cols)
                if index == 0
                else slice(tile_cols + (index - 1) * half, tile_cols + index * half)
            )
            outs[3 * index][rows] = grad_ref[half : half + tile_rows, columns]
            outs[3 * index + 1][rows] = grad_ref[pl.ds(b_at, half), columns]
            outs[3 * index + 2][rows] = grad_ref[pl.ds(a_at, half), columns]
    for out in outs[:n_pieces]:
        out[2 * half :] = record_ref[:, : out.shape[1]]


def weight_kernel(sides, slots, z_count, x_count, weight_ref, *refs):
    pieces, out_ref = from_sent_order(refs[:-1]), refs[-1]
    tile_rows, tile_cols = out_ref.shape
    side = weight_ref.shape[0]
    half = side // 2
    z_index, x_index, parity = here()
    z_step_a = jnp.where(parity == 0, -1, 1)
    if sides == 1:
        x_steps = [0, jnp.where(x_index == 0, 1, -1)]
        x_shown = [True, True]
    else:
        x_steps = [0, 1, -1]
        x_shown = [True, x_index < x_count - 1, x_index > 0]
    weight = weight_ref[...]
    total = jnp.zeros((tile_rows, tile_cols), jnp.float32)
    for index, x_step in enumerate(x_steps):
        turns = []
        for turn, z_step in enumerate((0, z_step_a, -z_step_a)):
            part = jnp.zeros((tile_rows, tile_cols), jnp.float32)
            z_tile = z_index + z_step
            shown = (z_tile >= 0) & (z_tile < z_count) & x_shown[index]
            record = pieces[3 * index + turn][2 * half :].astype(jnp.float32)
            record = record.astype(jnp.int32)
            if record.shape[1] < side:
                record = jnp.concatenate([record] * (side // record.shape[1]), axis=1)
            count = record[2 * slots : 2 * slots + 1, :side]
            for slot in range(slots):
                row = record[2 * slot : 2 * slot + 1, :side] + (z_step * tile_rows - half)
                col = record[2 * slot + 1 : 2 * slot + 2, :side] + (x_step * tile_cols - half)
                row = jnp.where((count > slot) & shown, row, nowhere)
                put_rows = (
                    iota((tile_rows, side), 0) == iota((tile_rows, side), 1) + row
                ).astype(jnp.bfloat16)
                put_cols = (
                    iota((side, tile_cols), 1) == iota((side, tile_cols), 0) + col[:, :1]
                ).astype(jnp.bfloat16)
                placed = dot(put_rows, weight).astype(jnp.bfloat16)
                part = part + dot(placed, put_cols)
            turns.append(part)
        total = total + (turns[0] + (turns[1] + turns[2]))
    out_ref[...] = total + regularizer


def sum_kernel(sides, z_count, x_count, *refs):
    pieces, out_ref = from_sent_order(refs[:-1]), refs[-1]
    own_ref, rows_a, rows_b = pieces[:3]
    _, tile_rows, tile_cols = out_ref.shape
    half = pieces[3].shape[1]
    z_index, x_index, parity = here()
    below = z_index > 0
    above = z_index < z_count - 1
    a_on = jnp.where(parity == 0, below, above)
    b_on = jnp.where(parity == 0, above, below)

    for channel in range(2):
        rows = slice(channel * tile_rows, (channel + 1) * tile_rows)

        def gate(on, ref, rows=rows):
            return jnp.where(on, ref[rows].astype(jnp.float32), 0.0)

        total = own_ref[rows].astype(jnp.float32)
        total = total + gate(a_on, rows_a) + gate(b_on, rows_b)
        first = jnp.zeros((tile_rows, half), jnp.float32)
        last = first
        for index in range(sides):
            level, corner_a, corner_b = pieces[3 + 3 * index : 6 + 3 * index]
            edge = level[rows].astype(jnp.float32)
            edge = edge + gate(a_on, corner_a) + gate(b_on, corner_b)
            if sides == 1:
                first = jnp.where(x_index == 1, edge, 0.0)
                last = jnp.where(x_index == 0, edge, 0.0)
            elif index == 0:
                last = jnp.where(x_index < x_count - 1, edge, 0.0)
            else:
                first = jnp.where(x_index > 0, edge, 0.0)
        zero = jnp.zeros((tile_rows, tile_cols - 2 * half), jnp.float32)
        parts = [first, zero, last] if tile_cols > 2 * half else [first, last]
        total = total + jnp.concatenate(parts, axis=1)
        out_ref[channel] = total.astype(jnp.bfloat16)


def update_kernel(object_ref, own_ref, other_ref, weight_ref, out_ref):
    for channel in range(2):
        gradient = own_ref[channel].astype(jnp.float32) + other_ref[channel].astype(jnp.float32)
        out_ref[channel] = object_ref[channel] + gradient / weight_ref[...]


def in_hbm(array):
    return pltpu.with_memory_space_constraint(array, pltpu.HBM)


def smem():
    return pl.BlockSpec(memory_space=pltpu.SMEM)


def hbm():
    return pl.BlockSpec(memory_space=pltpu.HBM)


def vmem():
    return pl.BlockSpec(memory_space=pltpu.VMEM)


def on_device(object_field, probe, amplitudes, centers, live):
    side = probe.shape[2]
    half = side // 2
    _, tile_rows, tile_cols = object_field.shape
    slots = centers.shape[2]
    z_count = lax.axis_size("tx")
    x_count = lax.axis_size("ty")
    m_count = lax.axis_size("mode")
    modes = probe.shape[1]
    if tile_rows != half or slots != 2 or m_count != 4 or x_count % 2 or modes < 2:
        raise ValueError("unsupported sizes")
    sides = 1 if x_count == 2 else 2
    axes = ("tx", "ty", "mode")

    def zigzag(x_step, flip=False):
        def moved(z, m):
            down = (m % 2 == 0) != flip
            if down:
                return (z + 1, m) if z < z_count - 1 else (z, m ^ 1)
            return (z - 1, m) if z > 0 else (z, m ^ 1)

        pairs = []
        for z in range(z_count):
            for x in range(x_count):
                for m in range(m_count):
                    z_to, m_to = moved(z, m)
                    x_to = (x + x_step) % x_count
                    pairs.append(
                        (
                            (z * x_count + x) * m_count + m,
                            (z_to * x_count + x_to) * m_count + m_to,
                        )
                    )
        return pairs

    def level(step):
        return [(x, (x + step) % x_count) for x in range(x_count)]

    def exchange(array, flip):
        return lax.ppermute(array, "mode", [(m, m ^ flip) for m in range(m_count)])

    tables = [jnp.asarray(matrix) for matrix in dft_matrices(side)]
    probe_low, shared, rest, record, direct, swapped, *packed = pl.pallas_call(
        functools.partial(start_kernel, sides, slots),
        out_shape=[
            jax.ShapeDtypeStruct(probe.shape, jnp.bfloat16),
            jax.ShapeDtypeStruct((side, side), jnp.bfloat16),
            jax.ShapeDtypeStruct((2, modes - 1, side, side), jnp.bfloat16),
            jax.ShapeDtypeStruct((record_rows, tile_cols), jnp.bfloat16),
            jax.ShapeDtypeStruct((2 * side, 2 * side), jnp.bfloat16),
            jax.ShapeDtypeStruct((2 * side, 2 * side), jnp.bfloat16),
            jax.ShapeDtypeStruct(object_field.shape, jnp.bfloat16),
        ]
        + [jax.ShapeDtypeStruct((2, tile_rows, half), jnp.bfloat16)] * sides,
        in_specs=[hbm()] * 5,
        out_specs=[vmem()] * (7 + sides),
        scratch_shapes=[
            pltpu.VMEM(object_field.shape, jnp.float32),
            pltpu.VMEM(probe.shape, jnp.float32),
            pltpu.SMEM(centers.shape, jnp.int32),
            pltpu.SemaphoreType.DMA((5,)),
        ],
        compiler_params=pltpu.CompilerParams(vmem_limit_bytes=small_bytes),
        name="start",
    )(*(in_hbm(array) for array in (object_field, probe, centers, *tables)))
    over_y = exchange(shared, 2)
    probe_core = exchange(probe_low, 1)
    probe_core, rest, live = lax.optimization_barrier((probe_core, rest, live))
    rest = exchange(rest, 2)
    over_x = lax.ppermute(over_y, "ty", [(x, x ^ 1) for x in range(x_count)])
    x_steps = [1] if sides == 1 else [1, -1]
    rows = lax.ppermute(packed[0], axes, zigzag(0))
    corners = [lax.ppermute(edge, axes, zigzag(step)) for step, edge in zip(x_steps, packed[1:])]
    levels = [lax.ppermute(edge, "ty", level(step)) for step, edge in zip(x_steps, packed[1:])]
    record = pl.pallas_call(
        functools.partial(live_kernel, slots),
        out_shape=jax.ShapeDtypeStruct(record.shape, jnp.bfloat16),
        in_specs=[vmem(), smem()],
        out_specs=vmem(),
        compiler_params=pltpu.CompilerParams(vmem_limit_bytes=small_bytes),
        name="live",
    )(record, live)
    rows, record, *levels = lax.optimization_barrier((rows, record, *levels))
    pieces = [packed[0], rows, exchange(rows, 1)]
    for at_level, corner in zip(levels, corners):
        pieces += [at_level, corner, exchange(corner, 1)]
    n_pieces = len(pieces)
    ext_rows = tile_rows + side
    ext_cols = tile_cols + sides * half

    def waves(count):
        return [
            jax.ShapeDtypeStruct((count, side, 2 * side), jnp.float32),
            jax.ShapeDtypeStruct((count, 2 * side, side), jnp.bfloat16),
            jax.ShapeDtypeStruct((2, side, side), jnp.float32),
        ]

    patch, *near = pl.pallas_call(
        functools.partial(near_kernel, sides, slots, z_count, x_count),
        out_shape=[jax.ShapeDtypeStruct((2, side, side), jnp.float32)] + waves(2 * modes),
        in_specs=[vmem()] * (n_pieces + 5),
        out_specs=[vmem()] * 4,
        scratch_shapes=[pltpu.VMEM((2 * ext_rows, ext_cols), jnp.bfloat16)],
        compiler_params=pltpu.CompilerParams(vmem_limit_bytes=wave_bytes),
        name="near",
    )(record, *in_sent_order(pieces), probe_low, probe_core, direct, swapped)
    over_x, rest, patch = lax.optimization_barrier((over_x, rest, patch))
    over_group = (over_y, over_x, rest)
    last_group = [exchange(part, 1) for part in over_group]
    over = pl.pallas_call(
        over_kernel,
        out_shape=waves(modes),
        in_specs=[vmem()] * 6,
        out_specs=[vmem()] * 3,
        compiler_params=pltpu.CompilerParams(vmem_limit_bytes=wave_bytes),
        name="over",
    )(patch, *over_group, direct, swapped)
    shapes = [(2 * half + record_rows, tile_cols)] * 3
    shapes += [(2 * half + record_rows, half)] * (3 * sides)
    results = pl.pallas_call(
        functools.partial(back_kernel, sides, slots, x_count, tile_rows, tile_cols),
        out_shape=[jax.ShapeDtypeStruct(shape, jnp.bfloat16) for shape in shapes]
        + [jax.ShapeDtypeStruct((side, side), jnp.bfloat16)],
        in_specs=[vmem()] * 19,
        out_specs=[vmem()] * (n_pieces + 1),
        scratch_shapes=[
            pltpu.VMEM((modes, side, 2 * side), jnp.float32),
            pltpu.VMEM((modes, 2 * side, side), jnp.bfloat16),
            pltpu.VMEM((ext_rows, ext_cols), jnp.bfloat16),
        ],
        compiler_params=pltpu.CompilerParams(vmem_limit_bytes=wave_bytes),
        name="back",
    )(
        record,
        amplitudes,
        patch,
        probe_low,
        probe_core,
        *over_group,
        *last_group,
        direct,
        swapped,
        *near,
        *over,
    )
    received = [results[0]] + [None] * (n_pieces - 1)
    for index, step in enumerate(x_steps):
        at = 3 + 3 * index
        for turn, flip in enumerate((False, True)):
            received[at + 1 + turn] = lax.ppermute(results[at + 1 + turn], axes, zigzag(-step, flip))
    for turn, flip in enumerate((False, True)):
        received[1 + turn] = lax.ppermute(results[1 + turn], axes, zigzag(0, flip))
    for index, step in enumerate(x_steps):
        received[3 + 3 * index] = lax.ppermute(results[3 + 3 * index], "ty", level(-step))
    summed = pl.pallas_call(
        functools.partial(sum_kernel, sides, z_count, x_count),
        out_shape=jax.ShapeDtypeStruct(object_field.shape, jnp.bfloat16),
        in_specs=[vmem()] * n_pieces,
        out_specs=vmem(),
        compiler_params=pltpu.CompilerParams(vmem_limit_bytes=small_bytes),
        name="sums",
    )(*in_sent_order(received))
    weight = pl.pallas_call(
        functools.partial(weight_kernel, sides, slots, z_count, x_count),
        out_shape=jax.ShapeDtypeStruct((tile_rows, tile_cols), jnp.float32),
        in_specs=[vmem()] * (n_pieces + 1),
        out_specs=vmem(),
        compiler_params=pltpu.CompilerParams(vmem_limit_bytes=small_bytes),
        name="weights",
    )(results[-1], *in_sent_order(received))
    other = exchange(summed, 1)
    return pl.pallas_call(
        update_kernel,
        out_shape=jax.ShapeDtypeStruct(object_field.shape, jnp.float32),
        in_specs=[vmem()] * 4,
        out_specs=vmem(),
        compiler_params=pltpu.CompilerParams(vmem_limit_bytes=small_bytes),
        name="update",
    )(object_field, summed, other, weight)


def solution(mesh):
    return jax.shard_map(
        on_device,
        mesh=mesh,
        in_specs=(
            P(None, "tx", "ty"),
            P(None, "mode", None, None),
            P("tx", "ty", None, None, None),
            P("tx", "ty", None, None),
            P("tx", "ty"),
        ),
        out_specs=P(None, "tx", "ty"),
        check_vma=False,
    )
```

```python
import functools
import math

import jax
import jax.numpy as jnp
import numpy as np
from jax import lax
from jax.experimental import pallas as pl
from jax.experimental.pallas import tpu as pltpu
from jax.sharding import PartitionSpec as P

power_floor = 0.01
regularizer = 0.1
nowhere = -(1 << 20)
record_rows = 16
wave_bytes = 32 * 1024 * 1024
small_bytes = 8 * 1024 * 1024


def dft_matrices(side):
    line = np.arange(side, dtype=np.int32)
    angle = (line[:, None] * line[None, :] % side).astype(np.float32) * np.float32(
        2.0 * math.pi / side
    )
    scaling = np.float32(1.0 / math.sqrt(side))
    real = (np.cos(angle) * scaling).astype(jnp.bfloat16)
    imag = (-np.sin(angle) * scaling).astype(jnp.bfloat16)
    direct = np.block([[real, -imag], [imag, real]])
    swapped = np.block([[real, imag], [-imag, real]])
    return direct, swapped


def dot(left, right):
    return jnp.dot(left, right, preferred_element_type=jnp.float32)


def iota(shape, dim):
    return lax.broadcasted_iota(jnp.int32, shape, dim)


def column_coordinate(at, tile_cols, half, sides, x_index, x_count):
    own = at + half
    if sides == 1:
        side = at - tile_cols + jnp.where(x_index == 0, half + tile_cols, 0)
        return jnp.where(at < tile_cols, own, side)
    left = jnp.where(x_index > 0, at - tile_cols, nowhere)
    right = jnp.where(x_index < x_count - 1, at, nowhere)
    return jnp.where(at < tile_cols, own, jnp.where(at < tile_cols + half, left, right))


def sent_order(sides):
    corners = [at for index in range(sides) for at in (4 + 3 * index, 5 + 3 * index)]
    return [0] + corners + [1, 2] + [3 + 3 * index for index in range(sides)]


def in_sent_order(pieces):
    return [pieces[at] for at in sent_order(len(pieces) // 3 - 1)]


def from_sent_order(pieces):
    order = sent_order(len(pieces) // 3 - 1)
    return [pieces[order.index(at)] for at in range(len(pieces))]


def wide(tall):
    side = tall.shape[0] // 2
    return jnp.concatenate([tall[:side], tall[side:]], axis=1)


def tall(wide):
    side = wide.shape[1] // 2
    return jnp.concatenate([wide[:, :side], wide[:, side:]], axis=0)


def here():
    return (lax.axis_index("tx"), lax.axis_index("ty"), lax.axis_index("mode") % 2)


def start_kernel(
    sides,
    slots,
    object_hbm,
    probe_hbm,
    centers_hbm,
    direct_hbm,
    swapped_hbm,
    low_ref,
    shared_ref,
    rest_ref,
    record_ref,
    direct_ref,
    swapped_ref,
    packed_ref,
    *refs,
):
    edges = refs[:sides]
    object_ref, probe_ref, centers_ref, sems = refs[sides:]
    copies = [
        pltpu.make_async_copy(source, target, sems.at[index])
        for index, (source, target) in enumerate(
            (
                (probe_hbm, probe_ref),
                (object_hbm, object_ref),
                (centers_hbm, centers_ref),
                (direct_hbm, direct_ref),
                (swapped_hbm, swapped_ref),
            )
        )
    ]
    for copy in copies:
        copy.start()
    tile_cols = object_ref.shape[2]
    half = edges[0].shape[2]
    _, x_index, _ = here()
    copies[0].wait()
    low_ref[...] = probe_ref[...].astype(jnp.bfloat16)
    shared_ref[...] = jnp.where(x_index % 2 == 0, low_ref[0, 0], low_ref[1, 0])
    rest_ref[...] = low_ref[:, 1:]
    copies[1].wait()
    first, last = slice(0, half), slice(tile_cols - half, tile_cols)
    for channel in range(2):
        values = object_ref[channel].astype(jnp.bfloat16)
        packed_ref[channel] = values
        if sides == 1:
            edges[0][channel] = jnp.where(x_index == 0, values[:, last], values[:, first])
        else:
            edges[0][channel] = values[:, last]
            edges[1][channel] = values[:, first]
    copies[2].wait()
    record = jnp.zeros(record_ref.shape, jnp.float32)
    line = iota(record_ref.shape, 0)
    for slot in range(slots):
        for axis in range(2):
            value = centers_ref[0, 0, slot, axis].astype(jnp.float32)
            record = jnp.where(line == 2 * slot + axis, value, record)
    record_ref[...] = record.astype(jnp.bfloat16)
    copies[3].wait()
    copies[4].wait()


def live_kernel(slots, record_ref, live_ref, out_ref):
    line = iota(record_ref.shape, 0)
    record = record_ref[...].astype(jnp.float32)
    record = jnp.where(line == 2 * slots, live_ref[0, 0].astype(jnp.float32), record)
    out_ref[...] = record.astype(jnp.bfloat16)


def position_of(record, slots, wanted):
    record = record[:, :128].astype(jnp.float32).astype(jnp.int32)[:, :1]

    def of_slot(axis):
        value = record[axis : axis + 1]
        for slot in range(1, slots):
            value = jnp.where(wanted == slot, record[2 * slot + axis : 2 * slot + axis + 1], value)
        return value

    return of_slot(0), of_slot(1), record[2 * slots : 2 * slots + 1] > wanted


def row_starts(half, tile_rows, parity):
    low, high = 0, half + tile_rows
    return (
        pl.multiple_of(jnp.where(parity == 0, low, high), half),
        pl.multiple_of(jnp.where(parity == 0, high, low), half),
    )


def patch_of(sides, slots, z_count, x_count, side, record_ref, pieces, ext_ref):
    z_index, x_index, parity = here()
    row_at, col_at, _ = position_of(record_ref, slots, parity)
    half = side // 2
    _, tile_rows, tile_cols = pieces[0].shape
    ext_rows = tile_rows + side
    ext_cols = tile_cols + sides * half
    a_at, b_at = row_starts(half, tile_rows, parity)
    for channel in range(2):
        base = channel * ext_rows
        for index in range(1 + sides):
            columns = (
                slice(0, tile_cols)
                if index == 0
                else slice(tile_cols + (index - 1) * half, tile_cols + index * half)
            )
            level, turn_a, turn_b = pieces[3 * index : 3 * index + 3]
            ext_ref[pl.ds(base + half, tile_rows), columns] = level[channel]
            ext_ref[pl.ds(base + a_at, half), columns] = turn_a[channel]
            ext_ref[pl.ds(base + b_at, half), columns] = turn_b[channel]
    at = iota((ext_cols, side), 0)
    column = column_coordinate(at, tile_cols, half, sides, x_index, x_count)
    pick_cols = (column == iota((ext_cols, side), 1) + col_at).astype(jnp.bfloat16)
    at = iota((side, ext_rows), 1)
    first = jnp.where(z_index > 0, 0, half)
    last = jnp.where(z_index < z_count - 1, ext_rows, half + tile_rows)
    row = jnp.where((at >= first) & (at < last), at, nowhere)
    pick_rows = (row == iota((side, ext_rows), 0) + row_at).astype(jnp.bfloat16)
    narrow = dot(ext_ref[...], pick_cols).astype(jnp.bfloat16)
    return dot(pick_rows, narrow[:ext_rows]), dot(pick_rows, narrow[ext_rows:])


def modes_of(group):
    def reader(k):
        return lambda: (group[0, k].astype(jnp.float32), group[1, k].astype(jnp.float32))

    return [reader(k) for k in range(group.shape[1])]


def shared_mode(over_y, over_x):
    def read():
        _, x_index, _ = here()
        even = x_index % 2 == 0
        over_y_values = over_y[...].astype(jnp.float32)
        over_x_values = over_x[...].astype(jnp.float32)
        return (
            jnp.where(even, over_y_values, over_x_values),
            jnp.where(even, over_x_values, over_y_values),
        )

    return read


def forward(modes, patch, direct, swapped, far_ref, exit_ref, at):
    patch_real, patch_imag = patch
    side = patch_real.shape[0]
    power = jnp.zeros((side, side), jnp.float32)
    weight = jnp.zeros((side, side), jnp.float32)
    halves = []
    for k, mode in enumerate(modes):
        real, imag = mode()
        exit_wave = jnp.concatenate(
            [
                (real * patch_real - imag * patch_imag).astype(jnp.bfloat16),
                (real * patch_imag + imag * patch_real).astype(jnp.bfloat16),
            ],
            axis=0,
        )
        exit_ref[at + k] = exit_wave
        halves.append(wide(dot(direct, exit_wave).astype(jnp.bfloat16)))
        weight = weight + (real * real + imag * imag)
    far_all = dot(jnp.concatenate(halves, axis=0), swapped)
    for k in range(len(modes)):
        far = far_all[k * side : (k + 1) * side]
        far_ref[at + k] = far
        power = power + (far[:, :side] * far[:, :side] + far[:, side:] * far[:, side:])
    return power, weight


def backward(modes, factor, direct, swapped, far_ref, exit_ref, at):
    side = factor.shape[0]
    grad_real = jnp.zeros((side, side), jnp.float32)
    grad_imag = jnp.zeros((side, side), jnp.float32)
    halves = []
    for k in range(len(modes)):
        fixed = (far_ref[at + k] * factor).astype(jnp.bfloat16)
        halves.append(wide(dot(swapped, tall(fixed)).astype(jnp.bfloat16)))
    back_all = dot(jnp.concatenate(halves, axis=0), direct)
    for k, mode in enumerate(modes):
        back = back_all[k * side : (k + 1) * side]
        exit_wave = exit_ref[at + k].astype(jnp.float32)
        real, imag = mode()
        diff_real = back[:, :side] - exit_wave[:side]
        diff_imag = back[:, side:] - exit_wave[side:]
        grad_real = grad_real + (real * diff_real + imag * diff_imag)
        grad_imag = grad_imag + (real * diff_imag - imag * diff_real)
    return grad_real, grad_imag


def near_kernel(sides, slots, z_count, x_count, record_ref, *refs):
    n_pieces = 3 + 3 * sides
    pieces = from_sent_order(refs[:n_pieces])
    own, core, direct, swapped = refs[n_pieces : n_pieces + 4]
    patch_ref, far_ref, exit_ref, sum_ref, ext_ref = refs[n_pieces + 4 :]
    side = own.shape[2]
    patch = patch_of(sides, slots, z_count, x_count, side, record_ref, pieces, ext_ref)
    patch_ref[0], patch_ref[1] = patch
    tables = (direct[...], swapped[...], far_ref, exit_ref)
    first = forward(modes_of(own), patch, *tables, 0)
    second = forward(modes_of(core), patch, *tables, own.shape[1])
    sum_ref[0] = first[0] + second[0]
    sum_ref[1] = first[1] + second[1]


def over_kernel(patch_ref, over_y, over_x, rest, direct, swapped, far_ref, exit_ref, sum_ref):
    patch = (patch_ref[0], patch_ref[1])
    modes = [shared_mode(over_y, over_x)] + modes_of(rest)
    sum_ref[0], sum_ref[1] = forward(
        modes, patch, direct[...], swapped[...], far_ref, exit_ref, 0
    )


def back_kernel(sides, slots, x_count, tile_rows, tile_cols, record_ref, *refs):
    amplitude_ref, patch_ref, own, core = refs[:4]
    over_modes = [shared_mode(*refs[4:6])] + modes_of(refs[6])
    last_modes = [shared_mode(*refs[7:9])] + modes_of(refs[9])
    direct_ref, swapped_ref = refs[10:12]
    near_far, near_exit, near_sum, over_far, over_exit, over_sum = refs[12:18]
    weight_out, own_out, keep_out, swap_out = refs[18:22]
    side_outs = refs[22 : 22 + sides]
    last_far, last_exit, grad_ref = refs[22 + sides :]
    side = own.shape[2]
    half = side // 2
    modes = own.shape[1]
    ext_rows = tile_rows + side
    ext_cols = tile_cols + sides * half
    _, x_index, parity = here()
    row_at, col_at, is_live = position_of(record_ref, slots, parity)
    direct = direct_ref[...]
    swapped = swapped_ref[...]
    patch = (patch_ref[0], patch_ref[1])
    power, weight = forward(last_modes, patch, direct, swapped, last_far, last_exit, 0)
    power = near_sum[0] + (over_sum[0] + power)
    weight = near_sum[1] + (over_sum[1] + weight)
    weight_out[...] = weight.astype(jnp.bfloat16)
    amplitude = amplitude_ref[0, 0, parity].astype(jnp.float32)
    factor = amplitude / jnp.sqrt(power + power_floor)
    factor = jnp.concatenate([factor, factor], axis=1)
    tables = (factor, direct, swapped)
    grads = [
        backward(modes_of(own), *tables, near_far, near_exit, 0),
        backward(modes_of(core), *tables, near_far, near_exit, modes),
        backward(over_modes, *tables, over_far, over_exit, 0),
        backward(last_modes, *tables, last_far, last_exit, 0),
    ]
    at = iota((side, ext_cols), 1)
    column = column_coordinate(at, tile_cols, half, sides, x_index, x_count)
    put_cols = ((column == iota((side, ext_cols), 0) + col_at) & is_live).astype(jnp.bfloat16)
    put_rows = (iota((ext_rows, side), 0) == iota((ext_rows, side), 1) + row_at).astype(
        jnp.bfloat16
    )
    a_at, b_at = row_starts(half, tile_rows, parity)
    for channel in range(2):
        gradient = (grads[0][channel] + grads[1][channel]) + (grads[2][channel] + grads[3][channel])
        placed = dot(put_rows, gradient.astype(jnp.bfloat16)).astype(jnp.bfloat16)
        grad_ref[...] = dot(placed, put_cols).astype(jnp.bfloat16)
        rows = slice(channel * half, (channel + 1) * half)
        own_out[rows] = grad_ref[half : half + tile_rows, :tile_cols]
        keep_out[rows] = grad_ref[pl.ds(b_at, half), :]
        swap_out[rows] = grad_ref[pl.ds(a_at, half), :]
        for index, out in enumerate(side_outs):
            columns = slice(tile_cols + index * half, tile_cols + (index + 1) * half)
            out[rows] = grad_ref[half : half + tile_rows, columns]
    for out in side_outs:
        out[2 * half :] = record_ref[:, :half]


def meet_kernel(record_ref, keep_ref, swap_ref, rows_out, *corner_outs):
    total = keep_ref[...].astype(jnp.float32) + swap_ref[...].astype(jnp.float32)
    total = total.astype(jnp.bfloat16)
    height = total.shape[0]
    tile_cols = rows_out.shape[1]
    rows_out[:height] = total[:, :tile_cols]
    rows_out[height:] = record_ref[...]
    for index, out in enumerate(corner_outs):
        half = out.shape[1]
        out[:height] = total[:, tile_cols + index * half : tile_cols + (index + 1) * half]
        out[height:] = record_ref[:, :half]


def sum_kernel(sides, slots, z_count, x_count, weight_ref, record_ref, own_ref, rows_ref, *refs):
    corners, levels, out_ref = refs[:sides], refs[sides:-1], refs[-1]
    _, tile_rows, tile_cols = out_ref.shape
    side = weight_ref.shape[0]
    half = side // 2
    z_index, x_index, parity = here()
    z_step = jnp.where(parity == 0, -1, 1)
    z_shown = jnp.where(parity == 0, z_index > 0, z_index < z_count - 1)
    if sides == 1:
        x_steps = [jnp.where(x_index == 0, 1, -1)]
        x_shown = [z_index >= 0]
    else:
        x_steps = [1, -1]
        x_shown = [x_index < x_count - 1, x_index > 0]
    weight = weight_ref[...]

    def placed(position, z_step, x_step, shown):
        row, col, is_live = position
        row = jnp.where(is_live & shown, row + (z_step * tile_rows - half), nowhere)
        col = col + (x_step * tile_cols - half)
        put_rows = (iota((tile_rows, side), 0) == iota((tile_rows, side), 1) + row).astype(
            jnp.bfloat16
        )
        put_cols = (iota((side, tile_cols), 1) == iota((side, tile_cols), 0) + col).astype(
            jnp.bfloat16
        )
        return dot(dot(put_rows, weight).astype(jnp.bfloat16), put_cols)

    total = placed(position_of(record_ref, slots, parity), 0, 0, z_index >= 0)
    for level, x_step, shown in zip(levels, x_steps, x_shown):
        record = level[2 * half :]
        total = total + placed(position_of(record, slots, parity), 0, x_step, shown)
    for piece, x_step, shown in zip(
        (rows_ref,) + corners, [0] + x_steps, [z_index >= 0] + x_shown
    ):
        record = piece[2 * half :]
        for slot in range(slots):
            position = position_of(record, slots, slot)
            total = total + placed(position, z_step, x_step, shown & z_shown)
    out_ref[2] = total.astype(jnp.bfloat16)

    for channel in range(2):
        rows = slice(channel * tile_rows, (channel + 1) * tile_rows)

        def values(ref, rows=rows):
            return ref[rows].astype(jnp.float32)

        total = values(own_ref) + jnp.where(z_shown, values(rows_ref), 0.0)
        first = jnp.zeros((tile_rows, half), jnp.float32)
        last = first
        for index in range(sides):
            edge = values(levels[index]) + jnp.where(z_shown, values(corners[index]), 0.0)
            if sides == 1:
                first = jnp.where(x_index == 1, edge, 0.0)
                last = jnp.where(x_index == 0, edge, 0.0)
            elif index == 0:
                last = jnp.where(x_shown[0], edge, 0.0)
            else:
                first = jnp.where(x_shown[1], edge, 0.0)
        zero = jnp.zeros((tile_rows, tile_cols - 2 * half), jnp.float32)
        parts = [first, zero, last] if tile_cols > 2 * half else [first, last]
        total = total + jnp.concatenate(parts, axis=1)
        out_ref[channel] = total.astype(jnp.bfloat16)


def update_kernel(object_ref, own_ref, other_ref, out_ref):
    weight = own_ref[2].astype(jnp.float32) + other_ref[2].astype(jnp.float32) + regularizer
    for channel in range(2):
        gradient = own_ref[channel].astype(jnp.float32) + other_ref[channel].astype(jnp.float32)
        out_ref[channel] = object_ref[channel] + gradient / weight


def in_hbm(array):
    return pltpu.with_memory_space_constraint(array, pltpu.HBM)


def smem():
    return pl.BlockSpec(memory_space=pltpu.SMEM)


def hbm():
    return pl.BlockSpec(memory_space=pltpu.HBM)


def vmem():
    return pl.BlockSpec(memory_space=pltpu.VMEM)


def on_device(object_field, probe, amplitudes, centers, live):
    side = probe.shape[2]
    half = side // 2
    _, tile_rows, tile_cols = object_field.shape
    slots = centers.shape[2]
    z_count = lax.axis_size("tx")
    x_count = lax.axis_size("ty")
    m_count = lax.axis_size("mode")
    modes = probe.shape[1]
    if tile_rows != half or slots != 2 or m_count != 4 or x_count % 2 or modes < 2:
        raise ValueError("unsupported sizes")
    sides = 1 if x_count == 2 else 2
    axes = ("tx", "ty", "mode")

    def zigzag(x_step):
        def moved(z, m):
            if m % 2 == 0:
                return (z + 1, m) if z < z_count - 1 else (z, m ^ 1)
            return (z - 1, m) if z > 0 else (z, m ^ 1)

        pairs = []
        for z in range(z_count):
            for x in range(x_count):
                for m in range(m_count):
                    z_to, m_to = moved(z, m)
                    x_to = (x + x_step) % x_count
                    pairs.append(
                        (
                            (z * x_count + x) * m_count + m,
                            (z_to * x_count + x_to) * m_count + m_to,
                        )
                    )
        return pairs

    def level(step):
        return [(x, (x + step) % x_count) for x in range(x_count)]

    def exchange(array, flip):
        return lax.ppermute(array, "mode", [(m, m ^ flip) for m in range(m_count)])

    tables = [jnp.asarray(matrix) for matrix in dft_matrices(side)]
    probe_low, shared, rest, record, direct, swapped, *packed = pl.pallas_call(
        functools.partial(start_kernel, sides, slots),
        out_shape=[
            jax.ShapeDtypeStruct(probe.shape, jnp.bfloat16),
            jax.ShapeDtypeStruct((side, side), jnp.bfloat16),
            jax.ShapeDtypeStruct((2, modes - 1, side, side), jnp.bfloat16),
            jax.ShapeDtypeStruct((record_rows, tile_cols), jnp.bfloat16),
            jax.ShapeDtypeStruct((2 * side, 2 * side), jnp.bfloat16),
            jax.ShapeDtypeStruct((2 * side, 2 * side), jnp.bfloat16),
            jax.ShapeDtypeStruct(object_field.shape, jnp.bfloat16),
        ]
        + [jax.ShapeDtypeStruct((2, tile_rows, half), jnp.bfloat16)] * sides,
        in_specs=[hbm()] * 5,
        out_specs=[vmem()] * (7 + sides),
        scratch_shapes=[
            pltpu.VMEM(object_field.shape, jnp.float32),
            pltpu.VMEM(probe.shape, jnp.float32),
            pltpu.SMEM(centers.shape, jnp.int32),
            pltpu.SemaphoreType.DMA((5,)),
        ],
        compiler_params=pltpu.CompilerParams(vmem_limit_bytes=small_bytes),
        name="start",
    )(*(in_hbm(array) for array in (object_field, probe, centers, *tables)))
    over_y = exchange(shared, 2)
    probe_core = exchange(probe_low, 1)
    probe_core, rest, live = lax.optimization_barrier((probe_core, rest, live))
    rest = exchange(rest, 2)
    over_x = lax.ppermute(over_y, "ty", [(x, x ^ 1) for x in range(x_count)])
    x_steps = [1] if sides == 1 else [1, -1]
    rows = lax.ppermute(packed[0], axes, zigzag(0))
    corners = [lax.ppermute(edge, axes, zigzag(step)) for step, edge in zip(x_steps, packed[1:])]
    levels = [lax.ppermute(edge, "ty", level(step)) for step, edge in zip(x_steps, packed[1:])]
    record = pl.pallas_call(
        functools.partial(live_kernel, slots),
        out_shape=jax.ShapeDtypeStruct(record.shape, jnp.bfloat16),
        in_specs=[vmem(), smem()],
        out_specs=vmem(),
        compiler_params=pltpu.CompilerParams(vmem_limit_bytes=small_bytes),
        name="live",
    )(record, live)
    rows, record, *levels = lax.optimization_barrier((rows, record, *levels))
    pieces = [packed[0], rows, exchange(rows, 1)]
    for at_level, corner in zip(levels, corners):
        pieces += [at_level, corner, exchange(corner, 1)]
    n_pieces = len(pieces)
    ext_rows = tile_rows + side
    ext_cols = tile_cols + sides * half

    def waves(count):
        return [
            jax.ShapeDtypeStruct((count, side, 2 * side), jnp.float32),
            jax.ShapeDtypeStruct((count, 2 * side, side), jnp.bfloat16),
            jax.ShapeDtypeStruct((2, side, side), jnp.float32),
        ]

    patch, *near = pl.pallas_call(
        functools.partial(near_kernel, sides, slots, z_count, x_count),
        out_shape=[jax.ShapeDtypeStruct((2, side, side), jnp.float32)] + waves(2 * modes),
        in_specs=[vmem()] * (n_pieces + 5),
        out_specs=[vmem()] * 4,
        scratch_shapes=[pltpu.VMEM((2 * ext_rows, ext_cols), jnp.bfloat16)],
        compiler_params=pltpu.CompilerParams(vmem_limit_bytes=wave_bytes),
        name="near",
    )(record, *in_sent_order(pieces), probe_low, probe_core, direct, swapped)
    over_x, rest, patch = lax.optimization_barrier((over_x, rest, patch))
    over_group = (over_y, over_x, rest)
    last_group = [exchange(part, 1) for part in over_group]
    over = pl.pallas_call(
        over_kernel,
        out_shape=waves(modes),
        in_specs=[vmem()] * 6,
        out_specs=[vmem()] * 3,
        compiler_params=pltpu.CompilerParams(vmem_limit_bytes=wave_bytes),
        name="over",
    )(patch, *over_group, direct, swapped)
    piece_rows = 2 * half + record_rows
    shapes = [(side, side), (2 * half, tile_cols)] + [(2 * half, ext_cols)] * 2
    shapes += [(piece_rows, half)] * sides
    weight, own, keep, swap, *levels = pl.pallas_call(
        functools.partial(back_kernel, sides, slots, x_count, tile_rows, tile_cols),
        out_shape=[jax.ShapeDtypeStruct(shape, jnp.bfloat16) for shape in shapes],
        in_specs=[vmem()] * 19,
        out_specs=[vmem()] * (4 + sides),
        scratch_shapes=[
            pltpu.VMEM((modes, side, 2 * side), jnp.float32),
            pltpu.VMEM((modes, 2 * side, side), jnp.bfloat16),
            pltpu.VMEM((ext_rows, ext_cols), jnp.bfloat16),
        ],
        compiler_params=pltpu.CompilerParams(vmem_limit_bytes=wave_bytes),
        name="back",
    )(
        record,
        amplitudes,
        patch,
        probe_low,
        probe_core,
        *over_group,
        *last_group,
        direct,
        swapped,
        *near,
        *over,
    )
    levels = [lax.ppermute(piece, "ty", level(-step)) for piece, step in zip(levels, x_steps)]
    rows, *corners = pl.pallas_call(
        meet_kernel,
        out_shape=[jax.ShapeDtypeStruct((piece_rows, tile_cols), jnp.bfloat16)]
        + [jax.ShapeDtypeStruct((piece_rows, half), jnp.bfloat16)] * sides,
        in_specs=[vmem()] * 3,
        out_specs=[vmem()] * (1 + sides),
        compiler_params=pltpu.CompilerParams(vmem_limit_bytes=small_bytes),
        name="meet",
    )(record, keep, exchange(swap, 1))
    corners = [
        lax.ppermute(piece, axes, zigzag(-step)) for piece, step in zip(corners, x_steps)
    ]
    rows = lax.ppermute(rows, axes, zigzag(0))
    summed = pl.pallas_call(
        functools.partial(sum_kernel, sides, slots, z_count, x_count),
        out_shape=jax.ShapeDtypeStruct((3, tile_rows, tile_cols), jnp.bfloat16),
        in_specs=[vmem()] * (4 + 2 * sides),
        out_specs=vmem(),
        compiler_params=pltpu.CompilerParams(vmem_limit_bytes=small_bytes),
        name="sums",
    )(weight, record, own, rows, *corners, *levels)
    return pl.pallas_call(
        update_kernel,
        out_shape=jax.ShapeDtypeStruct(object_field.shape, jnp.float32),
        in_specs=[vmem()] * 3,
        out_specs=vmem(),
        compiler_params=pltpu.CompilerParams(vmem_limit_bytes=small_bytes),
        name="update",
    )(object_field, summed, exchange(summed, 1))


def solution(mesh):
    return jax.shard_map(
        on_device,
        mesh=mesh,
        in_specs=(
            P(None, "tx", "ty"),
            P(None, "mode", None, None),
            P("tx", "ty", None, None, None),
            P("tx", "ty", None, None),
            P("tx", "ty"),
        ),
        out_specs=P(None, "tx", "ty"),
        check_vma=False,
    )
```

```python
import functools
import math

import jax
import jax.numpy as jnp
import numpy as np
from jax import lax
from jax.experimental import pallas as pl
from jax.experimental.pallas import tpu as pltpu
from jax.sharding import PartitionSpec as P

power_floor = 0.01
regularizer = 0.1
nowhere = -(1 << 20)
record_rows = 16
wave_bytes = 32 * 1024 * 1024
small_bytes = 8 * 1024 * 1024


def dft_matrices(side):
    line = np.arange(side, dtype=np.int32)
    angle = (line[:, None] * line[None, :] % side).astype(np.float32) * np.float32(
        2.0 * math.pi / side
    )
    scaling = np.float32(1.0 / math.sqrt(side))
    real = (np.cos(angle) * scaling).astype(jnp.bfloat16)
    imag = (-np.sin(angle) * scaling).astype(jnp.bfloat16)
    direct = np.block([[real, -imag], [imag, real]])
    swapped = np.block([[real, imag], [-imag, real]])
    return direct, swapped


def dot(left, right):
    return jnp.dot(left, right, preferred_element_type=jnp.float32)


def iota(shape, dim):
    return lax.broadcasted_iota(jnp.int32, shape, dim)


def sent_order(sides):
    corners = [at for index in range(sides) for at in (4 + 3 * index, 5 + 3 * index)]
    return [0] + corners + [1, 2] + [3 + 3 * index for index in range(sides)]


def in_sent_order(pieces):
    return [pieces[at] for at in sent_order(len(pieces) // 3 - 1)]


def from_sent_order(pieces):
    order = sent_order(len(pieces) // 3 - 1)
    return [pieces[order.index(at)] for at in range(len(pieces))]


def wide(tall):
    side = tall.shape[0] // 2
    return jnp.concatenate([tall[:side], tall[side:]], axis=1)


def tall(wide):
    side = wide.shape[1] // 2
    return jnp.concatenate([wide[:, :side], wide[:, side:]], axis=0)


def here():
    return (lax.axis_index("tx"), lax.axis_index("ty"), lax.axis_index("mode") % 2)


def start_kernel(
    sides,
    slots,
    object_hbm,
    probe_hbm,
    centers_hbm,
    direct_hbm,
    swapped_hbm,
    low_ref,
    shared_ref,
    rest_ref,
    record_ref,
    spot_ref,
    direct_ref,
    swapped_ref,
    packed_ref,
    *refs,
):
    edges = refs[:sides]
    object_ref, probe_ref, centers_ref, sems = refs[sides:]
    copies = [
        pltpu.make_async_copy(source, target, sems.at[index])
        for index, (source, target) in enumerate(
            (
                (probe_hbm, probe_ref),
                (object_hbm, object_ref),
                (centers_hbm, centers_ref),
                (direct_hbm, direct_ref),
                (swapped_hbm, swapped_ref),
            )
        )
    ]
    for copy in copies:
        copy.start()
    tile_cols = object_ref.shape[2]
    half = edges[0].shape[2]
    z_index, x_index, parity = here()
    copies[0].wait()
    low_ref[...] = probe_ref[...].astype(jnp.bfloat16)
    shared_ref[...] = jnp.where(z_index % 2 == 0, low_ref[0, 0], low_ref[1, 0])
    rest_ref[...] = low_ref[:, 1:]
    copies[1].wait()
    first, last = slice(0, half), slice(tile_cols - half, tile_cols)
    for channel in range(2):
        values = object_ref[channel].astype(jnp.bfloat16)
        packed_ref[channel] = values
        if sides == 1:
            edges[0][channel] = jnp.where(x_index == 0, values[:, last], values[:, first])
        else:
            edges[0][channel] = values[:, last]
            edges[1][channel] = values[:, first]
    copies[2].wait()
    spot_ref[...] = jnp.where(
        iota(spot_ref.shape, 0) == 0, centers_ref[0, 0, parity, 0], centers_ref[0, 0, parity, 1]
    )
    record = jnp.zeros(record_ref.shape, jnp.float32)
    line = iota(record_ref.shape, 0)
    for slot in range(slots):
        for axis in range(2):
            value = centers_ref[0, 0, slot, axis].astype(jnp.float32)
            record = jnp.where(line == 2 * slot + axis, value, record)
    record_ref[...] = record.astype(jnp.bfloat16)
    copies[3].wait()
    copies[4].wait()


def live_kernel(slots, record_ref, live_ref, out_ref):
    line = iota(record_ref.shape, 0)
    record = record_ref[...].astype(jnp.float32)
    record = jnp.where(line == 2 * slots, live_ref[0, 0].astype(jnp.float32), record)
    out_ref[...] = record.astype(jnp.bfloat16)


def position_of(record, slots, wanted):
    record = record[:, :128].astype(jnp.float32).astype(jnp.int32)[:, :1]

    def of_slot(axis):
        value = record[axis : axis + 1]
        for slot in range(1, slots):
            value = jnp.where(wanted == slot, record[2 * slot + axis : 2 * slot + axis + 1], value)
        return value

    return of_slot(0), of_slot(1), record[2 * slots : 2 * slots + 1] > wanted


def turned_back(value, side):
    return jnp.where(value == 0, 0, side - value)


def patch_of(sides, z_count, x_count, side, spot_ref, pieces):
    z_index, x_index, parity = here()
    row_at, col_at = spot_ref[0, 0], spot_ref[1, 0]
    half = side // 2
    even = parity == 0
    low_shown = z_index > 0
    high_shown = z_index < z_count - 1

    def joined(piece, a, b, channel):
        level = piece[channel].astype(jnp.float32)
        turn_a = a[channel].astype(jnp.float32)
        turn_b = b[channel].astype(jnp.float32)
        low = jnp.where(even & low_shown, turn_a, jnp.where(low_shown, turn_b, 0.0))
        high = jnp.where(even & high_shown, turn_b, jnp.where(high_shown, turn_a, 0.0))
        first = jnp.where(iota(low.shape, 0) >= row_at, low, high)
        return jnp.concatenate([first, level], axis=0)

    out = []
    for channel in range(2):
        own = joined(*pieces[:3], channel)
        sides_joined = [
            joined(*pieces[3 + 3 * index : 6 + 3 * index], channel) for index in range(sides)
        ]
        if sides == 1:
            left = jnp.where(x_index == 1, sides_joined[0], 0.0)
            right = jnp.where(x_index == 0, sides_joined[0], 0.0)
        else:
            left = jnp.where(x_index > 0, sides_joined[0], 0.0)
            right = jnp.where(x_index < x_count - 1, sides_joined[1], 0.0)
        at = iota(left.shape, 1)
        window = jnp.concatenate(
            [
                jnp.where(at >= col_at, left, own[:, half:]),
                jnp.where(at + half >= col_at, own[:, :half], right),
            ],
            axis=1,
        )
        window = pltpu.roll(window, turned_back(row_at, side), 0)
        out.append(pltpu.roll(window, turned_back(col_at, side), 1))
    return out


def modes_of(group):
    def reader(k):
        return lambda: (group[0, k].astype(jnp.float32), group[1, k].astype(jnp.float32))

    return [reader(k) for k in range(group.shape[1])]


def shared_mode(over_y, over_z):
    def read():
        z_index, _, _ = here()
        even = z_index % 2 == 0
        over_y_values = over_y[...].astype(jnp.float32)
        over_z_values = over_z[...].astype(jnp.float32)
        return (
            jnp.where(even, over_y_values, over_z_values),
            jnp.where(even, over_z_values, over_y_values),
        )

    return read


def forward(modes, patch, direct, swapped, far_ref, exit_ref, at):
    patch_real, patch_imag = patch
    side = patch_real.shape[0]
    power = jnp.zeros((side, side), jnp.float32)
    weight = jnp.zeros((side, side), jnp.float32)
    halves = []
    for k, mode in enumerate(modes):
        real, imag = mode()
        exit_wave = jnp.concatenate(
            [
                (real * patch_real - imag * patch_imag).astype(jnp.bfloat16),
                (real * patch_imag + imag * patch_real).astype(jnp.bfloat16),
            ],
            axis=0,
        )
        exit_ref[at + k] = exit_wave
        halves.append(wide(dot(direct, exit_wave).astype(jnp.bfloat16)))
        weight = weight + (real * real + imag * imag)
    far_all = dot(jnp.concatenate(halves, axis=0), swapped)
    for k in range(len(modes)):
        far = far_all[k * side : (k + 1) * side]
        far_ref[at + k] = far
        power = power + (far[:, :side] * far[:, :side] + far[:, side:] * far[:, side:])
    return power, weight


def backward(modes, factor, direct, swapped, far_ref, exit_ref, at):
    side = factor.shape[0]
    grad_real = jnp.zeros((side, side), jnp.float32)
    grad_imag = jnp.zeros((side, side), jnp.float32)
    halves = []
    for k in range(len(modes)):
        fixed = (far_ref[at + k] * factor).astype(jnp.bfloat16)
        halves.append(wide(dot(swapped, tall(fixed)).astype(jnp.bfloat16)))
    back_all = dot(jnp.concatenate(halves, axis=0), direct)
    for k, mode in enumerate(modes):
        back = back_all[k * side : (k + 1) * side]
        exit_wave = exit_ref[at + k].astype(jnp.float32)
        real, imag = mode()
        diff_real = back[:, :side] - exit_wave[:side]
        diff_imag = back[:, side:] - exit_wave[side:]
        grad_real = grad_real + (real * diff_real + imag * diff_imag)
        grad_imag = grad_imag + (real * diff_imag - imag * diff_real)
    return grad_real, grad_imag


def near_kernel(sides, z_count, x_count, spot_ref, *refs):
    n_pieces = 3 + 3 * sides
    pieces = from_sent_order(refs[:n_pieces])
    own, core, direct, swapped = refs[n_pieces : n_pieces + 4]
    patch_ref, far_ref, exit_ref, sum_ref = refs[n_pieces + 4 :]
    side = own.shape[2]
    patch = patch_of(sides, z_count, x_count, side, spot_ref, pieces)
    patch_ref[0], patch_ref[1] = patch
    tables = (direct[...], swapped[...], far_ref, exit_ref)
    first = forward(modes_of(own), patch, *tables, 0)
    second = forward(modes_of(core), patch, *tables, own.shape[1])
    sum_ref[0] = first[0] + second[0]
    sum_ref[1] = first[1] + second[1]


def over_kernel(patch_ref, over_y, over_z, rest, direct, swapped, far_ref, exit_ref, sum_ref):
    patch = (patch_ref[0], patch_ref[1])
    modes = [shared_mode(over_y, over_z)] + modes_of(rest)
    sum_ref[0], sum_ref[1] = forward(
        modes, patch, direct[...], swapped[...], far_ref, exit_ref, 0
    )


def back_kernel(sides, slots, tile_cols, record_ref, spot_ref, *refs):
    amplitude_ref, patch_ref, own, core = refs[:4]
    over_modes = [shared_mode(*refs[4:6])] + modes_of(refs[6])
    last_modes = [shared_mode(*refs[7:9])] + modes_of(refs[9])
    direct_ref, swapped_ref = refs[10:12]
    near_far, near_exit, near_sum, over_far, over_exit, over_sum = refs[12:18]
    weight_out, own_out, keep_out, swap_out = refs[18:22]
    side_outs = refs[22 : 22 + sides]
    last_far, last_exit = refs[22 + sides :]
    side = own.shape[2]
    half = side // 2
    modes = own.shape[1]
    _, x_index, parity = here()
    row_at, col_at = spot_ref[0, 0], spot_ref[1, 0]
    _, _, is_live = position_of(record_ref, slots, parity)
    direct = direct_ref[...]
    swapped = swapped_ref[...]
    patch = (patch_ref[0], patch_ref[1])
    power, weight = forward(last_modes, patch, direct, swapped, last_far, last_exit, 0)
    power = near_sum[0] + (over_sum[0] + power)
    weight = near_sum[1] + (over_sum[1] + weight)
    weight_out[...] = weight.astype(jnp.bfloat16)
    amplitude = amplitude_ref[0, 0, parity].astype(jnp.float32)
    factor = amplitude / jnp.sqrt(power + power_floor)
    factor = jnp.concatenate([factor, factor], axis=1)
    tables = (factor, direct, swapped)
    grads = [
        backward(modes_of(own), *tables, near_far, near_exit, 0),
        backward(modes_of(core), *tables, near_far, near_exit, modes),
        backward(over_modes, *tables, over_far, over_exit, 0),
        backward(last_modes, *tables, last_far, last_exit, 0),
    ]
    even = parity == 0
    for channel in range(2):
        gradient = (grads[0][channel] + grads[1][channel]) + (grads[2][channel] + grads[3][channel])
        gradient = jnp.where(is_live, gradient, 0.0)
        gradient = pltpu.roll(pltpu.roll(gradient, col_at, 1), row_at, 0)
        first, second = gradient[:, :half], gradient[:, half:]
        at = iota(first.shape, 1)
        left = jnp.where(at >= col_at, first, 0.0)
        own = [
            jnp.where(at + half >= col_at, second, 0.0),
            jnp.where(at < col_at, first, 0.0),
        ]
        right = jnp.where(at + half < col_at, second, 0.0)
        if sides == 1:
            beside = [jnp.where(x_index == 0, right, left)]
        else:
            beside = [left, right]
        placed = jnp.concatenate(own + beside, axis=1)
        row = iota((half, placed.shape[1]), 0)
        low = jnp.where(row >= row_at, placed[:half], 0.0).astype(jnp.bfloat16)
        high = jnp.where(row < row_at, placed[:half], 0.0).astype(jnp.bfloat16)
        inner = placed[half:].astype(jnp.bfloat16)
        rows = slice(channel * half, (channel + 1) * half)
        own_out[rows] = inner[:, :tile_cols]
        keep_out[rows] = jnp.where(even, high, low)
        swap_out[rows] = jnp.where(even, low, high)
        for index, out in enumerate(side_outs):
            out[rows] = inner[:, tile_cols + index * half : tile_cols + (index + 1) * half]
    for out in side_outs:
        out[2 * half :] = record_ref[:, :half]


def meet_kernel(first_column, record_ref, keep_ref, swap_ref, *outs):
    at = first_column
    for out in outs:
        height, width = keep_ref.shape[0], out.shape[1]
        columns = slice(at, at + width)
        total = keep_ref[:, columns].astype(jnp.float32) + swap_ref[:, columns].astype(jnp.float32)
        out[:height] = total.astype(jnp.bfloat16)
        out[height:] = record_ref[:, :width]
        at += width


def sum_kernel(sides, slots, z_count, x_count, weight_ref, record_ref, own_ref, rows_ref, *refs):
    corners, levels, out_ref = refs[:sides], refs[sides:-1], refs[-1]
    _, tile_rows, tile_cols = out_ref.shape
    side = weight_ref.shape[0]
    half = side // 2
    z_index, x_index, parity = here()
    z_step = jnp.where(parity == 0, -1, 1)
    z_shown = jnp.where(parity == 0, z_index > 0, z_index < z_count - 1)
    if sides == 1:
        x_steps = [jnp.where(x_index == 0, 1, -1)]
        x_shown = [z_index >= 0]
    else:
        x_steps = [1, -1]
        x_shown = [x_index < x_count - 1, x_index > 0]
    weight = weight_ref[...]

    def placed(position, z_step, x_step, shown):
        row, col, is_live = position
        row = jnp.where(is_live & shown, row + (z_step * tile_rows - half), nowhere)
        col = col + (x_step * tile_cols - half)
        put_rows = (iota((tile_rows, side), 0) == iota((tile_rows, side), 1) + row).astype(
            jnp.bfloat16
        )
        put_cols = (iota((side, tile_cols), 1) == iota((side, tile_cols), 0) + col).astype(
            jnp.bfloat16
        )
        return dot(dot(put_rows, weight).astype(jnp.bfloat16), put_cols)

    total = placed(position_of(record_ref, slots, parity), 0, 0, z_index >= 0)
    for level, x_step, shown in zip(levels, x_steps, x_shown):
        record = level[2 * half :]
        total = total + placed(position_of(record, slots, parity), 0, x_step, shown)
    for piece, x_step, shown in zip(
        (rows_ref,) + corners, [0] + x_steps, [z_index >= 0] + x_shown
    ):
        record = piece[2 * half :]
        for slot in range(slots):
            position = position_of(record, slots, slot)
            total = total + placed(position, z_step, x_step, shown & z_shown)
    out_ref[2] = total.astype(jnp.bfloat16)

    for channel in range(2):
        rows = slice(channel * tile_rows, (channel + 1) * tile_rows)

        def values(ref, rows=rows):
            return ref[rows].astype(jnp.float32)

        total = values(own_ref) + jnp.where(z_shown, values(rows_ref), 0.0)
        first = jnp.zeros((tile_rows, half), jnp.float32)
        last = first
        for index in range(sides):
            edge = values(levels[index]) + jnp.where(z_shown, values(corners[index]), 0.0)
            if sides == 1:
                first = jnp.where(x_index == 1, edge, 0.0)
                last = jnp.where(x_index == 0, edge, 0.0)
            elif index == 0:
                last = jnp.where(x_shown[0], edge, 0.0)
            else:
                first = jnp.where(x_shown[1], edge, 0.0)
        zero = jnp.zeros((tile_rows, tile_cols - 2 * half), jnp.float32)
        parts = [first, zero, last] if tile_cols > 2 * half else [first, last]
        total = total + jnp.concatenate(parts, axis=1)
        out_ref[channel] = total.astype(jnp.bfloat16)


def update_kernel(object_ref, own_ref, other_ref, out_ref):
    weight = own_ref[2].astype(jnp.float32) + other_ref[2].astype(jnp.float32) + regularizer
    for channel in range(2):
        gradient = own_ref[channel].astype(jnp.float32) + other_ref[channel].astype(jnp.float32)
        out_ref[channel] = object_ref[channel] + gradient / weight


def in_hbm(array):
    return pltpu.with_memory_space_constraint(array, pltpu.HBM)


def smem():
    return pl.BlockSpec(memory_space=pltpu.SMEM)


def hbm():
    return pl.BlockSpec(memory_space=pltpu.HBM)


def vmem():
    return pl.BlockSpec(memory_space=pltpu.VMEM)


def on_device(object_field, probe, amplitudes, centers, live):
    side = probe.shape[2]
    half = side // 2
    _, tile_rows, tile_cols = object_field.shape
    slots = centers.shape[2]
    z_count = lax.axis_size("tx")
    x_count = lax.axis_size("ty")
    m_count = lax.axis_size("mode")
    modes = probe.shape[1]
    if tile_rows != half or slots != 2 or m_count != 4 or z_count % 2 or x_count < 2 or modes < 2:
        raise ValueError("unsupported sizes")
    sides = 1 if x_count == 2 else 2
    axes = ("tx", "ty", "mode")

    def zigzag(x_step):
        def moved(z, m):
            if m % 2 == 0:
                return (z + 1, m) if z < z_count - 1 else (z, m ^ 1)
            return (z - 1, m) if z > 0 else (z, m ^ 1)

        pairs = []
        for z in range(z_count):
            for x in range(x_count):
                for m in range(m_count):
                    z_to, m_to = moved(z, m)
                    x_to = (x + x_step) % x_count
                    pairs.append(
                        (
                            (z * x_count + x) * m_count + m,
                            (z_to * x_count + x_to) * m_count + m_to,
                        )
                    )
        return pairs

    def level(step):
        return [(x, (x + step) % x_count) for x in range(x_count)]

    def exchange(array, flip):
        return lax.ppermute(array, "mode", [(m, m ^ flip) for m in range(m_count)])

    tables = [jnp.asarray(matrix) for matrix in dft_matrices(side)]
    probe_low, shared, rest, record, spot, direct, swapped, *packed = pl.pallas_call(
        functools.partial(start_kernel, sides, slots),
        out_shape=[
            jax.ShapeDtypeStruct(probe.shape, jnp.bfloat16),
            jax.ShapeDtypeStruct((side, side), jnp.bfloat16),
            jax.ShapeDtypeStruct((2, modes - 1, side, side), jnp.bfloat16),
            jax.ShapeDtypeStruct((record_rows, tile_cols), jnp.bfloat16),
            jax.ShapeDtypeStruct((8, 128), jnp.int32),
            jax.ShapeDtypeStruct((2 * side, 2 * side), jnp.bfloat16),
            jax.ShapeDtypeStruct((2 * side, 2 * side), jnp.bfloat16),
            jax.ShapeDtypeStruct(object_field.shape, jnp.bfloat16),
        ]
        + [jax.ShapeDtypeStruct((2, tile_rows, half), jnp.bfloat16)] * sides,
        in_specs=[hbm()] * 5,
        out_specs=[vmem()] * (8 + sides),
        scratch_shapes=[
            pltpu.VMEM(object_field.shape, jnp.float32),
            pltpu.VMEM(probe.shape, jnp.float32),
            pltpu.SMEM(centers.shape, jnp.int32),
            pltpu.SemaphoreType.DMA((5,)),
        ],
        compiler_params=pltpu.CompilerParams(vmem_limit_bytes=small_bytes),
        name="start",
    )(*(in_hbm(array) for array in (object_field, probe, centers, *tables)))
    over_y = exchange(shared, 2)
    probe_core = exchange(probe_low, 1)
    probe_core, rest, live = lax.optimization_barrier((probe_core, rest, live))
    rest = exchange(rest, 2)
    over_z = lax.ppermute(over_y, "tx", [(z, z ^ 1) for z in range(z_count)])
    x_steps = [1] if sides == 1 else [1, -1]
    rows = lax.ppermute(packed[0], axes, zigzag(0))
    corners = [lax.ppermute(edge, axes, zigzag(step)) for step, edge in zip(x_steps, packed[1:])]
    levels = [lax.ppermute(edge, "ty", level(step)) for step, edge in zip(x_steps, packed[1:])]
    record = pl.pallas_call(
        functools.partial(live_kernel, slots),
        out_shape=jax.ShapeDtypeStruct(record.shape, jnp.bfloat16),
        in_specs=[vmem(), smem()],
        out_specs=vmem(),
        compiler_params=pltpu.CompilerParams(vmem_limit_bytes=small_bytes),
        name="live",
    )(record, live)
    rows, record = lax.optimization_barrier((rows, record))
    corners, levels = lax.optimization_barrier((corners, levels))
    pieces = [packed[0], rows, exchange(rows, 1)]
    for at_level, corner in zip(levels, corners):
        pieces += [at_level, corner, exchange(corner, 1)]
    n_pieces = len(pieces)
    ext_cols = tile_cols + sides * half

    def waves(count):
        return [
            jax.ShapeDtypeStruct((count, side, 2 * side), jnp.float32),
            jax.ShapeDtypeStruct((count, 2 * side, side), jnp.bfloat16),
            jax.ShapeDtypeStruct((2, side, side), jnp.float32),
        ]

    patch, *near = pl.pallas_call(
        functools.partial(near_kernel, sides, z_count, x_count),
        out_shape=[jax.ShapeDtypeStruct((2, side, side), jnp.float32)] + waves(2 * modes),
        in_specs=[vmem()] * (n_pieces + 5),
        out_specs=[vmem()] * 4,
        compiler_params=pltpu.CompilerParams(vmem_limit_bytes=wave_bytes),
        name="near",
    )(spot, *in_sent_order(pieces), probe_low, probe_core, direct, swapped)
    over_z, rest, patch = lax.optimization_barrier((over_z, rest, patch))
    over_group = (over_y, over_z, rest)
    last_group = [exchange(part, 1) for part in over_group]
    over = pl.pallas_call(
        over_kernel,
        out_shape=waves(modes),
        in_specs=[vmem()] * 6,
        out_specs=[vmem()] * 3,
        compiler_params=pltpu.CompilerParams(vmem_limit_bytes=wave_bytes),
        name="over",
    )(patch, *over_group, direct, swapped)
    piece_rows = 2 * half + record_rows
    shapes = [(side, side), (2 * half, tile_cols)] + [(2 * half, ext_cols)] * 2
    shapes += [(piece_rows, half)] * sides
    weight, own, keep, swap, *levels = pl.pallas_call(
        functools.partial(back_kernel, sides, slots, tile_cols),
        out_shape=[jax.ShapeDtypeStruct(shape, jnp.bfloat16) for shape in shapes],
        in_specs=[vmem()] * 20,
        out_specs=[vmem()] * (4 + sides),
        scratch_shapes=[
            pltpu.VMEM((modes, side, 2 * side), jnp.float32),
            pltpu.VMEM((modes, 2 * side, side), jnp.bfloat16),
        ],
        compiler_params=pltpu.CompilerParams(vmem_limit_bytes=wave_bytes),
        name="back",
    )(
        record,
        spot,
        amplitudes,
        patch,
        probe_low,
        probe_core,
        *over_group,
        *last_group,
        direct,
        swapped,
        *near,
        *over,
    )
    levels = [lax.ppermute(piece, "ty", level(-step)) for piece, step in zip(levels, x_steps)]
    rows, *corners = pl.pallas_call(
        functools.partial(meet_kernel, 0),
        out_shape=[
            jax.ShapeDtypeStruct((piece_rows, width), jnp.bfloat16)
            for width in [tile_cols] + [half] * sides
        ],
        in_specs=[vmem()] * 3,
        out_specs=[vmem()] * (1 + sides),
        compiler_params=pltpu.CompilerParams(vmem_limit_bytes=small_bytes),
        name="meet",
    )(record, keep, exchange(swap, 1))
    rows = lax.ppermute(rows, axes, zigzag(0))
    corners, levels = lax.optimization_barrier((corners, levels))
    corners = [
        lax.ppermute(piece, axes, zigzag(-step)) for piece, step in zip(corners, x_steps)
    ]
    summed = pl.pallas_call(
        functools.partial(sum_kernel, sides, slots, z_count, x_count),
        out_shape=jax.ShapeDtypeStruct((3, tile_rows, tile_cols), jnp.bfloat16),
        in_specs=[vmem()] * (4 + 2 * sides),
        out_specs=vmem(),
        compiler_params=pltpu.CompilerParams(vmem_limit_bytes=small_bytes),
        name="sums",
    )(weight, record, own, rows, *corners, *levels)
    return pl.pallas_call(
        update_kernel,
        out_shape=jax.ShapeDtypeStruct(object_field.shape, jnp.float32),
        in_specs=[vmem()] * 3,
        out_specs=vmem(),
        compiler_params=pltpu.CompilerParams(vmem_limit_bytes=small_bytes),
        name="update",
    )(object_field, summed, exchange(summed, 1))


def solution(mesh):
    return jax.shard_map(
        on_device,
        mesh=mesh,
        in_specs=(
            P(None, "tx", "ty"),
            P(None, "mode", None, None),
            P("tx", "ty", None, None, None),
            P("tx", "ty", None, None),
            P("tx", "ty"),
        ),
        out_specs=P(None, "tx", "ty"),
        check_vma=False,
    )
```

```python
import functools
import math

import jax
import jax.numpy as jnp
import numpy as np
from jax import lax
from jax.experimental import pallas as pl
from jax.experimental.pallas import tpu as pltpu
from jax.sharding import PartitionSpec as P

power_floor = 0.01
regularizer = 0.1
nowhere = -(1 << 20)
record_rows = 16
wave_bytes = 32 * 1024 * 1024
small_bytes = 8 * 1024 * 1024


def dft_matrices(side):
    line = np.arange(side, dtype=np.int32)
    angle = (line[:, None] * line[None, :] % side).astype(np.float32) * np.float32(
        2.0 * math.pi / side
    )
    scaling = np.float32(1.0 / math.sqrt(side))
    real = (np.cos(angle) * scaling).astype(jnp.bfloat16)
    imag = (-np.sin(angle) * scaling).astype(jnp.bfloat16)
    direct = np.block([[real, -imag], [imag, real]])
    swapped = np.block([[real, imag], [-imag, real]])
    return direct, swapped


def dot(left, right):
    return jnp.dot(left, right, preferred_element_type=jnp.float32)


def iota(shape, dim):
    return lax.broadcasted_iota(jnp.int32, shape, dim)


def sent_order(sides):
    corners = [at for index in range(sides) for at in (4 + 3 * index, 5 + 3 * index)]
    return [0] + corners + [1, 2] + [3 + 3 * index for index in range(sides)]


def in_sent_order(pieces):
    return [pieces[at] for at in sent_order(len(pieces) // 3 - 1)]


def from_sent_order(pieces):
    order = sent_order(len(pieces) // 3 - 1)
    return [pieces[order.index(at)] for at in range(len(pieces))]


def wide(tall):
    side = tall.shape[0] // 2
    return jnp.concatenate([tall[:side], tall[side:]], axis=1)


def tall(wide):
    side = wide.shape[1] // 2
    return jnp.concatenate([wide[:, :side], wide[:, side:]], axis=0)


def here():
    return (lax.axis_index("tx"), lax.axis_index("ty"), lax.axis_index("mode") % 2)


def start_kernel(
    sides,
    slots,
    object_hbm,
    probe_hbm,
    centers_hbm,
    direct_hbm,
    swapped_hbm,
    low_ref,
    shared_ref,
    rest_ref,
    record_ref,
    spot_ref,
    direct_ref,
    swapped_ref,
    packed_ref,
    *refs,
):
    edges = refs[:sides]
    object_ref, probe_ref, centers_ref, sems = refs[sides:]
    copies = [
        pltpu.make_async_copy(source, target, sems.at[index])
        for index, (source, target) in enumerate(
            (
                (probe_hbm, probe_ref),
                (object_hbm, object_ref),
                (centers_hbm, centers_ref),
                (direct_hbm, direct_ref),
                (swapped_hbm, swapped_ref),
            )
        )
    ]
    for copy in copies:
        copy.start()
    tile_cols = object_ref.shape[2]
    half = edges[0].shape[2]
    z_index, x_index, parity = here()
    copies[0].wait()
    low_ref[...] = probe_ref[...].astype(jnp.bfloat16)
    shared_ref[...] = jnp.where(z_index % 2 == 0, low_ref[0, 0], low_ref[1, 0])
    rest_ref[...] = low_ref[:, 1:]
    copies[1].wait()
    first, last = slice(0, half), slice(tile_cols - half, tile_cols)
    for channel in range(2):
        values = object_ref[channel].astype(jnp.bfloat16)
        packed_ref[channel] = values
        if sides == 1:
            edges[0][channel] = jnp.where(x_index == 0, values[:, last], values[:, first])
        else:
            edges[0][channel] = values[:, last]
            edges[1][channel] = values[:, first]
    copies[2].wait()
    spot_ref[...] = jnp.where(
        iota(spot_ref.shape, 0) == 0, centers_ref[0, 0, parity, 0], centers_ref[0, 0, parity, 1]
    )
    record = jnp.zeros(record_ref.shape, jnp.float32)
    line = iota(record_ref.shape, 0)
    for slot in range(slots):
        for axis in range(2):
            value = centers_ref[0, 0, slot, axis].astype(jnp.float32)
            record = jnp.where(line == 2 * slot + axis, value, record)
    record_ref[...] = record.astype(jnp.bfloat16)
    copies[3].wait()
    copies[4].wait()


def live_kernel(slots, record_ref, live_ref, out_ref):
    line = iota(record_ref.shape, 0)
    record = record_ref[...].astype(jnp.float32)
    record = jnp.where(line == 2 * slots, live_ref[0, 0].astype(jnp.float32), record)
    out_ref[...] = record.astype(jnp.bfloat16)


def position_of(record, slots, wanted):
    record = record[:, :128].astype(jnp.float32).astype(jnp.int32)[:, :1]

    def of_slot(axis):
        value = record[axis : axis + 1]
        for slot in range(1, slots):
            value = jnp.where(wanted == slot, record[2 * slot + axis : 2 * slot + axis + 1], value)
        return value

    return of_slot(0), of_slot(1), record[2 * slots : 2 * slots + 1] > wanted


def turned_back(value, side):
    return jnp.where(value == 0, 0, side - value)


def patch_of(sides, z_count, x_count, side, spot_ref, pieces):
    z_index, x_index, parity = here()
    row_at, col_at = spot_ref[0, 0], spot_ref[1, 0]
    half = side // 2
    even = parity == 0
    low_shown = z_index > 0
    high_shown = z_index < z_count - 1

    def joined(piece, a, b, channel):
        level = piece[channel].astype(jnp.float32)
        turn_a = a[channel].astype(jnp.float32)
        turn_b = b[channel].astype(jnp.float32)
        low = jnp.where(even & low_shown, turn_a, jnp.where(low_shown, turn_b, 0.0))
        high = jnp.where(even & high_shown, turn_b, jnp.where(high_shown, turn_a, 0.0))
        first = jnp.where(iota(low.shape, 0) >= row_at, low, high)
        return jnp.concatenate([first, level], axis=0)

    out = []
    for channel in range(2):
        own = joined(*pieces[:3], channel)
        sides_joined = [
            joined(*pieces[3 + 3 * index : 6 + 3 * index], channel) for index in range(sides)
        ]
        if sides == 1:
            left = jnp.where(x_index == 1, sides_joined[0], 0.0)
            right = jnp.where(x_index == 0, sides_joined[0], 0.0)
        else:
            left = jnp.where(x_index > 0, sides_joined[0], 0.0)
            right = jnp.where(x_index < x_count - 1, sides_joined[1], 0.0)
        at = iota(left.shape, 1)
        window = jnp.concatenate(
            [
                jnp.where(at >= col_at, left, own[:, half:]),
                jnp.where(at + half >= col_at, own[:, :half], right),
            ],
            axis=1,
        )
        window = pltpu.roll(window, turned_back(row_at, side), 0)
        out.append(pltpu.roll(window, turned_back(col_at, side), 1))
    return out


def modes_of(group):
    def reader(k):
        return lambda: (group[0, k].astype(jnp.float32), group[1, k].astype(jnp.float32))

    return [reader(k) for k in range(group.shape[1])]


def shared_mode(over_y, over_z):
    def read():
        z_index, _, _ = here()
        even = z_index % 2 == 0
        over_y_values = over_y[...].astype(jnp.float32)
        over_z_values = over_z[...].astype(jnp.float32)
        return (
            jnp.where(even, over_y_values, over_z_values),
            jnp.where(even, over_z_values, over_y_values),
        )

    return read


def forward(modes, patch, direct, swapped, far_ref, exit_ref, at):
    patch_real, patch_imag = patch
    side = patch_real.shape[0]
    power = jnp.zeros((side, side), jnp.float32)
    weight = jnp.zeros((side, side), jnp.float32)
    halves = []
    for k, mode in enumerate(modes):
        real, imag = mode()
        exit_wave = jnp.concatenate(
            [
                (real * patch_real - imag * patch_imag).astype(jnp.bfloat16),
                (real * patch_imag + imag * patch_real).astype(jnp.bfloat16),
            ],
            axis=0,
        )
        exit_ref[at + k] = exit_wave
        halves.append(wide(dot(direct, exit_wave).astype(jnp.bfloat16)))
        weight = weight + (real * real + imag * imag)
    far_all = dot(jnp.concatenate(halves, axis=0), swapped)
    for k in range(len(modes)):
        far = far_all[k * side : (k + 1) * side]
        far_ref[at + k] = far
        power = power + (far[:, :side] * far[:, :side] + far[:, side:] * far[:, side:])
    return power, weight


def backward(modes, factor, direct, swapped, far_ref, exit_ref, at):
    side = factor.shape[0]
    grad_real = jnp.zeros((side, side), jnp.float32)
    grad_imag = jnp.zeros((side, side), jnp.float32)
    halves = []
    for k in range(len(modes)):
        fixed = (far_ref[at + k] * factor).astype(jnp.bfloat16)
        halves.append(wide(dot(swapped, tall(fixed)).astype(jnp.bfloat16)))
    back_all = dot(jnp.concatenate(halves, axis=0), direct)
    for k, mode in enumerate(modes):
        back = back_all[k * side : (k + 1) * side]
        exit_wave = exit_ref[at + k].astype(jnp.float32)
        real, imag = mode()
        diff_real = back[:, :side] - exit_wave[:side]
        diff_imag = back[:, side:] - exit_wave[side:]
        grad_real = grad_real + (real * diff_real + imag * diff_imag)
        grad_imag = grad_imag + (real * diff_imag - imag * diff_real)
    return grad_real, grad_imag


def near_kernel(sides, z_count, x_count, spot_ref, *refs):
    n_pieces = 3 + 3 * sides
    pieces = from_sent_order(refs[:n_pieces])
    own, direct, swapped = refs[n_pieces : n_pieces + 3]
    patch_ref, far_ref, exit_ref, sum_ref = refs[n_pieces + 3 :]
    side = own.shape[2]
    patch = patch_of(sides, z_count, x_count, side, spot_ref, pieces)
    patch_ref[0], patch_ref[1] = patch
    sum_ref[0], sum_ref[1] = forward(
        modes_of(own), patch, direct[...], swapped[...], far_ref, exit_ref, 0
    )


def over_kernel(patch_ref, core, over_y, over_z, rest, direct, swapped, far_ref, exit_ref, sum_ref):
    patch = (patch_ref[0], patch_ref[1])
    tables = (direct[...], swapped[...], far_ref, exit_ref)
    modes = modes_of(core)
    sum_ref[0], sum_ref[1] = forward(modes, patch, *tables, 0)
    over_modes = [shared_mode(over_y, over_z)] + modes_of(rest)
    sum_ref[2], sum_ref[3] = forward(over_modes, patch, *tables, len(modes))


def back_kernel(sides, slots, tile_cols, record_ref, spot_ref, *refs):
    amplitude_ref, patch_ref, own, core = refs[:4]
    over_modes = [shared_mode(*refs[4:6])] + modes_of(refs[6])
    last_modes = [shared_mode(*refs[7:9])] + modes_of(refs[9])
    direct_ref, swapped_ref = refs[10:12]
    near_far, near_exit, near_sum, over_far, over_exit, over_sum = refs[12:18]
    weight_out, own_out, keep_out, swap_out = refs[18:22]
    side_outs = refs[22 : 22 + sides]
    last_far, last_exit = refs[22 + sides :]
    side = own.shape[2]
    half = side // 2
    modes = own.shape[1]
    _, x_index, parity = here()
    row_at, col_at = spot_ref[0, 0], spot_ref[1, 0]
    _, _, is_live = position_of(record_ref, slots, parity)
    direct = direct_ref[...]
    swapped = swapped_ref[...]
    patch = (patch_ref[0], patch_ref[1])
    power, weight = forward(last_modes, patch, direct, swapped, last_far, last_exit, 0)
    power = (near_sum[0] + over_sum[0]) + (over_sum[2] + power)
    weight = (near_sum[1] + over_sum[1]) + (over_sum[3] + weight)
    weight_out[...] = weight.astype(jnp.bfloat16)
    amplitude = amplitude_ref[0, 0, parity].astype(jnp.float32)
    factor = amplitude / jnp.sqrt(power + power_floor)
    factor = jnp.concatenate([factor, factor], axis=1)
    tables = (factor, direct, swapped)
    grads = [
        backward(modes_of(own), *tables, near_far, near_exit, 0),
        backward(modes_of(core), *tables, over_far, over_exit, 0),
        backward(over_modes, *tables, over_far, over_exit, modes),
        backward(last_modes, *tables, last_far, last_exit, 0),
    ]
    even = parity == 0
    for channel in range(2):
        gradient = (grads[0][channel] + grads[1][channel]) + (grads[2][channel] + grads[3][channel])
        gradient = jnp.where(is_live, gradient, 0.0)
        gradient = pltpu.roll(pltpu.roll(gradient, col_at, 1), row_at, 0)
        first, second = gradient[:, :half], gradient[:, half:]
        at = iota(first.shape, 1)
        left = jnp.where(at >= col_at, first, 0.0)
        own = [
            jnp.where(at + half >= col_at, second, 0.0),
            jnp.where(at < col_at, first, 0.0),
        ]
        right = jnp.where(at + half < col_at, second, 0.0)
        if sides == 1:
            beside = [jnp.where(x_index == 0, right, left)]
        else:
            beside = [left, right]
        placed = jnp.concatenate(own + beside, axis=1)
        row = iota((half, placed.shape[1]), 0)
        low = jnp.where(row >= row_at, placed[:half], 0.0).astype(jnp.bfloat16)
        high = jnp.where(row < row_at, placed[:half], 0.0).astype(jnp.bfloat16)
        inner = placed[half:].astype(jnp.bfloat16)
        rows = slice(channel * half, (channel + 1) * half)
        own_out[rows] = inner[:, :tile_cols]
        keep_out[rows] = jnp.where(even, high, low)
        swap_out[rows] = jnp.where(even, low, high)
        for index, out in enumerate(side_outs):
            out[rows] = inner[:, tile_cols + index * half : tile_cols + (index + 1) * half]
    for out in side_outs:
        out[2 * half :] = record_ref[:, :half]


def meet_kernel(first_column, record_ref, keep_ref, swap_ref, *outs):
    at = first_column
    for out in outs:
        height, width = keep_ref.shape[0], out.shape[1]
        columns = slice(at, at + width)
        total = keep_ref[:, columns].astype(jnp.float32) + swap_ref[:, columns].astype(jnp.float32)
        out[:height] = total.astype(jnp.bfloat16)
        out[height:] = record_ref[:, :width]
        at += width


def placed_weight(weight, position, z_step, x_step, shown, shape):
    tile_rows, tile_cols = shape
    side = weight.shape[0]
    half = side // 2
    row, col, is_live = position
    row = jnp.where(is_live & shown, row + (z_step * tile_rows - half), nowhere)
    col = col + (x_step * tile_cols - half)
    put_rows = (iota((tile_rows, side), 0) == iota((tile_rows, side), 1) + row).astype(jnp.bfloat16)
    put_cols = (iota((side, tile_cols), 1) == iota((side, tile_cols), 0) + col).astype(jnp.bfloat16)
    return dot(dot(put_rows, weight).astype(jnp.bfloat16), put_cols)


def beside(sides, x_count):
    z_index, x_index, _ = here()
    if sides == 1:
        return [jnp.where(x_index == 0, 1, -1)], [z_index >= 0]
    return [1, -1], [x_index < x_count - 1, x_index > 0]


def edges_added(inner, edges, sides, shown):
    _, x_index, _ = here()
    half = edges[0].shape[1]
    first = jnp.zeros(edges[0].shape, jnp.float32)
    last = first
    for index, edge in enumerate(edges):
        if sides == 1:
            first = jnp.where(x_index == 1, edge, 0.0)
            last = jnp.where(x_index == 0, edge, 0.0)
        elif index == 0:
            last = jnp.where(shown[0], edge, 0.0)
        else:
            first = jnp.where(shown[1], edge, 0.0)
    middle = inner.shape[1] - 2 * half
    parts = [inner[:, :half] + first]
    if middle:
        parts.append(inner[:, half : half + middle])
    parts.append(inner[:, half + middle :] + last)
    return jnp.concatenate(parts, axis=1)


def level_kernel(sides, slots, x_count, weight_ref, record_ref, own_ref, *refs):
    levels, out_ref = refs[:sides], refs[-1]
    shape = out_ref.shape[1:]
    half = levels[0].shape[1]
    z_index, _, parity = here()
    x_steps, shown = beside(sides, x_count)
    weight = weight_ref[...]
    position = position_of(record_ref, slots, parity)
    total = placed_weight(weight, position, 0, 0, z_index >= 0, shape)
    for level, x_step, is_shown in zip(levels, x_steps, shown):
        position = position_of(level[2 * half :], slots, parity)
        total = total + placed_weight(weight, position, 0, x_step, is_shown, shape)
    out_ref[2] = total
    for channel in range(2):
        rows = slice(channel * half, (channel + 1) * half)
        edges = [level[rows].astype(jnp.float32) for level in levels]
        out_ref[channel] = edges_added(own_ref[rows].astype(jnp.float32), edges, sides, shown)


def sum_kernel(sides, slots, z_count, x_count, weight_ref, level_ref, rows_ref, *refs):
    corners, out_ref = refs[:sides], refs[-1]
    shape = out_ref.shape[1:]
    half = corners[0].shape[1]
    z_index, _, parity = here()
    z_step = jnp.where(parity == 0, -1, 1)
    z_shown = jnp.where(parity == 0, z_index > 0, z_index < z_count - 1)
    x_steps, shown = beside(sides, x_count)
    weight = weight_ref[...]
    total = level_ref[2]
    for piece, x_step, is_shown in zip(
        (rows_ref,) + corners, [0] + x_steps, [z_index >= 0] + shown
    ):
        for slot in range(slots):
            position = position_of(piece[2 * half :], slots, slot)
            total = total + placed_weight(
                weight, position, z_step, x_step, is_shown & z_shown, shape
            )
    out_ref[2] = total.astype(jnp.bfloat16)
    for channel in range(2):
        rows = slice(channel * half, (channel + 1) * half)
        edges = [corner[rows].astype(jnp.float32) for corner in corners]
        above = edges_added(rows_ref[rows].astype(jnp.float32), edges, sides, shown)
        total = level_ref[channel] + jnp.where(z_shown, above, 0.0)
        out_ref[channel] = total.astype(jnp.bfloat16)


def update_kernel(object_ref, own_ref, other_ref, out_ref):
    weight = own_ref[2].astype(jnp.float32) + other_ref[2].astype(jnp.float32) + regularizer
    for channel in range(2):
        gradient = own_ref[channel].astype(jnp.float32) + other_ref[channel].astype(jnp.float32)
        out_ref[channel] = object_ref[channel] + gradient / weight


def cost(products):
    return pl.CostEstimate(flops=products * 2 * 256**3, bytes_accessed=0, transcendentals=0)


def in_hbm(array):
    return pltpu.with_memory_space_constraint(array, pltpu.HBM)


def smem():
    return pl.BlockSpec(memory_space=pltpu.SMEM)


def hbm():
    return pl.BlockSpec(memory_space=pltpu.HBM)


def vmem():
    return pl.BlockSpec(memory_space=pltpu.VMEM)


def on_device(object_field, probe, amplitudes, centers, live):
    side = probe.shape[2]
    half = side // 2
    _, tile_rows, tile_cols = object_field.shape
    slots = centers.shape[2]
    z_count = lax.axis_size("tx")
    x_count = lax.axis_size("ty")
    m_count = lax.axis_size("mode")
    modes = probe.shape[1]
    if tile_rows != half or slots != 2 or m_count != 4 or z_count % 2 or x_count < 2 or modes < 2:
        raise ValueError("unsupported sizes")
    sides = 1 if x_count == 2 else 2
    axes = ("tx", "ty", "mode")

    def zigzag(x_step):
        def moved(z, m):
            if m % 2 == 0:
                return (z + 1, m) if z < z_count - 1 else (z, m ^ 1)
            return (z - 1, m) if z > 0 else (z, m ^ 1)

        pairs = []
        for z in range(z_count):
            for x in range(x_count):
                for m in range(m_count):
                    z_to, m_to = moved(z, m)
                    x_to = (x + x_step) % x_count
                    pairs.append(
                        (
                            (z * x_count + x) * m_count + m,
                            (z_to * x_count + x_to) * m_count + m_to,
                        )
                    )
        return pairs

    def level(step):
        return [(x, (x + step) % x_count) for x in range(x_count)]

    def exchange(array, flip):
        return lax.ppermute(array, "mode", [(m, m ^ flip) for m in range(m_count)])

    tables = [jnp.asarray(matrix) for matrix in dft_matrices(side)]
    probe_low, shared, rest, record, spot, direct, swapped, *packed = pl.pallas_call(
        functools.partial(start_kernel, sides, slots),
        out_shape=[
            jax.ShapeDtypeStruct(probe.shape, jnp.bfloat16),
            jax.ShapeDtypeStruct((side, side), jnp.bfloat16),
            jax.ShapeDtypeStruct((2, modes - 1, side, side), jnp.bfloat16),
            jax.ShapeDtypeStruct((record_rows, tile_cols), jnp.bfloat16),
            jax.ShapeDtypeStruct((8, 128), jnp.int32),
            jax.ShapeDtypeStruct((2 * side, 2 * side), jnp.bfloat16),
            jax.ShapeDtypeStruct((2 * side, 2 * side), jnp.bfloat16),
            jax.ShapeDtypeStruct(object_field.shape, jnp.bfloat16),
        ]
        + [jax.ShapeDtypeStruct((2, tile_rows, half), jnp.bfloat16)] * sides,
        in_specs=[hbm()] * 5,
        out_specs=[vmem()] * (8 + sides),
        scratch_shapes=[
            pltpu.VMEM(object_field.shape, jnp.float32),
            pltpu.VMEM(probe.shape, jnp.float32),
            pltpu.SMEM(centers.shape, jnp.int32),
            pltpu.SemaphoreType.DMA((5,)),
        ],
        compiler_params=pltpu.CompilerParams(vmem_limit_bytes=small_bytes),
        name="start",
    )(*(in_hbm(array) for array in (object_field, probe, centers, *tables)))
    over_y = exchange(shared, 2)
    rest = exchange(rest, 2)
    over_z = lax.ppermute(over_y, "tx", [(z, z ^ 1) for z in range(z_count)])
    x_steps = [1] if sides == 1 else [1, -1]
    rows = lax.ppermute(packed[0], axes, zigzag(0))
    corners = [lax.ppermute(edge, axes, zigzag(step)) for step, edge in zip(x_steps, packed[1:])]
    levels = [lax.ppermute(edge, "ty", level(step)) for step, edge in zip(x_steps, packed[1:])]
    probe_core = exchange(probe_low, 1)
    corners, record = lax.optimization_barrier((corners, record))
    record = pl.pallas_call(
        functools.partial(live_kernel, slots),
        out_shape=jax.ShapeDtypeStruct(record.shape, jnp.bfloat16),
        in_specs=[vmem(), smem()],
        out_specs=vmem(),
        compiler_params=pltpu.CompilerParams(vmem_limit_bytes=small_bytes),
        cost_estimate=cost(80),
        name="live",
    )(record, live)
    corners, record = lax.optimization_barrier((corners, record))
    pieces = [packed[0], rows, exchange(rows, 1)]
    for at_level, corner in zip(levels, corners):
        pieces += [at_level, corner, exchange(corner, 1)]
    n_pieces = len(pieces)
    ext_cols = tile_cols + sides * half

    def waves(groups):
        count = groups * modes
        return [
            jax.ShapeDtypeStruct((count, side, 2 * side), jnp.float32),
            jax.ShapeDtypeStruct((count, 2 * side, side), jnp.bfloat16),
            jax.ShapeDtypeStruct((2 * groups, side, side), jnp.float32),
        ]

    patch, *near = pl.pallas_call(
        functools.partial(near_kernel, sides, z_count, x_count),
        out_shape=[jax.ShapeDtypeStruct((2, side, side), jnp.float32)] + waves(1),
        in_specs=[vmem()] * (n_pieces + 4),
        out_specs=[vmem()] * 4,
        compiler_params=pltpu.CompilerParams(vmem_limit_bytes=wave_bytes),
        cost_estimate=cost(20),
        name="near",
    )(spot, *in_sent_order(pieces), probe_low, direct, swapped)
    over_z, rest, patch = lax.optimization_barrier((over_z, rest, patch))
    over_group = (over_y, over_z, rest)
    last_group = [exchange(part, 1) for part in over_group]
    over = pl.pallas_call(
        over_kernel,
        out_shape=waves(2),
        in_specs=[vmem()] * 7,
        out_specs=[vmem()] * 3,
        compiler_params=pltpu.CompilerParams(vmem_limit_bytes=wave_bytes),
        cost_estimate=cost(32),
        name="over",
    )(patch, probe_core, *over_group, direct, swapped)
    piece_rows = 2 * half + record_rows
    shapes = [(side, side), (2 * half, tile_cols)] + [(2 * half, ext_cols)] * 2
    shapes += [(piece_rows, half)] * sides
    weight, own, keep, swap, *levels = pl.pallas_call(
        functools.partial(back_kernel, sides, slots, tile_cols),
        out_shape=[jax.ShapeDtypeStruct(shape, jnp.bfloat16) for shape in shapes],
        in_specs=[vmem()] * 20,
        out_specs=[vmem()] * (4 + sides),
        scratch_shapes=[
            pltpu.VMEM((modes, side, 2 * side), jnp.float32),
            pltpu.VMEM((modes, 2 * side, side), jnp.bfloat16),
        ],
        compiler_params=pltpu.CompilerParams(vmem_limit_bytes=wave_bytes),
        cost_estimate=cost(80),
        name="back",
    )(
        record,
        spot,
        amplitudes,
        patch,
        probe_low,
        probe_core,
        *over_group,
        *last_group,
        direct,
        swapped,
        *near,
        *over,
    )
    levels = [lax.ppermute(piece, "ty", level(-step)) for piece, step in zip(levels, x_steps)]
    rows, *corners = pl.pallas_call(
        functools.partial(meet_kernel, 0),
        out_shape=[
            jax.ShapeDtypeStruct((piece_rows, width), jnp.bfloat16)
            for width in [tile_cols] + [half] * sides
        ],
        in_specs=[vmem()] * 3,
        out_specs=[vmem()] * (1 + sides),
        compiler_params=pltpu.CompilerParams(vmem_limit_bytes=small_bytes),
        name="meet",
    )(record, keep, exchange(swap, 1))
    rows = lax.ppermute(rows, axes, zigzag(0))
    corners = [
        lax.ppermute(piece, axes, zigzag(-step)) for piece, step in zip(corners, x_steps)
    ]
    leveled = pl.pallas_call(
        functools.partial(level_kernel, sides, slots, x_count),
        out_shape=jax.ShapeDtypeStruct((3, tile_rows, tile_cols), jnp.float32),
        in_specs=[vmem()] * (3 + sides),
        out_specs=vmem(),
        compiler_params=pltpu.CompilerParams(vmem_limit_bytes=small_bytes),
        cost_estimate=cost(80),
        name="levels",
    )(weight, record, own, *levels)
    summed = pl.pallas_call(
        functools.partial(sum_kernel, sides, slots, z_count, x_count),
        out_shape=jax.ShapeDtypeStruct((3, tile_rows, tile_cols), jnp.bfloat16),
        in_specs=[vmem()] * (3 + sides),
        out_specs=vmem(),
        compiler_params=pltpu.CompilerParams(vmem_limit_bytes=small_bytes),
        name="sums",
    )(weight, leveled, rows, *corners)
    return pl.pallas_call(
        update_kernel,
        out_shape=jax.ShapeDtypeStruct(object_field.shape, jnp.float32),
        in_specs=[vmem()] * 3,
        out_specs=vmem(),
        compiler_params=pltpu.CompilerParams(vmem_limit_bytes=small_bytes),
        name="update",
    )(object_field, summed, exchange(summed, 1))


def solution(mesh):
    return jax.shard_map(
        on_device,
        mesh=mesh,
        in_specs=(
            P(None, "tx", "ty"),
            P(None, "mode", None, None),
            P("tx", "ty", None, None, None),
            P("tx", "ty", None, None),
            P("tx", "ty"),
        ),
        out_specs=P(None, "tx", "ty"),
        check_vma=False,
    )
```

```python
import functools
import math

import jax
import jax.numpy as jnp
import numpy as np
from jax import lax
from jax.experimental import pallas as pl
from jax.experimental.pallas import tpu as pltpu
from jax.sharding import PartitionSpec as P

power_floor = 0.01
regularizer = 0.1
nowhere = -(1 << 20)
record_rows = 16
wave_bytes = 32 * 1024 * 1024
small_bytes = 8 * 1024 * 1024


def dft_matrices(side):
    line = np.arange(side, dtype=np.int32)
    angle = (line[:, None] * line[None, :] % side).astype(np.float32) * np.float32(
        2.0 * math.pi / side
    )
    scaling = np.float32(1.0 / math.sqrt(side))
    real = (np.cos(angle) * scaling).astype(jnp.bfloat16)
    imag = (-np.sin(angle) * scaling).astype(jnp.bfloat16)
    direct = np.block([[real, -imag], [imag, real]])
    swapped = np.block([[real, imag], [-imag, real]])
    return direct, swapped


def dot(left, right):
    return jnp.dot(left, right, preferred_element_type=jnp.float32)


def iota(shape, dim):
    return lax.broadcasted_iota(jnp.int32, shape, dim)


def sent_order(sides):
    corners = [at for index in range(sides) for at in (4 + 3 * index, 5 + 3 * index)]
    return [0] + corners + [1, 2] + [3 + 3 * index for index in range(sides)]


def in_sent_order(pieces):
    return [pieces[at] for at in sent_order(len(pieces) // 3 - 1)]


def from_sent_order(pieces):
    order = sent_order(len(pieces) // 3 - 1)
    return [pieces[order.index(at)] for at in range(len(pieces))]


def wide(tall):
    side = tall.shape[0] // 2
    return jnp.concatenate([tall[:side], tall[side:]], axis=1)


def tall(wide):
    side = wide.shape[1] // 2
    return jnp.concatenate([wide[:, :side], wide[:, side:]], axis=0)


def here():
    return (lax.axis_index("tx"), lax.axis_index("ty"), lax.axis_index("mode") % 2)


def start_kernel(
    sides,
    slots,
    object_hbm,
    probe_hbm,
    centers_hbm,
    direct_hbm,
    swapped_hbm,
    low_ref,
    shared_ref,
    rest_ref,
    record_ref,
    spot_ref,
    direct_ref,
    swapped_ref,
    packed_ref,
    *refs,
):
    edges = refs[:sides]
    object_ref, probe_ref, centers_ref, sems = refs[sides:]
    copies = [
        pltpu.make_async_copy(source, target, sems.at[index])
        for index, (source, target) in enumerate(
            (
                (probe_hbm, probe_ref),
                (object_hbm, object_ref),
                (centers_hbm, centers_ref),
                (direct_hbm, direct_ref),
                (swapped_hbm, swapped_ref),
            )
        )
    ]
    for copy in copies:
        copy.start()
    tile_cols = object_ref.shape[2]
    half = edges[0].shape[2]
    z_index, x_index, parity = here()
    copies[0].wait()
    low_ref[...] = probe_ref[...].astype(jnp.bfloat16)
    shared_ref[...] = jnp.where(z_index % 2 == 0, low_ref[0, 0], low_ref[1, 0])
    rest_ref[...] = low_ref[:, 1:]
    copies[1].wait()
    first, last = slice(0, half), slice(tile_cols - half, tile_cols)
    for channel in range(2):
        values = object_ref[channel].astype(jnp.bfloat16)
        packed_ref[channel] = values
        if sides == 1:
            edges[0][channel] = jnp.where(x_index == 0, values[:, last], values[:, first])
        else:
            edges[0][channel] = values[:, last]
            edges[1][channel] = values[:, first]
    copies[2].wait()
    spot_ref[...] = jnp.where(
        iota(spot_ref.shape, 0) == 0, centers_ref[0, 0, parity, 0], centers_ref[0, 0, parity, 1]
    )
    record = jnp.zeros(record_ref.shape, jnp.float32)
    line = iota(record_ref.shape, 0)
    for slot in range(slots):
        for axis in range(2):
            value = centers_ref[0, 0, slot, axis].astype(jnp.float32)
            record = jnp.where(line == 2 * slot + axis, value, record)
    record_ref[...] = record.astype(jnp.bfloat16)
    copies[3].wait()
    copies[4].wait()


def live_kernel(slots, record_ref, live_ref, out_ref):
    line = iota(record_ref.shape, 0)
    record = record_ref[...].astype(jnp.float32)
    record = jnp.where(line == 2 * slots, live_ref[0, 0].astype(jnp.float32), record)
    out_ref[...] = record.astype(jnp.bfloat16)


def position_of(record, slots, wanted):
    record = record[:, :128].astype(jnp.float32).astype(jnp.int32)[:, :1]

    def of_slot(axis):
        value = record[axis : axis + 1]
        for slot in range(1, slots):
            value = jnp.where(wanted == slot, record[2 * slot + axis : 2 * slot + axis + 1], value)
        return value

    return of_slot(0), of_slot(1), record[2 * slots : 2 * slots + 1] > wanted


def turned_back(value, side):
    return jnp.where(value == 0, 0, side - value)


def patch_of(sides, z_count, x_count, side, spot_ref, pieces):
    z_index, x_index, parity = here()
    row_at, col_at = spot_ref[0, 0], spot_ref[1, 0]
    half = side // 2
    even = parity == 0
    low_shown = z_index > 0
    high_shown = z_index < z_count - 1

    def joined(piece, a, b, channel):
        level = piece[channel].astype(jnp.float32)
        turn_a = a[channel].astype(jnp.float32)
        turn_b = b[channel].astype(jnp.float32)
        low = jnp.where(even & low_shown, turn_a, jnp.where(low_shown, turn_b, 0.0))
        high = jnp.where(even & high_shown, turn_b, jnp.where(high_shown, turn_a, 0.0))
        first = jnp.where(iota(low.shape, 0) >= row_at, low, high)
        return jnp.concatenate([first, level], axis=0)

    out = []
    for channel in range(2):
        own = joined(*pieces[:3], channel)
        sides_joined = [
            joined(*pieces[3 + 3 * index : 6 + 3 * index], channel) for index in range(sides)
        ]
        if sides == 1:
            left = jnp.where(x_index == 1, sides_joined[0], 0.0)
            right = jnp.where(x_index == 0, sides_joined[0], 0.0)
        else:
            left = jnp.where(x_index > 0, sides_joined[0], 0.0)
            right = jnp.where(x_index < x_count - 1, sides_joined[1], 0.0)
        at = iota(left.shape, 1)
        window = jnp.concatenate(
            [
                jnp.where(at >= col_at, left, own[:, half:]),
                jnp.where(at + half >= col_at, own[:, :half], right),
            ],
            axis=1,
        )
        window = pltpu.roll(window, turned_back(row_at, side), 0)
        out.append(pltpu.roll(window, turned_back(col_at, side), 1))
    return out


def modes_of(group):
    def reader(k):
        return lambda: (group[0, k].astype(jnp.float32), group[1, k].astype(jnp.float32))

    return [reader(k) for k in range(group.shape[1])]


def shared_mode(over_y, over_z):
    def read():
        z_index, _, _ = here()
        even = z_index % 2 == 0
        over_y_values = over_y[...].astype(jnp.float32)
        over_z_values = over_z[...].astype(jnp.float32)
        return (
            jnp.where(even, over_y_values, over_z_values),
            jnp.where(even, over_z_values, over_y_values),
        )

    return read


def forward(modes, patch, direct, swapped, far_ref, exit_ref, at):
    patch_real, patch_imag = patch
    side = patch_real.shape[0]
    power = jnp.zeros((side, side), jnp.float32)
    weight = jnp.zeros((side, side), jnp.float32)
    halves = []
    for k, mode in enumerate(modes):
        real, imag = mode()
        exit_wave = jnp.concatenate(
            [
                (real * patch_real - imag * patch_imag).astype(jnp.bfloat16),
                (real * patch_imag + imag * patch_real).astype(jnp.bfloat16),
            ],
            axis=0,
        )
        exit_ref[at + k] = exit_wave
        halves.append(wide(dot(direct, exit_wave).astype(jnp.bfloat16)))
        weight = weight + (real * real + imag * imag)
    far_all = dot(jnp.concatenate(halves, axis=0), swapped)
    for k in range(len(modes)):
        far = far_all[k * side : (k + 1) * side]
        far_ref[at + k] = far
        power = power + (far[:, :side] * far[:, :side] + far[:, side:] * far[:, side:])
    return power, weight


def backward(modes, factor, direct, swapped, far_ref, exit_ref, at):
    side = factor.shape[0]
    grad_real = jnp.zeros((side, side), jnp.float32)
    grad_imag = jnp.zeros((side, side), jnp.float32)
    halves = []
    for k in range(len(modes)):
        fixed = (far_ref[at + k] * factor).astype(jnp.bfloat16)
        halves.append(wide(dot(swapped, tall(fixed)).astype(jnp.bfloat16)))
    back_all = dot(jnp.concatenate(halves, axis=0), direct)
    for k, mode in enumerate(modes):
        back = back_all[k * side : (k + 1) * side]
        exit_wave = exit_ref[at + k].astype(jnp.float32)
        real, imag = mode()
        diff_real = back[:, :side] - exit_wave[:side]
        diff_imag = back[:, side:] - exit_wave[side:]
        grad_real = grad_real + (real * diff_real + imag * diff_imag)
        grad_imag = grad_imag + (real * diff_imag - imag * diff_real)
    return grad_real, grad_imag


def near_kernel(sides, z_count, x_count, spot_ref, *refs):
    n_pieces = 3 + 3 * sides
    pieces = from_sent_order(refs[:n_pieces])
    own, direct, swapped = refs[n_pieces : n_pieces + 3]
    patch_ref, far_ref, exit_ref, sum_ref = refs[n_pieces + 3 :]
    side = own.shape[2]
    patch = patch_of(sides, z_count, x_count, side, spot_ref, pieces)
    patch_ref[0], patch_ref[1] = patch
    sum_ref[0], sum_ref[1] = forward(
        modes_of(own), patch, direct[...], swapped[...], far_ref, exit_ref, 0
    )


def core_kernel(patch_ref, core, direct, swapped, far_ref, exit_ref, sum_ref):
    patch = (patch_ref[0], patch_ref[1])
    sum_ref[0], sum_ref[1] = forward(
        modes_of(core), patch, direct[...], swapped[...], far_ref, exit_ref, 0
    )


def over_kernel(patch_ref, over_y, over_z, rest, direct, swapped, far_ref, exit_ref, sum_ref):
    patch = (patch_ref[0], patch_ref[1])
    modes = [shared_mode(over_y, over_z)] + modes_of(rest)
    sum_ref[0], sum_ref[1] = forward(modes, patch, direct[...], swapped[...], far_ref, exit_ref, 0)


def back_kernel(sides, slots, tile_cols, record_ref, spot_ref, *refs):
    amplitude_ref, patch_ref, own, core = refs[:4]
    over_modes = [shared_mode(*refs[4:6])] + modes_of(refs[6])
    last_modes = [shared_mode(*refs[7:9])] + modes_of(refs[9])
    direct_ref, swapped_ref = refs[10:12]
    near_far, near_exit, near_sum, core_far, core_exit, core_sum = refs[12:18]
    over_far, over_exit, over_sum = refs[18:21]
    weight_out, own_out, keep_out, swap_out = refs[21:25]
    side_outs = refs[25 : 25 + sides]
    last_far, last_exit = refs[25 + sides :]
    side = own.shape[2]
    half = side // 2
    _, x_index, parity = here()
    row_at, col_at = spot_ref[0, 0], spot_ref[1, 0]
    _, _, is_live = position_of(record_ref, slots, parity)
    direct = direct_ref[...]
    swapped = swapped_ref[...]
    patch = (patch_ref[0], patch_ref[1])
    power, weight = forward(last_modes, patch, direct, swapped, last_far, last_exit, 0)
    power = (near_sum[0] + core_sum[0]) + (over_sum[0] + power)
    weight = (near_sum[1] + core_sum[1]) + (over_sum[1] + weight)
    weight_out[...] = weight.astype(jnp.bfloat16)
    amplitude = amplitude_ref[0, 0, parity].astype(jnp.float32)
    factor = amplitude / jnp.sqrt(power + power_floor)
    factor = jnp.concatenate([factor, factor], axis=1)
    tables = (factor, direct, swapped)
    grads = [
        backward(modes_of(own), *tables, near_far, near_exit, 0),
        backward(modes_of(core), *tables, core_far, core_exit, 0),
        backward(over_modes, *tables, over_far, over_exit, 0),
        backward(last_modes, *tables, last_far, last_exit, 0),
    ]
    even = parity == 0
    for channel in range(2):
        gradient = (grads[0][channel] + grads[1][channel]) + (grads[2][channel] + grads[3][channel])
        gradient = jnp.where(is_live, gradient, 0.0)
        gradient = pltpu.roll(pltpu.roll(gradient, col_at, 1), row_at, 0)
        first, second = gradient[:, :half], gradient[:, half:]
        at = iota(first.shape, 1)
        left = jnp.where(at >= col_at, first, 0.0)
        own = [
            jnp.where(at + half >= col_at, second, 0.0),
            jnp.where(at < col_at, first, 0.0),
        ]
        right = jnp.where(at + half < col_at, second, 0.0)
        if sides == 1:
            beside = [jnp.where(x_index == 0, right, left)]
        else:
            beside = [left, right]
        placed = jnp.concatenate(own + beside, axis=1)
        row = iota((half, placed.shape[1]), 0)
        low = jnp.where(row >= row_at, placed[:half], 0.0).astype(jnp.bfloat16)
        high = jnp.where(row < row_at, placed[:half], 0.0).astype(jnp.bfloat16)
        inner = placed[half:].astype(jnp.bfloat16)
        rows = slice(channel * half, (channel + 1) * half)
        own_out[rows] = inner[:, :tile_cols]
        keep_out[rows] = jnp.where(even, high, low)
        swap_out[rows] = jnp.where(even, low, high)
        for index, out in enumerate(side_outs):
            out[rows] = inner[:, tile_cols + index * half : tile_cols + (index + 1) * half]
    for out in side_outs:
        out[2 * half :] = record_ref[:, :half]


def meet_kernel(first_column, record_ref, keep_ref, swap_ref, *outs):
    at = first_column
    for out in outs:
        height, width = keep_ref.shape[0], out.shape[1]
        columns = slice(at, at + width)
        total = keep_ref[:, columns].astype(jnp.float32) + swap_ref[:, columns].astype(jnp.float32)
        out[:height] = total.astype(jnp.bfloat16)
        out[height:] = record_ref[:, :width]
        at += width


def placed_weight(weight, position, z_step, x_step, shown, shape):
    tile_rows, tile_cols = shape
    side = weight.shape[0]
    half = side // 2
    row, col, is_live = position
    row = jnp.where(is_live & shown, row + (z_step * tile_rows - half), nowhere)
    col = col + (x_step * tile_cols - half)
    put_rows = (iota((tile_rows, side), 0) == iota((tile_rows, side), 1) + row).astype(jnp.bfloat16)
    put_cols = (iota((side, tile_cols), 1) == iota((side, tile_cols), 0) + col).astype(jnp.bfloat16)
    return dot(dot(put_rows, weight).astype(jnp.bfloat16), put_cols)


def beside(sides, x_count):
    z_index, x_index, _ = here()
    if sides == 1:
        return [jnp.where(x_index == 0, 1, -1)], [z_index >= 0]
    return [1, -1], [x_index < x_count - 1, x_index > 0]


def edges_added(inner, edges, sides, shown):
    _, x_index, _ = here()
    half = edges[0].shape[1]
    first = jnp.zeros(edges[0].shape, jnp.float32)
    last = first
    for index, edge in enumerate(edges):
        if sides == 1:
            first = jnp.where(x_index == 1, edge, 0.0)
            last = jnp.where(x_index == 0, edge, 0.0)
        elif index == 0:
            last = jnp.where(shown[0], edge, 0.0)
        else:
            first = jnp.where(shown[1], edge, 0.0)
    middle = inner.shape[1] - 2 * half
    parts = [inner[:, :half] + first]
    if middle:
        parts.append(inner[:, half : half + middle])
    parts.append(inner[:, half + middle :] + last)
    return jnp.concatenate(parts, axis=1)


def level_kernel(sides, slots, x_count, weight_ref, record_ref, own_ref, *refs):
    levels, out_ref = refs[:sides], refs[-1]
    shape = out_ref.shape[1:]
    half = levels[0].shape[1]
    z_index, _, parity = here()
    x_steps, shown = beside(sides, x_count)
    weight = weight_ref[...]
    position = position_of(record_ref, slots, parity)
    total = placed_weight(weight, position, 0, 0, z_index >= 0, shape)
    for level, x_step, is_shown in zip(levels, x_steps, shown):
        position = position_of(level[2 * half :], slots, parity)
        total = total + placed_weight(weight, position, 0, x_step, is_shown, shape)
    out_ref[2] = total
    for channel in range(2):
        rows = slice(channel * half, (channel + 1) * half)
        edges = [level[rows].astype(jnp.float32) for level in levels]
        out_ref[channel] = edges_added(own_ref[rows].astype(jnp.float32), edges, sides, shown)


def sum_kernel(sides, slots, z_count, x_count, weight_ref, level_ref, rows_ref, *refs):
    corners, out_ref = refs[:sides], refs[-1]
    shape = out_ref.shape[1:]
    half = corners[0].shape[1]
    z_index, _, parity = here()
    z_step = jnp.where(parity == 0, -1, 1)
    z_shown = jnp.where(parity == 0, z_index > 0, z_index < z_count - 1)
    x_steps, shown = beside(sides, x_count)
    weight = weight_ref[...]
    total = level_ref[2]
    for piece, x_step, is_shown in zip(
        (rows_ref,) + corners, [0] + x_steps, [z_index >= 0] + shown
    ):
        for slot in range(slots):
            position = position_of(piece[2 * half :], slots, slot)
            total = total + placed_weight(
                weight, position, z_step, x_step, is_shown & z_shown, shape
            )
    out_ref[2] = total.astype(jnp.bfloat16)
    for channel in range(2):
        rows = slice(channel * half, (channel + 1) * half)
        edges = [corner[rows].astype(jnp.float32) for corner in corners]
        above = edges_added(rows_ref[rows].astype(jnp.float32), edges, sides, shown)
        total = level_ref[channel] + jnp.where(z_shown, above, 0.0)
        out_ref[channel] = total.astype(jnp.bfloat16)


def update_kernel(object_ref, own_ref, other_ref, out_ref):
    weight = own_ref[2].astype(jnp.float32) + other_ref[2].astype(jnp.float32) + regularizer
    for channel in range(2):
        gradient = own_ref[channel].astype(jnp.float32) + other_ref[channel].astype(jnp.float32)
        out_ref[channel] = object_ref[channel] + gradient / weight


def cost(products):
    return pl.CostEstimate(flops=products * 2 * 256**3, bytes_accessed=0, transcendentals=0)


def in_hbm(array):
    return pltpu.with_memory_space_constraint(array, pltpu.HBM)


def smem():
    return pl.BlockSpec(memory_space=pltpu.SMEM)


def hbm():
    return pl.BlockSpec(memory_space=pltpu.HBM)


def vmem():
    return pl.BlockSpec(memory_space=pltpu.VMEM)


def on_device(object_field, probe, amplitudes, centers, live):
    side = probe.shape[2]
    half = side // 2
    _, tile_rows, tile_cols = object_field.shape
    slots = centers.shape[2]
    z_count = lax.axis_size("tx")
    x_count = lax.axis_size("ty")
    m_count = lax.axis_size("mode")
    modes = probe.shape[1]
    if tile_rows != half or slots != 2 or m_count != 4 or z_count % 2 or x_count < 2 or modes < 2:
        raise ValueError("unsupported sizes")
    sides = 1 if x_count == 2 else 2
    axes = ("tx", "ty", "mode")

    def zigzag(x_step):
        def moved(z, m):
            if m % 2 == 0:
                return (z + 1, m) if z < z_count - 1 else (z, m ^ 1)
            return (z - 1, m) if z > 0 else (z, m ^ 1)

        pairs = []
        for z in range(z_count):
            for x in range(x_count):
                for m in range(m_count):
                    z_to, m_to = moved(z, m)
                    x_to = (x + x_step) % x_count
                    pairs.append(
                        (
                            (z * x_count + x) * m_count + m,
                            (z_to * x_count + x_to) * m_count + m_to,
                        )
                    )
        return pairs

    def level(step):
        return [(x, (x + step) % x_count) for x in range(x_count)]

    def exchange(array, flip):
        return lax.ppermute(array, "mode", [(m, m ^ flip) for m in range(m_count)])

    tables = [jnp.asarray(matrix) for matrix in dft_matrices(side)]
    probe_low, shared, rest, record, spot, direct, swapped, *packed = pl.pallas_call(
        functools.partial(start_kernel, sides, slots),
        out_shape=[
            jax.ShapeDtypeStruct(probe.shape, jnp.bfloat16),
            jax.ShapeDtypeStruct((side, side), jnp.bfloat16),
            jax.ShapeDtypeStruct((2, modes - 1, side, side), jnp.bfloat16),
            jax.ShapeDtypeStruct((record_rows, tile_cols), jnp.bfloat16),
            jax.ShapeDtypeStruct((8, 128), jnp.int32),
            jax.ShapeDtypeStruct((2 * side, 2 * side), jnp.bfloat16),
            jax.ShapeDtypeStruct((2 * side, 2 * side), jnp.bfloat16),
            jax.ShapeDtypeStruct(object_field.shape, jnp.bfloat16),
        ]
        + [jax.ShapeDtypeStruct((2, tile_rows, half), jnp.bfloat16)] * sides,
        in_specs=[hbm()] * 5,
        out_specs=[vmem()] * (8 + sides),
        scratch_shapes=[
            pltpu.VMEM(object_field.shape, jnp.float32),
            pltpu.VMEM(probe.shape, jnp.float32),
            pltpu.SMEM(centers.shape, jnp.int32),
            pltpu.SemaphoreType.DMA((5,)),
        ],
        compiler_params=pltpu.CompilerParams(vmem_limit_bytes=small_bytes),
        name="start",
    )(*(in_hbm(array) for array in (object_field, probe, centers, *tables)))
    over_y = exchange(shared, 2)
    probe_core = exchange(probe_low, 1)
    probe_core, rest = lax.optimization_barrier((probe_core, rest))
    rest = exchange(rest, 2)
    over_z = lax.ppermute(over_y, "tx", [(z, z ^ 1) for z in range(z_count)])
    x_steps = [1] if sides == 1 else [1, -1]
    rows = lax.ppermute(packed[0], axes, zigzag(0))
    corners = [lax.ppermute(edge, axes, zigzag(step)) for step, edge in zip(x_steps, packed[1:])]
    levels = [lax.ppermute(edge, "ty", level(step)) for step, edge in zip(x_steps, packed[1:])]
    corners, record = lax.optimization_barrier((corners, record))
    record = pl.pallas_call(
        functools.partial(live_kernel, slots),
        out_shape=jax.ShapeDtypeStruct(record.shape, jnp.bfloat16),
        in_specs=[vmem(), smem()],
        out_specs=vmem(),
        compiler_params=pltpu.CompilerParams(vmem_limit_bytes=small_bytes),
        cost_estimate=cost(40),
        name="live",
    )(record, live)
    corners, record = lax.optimization_barrier((corners, record))
    pieces = [packed[0], rows, exchange(rows, 1)]
    for at_level, corner in zip(levels, corners):
        pieces += [at_level, corner, exchange(corner, 1)]
    n_pieces = len(pieces)
    ext_cols = tile_cols + sides * half

    waves = [
        jax.ShapeDtypeStruct((modes, side, 2 * side), jnp.float32),
        jax.ShapeDtypeStruct((modes, 2 * side, side), jnp.bfloat16),
        jax.ShapeDtypeStruct((2, side, side), jnp.float32),
    ]
    patch, *near = pl.pallas_call(
        functools.partial(near_kernel, sides, z_count, x_count),
        out_shape=[jax.ShapeDtypeStruct((2, side, side), jnp.float32)] + waves,
        in_specs=[vmem()] * (n_pieces + 4),
        out_specs=[vmem()] * 4,
        compiler_params=pltpu.CompilerParams(vmem_limit_bytes=wave_bytes),
        cost_estimate=cost(1),
        name="near",
    )(spot, *in_sent_order(pieces), probe_low, direct, swapped)
    other = pl.pallas_call(
        core_kernel,
        out_shape=waves,
        in_specs=[vmem()] * 4,
        out_specs=[vmem()] * 3,
        compiler_params=pltpu.CompilerParams(vmem_limit_bytes=wave_bytes),
        cost_estimate=cost(1),
        name="core",
    )(patch, probe_core, direct, swapped)
    last_y = exchange(over_y, 1)
    over_z, rest, other = lax.optimization_barrier((over_z, rest, other))
    over_group = (over_y, over_z, rest)
    last_group = [last_y, exchange(over_z, 1), exchange(rest, 1)]
    over = pl.pallas_call(
        over_kernel,
        out_shape=waves,
        in_specs=[vmem()] * 6,
        out_specs=[vmem()] * 3,
        compiler_params=pltpu.CompilerParams(vmem_limit_bytes=wave_bytes),
        cost_estimate=cost(100),
        name="over",
    )(patch, *over_group, direct, swapped)
    piece_rows = 2 * half + record_rows
    shapes = [(side, side), (2 * half, tile_cols)] + [(2 * half, ext_cols)] * 2
    shapes += [(piece_rows, half)] * sides
    weight, own, keep, swap, *levels = pl.pallas_call(
        functools.partial(back_kernel, sides, slots, tile_cols),
        out_shape=[jax.ShapeDtypeStruct(shape, jnp.bfloat16) for shape in shapes],
        in_specs=[vmem()] * 23,
        out_specs=[vmem()] * (4 + sides),
        scratch_shapes=[
            pltpu.VMEM((modes, side, 2 * side), jnp.float32),
            pltpu.VMEM((modes, 2 * side, side), jnp.bfloat16),
        ],
        compiler_params=pltpu.CompilerParams(vmem_limit_bytes=wave_bytes),
        cost_estimate=cost(80),
        name="back",
    )(
        record,
        spot,
        amplitudes,
        patch,
        probe_low,
        probe_core,
        *over_group,
        *last_group,
        direct,
        swapped,
        *near,
        *other,
        *over,
    )
    levels = [lax.ppermute(piece, "ty", level(-step)) for piece, step in zip(levels, x_steps)]
    rows, *corners = pl.pallas_call(
        functools.partial(meet_kernel, 0),
        out_shape=[
            jax.ShapeDtypeStruct((piece_rows, width), jnp.bfloat16)
            for width in [tile_cols] + [half] * sides
        ],
        in_specs=[vmem()] * 3,
        out_specs=[vmem()] * (1 + sides),
        compiler_params=pltpu.CompilerParams(vmem_limit_bytes=small_bytes),
        name="meet",
    )(record, keep, exchange(swap, 1))
    rows = lax.ppermute(rows, axes, zigzag(0))
    corners = [
        lax.ppermute(piece, axes, zigzag(-step)) for piece, step in zip(corners, x_steps)
    ]
    leveled = pl.pallas_call(
        functools.partial(level_kernel, sides, slots, x_count),
        out_shape=jax.ShapeDtypeStruct((3, tile_rows, tile_cols), jnp.float32),
        in_specs=[vmem()] * (3 + sides),
        out_specs=vmem(),
        compiler_params=pltpu.CompilerParams(vmem_limit_bytes=small_bytes),
        cost_estimate=cost(80),
        name="levels",
    )(weight, record, own, *levels)
    summed = pl.pallas_call(
        functools.partial(sum_kernel, sides, slots, z_count, x_count),
        out_shape=jax.ShapeDtypeStruct((3, tile_rows, tile_cols), jnp.bfloat16),
        in_specs=[vmem()] * (3 + sides),
        out_specs=vmem(),
        compiler_params=pltpu.CompilerParams(vmem_limit_bytes=small_bytes),
        name="sums",
    )(weight, leveled, rows, *corners)
    return pl.pallas_call(
        update_kernel,
        out_shape=jax.ShapeDtypeStruct(object_field.shape, jnp.float32),
        in_specs=[vmem()] * 3,
        out_specs=vmem(),
        compiler_params=pltpu.CompilerParams(vmem_limit_bytes=small_bytes),
        name="update",
    )(object_field, summed, exchange(summed, 1))


def solution(mesh):
    return jax.shard_map(
        on_device,
        mesh=mesh,
        in_specs=(
            P(None, "tx", "ty"),
            P(None, "mode", None, None),
            P("tx", "ty", None, None, None),
            P("tx", "ty", None, None),
            P("tx", "ty"),
        ),
        out_specs=P(None, "tx", "ty"),
        check_vma=False,
    )
```

```python
import functools
import math

import jax
import jax.numpy as jnp
import numpy as np
from jax import lax
from jax.experimental import pallas as pl
from jax.experimental.pallas import tpu as pltpu
from jax.sharding import PartitionSpec as P

power_floor = 0.01
regularizer = 0.1
nowhere = -(1 << 20)
record_rows = 16
wave_bytes = 32 * 1024 * 1024
small_bytes = 8 * 1024 * 1024


def dft_matrices(side):
    line = np.arange(side, dtype=np.int32)
    angle = (line[:, None] * line[None, :] % side).astype(np.float32) * np.float32(
        2.0 * math.pi / side
    )
    scaling = np.float32(1.0 / math.sqrt(side))
    real = (np.cos(angle) * scaling).astype(jnp.bfloat16)
    imag = (-np.sin(angle) * scaling).astype(jnp.bfloat16)
    direct = np.block([[real, -imag], [imag, real]])
    swapped = np.block([[real, imag], [-imag, real]])
    return direct, swapped


def dot(left, right):
    return jnp.dot(left, right, preferred_element_type=jnp.float32)


def iota(shape, dim):
    return lax.broadcasted_iota(jnp.int32, shape, dim)


def sent_order(sides):
    corners = [at for index in range(sides) for at in (4 + 3 * index, 5 + 3 * index)]
    return [0] + corners + [1, 2] + [3 + 3 * index for index in range(sides)]


def in_sent_order(pieces):
    return [pieces[at] for at in sent_order(len(pieces) // 3 - 1)]


def from_sent_order(pieces):
    order = sent_order(len(pieces) // 3 - 1)
    return [pieces[order.index(at)] for at in range(len(pieces))]


def wide(tall):
    side = tall.shape[0] // 2
    return jnp.concatenate([tall[:side], tall[side:]], axis=1)


def tall(wide):
    side = wide.shape[1] // 2
    return jnp.concatenate([wide[:, :side], wide[:, side:]], axis=0)


def here():
    return (lax.axis_index("tx"), lax.axis_index("ty"), lax.axis_index("mode") % 2)


def start_kernel(
    sides,
    slots,
    object_hbm,
    probe_hbm,
    centers_hbm,
    direct_hbm,
    swapped_hbm,
    low_ref,
    shared_ref,
    rest_ref,
    record_ref,
    spot_ref,
    direct_ref,
    swapped_ref,
    packed_ref,
    *refs,
):
    edges = refs[:sides]
    object_ref, probe_ref, centers_ref, sems = refs[sides:]
    copies = [
        pltpu.make_async_copy(source, target, sems.at[index])
        for index, (source, target) in enumerate(
            (
                (probe_hbm, probe_ref),
                (object_hbm, object_ref),
                (centers_hbm, centers_ref),
                (direct_hbm, direct_ref),
                (swapped_hbm, swapped_ref),
            )
        )
    ]
    for copy in copies:
        copy.start()
    tile_cols = object_ref.shape[2]
    half = edges[0].shape[2]
    z_index, x_index, parity = here()
    copies[0].wait()
    low_ref[...] = probe_ref[...].astype(jnp.bfloat16)
    shared_ref[...] = jnp.where(z_index % 2 == 0, low_ref[0, 0], low_ref[1, 0])
    rest_ref[...] = low_ref[:, 1:]
    copies[1].wait()
    first, last = slice(0, half), slice(tile_cols - half, tile_cols)
    for channel in range(2):
        values = object_ref[channel].astype(jnp.bfloat16)
        packed_ref[channel] = values
        if sides == 1:
            edges[0][channel] = jnp.where(x_index == 0, values[:, last], values[:, first])
        else:
            edges[0][channel] = values[:, last]
            edges[1][channel] = values[:, first]
    copies[2].wait()
    spot_ref[...] = jnp.where(
        iota(spot_ref.shape, 0) == 0, centers_ref[0, 0, parity, 0], centers_ref[0, 0, parity, 1]
    )
    record = jnp.zeros(record_ref.shape, jnp.float32)
    line = iota(record_ref.shape, 0)
    for slot in range(slots):
        for axis in range(2):
            value = centers_ref[0, 0, slot, axis].astype(jnp.float32)
            record = jnp.where(line == 2 * slot + axis, value, record)
    record_ref[...] = record.astype(jnp.bfloat16)
    copies[3].wait()
    copies[4].wait()


def live_kernel(slots, record_ref, live_ref, out_ref):
    line = iota(record_ref.shape, 0)
    record = record_ref[...].astype(jnp.float32)
    record = jnp.where(line == 2 * slots, live_ref[0, 0].astype(jnp.float32), record)
    out_ref[...] = record.astype(jnp.bfloat16)


def position_of(record, slots, wanted):
    record = record[:, :128].astype(jnp.float32).astype(jnp.int32)[:, :1]

    def of_slot(axis):
        value = record[axis : axis + 1]
        for slot in range(1, slots):
            value = jnp.where(wanted == slot, record[2 * slot + axis : 2 * slot + axis + 1], value)
        return value

    return of_slot(0), of_slot(1), record[2 * slots : 2 * slots + 1] > wanted


def turned_back(value, side):
    return jnp.where(value == 0, 0, side - value)


def patch_of(sides, z_count, x_count, side, spot_ref, pieces):
    z_index, x_index, parity = here()
    row_at, col_at = spot_ref[0, 0], spot_ref[1, 0]
    half = side // 2
    even = parity == 0
    low_shown = z_index > 0
    high_shown = z_index < z_count - 1

    def joined(piece, a, b, channel):
        level = piece[channel].astype(jnp.float32)
        turn_a = a[channel].astype(jnp.float32)
        turn_b = b[channel].astype(jnp.float32)
        low = jnp.where(even & low_shown, turn_a, jnp.where(low_shown, turn_b, 0.0))
        high = jnp.where(even & high_shown, turn_b, jnp.where(high_shown, turn_a, 0.0))
        first = jnp.where(iota(low.shape, 0) >= row_at, low, high)
        return jnp.concatenate([first, level], axis=0)

    out = []
    for channel in range(2):
        own = joined(*pieces[:3], channel)
        sides_joined = [
            joined(*pieces[3 + 3 * index : 6 + 3 * index], channel) for index in range(sides)
        ]
        if sides == 1:
            left = jnp.where(x_index == 1, sides_joined[0], 0.0)
            right = jnp.where(x_index == 0, sides_joined[0], 0.0)
        else:
            left = jnp.where(x_index > 0, sides_joined[0], 0.0)
            right = jnp.where(x_index < x_count - 1, sides_joined[1], 0.0)
        at = iota(left.shape, 1)
        window = jnp.concatenate(
            [
                jnp.where(at >= col_at, left, own[:, half:]),
                jnp.where(at + half >= col_at, own[:, :half], right),
            ],
            axis=1,
        )
        window = pltpu.roll(window, turned_back(row_at, side), 0)
        out.append(pltpu.roll(window, turned_back(col_at, side), 1))
    return out


def modes_of(group):
    def reader(k):
        return lambda: (group[0, k].astype(jnp.float32), group[1, k].astype(jnp.float32))

    return [reader(k) for k in range(group.shape[1])]


def shared_mode(over_y, over_z):
    def read():
        z_index, _, _ = here()
        even = z_index % 2 == 0
        over_y_values = over_y[...].astype(jnp.float32)
        over_z_values = over_z[...].astype(jnp.float32)
        return (
            jnp.where(even, over_y_values, over_z_values),
            jnp.where(even, over_z_values, over_y_values),
        )

    return read


def forward(modes, patch, direct, swapped, far_ref, exit_ref, at):
    patch_real, patch_imag = patch
    side = patch_real.shape[0]
    power = jnp.zeros((side, side), jnp.float32)
    weight = jnp.zeros((side, side), jnp.float32)
    halves = []
    for k, mode in enumerate(modes):
        real, imag = mode()
        exit_wave = jnp.concatenate(
            [
                (real * patch_real - imag * patch_imag).astype(jnp.bfloat16),
                (real * patch_imag + imag * patch_real).astype(jnp.bfloat16),
            ],
            axis=0,
        )
        exit_ref[at + k] = exit_wave
        halves.append(wide(dot(direct, exit_wave).astype(jnp.bfloat16)))
        weight = weight + (real * real + imag * imag)
    far_all = dot(jnp.concatenate(halves, axis=0), swapped)
    for k in range(len(modes)):
        far = far_all[k * side : (k + 1) * side]
        far_ref[at + k] = far
        power = power + (far[:, :side] * far[:, :side] + far[:, side:] * far[:, side:])
    return power, weight


def backward(modes, factor, direct, swapped, far_ref, exit_ref, at):
    side = factor.shape[0]
    grad_real = jnp.zeros((side, side), jnp.float32)
    grad_imag = jnp.zeros((side, side), jnp.float32)
    halves = []
    for k in range(len(modes)):
        fixed = (far_ref[at + k] * factor).astype(jnp.bfloat16)
        halves.append(wide(dot(swapped, tall(fixed)).astype(jnp.bfloat16)))
    back_all = dot(jnp.concatenate(halves, axis=0), direct)
    for k, mode in enumerate(modes):
        back = back_all[k * side : (k + 1) * side]
        exit_wave = exit_ref[at + k].astype(jnp.float32)
        real, imag = mode()
        diff_real = back[:, :side] - exit_wave[:side]
        diff_imag = back[:, side:] - exit_wave[side:]
        grad_real = grad_real + (real * diff_real + imag * diff_imag)
        grad_imag = grad_imag + (real * diff_imag - imag * diff_real)
    return grad_real, grad_imag


def near_kernel(sides, z_count, x_count, spot_ref, *refs):
    n_pieces = 3 + 3 * sides
    pieces = from_sent_order(refs[:n_pieces])
    own, direct, swapped = refs[n_pieces : n_pieces + 3]
    patch_ref, far_ref, exit_ref, sum_ref = refs[n_pieces + 3 :]
    side = own.shape[2]
    patch = patch_of(sides, z_count, x_count, side, spot_ref, pieces)
    patch_ref[0], patch_ref[1] = patch
    sum_ref[0], sum_ref[1] = forward(
        modes_of(own), patch, direct[...], swapped[...], far_ref, exit_ref, 0
    )


def core_kernel(patch_ref, core, direct, swapped, far_ref, exit_ref, sum_ref):
    patch = (patch_ref[0], patch_ref[1])
    sum_ref[0], sum_ref[1] = forward(
        modes_of(core), patch, direct[...], swapped[...], far_ref, exit_ref, 0
    )


def over_kernel(patch_ref, over_y, over_z, rest, direct, swapped, far_ref, exit_ref, sum_ref):
    patch = (patch_ref[0], patch_ref[1])
    modes = [shared_mode(over_y, over_z)] + modes_of(rest)
    sum_ref[0], sum_ref[1] = forward(modes, patch, direct[...], swapped[...], far_ref, exit_ref, 0)


def back_kernel(sides, slots, tile_cols, record_ref, spot_ref, *refs):
    amplitude_ref, patch_ref, own, core = refs[:4]
    over_modes = [shared_mode(*refs[4:6])] + modes_of(refs[6])
    last_modes = [shared_mode(*refs[7:9])] + modes_of(refs[9])
    direct_ref, swapped_ref = refs[10:12]
    near_far, near_exit, near_sum, core_far, core_exit, core_sum = refs[12:18]
    over_far, over_exit, over_sum = refs[18:21]
    weight_out, own_out, keep_out, swap_out = refs[21:25]
    side_outs = refs[25 : 25 + sides]
    last_far, last_exit = refs[25 + sides :]
    side = own.shape[2]
    half = side // 2
    _, x_index, parity = here()
    row_at, col_at = spot_ref[0, 0], spot_ref[1, 0]
    _, _, is_live = position_of(record_ref, slots, parity)
    direct = direct_ref[...]
    swapped = swapped_ref[...]
    patch = (patch_ref[0], patch_ref[1])
    power, weight = forward(last_modes, patch, direct, swapped, last_far, last_exit, 0)
    power = (near_sum[0] + core_sum[0]) + (over_sum[0] + power)
    weight = (near_sum[1] + core_sum[1]) + (over_sum[1] + weight)
    weight_out[...] = weight.astype(jnp.bfloat16)
    amplitude = amplitude_ref[0, 0, parity].astype(jnp.float32)
    factor = amplitude / jnp.sqrt(power + power_floor)
    factor = jnp.concatenate([factor, factor], axis=1)
    tables = (factor, direct, swapped)
    grads = [
        backward(modes_of(own), *tables, near_far, near_exit, 0),
        backward(modes_of(core), *tables, core_far, core_exit, 0),
        backward(over_modes, *tables, over_far, over_exit, 0),
        backward(last_modes, *tables, last_far, last_exit, 0),
    ]
    even = parity == 0
    for channel in range(2):
        gradient = (grads[0][channel] + grads[1][channel]) + (grads[2][channel] + grads[3][channel])
        gradient = jnp.where(is_live, gradient, 0.0)
        gradient = pltpu.roll(pltpu.roll(gradient, col_at, 1), row_at, 0)
        first, second = gradient[:, :half], gradient[:, half:]
        at = iota(first.shape, 1)
        left = jnp.where(at >= col_at, first, 0.0)
        own = [
            jnp.where(at + half >= col_at, second, 0.0),
            jnp.where(at < col_at, first, 0.0),
        ]
        right = jnp.where(at + half < col_at, second, 0.0)
        if sides == 1:
            beside = [jnp.where(x_index == 0, right, left)]
        else:
            beside = [left, right]
        placed = jnp.concatenate(own + beside, axis=1)
        row = iota((half, placed.shape[1]), 0)
        low = jnp.where(row >= row_at, placed[:half], 0.0).astype(jnp.bfloat16)
        high = jnp.where(row < row_at, placed[:half], 0.0).astype(jnp.bfloat16)
        inner = placed[half:].astype(jnp.bfloat16)
        rows = slice(channel * half, (channel + 1) * half)
        own_out[rows] = inner[:, :tile_cols]
        keep_out[rows] = jnp.where(even, high, low)
        swap_out[rows] = jnp.where(even, low, high)
        for index, out in enumerate(side_outs):
            out[rows] = inner[:, tile_cols + index * half : tile_cols + (index + 1) * half]
    for out in side_outs:
        out[2 * half :] = record_ref[:, :half]


def meet_kernel(first_column, record_ref, keep_ref, swap_ref, *outs):
    at = first_column
    for out in outs:
        height, width = keep_ref.shape[0], out.shape[1]
        columns = slice(at, at + width)
        total = keep_ref[:, columns].astype(jnp.float32) + swap_ref[:, columns].astype(jnp.float32)
        out[:height] = total.astype(jnp.bfloat16)
        out[height:] = record_ref[:, :width]
        at += width


def placed_weight(weight, position, z_step, x_step, shown, shape):
    tile_rows, tile_cols = shape
    side = weight.shape[0]
    half = side // 2
    row, col, is_live = position
    row = jnp.where(is_live & shown, row + (z_step * tile_rows - half), nowhere)
    col = col + (x_step * tile_cols - half)
    put_rows = (iota((tile_rows, side), 0) == iota((tile_rows, side), 1) + row).astype(jnp.bfloat16)
    put_cols = (iota((side, tile_cols), 1) == iota((side, tile_cols), 0) + col).astype(jnp.bfloat16)
    return dot(dot(put_rows, weight).astype(jnp.bfloat16), put_cols)


def beside(sides, x_count):
    z_index, x_index, _ = here()
    if sides == 1:
        return [jnp.where(x_index == 0, 1, -1)], [z_index >= 0]
    return [1, -1], [x_index < x_count - 1, x_index > 0]


def edges_added(inner, edges, sides, shown):
    _, x_index, _ = here()
    half = edges[0].shape[1]
    first = jnp.zeros(edges[0].shape, jnp.float32)
    last = first
    for index, edge in enumerate(edges):
        if sides == 1:
            first = jnp.where(x_index == 1, edge, 0.0)
            last = jnp.where(x_index == 0, edge, 0.0)
        elif index == 0:
            last = jnp.where(shown[0], edge, 0.0)
        else:
            first = jnp.where(shown[1], edge, 0.0)
    middle = inner.shape[1] - 2 * half
    parts = [inner[:, :half] + first]
    if middle:
        parts.append(inner[:, half : half + middle])
    parts.append(inner[:, half + middle :] + last)
    return jnp.concatenate(parts, axis=1)


def level_kernel(sides, slots, x_count, weight_ref, record_ref, own_ref, *refs):
    levels, out_ref = refs[:sides], refs[-1]
    shape = out_ref.shape[1:]
    half = levels[0].shape[1]
    z_index, _, parity = here()
    x_steps, shown = beside(sides, x_count)
    weight = weight_ref[...]
    position = position_of(record_ref, slots, parity)
    total = placed_weight(weight, position, 0, 0, z_index >= 0, shape)
    for level, x_step, is_shown in zip(levels, x_steps, shown):
        position = position_of(level[2 * half :], slots, parity)
        total = total + placed_weight(weight, position, 0, x_step, is_shown, shape)
    out_ref[2] = total
    for channel in range(2):
        rows = slice(channel * half, (channel + 1) * half)
        edges = [level[rows].astype(jnp.float32) for level in levels]
        out_ref[channel] = edges_added(own_ref[rows].astype(jnp.float32), edges, sides, shown)


def sum_kernel(sides, slots, z_count, x_count, weight_ref, level_ref, rows_ref, *refs):
    corners, out_ref = refs[:sides], refs[-1]
    shape = out_ref.shape[1:]
    half = corners[0].shape[1]
    z_index, _, parity = here()
    z_step = jnp.where(parity == 0, -1, 1)
    z_shown = jnp.where(parity == 0, z_index > 0, z_index < z_count - 1)
    x_steps, shown = beside(sides, x_count)
    weight = weight_ref[...]
    total = level_ref[2]
    for piece, x_step, is_shown in zip(
        (rows_ref,) + corners, [0] + x_steps, [z_index >= 0] + shown
    ):
        for slot in range(slots):
            position = position_of(piece[2 * half :], slots, slot)
            total = total + placed_weight(
                weight, position, z_step, x_step, is_shown & z_shown, shape
            )
    out_ref[2] = total.astype(jnp.bfloat16)
    for channel in range(2):
        rows = slice(channel * half, (channel + 1) * half)
        edges = [corner[rows].astype(jnp.float32) for corner in corners]
        above = edges_added(rows_ref[rows].astype(jnp.float32), edges, sides, shown)
        total = level_ref[channel] + jnp.where(z_shown, above, 0.0)
        out_ref[channel] = total.astype(jnp.bfloat16)


def update_kernel(object_ref, own_ref, other_ref, out_ref):
    weight = own_ref[2].astype(jnp.float32) + other_ref[2].astype(jnp.float32) + regularizer
    for channel in range(2):
        gradient = own_ref[channel].astype(jnp.float32) + other_ref[channel].astype(jnp.float32)
        out_ref[channel] = object_ref[channel] + gradient / weight


def cost(products):
    return pl.CostEstimate(flops=products * 2 * 256**3, bytes_accessed=0, transcendentals=0)


def in_hbm(array):
    return pltpu.with_memory_space_constraint(array, pltpu.HBM)


def smem():
    return pl.BlockSpec(memory_space=pltpu.SMEM)


def hbm():
    return pl.BlockSpec(memory_space=pltpu.HBM)


def vmem():
    return pl.BlockSpec(memory_space=pltpu.VMEM)


def on_device(object_field, probe, amplitudes, centers, live):
    side = probe.shape[2]
    half = side // 2
    _, tile_rows, tile_cols = object_field.shape
    slots = centers.shape[2]
    z_count = lax.axis_size("tx")
    x_count = lax.axis_size("ty")
    m_count = lax.axis_size("mode")
    modes = probe.shape[1]
    if tile_rows != half or slots != 2 or m_count != 4 or z_count % 2 or x_count < 2 or modes < 2:
        raise ValueError("unsupported sizes")
    sides = 1 if x_count == 2 else 2
    axes = ("tx", "ty", "mode")

    def zigzag(x_step):
        def moved(z, m):
            if m % 2 == 0:
                return (z + 1, m) if z < z_count - 1 else (z, m ^ 1)
            return (z - 1, m) if z > 0 else (z, m ^ 1)

        pairs = []
        for z in range(z_count):
            for x in range(x_count):
                for m in range(m_count):
                    z_to, m_to = moved(z, m)
                    x_to = (x + x_step) % x_count
                    pairs.append(
                        (
                            (z * x_count + x) * m_count + m,
                            (z_to * x_count + x_to) * m_count + m_to,
                        )
                    )
        return pairs

    def level(step):
        return [(x, (x + step) % x_count) for x in range(x_count)]

    def exchange(array, flip):
        return lax.ppermute(array, "mode", [(m, m ^ flip) for m in range(m_count)])

    tables = [jnp.asarray(matrix) for matrix in dft_matrices(side)]
    probe_low, shared, rest, record, spot, direct, swapped, *packed = pl.pallas_call(
        functools.partial(start_kernel, sides, slots),
        out_shape=[
            jax.ShapeDtypeStruct(probe.shape, jnp.bfloat16),
            jax.ShapeDtypeStruct((side, side), jnp.bfloat16),
            jax.ShapeDtypeStruct((2, modes - 1, side, side), jnp.bfloat16),
            jax.ShapeDtypeStruct((record_rows, tile_cols), jnp.bfloat16),
            jax.ShapeDtypeStruct((8, 128), jnp.int32),
            jax.ShapeDtypeStruct((2 * side, 2 * side), jnp.bfloat16),
            jax.ShapeDtypeStruct((2 * side, 2 * side), jnp.bfloat16),
            jax.ShapeDtypeStruct(object_field.shape, jnp.bfloat16),
        ]
        + [jax.ShapeDtypeStruct((2, tile_rows, half), jnp.bfloat16)] * sides,
        in_specs=[hbm()] * 5,
        out_specs=[vmem()] * (8 + sides),
        scratch_shapes=[
            pltpu.VMEM(object_field.shape, jnp.float32),
            pltpu.VMEM(probe.shape, jnp.float32),
            pltpu.SMEM(centers.shape, jnp.int32),
            pltpu.SemaphoreType.DMA((5,)),
        ],
        compiler_params=pltpu.CompilerParams(vmem_limit_bytes=small_bytes),
        name="start",
    )(*(in_hbm(array) for array in (object_field, probe, centers, *tables)))
    over_y = exchange(shared, 2)
    probe_core = exchange(probe_low, 1)
    probe_core, rest = lax.optimization_barrier((probe_core, rest))
    rest = exchange(rest, 2)
    over_z = lax.ppermute(over_y, "tx", [(z, z ^ 1) for z in range(z_count)])
    x_steps = [1] if sides == 1 else [1, -1]
    rows = lax.ppermute(packed[0], axes, zigzag(0))
    corners = [lax.ppermute(edge, axes, zigzag(step)) for step, edge in zip(x_steps, packed[1:])]
    levels = [lax.ppermute(edge, "ty", level(step)) for step, edge in zip(x_steps, packed[1:])]
    corners, record = lax.optimization_barrier((corners, record))
    record = pl.pallas_call(
        functools.partial(live_kernel, slots),
        out_shape=jax.ShapeDtypeStruct(record.shape, jnp.bfloat16),
        in_specs=[vmem(), smem()],
        out_specs=vmem(),
        compiler_params=pltpu.CompilerParams(vmem_limit_bytes=small_bytes),
        cost_estimate=cost(40),
        name="live",
    )(record, live)
    corners, record = lax.optimization_barrier((corners, record))
    pieces = [packed[0], rows, exchange(rows, 1)]
    for at_level, corner in zip(levels, corners):
        pieces += [at_level, corner, exchange(corner, 1)]
    n_pieces = len(pieces)
    ext_cols = tile_cols + sides * half

    waves = [
        jax.ShapeDtypeStruct((modes, side, 2 * side), jnp.float32),
        jax.ShapeDtypeStruct((modes, 2 * side, side), jnp.bfloat16),
        jax.ShapeDtypeStruct((2, side, side), jnp.float32),
    ]
    patch, *near = pl.pallas_call(
        functools.partial(near_kernel, sides, z_count, x_count),
        out_shape=[jax.ShapeDtypeStruct((2, side, side), jnp.float32)] + waves,
        in_specs=[vmem()] * (n_pieces + 4),
        out_specs=[vmem()] * 4,
        compiler_params=pltpu.CompilerParams(vmem_limit_bytes=wave_bytes),
        cost_estimate=cost(1),
        name="near",
    )(spot, *in_sent_order(pieces), probe_low, direct, swapped)
    other = pl.pallas_call(
        core_kernel,
        out_shape=waves,
        in_specs=[vmem()] * 4,
        out_specs=[vmem()] * 3,
        compiler_params=pltpu.CompilerParams(vmem_limit_bytes=wave_bytes),
        cost_estimate=cost(1),
        name="core",
    )(patch, probe_core, direct, swapped)
    last_y = exchange(over_y, 1)
    over_z, rest, other = lax.optimization_barrier((over_z, rest, other))
    over_group = (over_y, over_z, rest)
    last_group = [last_y, exchange(over_z, 1), exchange(rest, 1)]
    over = pl.pallas_call(
        over_kernel,
        out_shape=waves,
        in_specs=[vmem()] * 6,
        out_specs=[vmem()] * 3,
        compiler_params=pltpu.CompilerParams(vmem_limit_bytes=wave_bytes),
        cost_estimate=cost(100),
        name="over",
    )(patch, *over_group, direct, swapped)
    piece_rows = 2 * half + record_rows
    shapes = [(side, side), (2 * half, tile_cols)] + [(2 * half, ext_cols)] * 2
    shapes += [(piece_rows, half)] * sides
    weight, own, keep, swap, *levels = pl.pallas_call(
        functools.partial(back_kernel, sides, slots, tile_cols),
        out_shape=[jax.ShapeDtypeStruct(shape, jnp.bfloat16) for shape in shapes],
        in_specs=[vmem()] * 23,
        out_specs=[vmem()] * (4 + sides),
        scratch_shapes=[
            pltpu.VMEM((modes, side, 2 * side), jnp.float32),
            pltpu.VMEM((modes, 2 * side, side), jnp.bfloat16),
        ],
        compiler_params=pltpu.CompilerParams(vmem_limit_bytes=wave_bytes),
        cost_estimate=cost(80),
        name="back",
    )(
        record,
        spot,
        amplitudes,
        patch,
        probe_low,
        probe_core,
        *over_group,
        *last_group,
        direct,
        swapped,
        *near,
        *other,
        *over,
    )
    levels = [lax.ppermute(piece, "ty", level(-step)) for piece, step in zip(levels, x_steps)]
    rows, *corners = pl.pallas_call(
        functools.partial(meet_kernel, 0),
        out_shape=[
            jax.ShapeDtypeStruct((piece_rows, width), jnp.bfloat16)
            for width in [tile_cols] + [half] * sides
        ],
        in_specs=[vmem()] * 3,
        out_specs=[vmem()] * (1 + sides),
        compiler_params=pltpu.CompilerParams(vmem_limit_bytes=small_bytes),
        name="meet",
    )(record, keep, exchange(swap, 1))
    rows = lax.ppermute(rows, axes, zigzag(0))
    corners = [
        lax.ppermute(piece, axes, zigzag(-step)) for piece, step in zip(corners, x_steps)
    ]
    leveled = pl.pallas_call(
        functools.partial(level_kernel, sides, slots, x_count),
        out_shape=jax.ShapeDtypeStruct((3, tile_rows, tile_cols), jnp.float32),
        in_specs=[vmem()] * (3 + sides),
        out_specs=vmem(),
        compiler_params=pltpu.CompilerParams(vmem_limit_bytes=small_bytes),
        cost_estimate=cost(40),
        name="levels",
    )(weight, record, own, *levels)
    summed = pl.pallas_call(
        functools.partial(sum_kernel, sides, slots, z_count, x_count),
        out_shape=jax.ShapeDtypeStruct((3, tile_rows, tile_cols), jnp.bfloat16),
        in_specs=[vmem()] * (3 + sides),
        out_specs=vmem(),
        compiler_params=pltpu.CompilerParams(vmem_limit_bytes=small_bytes),
        name="sums",
    )(weight, leveled, rows, *corners)
    return pl.pallas_call(
        update_kernel,
        out_shape=jax.ShapeDtypeStruct(object_field.shape, jnp.float32),
        in_specs=[vmem()] * 3,
        out_specs=vmem(),
        compiler_params=pltpu.CompilerParams(vmem_limit_bytes=small_bytes),
        name="update",
    )(object_field, summed, exchange(summed, 1))


def solution(mesh):
    return jax.shard_map(
        on_device,
        mesh=mesh,
        in_specs=(
            P(None, "tx", "ty"),
            P(None, "mode", None, None),
            P("tx", "ty", None, None, None),
            P("tx", "ty", None, None),
            P("tx", "ty"),
        ),
        out_specs=P(None, "tx", "ty"),
        check_vma=False,
    )
```

```python
import functools
import math

import jax
import jax.numpy as jnp
import numpy as np
from jax import lax
from jax.experimental import pallas as pl
from jax.experimental.pallas import tpu as pltpu
from jax.sharding import PartitionSpec as P

power_floor = 0.01
regularizer = 0.1
nowhere = -(1 << 20)
record_rows = 16
wave_bytes = 32 * 1024 * 1024
small_bytes = 8 * 1024 * 1024


def dft_matrices(side):
    line = np.arange(side, dtype=np.int32)
    angle = (line[:, None] * line[None, :] % side).astype(np.float32) * np.float32(
        2.0 * math.pi / side
    )
    scaling = np.float32(1.0 / math.sqrt(side))
    real = (np.cos(angle) * scaling).astype(jnp.bfloat16)
    imag = (-np.sin(angle) * scaling).astype(jnp.bfloat16)
    direct = np.block([[real, -imag], [imag, real]])
    swapped = np.block([[real, imag], [-imag, real]])
    return direct, swapped


def dot(left, right):
    return jnp.dot(left, right, preferred_element_type=jnp.float32)


def iota(shape, dim):
    return lax.broadcasted_iota(jnp.int32, shape, dim)


def wide(tall):
    side = tall.shape[0] // 2
    return jnp.concatenate([tall[:side], tall[side:]], axis=1)


def tall(wide):
    side = wide.shape[1] // 2
    return jnp.concatenate([wide[:, :side], wide[:, side:]], axis=0)


def here():
    return (lax.axis_index("tx"), lax.axis_index("ty"), lax.axis_index("mode") % 2)


def start_kernel(
    sides,
    slots,
    object_hbm,
    probe_hbm,
    centers_hbm,
    direct_hbm,
    swapped_hbm,
    low_ref,
    shared_ref,
    rest_ref,
    record_ref,
    spot_ref,
    direct_ref,
    swapped_ref,
    packed_ref,
    *refs,
):
    edges = refs[:sides]
    object_ref, probe_ref, centers_ref, sems = refs[sides:]
    copies = [
        pltpu.make_async_copy(source, target, sems.at[index])
        for index, (source, target) in enumerate(
            (
                (probe_hbm, probe_ref),
                (object_hbm, object_ref),
                (centers_hbm, centers_ref),
                (direct_hbm, direct_ref),
                (swapped_hbm, swapped_ref),
            )
        )
    ]
    for copy in copies:
        copy.start()
    tile_cols = object_ref.shape[2]
    half = edges[0].shape[2]
    z_index, x_index, parity = here()
    copies[0].wait()
    low_ref[...] = probe_ref[...].astype(jnp.bfloat16)
    shared_ref[...] = jnp.where(z_index % 2 == 0, low_ref[0, 0], low_ref[1, 0])
    rest_ref[...] = low_ref[:, 1:]
    copies[1].wait()
    first, last = slice(0, half), slice(tile_cols - half, tile_cols)
    for channel in range(2):
        values = object_ref[channel].astype(jnp.bfloat16)
        packed_ref[channel] = values
        if sides == 1:
            edges[0][channel] = jnp.where(x_index == 0, values[:, last], values[:, first])
        else:
            edges[0][channel] = values[:, last]
            edges[1][channel] = values[:, first]
    copies[2].wait()
    spot_ref[...] = jnp.where(
        iota(spot_ref.shape, 0) == 0, centers_ref[0, 0, parity, 0], centers_ref[0, 0, parity, 1]
    )
    record = jnp.zeros(record_ref.shape, jnp.float32)
    line = iota(record_ref.shape, 0)
    for slot in range(slots):
        for axis in range(2):
            value = centers_ref[0, 0, slot, axis].astype(jnp.float32)
            record = jnp.where(line == 2 * slot + axis, value, record)
    record_ref[...] = record.astype(jnp.bfloat16)
    copies[3].wait()
    copies[4].wait()


def live_kernel(slots, record_ref, live_ref, out_ref):
    line = iota(record_ref.shape, 0)
    record = record_ref[...].astype(jnp.float32)
    record = jnp.where(line == 2 * slots, live_ref[0, 0].astype(jnp.float32), record)
    out_ref[...] = record.astype(jnp.bfloat16)


def position_of(record, slots, wanted):
    record = record[:, :128].astype(jnp.float32).astype(jnp.int32)[:, :1]

    def of_slot(axis):
        value = record[axis : axis + 1]
        for slot in range(1, slots):
            value = jnp.where(wanted == slot, record[2 * slot + axis : 2 * slot + axis + 1], value)
        return value

    return of_slot(0), of_slot(1), record[2 * slots : 2 * slots + 1] > wanted


def turned_back(value, side):
    return jnp.where(value == 0, 0, side - value)


def joined(piece, turn_a, turn_b, channel, z_count, row_at):
    z_index, _, parity = here()
    even = parity == 0
    low_shown = z_index > 0
    high_shown = z_index < z_count - 1
    level = piece[channel].astype(jnp.float32)
    first = turn_a[channel].astype(jnp.float32)
    second = turn_b[channel].astype(jnp.float32)
    low = jnp.where(even & low_shown, first, jnp.where(low_shown, second, 0.0))
    high = jnp.where(even & high_shown, second, jnp.where(high_shown, first, 0.0))
    upper = jnp.where(iota(low.shape, 0) >= row_at, low, high)
    return jnp.concatenate([upper, level], axis=0)


def edge_kernel(z_count, spot_ref, level_ref, turn_a, turn_b, out_ref):
    for channel in range(2):
        out_ref[channel] = joined(level_ref, turn_a, turn_b, channel, z_count, spot_ref[0, 0])


def patch_of(z_count, x_count, spot_ref, pieces, edges):
    _, x_index, _ = here()
    row_at, col_at = spot_ref[0, 0], spot_ref[1, 0]
    side, half = edges[0].shape[1:]
    out = []
    for channel in range(2):
        own = joined(*pieces, channel, z_count, row_at)
        if len(edges) == 1:
            left = jnp.where(x_index == 1, edges[0][channel], 0.0)
            right = jnp.where(x_index == 0, edges[0][channel], 0.0)
        else:
            left = jnp.where(x_index > 0, edges[0][channel], 0.0)
            right = jnp.where(x_index < x_count - 1, edges[1][channel], 0.0)
        at = iota(left.shape, 1)
        window = jnp.concatenate(
            [
                jnp.where(at >= col_at, left, own[:, half:]),
                jnp.where(at + half >= col_at, own[:, :half], right),
            ],
            axis=1,
        )
        window = pltpu.roll(window, turned_back(row_at, side), 0)
        out.append(pltpu.roll(window, turned_back(col_at, side), 1))
    return out


def modes_of(group):
    def reader(k):
        return lambda: (group[0, k].astype(jnp.float32), group[1, k].astype(jnp.float32))

    return [reader(k) for k in range(group.shape[1])]


def shared_mode(over_y, over_z):
    def read():
        z_index, _, _ = here()
        even = z_index % 2 == 0
        over_y_values = over_y[...].astype(jnp.float32)
        over_z_values = over_z[...].astype(jnp.float32)
        return (
            jnp.where(even, over_y_values, over_z_values),
            jnp.where(even, over_z_values, over_y_values),
        )

    return read


def forward(modes, patch, direct, swapped, far_ref, exit_ref, at):
    patch_real, patch_imag = patch
    side = patch_real.shape[0]
    power = jnp.zeros((side, side), jnp.float32)
    weight = jnp.zeros((side, side), jnp.float32)
    halves = []
    for k, mode in enumerate(modes):
        real, imag = mode()
        exit_wave = jnp.concatenate(
            [
                (real * patch_real - imag * patch_imag).astype(jnp.bfloat16),
                (real * patch_imag + imag * patch_real).astype(jnp.bfloat16),
            ],
            axis=0,
        )
        exit_ref[at + k] = exit_wave
        halves.append(wide(dot(direct, exit_wave).astype(jnp.bfloat16)))
        weight = weight + (real * real + imag * imag)
    far_all = dot(jnp.concatenate(halves, axis=0), swapped)
    for k in range(len(modes)):
        far = far_all[k * side : (k + 1) * side]
        far_ref[at + k] = far
        power = power + (far[:, :side] * far[:, :side] + far[:, side:] * far[:, side:])
    return power, weight


def backward(modes, factor, direct, swapped, far_ref, exit_ref, at):
    side = factor.shape[0]
    grad_real = jnp.zeros((side, side), jnp.float32)
    grad_imag = jnp.zeros((side, side), jnp.float32)
    halves = []
    for k in range(len(modes)):
        fixed = (far_ref[at + k] * factor).astype(jnp.bfloat16)
        halves.append(wide(dot(swapped, tall(fixed)).astype(jnp.bfloat16)))
    back_all = dot(jnp.concatenate(halves, axis=0), direct)
    for k, mode in enumerate(modes):
        back = back_all[k * side : (k + 1) * side]
        exit_wave = exit_ref[at + k].astype(jnp.float32)
        real, imag = mode()
        diff_real = back[:, :side] - exit_wave[:side]
        diff_imag = back[:, side:] - exit_wave[side:]
        grad_real = grad_real + (real * diff_real + imag * diff_imag)
        grad_imag = grad_imag + (real * diff_imag - imag * diff_real)
    return grad_real, grad_imag


def near_kernel(sides, z_count, x_count, spot_ref, *refs):
    pieces, edges = refs[:3], refs[3 : 3 + sides]
    own, direct, swapped, patch_ref, far_ref, exit_ref, sum_ref = refs[3 + sides :]
    patch = patch_of(z_count, x_count, spot_ref, pieces, edges)
    patch_ref[0], patch_ref[1] = patch
    sum_ref[0], sum_ref[1] = forward(
        modes_of(own), patch, direct[...], swapped[...], far_ref, exit_ref, 0
    )


def core_kernel(patch_ref, core, direct, swapped, far_ref, exit_ref, sum_ref):
    patch = (patch_ref[0], patch_ref[1])
    sum_ref[0], sum_ref[1] = forward(
        modes_of(core), patch, direct[...], swapped[...], far_ref, exit_ref, 0
    )


def over_kernel(patch_ref, over_y, over_z, rest, direct, swapped, far_ref, exit_ref, sum_ref):
    patch = (patch_ref[0], patch_ref[1])
    modes = [shared_mode(over_y, over_z)] + modes_of(rest)
    sum_ref[0], sum_ref[1] = forward(modes, patch, direct[...], swapped[...], far_ref, exit_ref, 0)


def back_kernel(sides, slots, tile_cols, record_ref, spot_ref, *refs):
    amplitude_ref, patch_ref, own, core = refs[:4]
    over_modes = [shared_mode(*refs[4:6])] + modes_of(refs[6])
    last_modes = [shared_mode(*refs[7:9])] + modes_of(refs[9])
    direct_ref, swapped_ref = refs[10:12]
    near_far, near_exit, near_sum, core_far, core_exit, core_sum = refs[12:18]
    over_far, over_exit, over_sum = refs[18:21]
    weight_out, own_out, keep_out, swap_out = refs[21:25]
    side_outs = refs[25 : 25 + sides]
    last_far, last_exit = refs[25 + sides :]
    side = own.shape[2]
    half = side // 2
    _, x_index, parity = here()
    row_at, col_at = spot_ref[0, 0], spot_ref[1, 0]
    _, _, is_live = position_of(record_ref, slots, parity)
    direct = direct_ref[...]
    swapped = swapped_ref[...]
    patch = (patch_ref[0], patch_ref[1])
    power, weight = forward(last_modes, patch, direct, swapped, last_far, last_exit, 0)
    power = (near_sum[0] + core_sum[0]) + (over_sum[0] + power)
    weight = (near_sum[1] + core_sum[1]) + (over_sum[1] + weight)
    weight_out[...] = weight.astype(jnp.bfloat16)
    amplitude = amplitude_ref[0, 0, parity].astype(jnp.float32)
    factor = amplitude / jnp.sqrt(power + power_floor)
    factor = jnp.concatenate([factor, factor], axis=1)
    tables = (factor, direct, swapped)
    grads = [
        backward(modes_of(own), *tables, near_far, near_exit, 0),
        backward(modes_of(core), *tables, core_far, core_exit, 0),
        backward(over_modes, *tables, over_far, over_exit, 0),
        backward(last_modes, *tables, last_far, last_exit, 0),
    ]
    even = parity == 0
    for channel in range(2):
        gradient = (grads[0][channel] + grads[1][channel]) + (grads[2][channel] + grads[3][channel])
        gradient = jnp.where(is_live, gradient, 0.0)
        gradient = pltpu.roll(pltpu.roll(gradient, col_at, 1), row_at, 0)
        first, second = gradient[:, :half], gradient[:, half:]
        at = iota(first.shape, 1)
        left = jnp.where(at >= col_at, first, 0.0)
        own = [
            jnp.where(at + half >= col_at, second, 0.0),
            jnp.where(at < col_at, first, 0.0),
        ]
        right = jnp.where(at + half < col_at, second, 0.0)
        if sides == 1:
            beside = [jnp.where(x_index == 0, right, left)]
        else:
            beside = [left, right]
        placed = jnp.concatenate(own + beside, axis=1)
        row = iota((half, placed.shape[1]), 0)
        low = jnp.where(row >= row_at, placed[:half], 0.0).astype(jnp.bfloat16)
        high = jnp.where(row < row_at, placed[:half], 0.0).astype(jnp.bfloat16)
        inner = placed[half:].astype(jnp.bfloat16)
        rows = slice(channel * half, (channel + 1) * half)
        own_out[rows] = inner[:, :tile_cols]
        keep_out[rows] = jnp.where(even, high, low)
        swap_out[rows] = jnp.where(even, low, high)
        for index, out in enumerate(side_outs):
            out[rows] = inner[:, tile_cols + index * half : tile_cols + (index + 1) * half]
    for out in side_outs:
        out[2 * half :] = record_ref[:, :half]


def meet_kernel(first_column, record_ref, keep_ref, swap_ref, *outs):
    at = first_column
    for out in outs:
        height, width = keep_ref.shape[0], out.shape[1]
        columns = slice(at, at + width)
        total = keep_ref[:, columns].astype(jnp.float32) + swap_ref[:, columns].astype(jnp.float32)
        out[:height] = total.astype(jnp.bfloat16)
        out[height:] = record_ref[:, :width]
        at += width


def placed_weight(weight, position, z_step, x_step, shown, shape):
    tile_rows, tile_cols = shape
    side = weight.shape[0]
    half = side // 2
    row, col, is_live = position
    row = jnp.where(is_live & shown, row + (z_step * tile_rows - half), nowhere)
    col = col + (x_step * tile_cols - half)
    put_rows = (iota((tile_rows, side), 0) == iota((tile_rows, side), 1) + row).astype(jnp.bfloat16)
    put_cols = (iota((side, tile_cols), 1) == iota((side, tile_cols), 0) + col).astype(jnp.bfloat16)
    return dot(dot(put_rows, weight).astype(jnp.bfloat16), put_cols)


def beside(sides, x_count):
    z_index, x_index, _ = here()
    if sides == 1:
        return [jnp.where(x_index == 0, 1, -1)], [z_index >= 0]
    return [1, -1], [x_index < x_count - 1, x_index > 0]


def edges_added(inner, edges, sides, shown):
    _, x_index, _ = here()
    half = edges[0].shape[1]
    first = jnp.zeros(edges[0].shape, jnp.float32)
    last = first
    for index, edge in enumerate(edges):
        if sides == 1:
            first = jnp.where(x_index == 1, edge, 0.0)
            last = jnp.where(x_index == 0, edge, 0.0)
        elif index == 0:
            last = jnp.where(shown[0], edge, 0.0)
        else:
            first = jnp.where(shown[1], edge, 0.0)
    middle = inner.shape[1] - 2 * half
    parts = [inner[:, :half] + first]
    if middle:
        parts.append(inner[:, half : half + middle])
    parts.append(inner[:, half + middle :] + last)
    return jnp.concatenate(parts, axis=1)


def level_kernel(sides, slots, x_count, weight_ref, record_ref, own_ref, *refs):
    levels, out_ref = refs[:sides], refs[-1]
    shape = out_ref.shape[1:]
    half = levels[0].shape[1]
    z_index, _, parity = here()
    x_steps, shown = beside(sides, x_count)
    weight = weight_ref[...]
    position = position_of(record_ref, slots, parity)
    total = placed_weight(weight, position, 0, 0, z_index >= 0, shape)
    for level, x_step, is_shown in zip(levels, x_steps, shown):
        position = position_of(level[2 * half :], slots, parity)
        total = total + placed_weight(weight, position, 0, x_step, is_shown, shape)
    out_ref[2] = total
    for channel in range(2):
        rows = slice(channel * half, (channel + 1) * half)
        edges = [level[rows].astype(jnp.float32) for level in levels]
        out_ref[channel] = edges_added(own_ref[rows].astype(jnp.float32), edges, sides, shown)


def sum_kernel(sides, slots, z_count, x_count, weight_ref, level_ref, rows_ref, *refs):
    corners, out_ref = refs[:sides], refs[-1]
    shape = out_ref.shape[1:]
    half = corners[0].shape[1]
    z_index, _, parity = here()
    z_step = jnp.where(parity == 0, -1, 1)
    z_shown = jnp.where(parity == 0, z_index > 0, z_index < z_count - 1)
    x_steps, shown = beside(sides, x_count)
    weight = weight_ref[...]
    total = level_ref[2]
    for piece, x_step, is_shown in zip(
        (rows_ref,) + corners, [0] + x_steps, [z_index >= 0] + shown
    ):
        for slot in range(slots):
            position = position_of(piece[2 * half :], slots, slot)
            total = total + placed_weight(
                weight, position, z_step, x_step, is_shown & z_shown, shape
            )
    out_ref[2] = total.astype(jnp.bfloat16)
    for channel in range(2):
        rows = slice(channel * half, (channel + 1) * half)
        edges = [corner[rows].astype(jnp.float32) for corner in corners]
        above = edges_added(rows_ref[rows].astype(jnp.float32), edges, sides, shown)
        total = level_ref[channel] + jnp.where(z_shown, above, 0.0)
        out_ref[channel] = total.astype(jnp.bfloat16)


def update_kernel(object_ref, own_ref, other_ref, out_ref):
    weight = own_ref[2].astype(jnp.float32) + other_ref[2].astype(jnp.float32) + regularizer
    for channel in range(2):
        gradient = own_ref[channel].astype(jnp.float32) + other_ref[channel].astype(jnp.float32)
        out_ref[channel] = object_ref[channel] + gradient / weight


def cost(products):
    return pl.CostEstimate(flops=products * 2 * 256**3, bytes_accessed=0, transcendentals=0)


def in_hbm(array):
    return pltpu.with_memory_space_constraint(array, pltpu.HBM)


def smem():
    return pl.BlockSpec(memory_space=pltpu.SMEM)


def hbm():
    return pl.BlockSpec(memory_space=pltpu.HBM)


def vmem():
    return pl.BlockSpec(memory_space=pltpu.VMEM)


def on_device(object_field, probe, amplitudes, centers, live):
    side = probe.shape[2]
    half = side // 2
    _, tile_rows, tile_cols = object_field.shape
    slots = centers.shape[2]
    z_count = lax.axis_size("tx")
    x_count = lax.axis_size("ty")
    m_count = lax.axis_size("mode")
    modes = probe.shape[1]
    if tile_rows != half or slots != 2 or m_count != 4 or z_count % 2 or x_count < 2 or modes < 2:
        raise ValueError("unsupported sizes")
    sides = 1 if x_count == 2 else 2
    axes = ("tx", "ty", "mode")

    def zigzag(x_step):
        def moved(z, m):
            if m % 2 == 0:
                return (z + 1, m) if z < z_count - 1 else (z, m ^ 1)
            return (z - 1, m) if z > 0 else (z, m ^ 1)

        pairs = []
        for z in range(z_count):
            for x in range(x_count):
                for m in range(m_count):
                    z_to, m_to = moved(z, m)
                    x_to = (x + x_step) % x_count
                    pairs.append(
                        (
                            (z * x_count + x) * m_count + m,
                            (z_to * x_count + x_to) * m_count + m_to,
                        )
                    )
        return pairs

    def level(step):
        return [(x, (x + step) % x_count) for x in range(x_count)]

    def exchange(array, flip):
        return lax.ppermute(array, "mode", [(m, m ^ flip) for m in range(m_count)])

    tables = [jnp.asarray(matrix) for matrix in dft_matrices(side)]
    probe_low, shared, rest, record, spot, direct, swapped, *packed = pl.pallas_call(
        functools.partial(start_kernel, sides, slots),
        out_shape=[
            jax.ShapeDtypeStruct(probe.shape, jnp.bfloat16),
            jax.ShapeDtypeStruct((side, side), jnp.bfloat16),
            jax.ShapeDtypeStruct((2, modes - 1, side, side), jnp.bfloat16),
            jax.ShapeDtypeStruct((record_rows, tile_cols), jnp.bfloat16),
            jax.ShapeDtypeStruct((8, 128), jnp.int32),
            jax.ShapeDtypeStruct((2 * side, 2 * side), jnp.bfloat16),
            jax.ShapeDtypeStruct((2 * side, 2 * side), jnp.bfloat16),
            jax.ShapeDtypeStruct(object_field.shape, jnp.bfloat16),
        ]
        + [jax.ShapeDtypeStruct((2, tile_rows, half), jnp.bfloat16)] * sides,
        in_specs=[hbm()] * 5,
        out_specs=[vmem()] * (8 + sides),
        scratch_shapes=[
            pltpu.VMEM(object_field.shape, jnp.float32),
            pltpu.VMEM(probe.shape, jnp.float32),
            pltpu.SMEM(centers.shape, jnp.int32),
            pltpu.SemaphoreType.DMA((5,)),
        ],
        compiler_params=pltpu.CompilerParams(vmem_limit_bytes=small_bytes),
        name="start",
    )(*(in_hbm(array) for array in (object_field, probe, centers, *tables)))
    over_y = exchange(shared, 2)
    probe_core = exchange(probe_low, 1)
    probe_core, rest = lax.optimization_barrier((probe_core, rest))
    rest = exchange(rest, 2)
    over_z = lax.ppermute(over_y, "tx", [(z, z ^ 1) for z in range(z_count)])
    x_steps = [1] if sides == 1 else [1, -1]
    rows = lax.ppermute(packed[0], axes, zigzag(0))
    corners = [lax.ppermute(edge, axes, zigzag(step)) for step, edge in zip(x_steps, packed[1:])]
    levels = [lax.ppermute(edge, "ty", level(step)) for step, edge in zip(x_steps, packed[1:])]
    corners, record = lax.optimization_barrier((corners, record))
    record = pl.pallas_call(
        functools.partial(live_kernel, slots),
        out_shape=jax.ShapeDtypeStruct(record.shape, jnp.bfloat16),
        in_specs=[vmem(), smem()],
        out_specs=vmem(),
        compiler_params=pltpu.CompilerParams(vmem_limit_bytes=small_bytes),
        cost_estimate=cost(1),
        name="live",
    )(record, live)
    corners, record = lax.optimization_barrier((corners, record))
    edges = [
        pl.pallas_call(
            functools.partial(edge_kernel, z_count),
            out_shape=jax.ShapeDtypeStruct((2, side, half), jnp.float32),
            in_specs=[vmem()] * 4,
            out_specs=vmem(),
            compiler_params=pltpu.CompilerParams(vmem_limit_bytes=small_bytes),
            cost_estimate=cost(50),
            name="edge",
        )(spot, at_level, corner, exchange(corner, 1))
        for at_level, corner in zip(levels, corners)
    ]
    ext_cols = tile_cols + sides * half

    waves = [
        jax.ShapeDtypeStruct((modes, side, 2 * side), jnp.float32),
        jax.ShapeDtypeStruct((modes, 2 * side, side), jnp.bfloat16),
        jax.ShapeDtypeStruct((2, side, side), jnp.float32),
    ]
    patch, *near = pl.pallas_call(
        functools.partial(near_kernel, sides, z_count, x_count),
        out_shape=[jax.ShapeDtypeStruct((2, side, side), jnp.float32)] + waves,
        in_specs=[vmem()] * (7 + sides),
        out_specs=[vmem()] * 4,
        compiler_params=pltpu.CompilerParams(vmem_limit_bytes=wave_bytes),
        cost_estimate=cost(1),
        name="near",
    )(spot, packed[0], rows, exchange(rows, 1), *edges, probe_low, direct, swapped)
    other = pl.pallas_call(
        core_kernel,
        out_shape=waves,
        in_specs=[vmem()] * 4,
        out_specs=[vmem()] * 3,
        compiler_params=pltpu.CompilerParams(vmem_limit_bytes=wave_bytes),
        cost_estimate=cost(1),
        name="core",
    )(patch, probe_core, direct, swapped)
    last_y = exchange(over_y, 1)
    over_z, rest, other = lax.optimization_barrier((over_z, rest, other))
    over_group = (over_y, over_z, rest)
    last_group = [last_y, exchange(over_z, 1), exchange(rest, 1)]
    over = pl.pallas_call(
        over_kernel,
        out_shape=waves,
        in_specs=[vmem()] * 6,
        out_specs=[vmem()] * 3,
        compiler_params=pltpu.CompilerParams(vmem_limit_bytes=wave_bytes),
        cost_estimate=cost(60),
        name="over",
    )(patch, *over_group, direct, swapped)
    piece_rows = 2 * half + record_rows
    shapes = [(side, side), (2 * half, tile_cols)] + [(2 * half, ext_cols)] * 2
    shapes += [(piece_rows, half)] * sides
    weight, own, keep, swap, *levels = pl.pallas_call(
        functools.partial(back_kernel, sides, slots, tile_cols),
        out_shape=[jax.ShapeDtypeStruct(shape, jnp.bfloat16) for shape in shapes],
        in_specs=[vmem()] * 23,
        out_specs=[vmem()] * (4 + sides),
        scratch_shapes=[
            pltpu.VMEM((modes, side, 2 * side), jnp.float32),
            pltpu.VMEM((modes, 2 * side, side), jnp.bfloat16),
        ],
        compiler_params=pltpu.CompilerParams(vmem_limit_bytes=wave_bytes),
        cost_estimate=cost(80),
        name="back",
    )(
        record,
        spot,
        amplitudes,
        patch,
        probe_low,
        probe_core,
        *over_group,
        *last_group,
        direct,
        swapped,
        *near,
        *other,
        *over,
    )
    levels = [lax.ppermute(piece, "ty", level(-step)) for piece, step in zip(levels, x_steps)]
    rows, *corners = pl.pallas_call(
        functools.partial(meet_kernel, 0),
        out_shape=[
            jax.ShapeDtypeStruct((piece_rows, width), jnp.bfloat16)
            for width in [tile_cols] + [half] * sides
        ],
        in_specs=[vmem()] * 3,
        out_specs=[vmem()] * (1 + sides),
        compiler_params=pltpu.CompilerParams(vmem_limit_bytes=small_bytes),
        name="meet",
    )(record, keep, exchange(swap, 1))
    rows = lax.ppermute(rows, axes, zigzag(0))
    corners = [
        lax.ppermute(piece, axes, zigzag(-step)) for piece, step in zip(corners, x_steps)
    ]
    leveled = pl.pallas_call(
        functools.partial(level_kernel, sides, slots, x_count),
        out_shape=jax.ShapeDtypeStruct((3, tile_rows, tile_cols), jnp.float32),
        in_specs=[vmem()] * (3 + sides),
        out_specs=vmem(),
        compiler_params=pltpu.CompilerParams(vmem_limit_bytes=small_bytes),
        cost_estimate=cost(40),
        name="levels",
    )(weight, record, own, *levels)
    summed = pl.pallas_call(
        functools.partial(sum_kernel, sides, slots, z_count, x_count),
        out_shape=jax.ShapeDtypeStruct((3, tile_rows, tile_cols), jnp.bfloat16),
        in_specs=[vmem()] * (3 + sides),
        out_specs=vmem(),
        compiler_params=pltpu.CompilerParams(vmem_limit_bytes=small_bytes),
        name="sums",
    )(weight, leveled, rows, *corners)
    return pl.pallas_call(
        update_kernel,
        out_shape=jax.ShapeDtypeStruct(object_field.shape, jnp.float32),
        in_specs=[vmem()] * 3,
        out_specs=vmem(),
        compiler_params=pltpu.CompilerParams(vmem_limit_bytes=small_bytes),
        name="update",
    )(object_field, summed, exchange(summed, 1))


def solution(mesh):
    return jax.shard_map(
        on_device,
        mesh=mesh,
        in_specs=(
            P(None, "tx", "ty"),
            P(None, "mode", None, None),
            P("tx", "ty", None, None, None),
            P("tx", "ty", None, None),
            P("tx", "ty"),
        ),
        out_specs=P(None, "tx", "ty"),
        check_vma=False,
    )
```

```python
import functools
import math

import jax
import jax.numpy as jnp
import numpy as np
from jax import lax
from jax.experimental import pallas as pl
from jax.experimental.pallas import tpu as pltpu
from jax.sharding import PartitionSpec as P

power_floor = 0.01
regularizer = 0.1
nowhere = -(1 << 20)
record_rows = 16
wave_bytes = 32 * 1024 * 1024
small_bytes = 8 * 1024 * 1024


def dft_matrices(side):
    line = np.arange(side, dtype=np.int32)
    angle = (line[:, None] * line[None, :] % side).astype(np.float32) * np.float32(
        2.0 * math.pi / side
    )
    scaling = np.float32(1.0 / math.sqrt(side))
    real = (np.cos(angle) * scaling).astype(jnp.bfloat16)
    imag = (-np.sin(angle) * scaling).astype(jnp.bfloat16)
    direct = np.block([[real, -imag], [imag, real]])
    swapped = np.block([[real, imag], [-imag, real]])
    return direct, swapped


def dot(left, right):
    return jnp.dot(left, right, preferred_element_type=jnp.float32)


def iota(shape, dim):
    return lax.broadcasted_iota(jnp.int32, shape, dim)


def sent_order(sides):
    corners = [at for index in range(sides) for at in (4 + 3 * index, 5 + 3 * index)]
    return [0] + corners + [1, 2] + [3 + 3 * index for index in range(sides)]


def in_sent_order(pieces):
    return [pieces[at] for at in sent_order(len(pieces) // 3 - 1)]


def from_sent_order(pieces):
    order = sent_order(len(pieces) // 3 - 1)
    return [pieces[order.index(at)] for at in range(len(pieces))]


def wide(tall):
    side = tall.shape[0] // 2
    return jnp.concatenate([tall[:side], tall[side:]], axis=1)


def tall(wide):
    side = wide.shape[1] // 2
    return jnp.concatenate([wide[:, :side], wide[:, side:]], axis=0)


def here():
    return (lax.axis_index("tx"), lax.axis_index("ty"), lax.axis_index("mode") % 2)


def start_kernel(
    sides,
    slots,
    object_hbm,
    probe_hbm,
    centers_hbm,
    direct_hbm,
    swapped_hbm,
    low_ref,
    shared_ref,
    rest_ref,
    record_ref,
    spot_ref,
    direct_ref,
    swapped_ref,
    packed_ref,
    *refs,
):
    edges = refs[:sides]
    object_ref, probe_ref, centers_ref, sems = refs[sides:]
    copies = [
        pltpu.make_async_copy(source, target, sems.at[index])
        for index, (source, target) in enumerate(
            (
                (probe_hbm, probe_ref),
                (object_hbm, object_ref),
                (centers_hbm, centers_ref),
                (direct_hbm, direct_ref),
                (swapped_hbm, swapped_ref),
            )
        )
    ]
    for copy in copies:
        copy.start()
    tile_cols = object_ref.shape[2]
    half = edges[0].shape[2]
    z_index, x_index, parity = here()
    copies[0].wait()
    low_ref[...] = probe_ref[...].astype(jnp.bfloat16)
    shared_ref[...] = jnp.where(z_index % 2 == 0, low_ref[0, 0], low_ref[1, 0])
    rest_ref[...] = low_ref[:, 1:]
    copies[1].wait()
    first, last = slice(0, half), slice(tile_cols - half, tile_cols)
    for channel in range(2):
        values = object_ref[channel].astype(jnp.bfloat16)
        packed_ref[channel] = values
        if sides == 1:
            edges[0][channel] = jnp.where(x_index == 0, values[:, last], values[:, first])
        else:
            edges[0][channel] = values[:, last]
            edges[1][channel] = values[:, first]
    copies[2].wait()
    spot_ref[...] = jnp.where(
        iota(spot_ref.shape, 0) == 0, centers_ref[0, 0, parity, 0], centers_ref[0, 0, parity, 1]
    )
    record = jnp.zeros(record_ref.shape, jnp.float32)
    line = iota(record_ref.shape, 0)
    for slot in range(slots):
        for axis in range(2):
            value = centers_ref[0, 0, slot, axis].astype(jnp.float32)
            record = jnp.where(line == 2 * slot + axis, value, record)
    record_ref[...] = record.astype(jnp.bfloat16)
    copies[3].wait()
    copies[4].wait()


def live_kernel(slots, record_ref, live_ref, out_ref):
    line = iota(record_ref.shape, 0)
    record = record_ref[...].astype(jnp.float32)
    record = jnp.where(line == 2 * slots, live_ref[0, 0].astype(jnp.float32), record)
    out_ref[...] = record.astype(jnp.bfloat16)


def position_of(record, slots, wanted):
    record = record[:, :128].astype(jnp.float32).astype(jnp.int32)[:, :1]

    def of_slot(axis):
        value = record[axis : axis + 1]
        for slot in range(1, slots):
            value = jnp.where(wanted == slot, record[2 * slot + axis : 2 * slot + axis + 1], value)
        return value

    return of_slot(0), of_slot(1), record[2 * slots : 2 * slots + 1] > wanted


def turned_back(value, side):
    return jnp.where(value == 0, 0, side - value)


def patch_of(sides, z_count, x_count, side, spot_ref, pieces):
    z_index, x_index, parity = here()
    row_at, col_at = spot_ref[0, 0], spot_ref[1, 0]
    half = side // 2
    even = parity == 0
    low_shown = z_index > 0
    high_shown = z_index < z_count - 1

    def joined(piece, a, b, channel):
        level = piece[channel].astype(jnp.float32)
        turn_a = a[channel].astype(jnp.float32)
        turn_b = b[channel].astype(jnp.float32)
        low = jnp.where(even & low_shown, turn_a, jnp.where(low_shown, turn_b, 0.0))
        high = jnp.where(even & high_shown, turn_b, jnp.where(high_shown, turn_a, 0.0))
        first = jnp.where(iota(low.shape, 0) >= row_at, low, high)
        return jnp.concatenate([first, level], axis=0)

    out = []
    for channel in range(2):
        own = joined(*pieces[:3], channel)
        sides_joined = [
            joined(*pieces[3 + 3 * index : 6 + 3 * index], channel) for index in range(sides)
        ]
        if sides == 1:
            left = jnp.where(x_index == 1, sides_joined[0], 0.0)
            right = jnp.where(x_index == 0, sides_joined[0], 0.0)
        else:
            left = jnp.where(x_index > 0, sides_joined[0], 0.0)
            right = jnp.where(x_index < x_count - 1, sides_joined[1], 0.0)
        at = iota(left.shape, 1)
        window = jnp.concatenate(
            [
                jnp.where(at >= col_at, left, own[:, half:]),
                jnp.where(at + half >= col_at, own[:, :half], right),
            ],
            axis=1,
        )
        window = pltpu.roll(window, turned_back(row_at, side), 0)
        out.append(pltpu.roll(window, turned_back(col_at, side), 1))
    return out


def modes_of(group):
    def reader(k):
        return lambda: (group[0, k].astype(jnp.float32), group[1, k].astype(jnp.float32))

    return [reader(k) for k in range(group.shape[1])]


def shared_mode(over_y, over_z):
    def read():
        z_index, _, _ = here()
        even = z_index % 2 == 0
        over_y_values = over_y[...].astype(jnp.float32)
        over_z_values = over_z[...].astype(jnp.float32)
        return (
            jnp.where(even, over_y_values, over_z_values),
            jnp.where(even, over_z_values, over_y_values),
        )

    return read


def forward(modes, patch, direct, swapped, far_ref, exit_ref, at):
    patch_real, patch_imag = patch
    side = patch_real.shape[0]
    power = jnp.zeros((side, side), jnp.float32)
    weight = jnp.zeros((side, side), jnp.float32)
    halves = []
    for k, mode in enumerate(modes):
        real, imag = mode()
        exit_wave = jnp.concatenate(
            [
                (real * patch_real - imag * patch_imag).astype(jnp.bfloat16),
                (real * patch_imag + imag * patch_real).astype(jnp.bfloat16),
            ],
            axis=0,
        )
        exit_ref[at + k] = exit_wave
        halves.append(wide(dot(direct, exit_wave).astype(jnp.bfloat16)))
        weight = weight + (real * real + imag * imag)
    far_all = dot(jnp.concatenate(halves, axis=0), swapped)
    for k in range(len(modes)):
        far = far_all[k * side : (k + 1) * side]
        far_ref[at + k] = far
        power = power + (far[:, :side] * far[:, :side] + far[:, side:] * far[:, side:])
    return power, weight


def backward(modes, factor, direct, swapped, far_ref, exit_ref, at):
    side = factor.shape[0]
    grad_real = jnp.zeros((side, side), jnp.float32)
    grad_imag = jnp.zeros((side, side), jnp.float32)
    halves = []
    for k in range(len(modes)):
        fixed = (far_ref[at + k] * factor).astype(jnp.bfloat16)
        halves.append(wide(dot(swapped, tall(fixed)).astype(jnp.bfloat16)))
    back_all = dot(jnp.concatenate(halves, axis=0), direct)
    for k, mode in enumerate(modes):
        back = back_all[k * side : (k + 1) * side]
        exit_wave = exit_ref[at + k].astype(jnp.float32)
        real, imag = mode()
        diff_real = back[:, :side] - exit_wave[:side]
        diff_imag = back[:, side:] - exit_wave[side:]
        grad_real = grad_real + (real * diff_real + imag * diff_imag)
        grad_imag = grad_imag + (real * diff_imag - imag * diff_real)
    return grad_real, grad_imag


def near_kernel(sides, z_count, x_count, spot_ref, *refs):
    n_pieces = 3 + 3 * sides
    pieces = from_sent_order(refs[:n_pieces])
    own, direct, swapped = refs[n_pieces : n_pieces + 3]
    patch_ref, far_ref, exit_ref, sum_ref = refs[n_pieces + 3 :]
    side = own.shape[2]
    patch = patch_of(sides, z_count, x_count, side, spot_ref, pieces)
    patch_ref[0], patch_ref[1] = patch
    sum_ref[0], sum_ref[1] = forward(
        modes_of(own), patch, direct[...], swapped[...], far_ref, exit_ref, 0
    )


def core_kernel(patch_ref, core, direct, swapped, far_ref, exit_ref, sum_ref):
    patch = (patch_ref[0], patch_ref[1])
    sum_ref[0], sum_ref[1] = forward(
        modes_of(core), patch, direct[...], swapped[...], far_ref, exit_ref, 0
    )


def over_kernel(patch_ref, over_y, over_z, rest, direct, swapped, far_ref, exit_ref, sum_ref):
    patch = (patch_ref[0], patch_ref[1])
    modes = [shared_mode(over_y, over_z)] + modes_of(rest)
    sum_ref[0], sum_ref[1] = forward(modes, patch, direct[...], swapped[...], far_ref, exit_ref, 0)


def back_kernel(sides, slots, tile_cols, record_ref, spot_ref, *refs):
    amplitude_ref, patch_ref, own, core = refs[:4]
    over_modes = [shared_mode(*refs[4:6])] + modes_of(refs[6])
    last_modes = [shared_mode(*refs[7:9])] + modes_of(refs[9])
    direct_ref, swapped_ref = refs[10:12]
    near_far, near_exit, near_sum, core_far, core_exit, core_sum = refs[12:18]
    over_far, over_exit, over_sum = refs[18:21]
    weight_out, own_out, keep_out, swap_out = refs[21:25]
    side_outs = refs[25 : 25 + sides]
    last_far, last_exit = refs[25 + sides :]
    side = own.shape[2]
    half = side // 2
    _, x_index, parity = here()
    row_at, col_at = spot_ref[0, 0], spot_ref[1, 0]
    _, _, is_live = position_of(record_ref, slots, parity)
    direct = direct_ref[...]
    swapped = swapped_ref[...]
    patch = (patch_ref[0], patch_ref[1])
    power, weight = forward(last_modes, patch, direct, swapped, last_far, last_exit, 0)
    power = (near_sum[0] + core_sum[0]) + (over_sum[0] + power)
    weight = (near_sum[1] + core_sum[1]) + (over_sum[1] + weight)
    weight_out[...] = weight.astype(jnp.bfloat16)
    amplitude = amplitude_ref[0, 0, parity].astype(jnp.float32)
    factor = amplitude / jnp.sqrt(power + power_floor)
    factor = jnp.concatenate([factor, factor], axis=1)
    tables = (factor, direct, swapped)
    grads = [
        backward(modes_of(own), *tables, near_far, near_exit, 0),
        backward(modes_of(core), *tables, core_far, core_exit, 0),
        backward(over_modes, *tables, over_far, over_exit, 0),
        backward(last_modes, *tables, last_far, last_exit, 0),
    ]
    even = parity == 0
    for channel in range(2):
        gradient = (grads[0][channel] + grads[1][channel]) + (grads[2][channel] + grads[3][channel])
        gradient = jnp.where(is_live, gradient, 0.0)
        gradient = pltpu.roll(pltpu.roll(gradient, col_at, 1), row_at, 0)
        first, second = gradient[:, :half], gradient[:, half:]
        at = iota(first.shape, 1)
        left = jnp.where(at >= col_at, first, 0.0)
        own = [
            jnp.where(at + half >= col_at, second, 0.0),
            jnp.where(at < col_at, first, 0.0),
        ]
        right = jnp.where(at + half < col_at, second, 0.0)
        if sides == 1:
            beside = [jnp.where(x_index == 0, right, left)]
        else:
            beside = [left, right]
        placed = jnp.concatenate(own + beside, axis=1)
        row = iota((half, placed.shape[1]), 0)
        low = jnp.where(row >= row_at, placed[:half], 0.0).astype(jnp.bfloat16)
        high = jnp.where(row < row_at, placed[:half], 0.0).astype(jnp.bfloat16)
        inner = placed[half:].astype(jnp.bfloat16)
        rows = slice(channel * half, (channel + 1) * half)
        own_out[rows] = inner[:, :tile_cols]
        keep_out[rows] = jnp.where(even, high, low)
        swap_out[rows] = jnp.where(even, low, high)
        for index, out in enumerate(side_outs):
            out[rows] = inner[:, tile_cols + index * half : tile_cols + (index + 1) * half]
    for out in side_outs:
        out[2 * half :] = record_ref[:, :half]


def meet_kernel(first_column, record_ref, keep_ref, swap_ref, *outs):
    at = first_column
    for out in outs:
        height, width = keep_ref.shape[0], out.shape[1]
        columns = slice(at, at + width)
        total = keep_ref[:, columns].astype(jnp.float32) + swap_ref[:, columns].astype(jnp.float32)
        out[:height] = total.astype(jnp.bfloat16)
        out[height:] = record_ref[:, :width]
        at += width


def placed_weight(weight, position, z_step, x_step, shown, shape):
    tile_rows, tile_cols = shape
    side = weight.shape[0]
    half = side // 2
    row, col, is_live = position
    row = jnp.where(is_live & shown, row + (z_step * tile_rows - half), nowhere)
    col = col + (x_step * tile_cols - half)
    put_rows = (iota((tile_rows, side), 0) == iota((tile_rows, side), 1) + row).astype(jnp.bfloat16)
    put_cols = (iota((side, tile_cols), 1) == iota((side, tile_cols), 0) + col).astype(jnp.bfloat16)
    return dot(dot(put_rows, weight).astype(jnp.bfloat16), put_cols)


def beside(sides, x_count):
    z_index, x_index, _ = here()
    if sides == 1:
        return [jnp.where(x_index == 0, 1, -1)], [z_index >= 0]
    return [1, -1], [x_index < x_count - 1, x_index > 0]


def edges_added(inner, edges, sides, shown):
    _, x_index, _ = here()
    half = edges[0].shape[1]
    first = jnp.zeros(edges[0].shape, jnp.float32)
    last = first
    for index, edge in enumerate(edges):
        if sides == 1:
            first = jnp.where(x_index == 1, edge, 0.0)
            last = jnp.where(x_index == 0, edge, 0.0)
        elif index == 0:
            last = jnp.where(shown[0], edge, 0.0)
        else:
            first = jnp.where(shown[1], edge, 0.0)
    middle = inner.shape[1] - 2 * half
    parts = [inner[:, :half] + first]
    if middle:
        parts.append(inner[:, half : half + middle])
    parts.append(inner[:, half + middle :] + last)
    return jnp.concatenate(parts, axis=1)


def level_kernel(sides, slots, x_count, weight_ref, record_ref, own_ref, *refs):
    levels, out_ref = refs[:sides], refs[-1]
    shape = out_ref.shape[1:]
    half = levels[0].shape[1]
    z_index, _, parity = here()
    x_steps, shown = beside(sides, x_count)
    weight = weight_ref[...]
    position = position_of(record_ref, slots, parity)
    total = placed_weight(weight, position, 0, 0, z_index >= 0, shape)
    for level, x_step, is_shown in zip(levels, x_steps, shown):
        position = position_of(level[2 * half :], slots, parity)
        total = total + placed_weight(weight, position, 0, x_step, is_shown, shape)
    out_ref[2] = total
    for channel in range(2):
        rows = slice(channel * half, (channel + 1) * half)
        edges = [level[rows].astype(jnp.float32) for level in levels]
        out_ref[channel] = edges_added(own_ref[rows].astype(jnp.float32), edges, sides, shown)


def sum_kernel(sides, slots, z_count, x_count, weight_ref, level_ref, rows_ref, *refs):
    corners, out_ref = refs[:sides], refs[-1]
    shape = out_ref.shape[1:]
    half = corners[0].shape[1]
    z_index, _, parity = here()
    z_step = jnp.where(parity == 0, -1, 1)
    z_shown = jnp.where(parity == 0, z_index > 0, z_index < z_count - 1)
    x_steps, shown = beside(sides, x_count)
    weight = weight_ref[...]
    total = level_ref[2]
    for piece, x_step, is_shown in zip(
        (rows_ref,) + corners, [0] + x_steps, [z_index >= 0] + shown
    ):
        for slot in range(slots):
            position = position_of(piece[2 * half :], slots, slot)
            total = total + placed_weight(
                weight, position, z_step, x_step, is_shown & z_shown, shape
            )
    out_ref[2] = total.astype(jnp.bfloat16)
    for channel in range(2):
        rows = slice(channel * half, (channel + 1) * half)
        edges = [corner[rows].astype(jnp.float32) for corner in corners]
        above = edges_added(rows_ref[rows].astype(jnp.float32), edges, sides, shown)
        total = level_ref[channel] + jnp.where(z_shown, above, 0.0)
        out_ref[channel] = total.astype(jnp.bfloat16)


def update_kernel(object_ref, own_ref, other_ref, out_ref):
    weight = own_ref[2].astype(jnp.float32) + other_ref[2].astype(jnp.float32) + regularizer
    for channel in range(2):
        gradient = own_ref[channel].astype(jnp.float32) + other_ref[channel].astype(jnp.float32)
        out_ref[channel] = object_ref[channel] + gradient / weight


def cost(products):
    return pl.CostEstimate(flops=products * 2 * 256**3, bytes_accessed=0, transcendentals=0)


def in_hbm(array):
    return pltpu.with_memory_space_constraint(array, pltpu.HBM)


def smem():
    return pl.BlockSpec(memory_space=pltpu.SMEM)


def hbm():
    return pl.BlockSpec(memory_space=pltpu.HBM)


def vmem():
    return pl.BlockSpec(memory_space=pltpu.VMEM)


def on_device(object_field, probe, amplitudes, centers, live):
    side = probe.shape[2]
    half = side // 2
    _, tile_rows, tile_cols = object_field.shape
    slots = centers.shape[2]
    z_count = lax.axis_size("tx")
    x_count = lax.axis_size("ty")
    m_count = lax.axis_size("mode")
    modes = probe.shape[1]
    if tile_rows != half or slots != 2 or m_count != 4 or z_count % 2 or x_count < 2 or modes < 2:
        raise ValueError("unsupported sizes")
    sides = 1 if x_count == 2 else 2
    axes = ("tx", "ty", "mode")

    def zigzag(x_step):
        def moved(z, m):
            if m % 2 == 0:
                return (z + 1, m) if z < z_count - 1 else (z, m ^ 1)
            return (z - 1, m) if z > 0 else (z, m ^ 1)

        pairs = []
        for z in range(z_count):
            for x in range(x_count):
                for m in range(m_count):
                    z_to, m_to = moved(z, m)
                    x_to = (x + x_step) % x_count
                    pairs.append(
                        (
                            (z * x_count + x) * m_count + m,
                            (z_to * x_count + x_to) * m_count + m_to,
                        )
                    )
        return pairs

    def level(step):
        return [(x, (x + step) % x_count) for x in range(x_count)]

    def exchange(array, flip):
        return lax.ppermute(array, "mode", [(m, m ^ flip) for m in range(m_count)])

    tables = [jnp.asarray(matrix) for matrix in dft_matrices(side)]
    probe_low, shared, rest, record, spot, direct, swapped, *packed = pl.pallas_call(
        functools.partial(start_kernel, sides, slots),
        out_shape=[
            jax.ShapeDtypeStruct(probe.shape, jnp.bfloat16),
            jax.ShapeDtypeStruct((side, side), jnp.bfloat16),
            jax.ShapeDtypeStruct((2, modes - 1, side, side), jnp.bfloat16),
            jax.ShapeDtypeStruct((record_rows, tile_cols), jnp.bfloat16),
            jax.ShapeDtypeStruct((8, 128), jnp.int32),
            jax.ShapeDtypeStruct((2 * side, 2 * side), jnp.bfloat16),
            jax.ShapeDtypeStruct((2 * side, 2 * side), jnp.bfloat16),
            jax.ShapeDtypeStruct(object_field.shape, jnp.bfloat16),
        ]
        + [jax.ShapeDtypeStruct((2, tile_rows, half), jnp.bfloat16)] * sides,
        in_specs=[hbm()] * 5,
        out_specs=[vmem()] * (8 + sides),
        scratch_shapes=[
            pltpu.VMEM(object_field.shape, jnp.float32),
            pltpu.VMEM(probe.shape, jnp.float32),
            pltpu.SMEM(centers.shape, jnp.int32),
            pltpu.SemaphoreType.DMA((5,)),
        ],
        compiler_params=pltpu.CompilerParams(vmem_limit_bytes=small_bytes),
        name="start",
    )(*(in_hbm(array) for array in (object_field, probe, centers, *tables)))
    over_y = exchange(shared, 2)
    probe_core = exchange(probe_low, 1)
    probe_core, rest = lax.optimization_barrier((probe_core, rest))
    rest = exchange(rest, 2)
    over_z = lax.ppermute(over_y, "tx", [(z, z ^ 1) for z in range(z_count)])
    x_steps = [1] if sides == 1 else [1, -1]
    rows = lax.ppermute(packed[0], axes, zigzag(0))
    corners = [lax.ppermute(edge, axes, zigzag(step)) for step, edge in zip(x_steps, packed[1:])]
    levels = [lax.ppermute(edge, "ty", level(step)) for step, edge in zip(x_steps, packed[1:])]
    corners, record = lax.optimization_barrier((corners, record))
    record = pl.pallas_call(
        functools.partial(live_kernel, slots),
        out_shape=jax.ShapeDtypeStruct(record.shape, jnp.bfloat16),
        in_specs=[vmem(), smem()],
        out_specs=vmem(),
        compiler_params=pltpu.CompilerParams(vmem_limit_bytes=small_bytes),
        cost_estimate=cost(50),
        name="live",
    )(record, live)
    corners, record = lax.optimization_barrier((corners, record))
    pieces = [packed[0], rows, exchange(rows, 1)]
    for at_level, corner in zip(levels, corners):
        pieces += [at_level, corner, exchange(corner, 1)]
    n_pieces = len(pieces)
    ext_cols = tile_cols + sides * half

    waves = [
        jax.ShapeDtypeStruct((modes, side, 2 * side), jnp.float32),
        jax.ShapeDtypeStruct((modes, 2 * side, side), jnp.bfloat16),
        jax.ShapeDtypeStruct((2, side, side), jnp.float32),
    ]
    patch, *near = pl.pallas_call(
        functools.partial(near_kernel, sides, z_count, x_count),
        out_shape=[jax.ShapeDtypeStruct((2, side, side), jnp.float32)] + waves,
        in_specs=[vmem()] * (n_pieces + 4),
        out_specs=[vmem()] * 4,
        compiler_params=pltpu.CompilerParams(vmem_limit_bytes=wave_bytes),
        cost_estimate=cost(1),
        name="near",
    )(spot, *in_sent_order(pieces), probe_low, direct, swapped)
    rest, patch = lax.optimization_barrier((rest, patch))
    other = pl.pallas_call(
        core_kernel,
        out_shape=waves,
        in_specs=[vmem()] * 4,
        out_specs=[vmem()] * 3,
        compiler_params=pltpu.CompilerParams(vmem_limit_bytes=wave_bytes),
        cost_estimate=cost(1),
        name="core",
    )(patch, probe_core, direct, swapped)
    last_y = exchange(over_y, 1)
    over_z, other = lax.optimization_barrier((over_z, other))
    over_group = (over_y, over_z, rest)
    last_group = [last_y, exchange(over_z, 1), exchange(rest, 1)]
    over = pl.pallas_call(
        over_kernel,
        out_shape=waves,
        in_specs=[vmem()] * 6,
        out_specs=[vmem()] * 3,
        compiler_params=pltpu.CompilerParams(vmem_limit_bytes=wave_bytes),
        cost_estimate=cost(100),
        name="over",
    )(patch, *over_group, direct, swapped)
    piece_rows = 2 * half + record_rows
    shapes = [(side, side), (2 * half, tile_cols)] + [(2 * half, ext_cols)] * 2
    shapes += [(piece_rows, half)] * sides
    weight, own, keep, swap, *levels = pl.pallas_call(
        functools.partial(back_kernel, sides, slots, tile_cols),
        out_shape=[jax.ShapeDtypeStruct(shape, jnp.bfloat16) for shape in shapes],
        in_specs=[vmem()] * 23,
        out_specs=[vmem()] * (4 + sides),
        scratch_shapes=[
            pltpu.VMEM((modes, side, 2 * side), jnp.float32),
            pltpu.VMEM((modes, 2 * side, side), jnp.bfloat16),
        ],
        compiler_params=pltpu.CompilerParams(vmem_limit_bytes=wave_bytes),
        cost_estimate=cost(80),
        name="back",
    )(
        record,
        spot,
        amplitudes,
        patch,
        probe_low,
        probe_core,
        *over_group,
        *last_group,
        direct,
        swapped,
        *near,
        *other,
        *over,
    )
    levels = [lax.ppermute(piece, "ty", level(-step)) for piece, step in zip(levels, x_steps)]
    rows, *corners = pl.pallas_call(
        functools.partial(meet_kernel, 0),
        out_shape=[
            jax.ShapeDtypeStruct((piece_rows, width), jnp.bfloat16)
            for width in [tile_cols] + [half] * sides
        ],
        in_specs=[vmem()] * 3,
        out_specs=[vmem()] * (1 + sides),
        compiler_params=pltpu.CompilerParams(vmem_limit_bytes=small_bytes),
        name="meet",
    )(record, keep, exchange(swap, 1))
    rows = lax.ppermute(rows, axes, zigzag(0))
    corners = [
        lax.ppermute(piece, axes, zigzag(-step)) for piece, step in zip(corners, x_steps)
    ]
    leveled = pl.pallas_call(
        functools.partial(level_kernel, sides, slots, x_count),
        out_shape=jax.ShapeDtypeStruct((3, tile_rows, tile_cols), jnp.float32),
        in_specs=[vmem()] * (3 + sides),
        out_specs=vmem(),
        compiler_params=pltpu.CompilerParams(vmem_limit_bytes=small_bytes),
        cost_estimate=cost(40),
        name="levels",
    )(weight, record, own, *levels)
    summed = pl.pallas_call(
        functools.partial(sum_kernel, sides, slots, z_count, x_count),
        out_shape=jax.ShapeDtypeStruct((3, tile_rows, tile_cols), jnp.bfloat16),
        in_specs=[vmem()] * (3 + sides),
        out_specs=vmem(),
        compiler_params=pltpu.CompilerParams(vmem_limit_bytes=small_bytes),
        name="sums",
    )(weight, leveled, rows, *corners)
    return pl.pallas_call(
        update_kernel,
        out_shape=jax.ShapeDtypeStruct(object_field.shape, jnp.float32),
        in_specs=[vmem()] * 3,
        out_specs=vmem(),
        compiler_params=pltpu.CompilerParams(vmem_limit_bytes=small_bytes),
        name="update",
    )(object_field, summed, exchange(summed, 1))


def solution(mesh):
    return jax.shard_map(
        on_device,
        mesh=mesh,
        in_specs=(
            P(None, "tx", "ty"),
            P(None, "mode", None, None),
            P("tx", "ty", None, None, None),
            P("tx", "ty", None, None),
            P("tx", "ty"),
        ),
        out_specs=P(None, "tx", "ty"),
        check_vma=False,
    )
```

```python
import functools
import math

import jax
import jax.numpy as jnp
import numpy as np
from jax import lax
from jax.experimental import pallas as pl
from jax.experimental.pallas import tpu as pltpu
from jax.sharding import PartitionSpec as P

power_floor = 0.01
regularizer = 0.1
nowhere = -(1 << 20)
record_rows = 16
wave_bytes = 32 * 1024 * 1024
small_bytes = 8 * 1024 * 1024


def dft_matrices(side):
    line = np.arange(side, dtype=np.int32)
    angle = (line[:, None] * line[None, :] % side).astype(np.float32) * np.float32(
        2.0 * math.pi / side
    )
    scaling = np.float32(1.0 / math.sqrt(side))
    real = (np.cos(angle) * scaling).astype(jnp.bfloat16)
    imag = (-np.sin(angle) * scaling).astype(jnp.bfloat16)
    direct = np.block([[real, -imag], [imag, real]])
    swapped = np.block([[real, imag], [-imag, real]])
    return direct, swapped


def dot(left, right):
    return jnp.dot(left, right, preferred_element_type=jnp.float32)


def iota(shape, dim):
    return lax.broadcasted_iota(jnp.int32, shape, dim)


def sent_order(sides):
    corners = [at for index in range(sides) for at in (4 + 3 * index, 5 + 3 * index)]
    return [0] + corners + [1, 2] + [3 + 3 * index for index in range(sides)]


def in_sent_order(pieces):
    return [pieces[at] for at in sent_order(len(pieces) // 3 - 1)]


def from_sent_order(pieces):
    order = sent_order(len(pieces) // 3 - 1)
    return [pieces[order.index(at)] for at in range(len(pieces))]


def wide(tall):
    side = tall.shape[0] // 2
    return jnp.concatenate([tall[:side], tall[side:]], axis=1)


def tall(wide):
    side = wide.shape[1] // 2
    return jnp.concatenate([wide[:, :side], wide[:, side:]], axis=0)


def here():
    return (lax.axis_index("tx"), lax.axis_index("ty"), lax.axis_index("mode") % 2)


def start_kernel(
    sides,
    slots,
    object_hbm,
    probe_hbm,
    centers_hbm,
    direct_hbm,
    swapped_hbm,
    low_ref,
    shared_ref,
    rest_ref,
    record_ref,
    spot_ref,
    direct_ref,
    swapped_ref,
    packed_ref,
    *refs,
):
    edges = refs[:sides]
    object_ref, probe_ref, centers_ref, sems = refs[sides:]
    copies = [
        pltpu.make_async_copy(source, target, sems.at[index])
        for index, (source, target) in enumerate(
            (
                (probe_hbm, probe_ref),
                (object_hbm, object_ref),
                (centers_hbm, centers_ref),
                (direct_hbm, direct_ref),
                (swapped_hbm, swapped_ref),
            )
        )
    ]
    for copy in copies:
        copy.start()
    tile_cols = object_ref.shape[2]
    half = edges[0].shape[2]
    z_index, x_index, parity = here()
    copies[0].wait()
    low_ref[...] = probe_ref[...].astype(jnp.bfloat16)
    shared_ref[...] = jnp.where(z_index % 2 == 0, low_ref[0, 0], low_ref[1, 0])
    rest_ref[...] = low_ref[:, 1:]
    copies[1].wait()
    first, last = slice(0, half), slice(tile_cols - half, tile_cols)
    for channel in range(2):
        values = object_ref[channel].astype(jnp.bfloat16)
        packed_ref[channel] = values
        if sides == 1:
            edges[0][channel] = jnp.where(x_index == 0, values[:, last], values[:, first])
        else:
            edges[0][channel] = values[:, last]
            edges[1][channel] = values[:, first]
    copies[2].wait()
    spot_ref[...] = jnp.where(
        iota(spot_ref.shape, 0) == 0, centers_ref[0, 0, parity, 0], centers_ref[0, 0, parity, 1]
    )
    record = jnp.zeros(record_ref.shape, jnp.float32)
    line = iota(record_ref.shape, 0)
    for slot in range(slots):
        for axis in range(2):
            value = centers_ref[0, 0, slot, axis].astype(jnp.float32)
            record = jnp.where(line == 2 * slot + axis, value, record)
    record_ref[...] = record.astype(jnp.bfloat16)
    copies[3].wait()
    copies[4].wait()


def live_kernel(slots, record_ref, live_ref, out_ref):
    line = iota(record_ref.shape, 0)
    record = record_ref[...].astype(jnp.float32)
    record = jnp.where(line == 2 * slots, live_ref[0, 0].astype(jnp.float32), record)
    out_ref[...] = record.astype(jnp.bfloat16)


def position_of(record, slots, wanted):
    record = record[:, :128].astype(jnp.float32).astype(jnp.int32)[:, :1]

    def of_slot(axis):
        value = record[axis : axis + 1]
        for slot in range(1, slots):
            value = jnp.where(wanted == slot, record[2 * slot + axis : 2 * slot + axis + 1], value)
        return value

    return of_slot(0), of_slot(1), record[2 * slots : 2 * slots + 1] > wanted


def turned_back(value, side):
    return jnp.where(value == 0, 0, side - value)


def patch_of(sides, z_count, x_count, side, spot_ref, pieces):
    z_index, x_index, parity = here()
    row_at, col_at = spot_ref[0, 0], spot_ref[1, 0]
    half = side // 2
    even = parity == 0
    low_shown = z_index > 0
    high_shown = z_index < z_count - 1

    def joined(piece, a, b, channel):
        level = piece[channel].astype(jnp.float32)
        turn_a = a[channel].astype(jnp.float32)
        turn_b = b[channel].astype(jnp.float32)
        low = jnp.where(even & low_shown, turn_a, jnp.where(low_shown, turn_b, 0.0))
        high = jnp.where(even & high_shown, turn_b, jnp.where(high_shown, turn_a, 0.0))
        first = jnp.where(iota(low.shape, 0) >= row_at, low, high)
        return jnp.concatenate([first, level], axis=0)

    out = []
    for channel in range(2):
        own = joined(*pieces[:3], channel)
        sides_joined = [
            joined(*pieces[3 + 3 * index : 6 + 3 * index], channel) for index in range(sides)
        ]
        if sides == 1:
            left = jnp.where(x_index == 1, sides_joined[0], 0.0)
            right = jnp.where(x_index == 0, sides_joined[0], 0.0)
        else:
            left = jnp.where(x_index > 0, sides_joined[0], 0.0)
            right = jnp.where(x_index < x_count - 1, sides_joined[1], 0.0)
        at = iota(left.shape, 1)
        window = jnp.concatenate(
            [
                jnp.where(at >= col_at, left, own[:, half:]),
                jnp.where(at + half >= col_at, own[:, :half], right),
            ],
            axis=1,
        )
        window = pltpu.roll(window, turned_back(row_at, side), 0)
        out.append(pltpu.roll(window, turned_back(col_at, side), 1))
    return out


def modes_of(group):
    def reader(k):
        return lambda: (group[0, k].astype(jnp.float32), group[1, k].astype(jnp.float32))

    return [reader(k) for k in range(group.shape[1])]


def shared_mode(over_y, over_z):
    def read():
        z_index, _, _ = here()
        even = z_index % 2 == 0
        over_y_values = over_y[...].astype(jnp.float32)
        over_z_values = over_z[...].astype(jnp.float32)
        return (
            jnp.where(even, over_y_values, over_z_values),
            jnp.where(even, over_z_values, over_y_values),
        )

    return read


def forward(modes, patch, direct, swapped, far_ref, exit_ref, at):
    patch_real, patch_imag = patch
    side = patch_real.shape[0]
    power = jnp.zeros((side, side), jnp.float32)
    weight = jnp.zeros((side, side), jnp.float32)
    halves = []
    for k, mode in enumerate(modes):
        real, imag = mode()
        exit_wave = jnp.concatenate(
            [
                (real * patch_real - imag * patch_imag).astype(jnp.bfloat16),
                (real * patch_imag + imag * patch_real).astype(jnp.bfloat16),
            ],
            axis=0,
        )
        exit_ref[at + k] = exit_wave
        halves.append(wide(dot(direct, exit_wave).astype(jnp.bfloat16)))
        weight = weight + (real * real + imag * imag)
    far_all = dot(jnp.concatenate(halves, axis=0), swapped)
    for k in range(len(modes)):
        far = far_all[k * side : (k + 1) * side]
        far_ref[at + k] = far
        power = power + (far[:, :side] * far[:, :side] + far[:, side:] * far[:, side:])
    return power, weight


def backward(modes, factor, direct, swapped, far_ref, exit_ref, at):
    side = factor.shape[0]
    grad_real = jnp.zeros((side, side), jnp.float32)
    grad_imag = jnp.zeros((side, side), jnp.float32)
    halves = []
    for k in range(len(modes)):
        fixed = (far_ref[at + k] * factor).astype(jnp.bfloat16)
        halves.append(wide(dot(swapped, tall(fixed)).astype(jnp.bfloat16)))
    back_all = dot(jnp.concatenate(halves, axis=0), direct)
    for k, mode in enumerate(modes):
        back = back_all[k * side : (k + 1) * side]
        exit_wave = exit_ref[at + k].astype(jnp.float32)
        real, imag = mode()
        diff_real = back[:, :side] - exit_wave[:side]
        diff_imag = back[:, side:] - exit_wave[side:]
        grad_real = grad_real + (real * diff_real + imag * diff_imag)
        grad_imag = grad_imag + (real * diff_imag - imag * diff_real)
    return grad_real, grad_imag


def near_kernel(sides, z_count, x_count, spot_ref, *refs):
    n_pieces = 3 + 3 * sides
    pieces = from_sent_order(refs[:n_pieces])
    own, direct, swapped = refs[n_pieces : n_pieces + 3]
    patch_ref, far_ref, exit_ref, sum_ref = refs[n_pieces + 3 :]
    side = own.shape[2]
    patch = patch_of(sides, z_count, x_count, side, spot_ref, pieces)
    patch_ref[0], patch_ref[1] = patch
    sum_ref[0], sum_ref[1] = forward(
        modes_of(own), patch, direct[...], swapped[...], far_ref, exit_ref, 0
    )


def core_kernel(patch_ref, core, direct, swapped, far_ref, exit_ref, sum_ref):
    patch = (patch_ref[0], patch_ref[1])
    sum_ref[0], sum_ref[1] = forward(
        modes_of(core), patch, direct[...], swapped[...], far_ref, exit_ref, 0
    )


def over_kernel(patch_ref, over_y, over_z, rest, direct, swapped, far_ref, exit_ref, sum_ref):
    patch = (patch_ref[0], patch_ref[1])
    modes = [shared_mode(over_y, over_z)] + modes_of(rest)
    sum_ref[0], sum_ref[1] = forward(modes, patch, direct[...], swapped[...], far_ref, exit_ref, 0)


def back_kernel(sides, slots, tile_cols, record_ref, spot_ref, *refs):
    amplitude_ref, patch_ref, own, core = refs[:4]
    over_modes = [shared_mode(*refs[4:6])] + modes_of(refs[6])
    last_modes = [shared_mode(*refs[7:9])] + modes_of(refs[9])
    direct_ref, swapped_ref = refs[10:12]
    near_far, near_exit, near_sum, core_far, core_exit, core_sum = refs[12:18]
    over_far, over_exit, over_sum = refs[18:21]
    weight_out, own_out, keep_out, swap_out = refs[21:25]
    side_outs = refs[25 : 25 + sides]
    last_far, last_exit = refs[25 + sides :]
    side = own.shape[2]
    half = side // 2
    _, x_index, parity = here()
    row_at, col_at = spot_ref[0, 0], spot_ref[1, 0]
    _, _, is_live = position_of(record_ref, slots, parity)
    direct = direct_ref[...]
    swapped = swapped_ref[...]
    patch = (patch_ref[0], patch_ref[1])
    power, weight = forward(last_modes, patch, direct, swapped, last_far, last_exit, 0)
    power = (near_sum[0] + core_sum[0]) + (over_sum[0] + power)
    weight = (near_sum[1] + core_sum[1]) + (over_sum[1] + weight)
    weight_out[...] = weight.astype(jnp.bfloat16)
    amplitude = amplitude_ref[0, 0, parity].astype(jnp.float32)
    factor = amplitude / jnp.sqrt(power + power_floor)
    factor = jnp.concatenate([factor, factor], axis=1)
    tables = (factor, direct, swapped)
    grads = [
        backward(modes_of(own), *tables, near_far, near_exit, 0),
        backward(modes_of(core), *tables, core_far, core_exit, 0),
        backward(over_modes, *tables, over_far, over_exit, 0),
        backward(last_modes, *tables, last_far, last_exit, 0),
    ]
    even = parity == 0
    for channel in range(2):
        gradient = (grads[0][channel] + grads[1][channel]) + (grads[2][channel] + grads[3][channel])
        gradient = jnp.where(is_live, gradient, 0.0)
        gradient = pltpu.roll(pltpu.roll(gradient, col_at, 1), row_at, 0)
        first, second = gradient[:, :half], gradient[:, half:]
        at = iota(first.shape, 1)
        left = jnp.where(at >= col_at, first, 0.0)
        own = [
            jnp.where(at + half >= col_at, second, 0.0),
            jnp.where(at < col_at, first, 0.0),
        ]
        right = jnp.where(at + half < col_at, second, 0.0)
        if sides == 1:
            beside = [jnp.where(x_index == 0, right, left)]
        else:
            beside = [left, right]
        placed = jnp.concatenate(own + beside, axis=1)
        row = iota((half, placed.shape[1]), 0)
        low = jnp.where(row >= row_at, placed[:half], 0.0).astype(jnp.bfloat16)
        high = jnp.where(row < row_at, placed[:half], 0.0).astype(jnp.bfloat16)
        inner = placed[half:].astype(jnp.bfloat16)
        rows = slice(channel * half, (channel + 1) * half)
        own_out[rows] = inner[:, :tile_cols]
        keep_out[rows] = jnp.where(even, high, low)
        swap_out[rows] = jnp.where(even, low, high)
        for index, out in enumerate(side_outs):
            out[rows] = inner[:, tile_cols + index * half : tile_cols + (index + 1) * half]
    for out in side_outs:
        out[2 * half :] = record_ref[:, :half]


def meet_kernel(first_column, record_ref, keep_ref, swap_ref, *outs):
    at = first_column
    for out in outs:
        height, width = keep_ref.shape[0], out.shape[1]
        columns = slice(at, at + width)
        total = keep_ref[:, columns].astype(jnp.float32) + swap_ref[:, columns].astype(jnp.float32)
        out[:height] = total.astype(jnp.bfloat16)
        out[height:] = record_ref[:, :width]
        at += width


def placed_weight(weight, position, z_step, x_step, shown, shape):
    tile_rows, tile_cols = shape
    side = weight.shape[0]
    half = side // 2
    row, col, is_live = position
    row = jnp.where(is_live & shown, row + (z_step * tile_rows - half), nowhere)
    col = col + (x_step * tile_cols - half)
    put_rows = (iota((tile_rows, side), 0) == iota((tile_rows, side), 1) + row).astype(jnp.bfloat16)
    put_cols = (iota((side, tile_cols), 1) == iota((side, tile_cols), 0) + col).astype(jnp.bfloat16)
    return dot(dot(put_rows, weight).astype(jnp.bfloat16), put_cols)


def beside(sides, x_count):
    z_index, x_index, _ = here()
    if sides == 1:
        return [jnp.where(x_index == 0, 1, -1)], [z_index >= 0]
    return [1, -1], [x_index < x_count - 1, x_index > 0]


def edges_added(inner, edges, sides, shown):
    _, x_index, _ = here()
    half = edges[0].shape[1]
    first = jnp.zeros(edges[0].shape, jnp.float32)
    last = first
    for index, edge in enumerate(edges):
        if sides == 1:
            first = jnp.where(x_index == 1, edge, 0.0)
            last = jnp.where(x_index == 0, edge, 0.0)
        elif index == 0:
            last = jnp.where(shown[0], edge, 0.0)
        else:
            first = jnp.where(shown[1], edge, 0.0)
    middle = inner.shape[1] - 2 * half
    parts = [inner[:, :half] + first]
    if middle:
        parts.append(inner[:, half : half + middle])
    parts.append(inner[:, half + middle :] + last)
    return jnp.concatenate(parts, axis=1)


def level_kernel(sides, slots, x_count, weight_ref, record_ref, own_ref, *refs):
    levels, out_ref = refs[:sides], refs[-1]
    shape = out_ref.shape[1:]
    half = levels[0].shape[1]
    z_index, _, parity = here()
    x_steps, shown = beside(sides, x_count)
    weight = weight_ref[...]
    position = position_of(record_ref, slots, parity)
    total = placed_weight(weight, position, 0, 0, z_index >= 0, shape)
    for level, x_step, is_shown in zip(levels, x_steps, shown):
        position = position_of(level[2 * half :], slots, parity)
        total = total + placed_weight(weight, position, 0, x_step, is_shown, shape)
    out_ref[2] = total
    for channel in range(2):
        rows = slice(channel * half, (channel + 1) * half)
        edges = [level[rows].astype(jnp.float32) for level in levels]
        out_ref[channel] = edges_added(own_ref[rows].astype(jnp.float32), edges, sides, shown)


def sum_kernel(sides, slots, z_count, x_count, weight_ref, level_ref, rows_ref, *refs):
    corners, out_ref = refs[:sides], refs[-1]
    shape = out_ref.shape[1:]
    half = corners[0].shape[1]
    z_index, _, parity = here()
    z_step = jnp.where(parity == 0, -1, 1)
    z_shown = jnp.where(parity == 0, z_index > 0, z_index < z_count - 1)
    x_steps, shown = beside(sides, x_count)
    weight = weight_ref[...]
    total = level_ref[2]
    for piece, x_step, is_shown in zip(
        (rows_ref,) + corners, [0] + x_steps, [z_index >= 0] + shown
    ):
        for slot in range(slots):
            position = position_of(piece[2 * half :], slots, slot)
            total = total + placed_weight(
                weight, position, z_step, x_step, is_shown & z_shown, shape
            )
    out_ref[2] = total.astype(jnp.bfloat16)
    for channel in range(2):
        rows = slice(channel * half, (channel + 1) * half)
        edges = [corner[rows].astype(jnp.float32) for corner in corners]
        above = edges_added(rows_ref[rows].astype(jnp.float32), edges, sides, shown)
        total = level_ref[channel] + jnp.where(z_shown, above, 0.0)
        out_ref[channel] = total.astype(jnp.bfloat16)


def update_kernel(object_ref, own_ref, other_ref, out_ref):
    weight = own_ref[2].astype(jnp.float32) + other_ref[2].astype(jnp.float32) + regularizer
    for channel in range(2):
        gradient = own_ref[channel].astype(jnp.float32) + other_ref[channel].astype(jnp.float32)
        out_ref[channel] = object_ref[channel] + gradient / weight


def cost(products):
    return pl.CostEstimate(flops=products * 2 * 256**3, bytes_accessed=0, transcendentals=0)


def in_hbm(array):
    return pltpu.with_memory_space_constraint(array, pltpu.HBM)


def smem():
    return pl.BlockSpec(memory_space=pltpu.SMEM)


def hbm():
    return pl.BlockSpec(memory_space=pltpu.HBM)


def vmem():
    return pl.BlockSpec(memory_space=pltpu.VMEM)


def on_device(object_field, probe, amplitudes, centers, live):
    side = probe.shape[2]
    half = side // 2
    _, tile_rows, tile_cols = object_field.shape
    slots = centers.shape[2]
    z_count = lax.axis_size("tx")
    x_count = lax.axis_size("ty")
    m_count = lax.axis_size("mode")
    modes = probe.shape[1]
    if tile_rows != half or slots != 2 or m_count != 4 or z_count % 2 or x_count < 2 or modes < 2:
        raise ValueError("unsupported sizes")
    sides = 1 if x_count == 2 else 2
    axes = ("tx", "ty", "mode")

    def zigzag(x_step):
        def moved(z, m):
            if m % 2 == 0:
                return (z + 1, m) if z < z_count - 1 else (z, m ^ 1)
            return (z - 1, m) if z > 0 else (z, m ^ 1)

        pairs = []
        for z in range(z_count):
            for x in range(x_count):
                for m in range(m_count):
                    z_to, m_to = moved(z, m)
                    x_to = (x + x_step) % x_count
                    pairs.append(
                        (
                            (z * x_count + x) * m_count + m,
                            (z_to * x_count + x_to) * m_count + m_to,
                        )
                    )
        return pairs

    def level(step):
        return [(x, (x + step) % x_count) for x in range(x_count)]

    def exchange(array, flip):
        return lax.ppermute(array, "mode", [(m, m ^ flip) for m in range(m_count)])

    tables = [jnp.asarray(matrix) for matrix in dft_matrices(side)]
    probe_low, shared, rest, record, spot, direct, swapped, *packed = pl.pallas_call(
        functools.partial(start_kernel, sides, slots),
        out_shape=[
            jax.ShapeDtypeStruct(probe.shape, jnp.bfloat16),
            jax.ShapeDtypeStruct((side, side), jnp.bfloat16),
            jax.ShapeDtypeStruct((2, modes - 1, side, side), jnp.bfloat16),
            jax.ShapeDtypeStruct((record_rows, tile_cols), jnp.bfloat16),
            jax.ShapeDtypeStruct((8, 128), jnp.int32),
            jax.ShapeDtypeStruct((2 * side, 2 * side), jnp.bfloat16),
            jax.ShapeDtypeStruct((2 * side, 2 * side), jnp.bfloat16),
            jax.ShapeDtypeStruct(object_field.shape, jnp.bfloat16),
        ]
        + [jax.ShapeDtypeStruct((2, tile_rows, half), jnp.bfloat16)] * sides,
        in_specs=[hbm()] * 5,
        out_specs=[vmem()] * (8 + sides),
        scratch_shapes=[
            pltpu.VMEM(object_field.shape, jnp.float32),
            pltpu.VMEM(probe.shape, jnp.float32),
            pltpu.SMEM(centers.shape, jnp.int32),
            pltpu.SemaphoreType.DMA((5,)),
        ],
        compiler_params=pltpu.CompilerParams(vmem_limit_bytes=small_bytes),
        name="start",
    )(*(in_hbm(array) for array in (object_field, probe, centers, *tables)))
    over_y = exchange(shared, 2)
    probe_core = exchange(probe_low, 1)
    rest = exchange(rest, 2)
    over_z = lax.ppermute(over_y, "tx", [(z, z ^ 1) for z in range(z_count)])
    x_steps = [1] if sides == 1 else [1, -1]
    rows = lax.ppermute(packed[0], axes, zigzag(0))
    probe_core, *corner_edges = lax.optimization_barrier((probe_core, *packed[1:]))
    corners = [lax.ppermute(edge, axes, zigzag(step)) for step, edge in zip(x_steps, corner_edges)]
    levels = [lax.ppermute(edge, "ty", level(step)) for step, edge in zip(x_steps, packed[1:])]
    corners, record = lax.optimization_barrier((corners, record))
    record = pl.pallas_call(
        functools.partial(live_kernel, slots),
        out_shape=jax.ShapeDtypeStruct(record.shape, jnp.bfloat16),
        in_specs=[vmem(), smem()],
        out_specs=vmem(),
        compiler_params=pltpu.CompilerParams(vmem_limit_bytes=small_bytes),
        cost_estimate=cost(50),
        name="live",
    )(record, live)
    corners, record = lax.optimization_barrier((corners, record))
    pieces = [packed[0], rows, exchange(rows, 1)]
    for at_level, corner in zip(levels, corners):
        pieces += [at_level, corner, exchange(corner, 1)]
    n_pieces = len(pieces)
    ext_cols = tile_cols + sides * half

    waves = [
        jax.ShapeDtypeStruct((modes, side, 2 * side), jnp.float32),
        jax.ShapeDtypeStruct((modes, 2 * side, side), jnp.bfloat16),
        jax.ShapeDtypeStruct((2, side, side), jnp.float32),
    ]
    patch, *near = pl.pallas_call(
        functools.partial(near_kernel, sides, z_count, x_count),
        out_shape=[jax.ShapeDtypeStruct((2, side, side), jnp.float32)] + waves,
        in_specs=[vmem()] * (n_pieces + 4),
        out_specs=[vmem()] * 4,
        compiler_params=pltpu.CompilerParams(vmem_limit_bytes=wave_bytes),
        cost_estimate=cost(1),
        name="near",
    )(spot, *in_sent_order(pieces), probe_low, direct, swapped)
    rest, patch = lax.optimization_barrier((rest, patch))
    other = pl.pallas_call(
        core_kernel,
        out_shape=waves,
        in_specs=[vmem()] * 4,
        out_specs=[vmem()] * 3,
        compiler_params=pltpu.CompilerParams(vmem_limit_bytes=wave_bytes),
        cost_estimate=cost(1),
        name="core",
    )(patch, probe_core, direct, swapped)
    last_y = exchange(over_y, 1)
    over_z, other = lax.optimization_barrier((over_z, other))
    over_group = (over_y, over_z, rest)
    last_group = [last_y, exchange(over_z, 1), exchange(rest, 1)]
    over = pl.pallas_call(
        over_kernel,
        out_shape=waves,
        in_specs=[vmem()] * 6,
        out_specs=[vmem()] * 3,
        compiler_params=pltpu.CompilerParams(vmem_limit_bytes=wave_bytes),
        cost_estimate=cost(100),
        name="over",
    )(patch, *over_group, direct, swapped)
    piece_rows = 2 * half + record_rows
    shapes = [(side, side), (2 * half, tile_cols)] + [(2 * half, ext_cols)] * 2
    shapes += [(piece_rows, half)] * sides
    weight, own, keep, swap, *levels = pl.pallas_call(
        functools.partial(back_kernel, sides, slots, tile_cols),
        out_shape=[jax.ShapeDtypeStruct(shape, jnp.bfloat16) for shape in shapes],
        in_specs=[vmem()] * 23,
        out_specs=[vmem()] * (4 + sides),
        scratch_shapes=[
            pltpu.VMEM((modes, side, 2 * side), jnp.float32),
            pltpu.VMEM((modes, 2 * side, side), jnp.bfloat16),
        ],
        compiler_params=pltpu.CompilerParams(vmem_limit_bytes=wave_bytes),
        cost_estimate=cost(80),
        name="back",
    )(
        record,
        spot,
        amplitudes,
        patch,
        probe_low,
        probe_core,
        *over_group,
        *last_group,
        direct,
        swapped,
        *near,
        *other,
        *over,
    )
    levels = [lax.ppermute(piece, "ty", level(-step)) for piece, step in zip(levels, x_steps)]
    rows, *corners = pl.pallas_call(
        functools.partial(meet_kernel, 0),
        out_shape=[
            jax.ShapeDtypeStruct((piece_rows, width), jnp.bfloat16)
            for width in [tile_cols] + [half] * sides
        ],
        in_specs=[vmem()] * 3,
        out_specs=[vmem()] * (1 + sides),
        compiler_params=pltpu.CompilerParams(vmem_limit_bytes=small_bytes),
        name="meet",
    )(record, keep, exchange(swap, 1))
    rows = lax.ppermute(rows, axes, zigzag(0))
    corners = [
        lax.ppermute(piece, axes, zigzag(-step)) for piece, step in zip(corners, x_steps)
    ]
    leveled = pl.pallas_call(
        functools.partial(level_kernel, sides, slots, x_count),
        out_shape=jax.ShapeDtypeStruct((3, tile_rows, tile_cols), jnp.float32),
        in_specs=[vmem()] * (3 + sides),
        out_specs=vmem(),
        compiler_params=pltpu.CompilerParams(vmem_limit_bytes=small_bytes),
        cost_estimate=cost(40),
        name="levels",
    )(weight, record, own, *levels)
    summed = pl.pallas_call(
        functools.partial(sum_kernel, sides, slots, z_count, x_count),
        out_shape=jax.ShapeDtypeStruct((3, tile_rows, tile_cols), jnp.bfloat16),
        in_specs=[vmem()] * (3 + sides),
        out_specs=vmem(),
        compiler_params=pltpu.CompilerParams(vmem_limit_bytes=small_bytes),
        name="sums",
    )(weight, leveled, rows, *corners)
    return pl.pallas_call(
        update_kernel,
        out_shape=jax.ShapeDtypeStruct(object_field.shape, jnp.float32),
        in_specs=[vmem()] * 3,
        out_specs=vmem(),
        compiler_params=pltpu.CompilerParams(vmem_limit_bytes=small_bytes),
        name="update",
    )(object_field, summed, exchange(summed, 1))


def solution(mesh):
    return jax.shard_map(
        on_device,
        mesh=mesh,
        in_specs=(
            P(None, "tx", "ty"),
            P(None, "mode", None, None),
            P("tx", "ty", None, None, None),
            P("tx", "ty", None, None),
            P("tx", "ty"),
        ),
        out_specs=P(None, "tx", "ty"),
        check_vma=False,
    )
```

```python
import functools
import math

import jax
import jax.numpy as jnp
import numpy as np
from jax import lax
from jax.experimental import pallas as pl
from jax.experimental.pallas import tpu as pltpu
from jax.sharding import PartitionSpec as P

power_floor = 0.01
regularizer = 0.1
nowhere = -(1 << 20)
record_rows = 16
wave_bytes = 32 * 1024 * 1024
small_bytes = 8 * 1024 * 1024


def dft_matrices(side):
    line = np.arange(side, dtype=np.int32)
    angle = (line[:, None] * line[None, :] % side).astype(np.float32) * np.float32(
        2.0 * math.pi / side
    )
    scaling = np.float32(1.0 / math.sqrt(side))
    real = (np.cos(angle) * scaling).astype(jnp.bfloat16)
    imag = (-np.sin(angle) * scaling).astype(jnp.bfloat16)
    direct = np.block([[real, -imag], [imag, real]])
    swapped = np.block([[real, imag], [-imag, real]])
    return direct, swapped


def dot(left, right):
    return jnp.dot(left, right, preferred_element_type=jnp.float32)


def iota(shape, dim):
    return lax.broadcasted_iota(jnp.int32, shape, dim)


def sent_order(sides):
    corners = [at for index in range(sides) for at in (4 + 3 * index, 5 + 3 * index)]
    return [0] + corners + [1, 2] + [3 + 3 * index for index in range(sides)]


def in_sent_order(pieces):
    return [pieces[at] for at in sent_order(len(pieces) // 3 - 1)]


def from_sent_order(pieces):
    order = sent_order(len(pieces) // 3 - 1)
    return [pieces[order.index(at)] for at in range(len(pieces))]


def wide(tall):
    side = tall.shape[0] // 2
    return jnp.concatenate([tall[:side], tall[side:]], axis=1)


def tall(wide):
    side = wide.shape[1] // 2
    return jnp.concatenate([wide[:, :side], wide[:, side:]], axis=0)


def here():
    return (lax.axis_index("tx"), lax.axis_index("ty"), lax.axis_index("mode") % 2)


def start_kernel(
    sides,
    slots,
    object_hbm,
    probe_hbm,
    centers_hbm,
    direct_hbm,
    swapped_hbm,
    low_ref,
    shared_ref,
    rest_ref,
    record_ref,
    spot_ref,
    direct_ref,
    swapped_ref,
    packed_ref,
    *refs,
):
    edges = refs[:sides]
    object_ref, probe_ref, centers_ref, sems = refs[sides:]
    copies = [
        pltpu.make_async_copy(source, target, sems.at[index])
        for index, (source, target) in enumerate(
            (
                (probe_hbm, probe_ref),
                (object_hbm, object_ref),
                (centers_hbm, centers_ref),
                (direct_hbm, direct_ref),
                (swapped_hbm, swapped_ref),
            )
        )
    ]
    for copy in copies:
        copy.start()
    tile_cols = object_ref.shape[2]
    half = edges[0].shape[2]
    z_index, x_index, parity = here()
    copies[0].wait()
    low_ref[...] = probe_ref[...].astype(jnp.bfloat16)
    shared_ref[...] = jnp.where(z_index % 2 == 0, low_ref[0, 0], low_ref[1, 0])
    rest_ref[...] = low_ref[:, 1:]
    copies[1].wait()
    first, last = slice(0, half), slice(tile_cols - half, tile_cols)
    for channel in range(2):
        values = object_ref[channel].astype(jnp.bfloat16)
        packed_ref[channel] = values
        if sides == 1:
            edges[0][channel] = jnp.where(x_index == 0, values[:, last], values[:, first])
        else:
            edges[0][channel] = values[:, last]
            edges[1][channel] = values[:, first]
    copies[2].wait()
    spot_ref[...] = jnp.where(
        iota(spot_ref.shape, 0) == 0, centers_ref[0, 0, parity, 0], centers_ref[0, 0, parity, 1]
    )
    record = jnp.zeros(record_ref.shape, jnp.float32)
    line = iota(record_ref.shape, 0)
    for slot in range(slots):
        for axis in range(2):
            value = centers_ref[0, 0, slot, axis].astype(jnp.float32)
            record = jnp.where(line == 2 * slot + axis, value, record)
    record_ref[...] = record.astype(jnp.bfloat16)
    copies[3].wait()
    copies[4].wait()


def live_kernel(slots, record_ref, live_ref, out_ref):
    line = iota(record_ref.shape, 0)
    record = record_ref[...].astype(jnp.float32)
    record = jnp.where(line == 2 * slots, live_ref[0, 0].astype(jnp.float32), record)
    out_ref[...] = record.astype(jnp.bfloat16)


def position_of(record, slots, wanted):
    record = record[:, :128].astype(jnp.float32).astype(jnp.int32)[:, :1]

    def of_slot(axis):
        value = record[axis : axis + 1]
        for slot in range(1, slots):
            value = jnp.where(wanted == slot, record[2 * slot + axis : 2 * slot + axis + 1], value)
        return value

    return of_slot(0), of_slot(1), record[2 * slots : 2 * slots + 1] > wanted


def turned_back(value, side):
    return jnp.where(value == 0, 0, side - value)


def patch_of(sides, z_count, x_count, side, spot_ref, pieces):
    z_index, x_index, parity = here()
    row_at, col_at = spot_ref[0, 0], spot_ref[1, 0]
    half = side // 2
    even = parity == 0
    low_shown = z_index > 0
    high_shown = z_index < z_count - 1

    def joined(piece, a, b, channel):
        level = piece[channel].astype(jnp.float32)
        turn_a = a[channel].astype(jnp.float32)
        turn_b = b[channel].astype(jnp.float32)
        low = jnp.where(even & low_shown, turn_a, jnp.where(low_shown, turn_b, 0.0))
        high = jnp.where(even & high_shown, turn_b, jnp.where(high_shown, turn_a, 0.0))
        first = jnp.where(iota(low.shape, 0) >= row_at, low, high)
        return jnp.concatenate([first, level], axis=0)

    out = []
    for channel in range(2):
        own = joined(*pieces[:3], channel)
        sides_joined = [
            joined(*pieces[3 + 3 * index : 6 + 3 * index], channel) for index in range(sides)
        ]
        if sides == 1:
            left = jnp.where(x_index == 1, sides_joined[0], 0.0)
            right = jnp.where(x_index == 0, sides_joined[0], 0.0)
        else:
            left = jnp.where(x_index > 0, sides_joined[0], 0.0)
            right = jnp.where(x_index < x_count - 1, sides_joined[1], 0.0)
        at = iota(left.shape, 1)
        window = jnp.concatenate(
            [
                jnp.where(at >= col_at, left, own[:, half:]),
                jnp.where(at + half >= col_at, own[:, :half], right),
            ],
            axis=1,
        )
        window = pltpu.roll(window, turned_back(row_at, side), 0)
        out.append(pltpu.roll(window, turned_back(col_at, side), 1))
    return out


def modes_of(group):
    def reader(k):
        return lambda: (group[0, k].astype(jnp.float32), group[1, k].astype(jnp.float32))

    return [reader(k) for k in range(group.shape[1])]


def shared_mode(over_y, over_z):
    def read():
        z_index, _, _ = here()
        even = z_index % 2 == 0
        over_y_values = over_y[...].astype(jnp.float32)
        over_z_values = over_z[...].astype(jnp.float32)
        return (
            jnp.where(even, over_y_values, over_z_values),
            jnp.where(even, over_z_values, over_y_values),
        )

    return read


def forward(modes, patch, direct, swapped, far_ref, exit_ref, at):
    patch_real, patch_imag = patch
    side = patch_real.shape[0]
    power = jnp.zeros((side, side), jnp.float32)
    weight = jnp.zeros((side, side), jnp.float32)
    halves = []
    for k, mode in enumerate(modes):
        real, imag = mode()
        exit_wave = jnp.concatenate(
            [
                (real * patch_real - imag * patch_imag).astype(jnp.bfloat16),
                (real * patch_imag + imag * patch_real).astype(jnp.bfloat16),
            ],
            axis=0,
        )
        exit_ref[at + k] = exit_wave
        halves.append(wide(dot(direct, exit_wave).astype(jnp.bfloat16)))
        weight = weight + (real * real + imag * imag)
    far_all = dot(jnp.concatenate(halves, axis=0), swapped)
    for k in range(len(modes)):
        far = far_all[k * side : (k + 1) * side]
        far_ref[at + k] = far
        power = power + (far[:, :side] * far[:, :side] + far[:, side:] * far[:, side:])
    return power, weight


def backward(modes, factor, direct, swapped, far_ref, exit_ref, at):
    side = factor.shape[0]
    grad_real = jnp.zeros((side, side), jnp.float32)
    grad_imag = jnp.zeros((side, side), jnp.float32)
    halves = []
    for k in range(len(modes)):
        fixed = (far_ref[at + k] * factor).astype(jnp.bfloat16)
        halves.append(wide(dot(swapped, tall(fixed)).astype(jnp.bfloat16)))
    back_all = dot(jnp.concatenate(halves, axis=0), direct)
    for k, mode in enumerate(modes):
        back = back_all[k * side : (k + 1) * side]
        exit_wave = exit_ref[at + k].astype(jnp.float32)
        real, imag = mode()
        diff_real = back[:, :side] - exit_wave[:side]
        diff_imag = back[:, side:] - exit_wave[side:]
        grad_real = grad_real + (real * diff_real + imag * diff_imag)
        grad_imag = grad_imag + (real * diff_imag - imag * diff_real)
    return grad_real, grad_imag


def near_kernel(sides, z_count, x_count, spot_ref, *refs):
    n_pieces = 3 + 3 * sides
    pieces = from_sent_order(refs[:n_pieces])
    own, direct, swapped = refs[n_pieces : n_pieces + 3]
    patch_ref, far_ref, exit_ref, sum_ref = refs[n_pieces + 3 :]
    side = own.shape[2]
    patch = patch_of(sides, z_count, x_count, side, spot_ref, pieces)
    patch_ref[0], patch_ref[1] = patch
    sum_ref[0], sum_ref[1] = forward(
        modes_of(own), patch, direct[...], swapped[...], far_ref, exit_ref, 0
    )


def core_kernel(patch_ref, core, direct, swapped, far_ref, exit_ref, sum_ref):
    patch = (patch_ref[0], patch_ref[1])
    sum_ref[0], sum_ref[1] = forward(
        modes_of(core), patch, direct[...], swapped[...], far_ref, exit_ref, 0
    )


def over_kernel(patch_ref, over_y, over_z, rest, direct, swapped, far_ref, exit_ref, sum_ref):
    patch = (patch_ref[0], patch_ref[1])
    modes = [shared_mode(over_y, over_z)] + modes_of(rest)
    sum_ref[0], sum_ref[1] = forward(modes, patch, direct[...], swapped[...], far_ref, exit_ref, 0)


def back_kernel(sides, slots, tile_cols, record_ref, spot_ref, *refs):
    amplitude_ref, patch_ref, own, core = refs[:4]
    over_modes = [shared_mode(*refs[4:6])] + modes_of(refs[6])
    last_modes = [shared_mode(*refs[7:9])] + modes_of(refs[9])
    direct_ref, swapped_ref = refs[10:12]
    near_far, near_exit, near_sum, core_far, core_exit, core_sum = refs[12:18]
    over_far, over_exit, over_sum = refs[18:21]
    weight_out, own_out, keep_out, swap_out = refs[21:25]
    side_outs = refs[25 : 25 + sides]
    last_far, last_exit = refs[25 + sides :]
    side = own.shape[2]
    half = side // 2
    _, x_index, parity = here()
    row_at, col_at = spot_ref[0, 0], spot_ref[1, 0]
    _, _, is_live = position_of(record_ref, slots, parity)
    direct = direct_ref[...]
    swapped = swapped_ref[...]
    patch = (patch_ref[0], patch_ref[1])
    power, weight = forward(last_modes, patch, direct, swapped, last_far, last_exit, 0)
    power = (near_sum[0] + core_sum[0]) + (over_sum[0] + power)
    weight = (near_sum[1] + core_sum[1]) + (over_sum[1] + weight)
    weight_out[...] = weight.astype(jnp.bfloat16)
    amplitude = amplitude_ref[0, 0, parity].astype(jnp.float32)
    factor = amplitude / jnp.sqrt(power + power_floor)
    factor = jnp.concatenate([factor, factor], axis=1)
    tables = (factor, direct, swapped)
    grads = [
        backward(modes_of(own), *tables, near_far, near_exit, 0),
        backward(modes_of(core), *tables, core_far, core_exit, 0),
        backward(over_modes, *tables, over_far, over_exit, 0),
        backward(last_modes, *tables, last_far, last_exit, 0),
    ]
    even = parity == 0
    for channel in range(2):
        gradient = (grads[0][channel] + grads[1][channel]) + (grads[2][channel] + grads[3][channel])
        gradient = jnp.where(is_live, gradient, 0.0)
        gradient = pltpu.roll(pltpu.roll(gradient, col_at, 1), row_at, 0)
        first, second = gradient[:, :half], gradient[:, half:]
        at = iota(first.shape, 1)
        left = jnp.where(at >= col_at, first, 0.0)
        own = [
            jnp.where(at + half >= col_at, second, 0.0),
            jnp.where(at < col_at, first, 0.0),
        ]
        right = jnp.where(at + half < col_at, second, 0.0)
        if sides == 1:
            beside = [jnp.where(x_index == 0, right, left)]
        else:
            beside = [left, right]
        placed = jnp.concatenate(own + beside, axis=1)
        row = iota((half, placed.shape[1]), 0)
        low = jnp.where(row >= row_at, placed[:half], 0.0).astype(jnp.bfloat16)
        high = jnp.where(row < row_at, placed[:half], 0.0).astype(jnp.bfloat16)
        inner = placed[half:].astype(jnp.bfloat16)
        rows = slice(channel * half, (channel + 1) * half)
        own_out[rows] = inner[:, :tile_cols]
        keep_out[rows] = jnp.where(even, high, low)
        swap_out[rows] = jnp.where(even, low, high)
        for index, out in enumerate(side_outs):
            out[rows] = inner[:, tile_cols + index * half : tile_cols + (index + 1) * half]
    for out in side_outs:
        out[2 * half :] = record_ref[:, :half]


def meet_kernel(first_column, record_ref, keep_ref, swap_ref, *outs):
    at = first_column
    for out in outs:
        height, width = keep_ref.shape[0], out.shape[1]
        columns = slice(at, at + width)
        total = keep_ref[:, columns].astype(jnp.float32) + swap_ref[:, columns].astype(jnp.float32)
        out[:height] = total.astype(jnp.bfloat16)
        out[height:] = record_ref[:, :width]
        at += width


def placed_weight(weight, position, z_step, x_step, shown, shape):
    tile_rows, tile_cols = shape
    side = weight.shape[0]
    half = side // 2
    row, col, is_live = position
    row = jnp.where(is_live & shown, row + (z_step * tile_rows - half), nowhere)
    col = col + (x_step * tile_cols - half)
    put_rows = (iota((tile_rows, side), 0) == iota((tile_rows, side), 1) + row).astype(jnp.bfloat16)
    put_cols = (iota((side, tile_cols), 1) == iota((side, tile_cols), 0) + col).astype(jnp.bfloat16)
    return dot(dot(put_rows, weight).astype(jnp.bfloat16), put_cols)


def beside(sides, x_count):
    z_index, x_index, _ = here()
    if sides == 1:
        return [jnp.where(x_index == 0, 1, -1)], [z_index >= 0]
    return [1, -1], [x_index < x_count - 1, x_index > 0]


def edges_added(inner, edges, sides, shown):
    _, x_index, _ = here()
    half = edges[0].shape[1]
    first = jnp.zeros(edges[0].shape, jnp.float32)
    last = first
    for index, edge in enumerate(edges):
        if sides == 1:
            first = jnp.where(x_index == 1, edge, 0.0)
            last = jnp.where(x_index == 0, edge, 0.0)
        elif index == 0:
            last = jnp.where(shown[0], edge, 0.0)
        else:
            first = jnp.where(shown[1], edge, 0.0)
    middle = inner.shape[1] - 2 * half
    parts = [inner[:, :half] + first]
    if middle:
        parts.append(inner[:, half : half + middle])
    parts.append(inner[:, half + middle :] + last)
    return jnp.concatenate(parts, axis=1)


def level_kernel(sides, slots, x_count, weight_ref, record_ref, own_ref, *refs):
    levels, out_ref = refs[:sides], refs[-1]
    shape = out_ref.shape[1:]
    half = levels[0].shape[1]
    z_index, _, parity = here()
    x_steps, shown = beside(sides, x_count)
    weight = weight_ref[...]
    position = position_of(record_ref, slots, parity)
    total = placed_weight(weight, position, 0, 0, z_index >= 0, shape)
    for level, x_step, is_shown in zip(levels, x_steps, shown):
        position = position_of(level[2 * half :], slots, parity)
        total = total + placed_weight(weight, position, 0, x_step, is_shown, shape)
    out_ref[2] = total
    for channel in range(2):
        rows = slice(channel * half, (channel + 1) * half)
        edges = [level[rows].astype(jnp.float32) for level in levels]
        out_ref[channel] = edges_added(own_ref[rows].astype(jnp.float32), edges, sides, shown)


def sum_kernel(sides, slots, z_count, x_count, weight_ref, level_ref, rows_ref, *refs):
    corners, out_ref = refs[:sides], refs[-1]
    shape = out_ref.shape[1:]
    half = corners[0].shape[1]
    z_index, _, parity = here()
    z_step = jnp.where(parity == 0, -1, 1)
    z_shown = jnp.where(parity == 0, z_index > 0, z_index < z_count - 1)
    x_steps, shown = beside(sides, x_count)
    weight = weight_ref[...]
    total = level_ref[2]
    for piece, x_step, is_shown in zip(
        (rows_ref,) + corners, [0] + x_steps, [z_index >= 0] + shown
    ):
        for slot in range(slots):
            position = position_of(piece[2 * half :], slots, slot)
            total = total + placed_weight(
                weight, position, z_step, x_step, is_shown & z_shown, shape
            )
    out_ref[2] = total.astype(jnp.bfloat16)
    for channel in range(2):
        rows = slice(channel * half, (channel + 1) * half)
        edges = [corner[rows].astype(jnp.float32) for corner in corners]
        above = edges_added(rows_ref[rows].astype(jnp.float32), edges, sides, shown)
        total = level_ref[channel] + jnp.where(z_shown, above, 0.0)
        out_ref[channel] = total.astype(jnp.bfloat16)


def update_kernel(object_ref, own_ref, other_ref, out_ref):
    weight = own_ref[2].astype(jnp.float32) + other_ref[2].astype(jnp.float32) + regularizer
    for channel in range(2):
        gradient = own_ref[channel].astype(jnp.float32) + other_ref[channel].astype(jnp.float32)
        out_ref[channel] = object_ref[channel] + gradient / weight


def cost(products):
    return pl.CostEstimate(flops=products * 2 * 256**3, bytes_accessed=0, transcendentals=0)


def in_hbm(array):
    return pltpu.with_memory_space_constraint(array, pltpu.HBM)


def smem():
    return pl.BlockSpec(memory_space=pltpu.SMEM)


def hbm():
    return pl.BlockSpec(memory_space=pltpu.HBM)


def vmem():
    return pl.BlockSpec(memory_space=pltpu.VMEM)


def on_device(object_field, probe, amplitudes, centers, live):
    side = probe.shape[2]
    half = side // 2
    _, tile_rows, tile_cols = object_field.shape
    slots = centers.shape[2]
    z_count = lax.axis_size("tx")
    x_count = lax.axis_size("ty")
    m_count = lax.axis_size("mode")
    modes = probe.shape[1]
    if tile_rows != half or slots != 2 or m_count != 4 or z_count % 2 or x_count < 2 or modes < 2:
        raise ValueError("unsupported sizes")
    sides = 1 if x_count == 2 else 2
    axes = ("tx", "ty", "mode")

    def zigzag(x_step):
        def moved(z, m):
            if m % 2 == 0:
                return (z + 1, m) if z < z_count - 1 else (z, m ^ 1)
            return (z - 1, m) if z > 0 else (z, m ^ 1)

        pairs = []
        for z in range(z_count):
            for x in range(x_count):
                for m in range(m_count):
                    z_to, m_to = moved(z, m)
                    x_to = (x + x_step) % x_count
                    pairs.append(
                        (
                            (z * x_count + x) * m_count + m,
                            (z_to * x_count + x_to) * m_count + m_to,
                        )
                    )
        return pairs

    def level(step):
        return [(x, (x + step) % x_count) for x in range(x_count)]

    def exchange(array, flip):
        return lax.ppermute(array, "mode", [(m, m ^ flip) for m in range(m_count)])

    tables = [jnp.asarray(matrix) for matrix in dft_matrices(side)]
    probe_low, shared, rest, record, spot, direct, swapped, *packed = pl.pallas_call(
        functools.partial(start_kernel, sides, slots),
        out_shape=[
            jax.ShapeDtypeStruct(probe.shape, jnp.bfloat16),
            jax.ShapeDtypeStruct((side, side), jnp.bfloat16),
            jax.ShapeDtypeStruct((2, modes - 1, side, side), jnp.bfloat16),
            jax.ShapeDtypeStruct((record_rows, tile_cols), jnp.bfloat16),
            jax.ShapeDtypeStruct((8, 128), jnp.int32),
            jax.ShapeDtypeStruct((2 * side, 2 * side), jnp.bfloat16),
            jax.ShapeDtypeStruct((2 * side, 2 * side), jnp.bfloat16),
            jax.ShapeDtypeStruct(object_field.shape, jnp.bfloat16),
        ]
        + [jax.ShapeDtypeStruct((2, tile_rows, half), jnp.bfloat16)] * sides,
        in_specs=[hbm()] * 5,
        out_specs=[vmem()] * (8 + sides),
        scratch_shapes=[
            pltpu.VMEM(object_field.shape, jnp.float32),
            pltpu.VMEM(probe.shape, jnp.float32),
            pltpu.SMEM(centers.shape, jnp.int32),
            pltpu.SemaphoreType.DMA((5,)),
        ],
        compiler_params=pltpu.CompilerParams(vmem_limit_bytes=small_bytes),
        name="start",
    )(*(in_hbm(array) for array in (object_field, probe, centers, *tables)))
    over_y = exchange(shared, 2)
    probe_core = exchange(probe_low, 1)
    rest = exchange(rest, 2)
    over_z = lax.ppermute(over_y, "tx", [(z, z ^ 1) for z in range(z_count)])
    x_steps = [1] if sides == 1 else [1, -1]
    rows = lax.ppermute(packed[0], axes, zigzag(0))
    probe_core, *corner_edges = lax.optimization_barrier((probe_core, *packed[1:]))
    corners = [lax.ppermute(edge, axes, zigzag(step)) for step, edge in zip(x_steps, corner_edges)]
    levels = [lax.ppermute(edge, "ty", level(step)) for step, edge in zip(x_steps, packed[1:])]
    corners, record = lax.optimization_barrier((corners, record))
    record = pl.pallas_call(
        functools.partial(live_kernel, slots),
        out_shape=jax.ShapeDtypeStruct(record.shape, jnp.bfloat16),
        in_specs=[vmem(), smem()],
        out_specs=vmem(),
        compiler_params=pltpu.CompilerParams(vmem_limit_bytes=small_bytes),
        cost_estimate=cost(40),
        name="live",
    )(record, live)
    corners, record = lax.optimization_barrier((corners, record))
    pieces = [packed[0], rows, exchange(rows, 1)]
    for at_level, corner in zip(levels, corners):
        pieces += [at_level, corner, exchange(corner, 1)]
    n_pieces = len(pieces)
    ext_cols = tile_cols + sides * half

    waves = [
        jax.ShapeDtypeStruct((modes, side, 2 * side), jnp.float32),
        jax.ShapeDtypeStruct((modes, 2 * side, side), jnp.bfloat16),
        jax.ShapeDtypeStruct((2, side, side), jnp.float32),
    ]
    patch, *near = pl.pallas_call(
        functools.partial(near_kernel, sides, z_count, x_count),
        out_shape=[jax.ShapeDtypeStruct((2, side, side), jnp.float32)] + waves,
        in_specs=[vmem()] * (n_pieces + 4),
        out_specs=[vmem()] * 4,
        compiler_params=pltpu.CompilerParams(vmem_limit_bytes=wave_bytes),
        cost_estimate=cost(1),
        name="near",
    )(spot, *in_sent_order(pieces), probe_low, direct, swapped)
    rest, patch = lax.optimization_barrier((rest, patch))
    other = pl.pallas_call(
        core_kernel,
        out_shape=waves,
        in_specs=[vmem()] * 4,
        out_specs=[vmem()] * 3,
        compiler_params=pltpu.CompilerParams(vmem_limit_bytes=wave_bytes),
        cost_estimate=cost(1),
        name="core",
    )(patch, probe_core, direct, swapped)
    last_y = exchange(over_y, 1)
    over_z, other = lax.optimization_barrier((over_z, other))
    over_group = (over_y, over_z, rest)
    last_group = [last_y, exchange(over_z, 1), exchange(rest, 1)]
    over = pl.pallas_call(
        over_kernel,
        out_shape=waves,
        in_specs=[vmem()] * 6,
        out_specs=[vmem()] * 3,
        compiler_params=pltpu.CompilerParams(vmem_limit_bytes=wave_bytes),
        cost_estimate=cost(100),
        name="over",
    )(patch, *over_group, direct, swapped)
    piece_rows = 2 * half + record_rows
    shapes = [(side, side), (2 * half, tile_cols)] + [(2 * half, ext_cols)] * 2
    shapes += [(piece_rows, half)] * sides
    weight, own, keep, swap, *levels = pl.pallas_call(
        functools.partial(back_kernel, sides, slots, tile_cols),
        out_shape=[jax.ShapeDtypeStruct(shape, jnp.bfloat16) for shape in shapes],
        in_specs=[vmem()] * 23,
        out_specs=[vmem()] * (4 + sides),
        scratch_shapes=[
            pltpu.VMEM((modes, side, 2 * side), jnp.float32),
            pltpu.VMEM((modes, 2 * side, side), jnp.bfloat16),
        ],
        compiler_params=pltpu.CompilerParams(vmem_limit_bytes=wave_bytes),
        cost_estimate=cost(80),
        name="back",
    )(
        record,
        spot,
        amplitudes,
        patch,
        probe_low,
        probe_core,
        *over_group,
        *last_group,
        direct,
        swapped,
        *near,
        *other,
        *over,
    )
    levels = [lax.ppermute(piece, "ty", level(-step)) for piece, step in zip(levels, x_steps)]
    rows, *corners = pl.pallas_call(
        functools.partial(meet_kernel, 0),
        out_shape=[
            jax.ShapeDtypeStruct((piece_rows, width), jnp.bfloat16)
            for width in [tile_cols] + [half] * sides
        ],
        in_specs=[vmem()] * 3,
        out_specs=[vmem()] * (1 + sides),
        compiler_params=pltpu.CompilerParams(vmem_limit_bytes=small_bytes),
        name="meet",
    )(record, keep, exchange(swap, 1))
    rows = lax.ppermute(rows, axes, zigzag(0))
    corners = [
        lax.ppermute(piece, axes, zigzag(-step)) for piece, step in zip(corners, x_steps)
    ]
    leveled = pl.pallas_call(
        functools.partial(level_kernel, sides, slots, x_count),
        out_shape=jax.ShapeDtypeStruct((3, tile_rows, tile_cols), jnp.float32),
        in_specs=[vmem()] * (3 + sides),
        out_specs=vmem(),
        compiler_params=pltpu.CompilerParams(vmem_limit_bytes=small_bytes),
        cost_estimate=cost(40),
        name="levels",
    )(weight, record, own, *levels)
    summed = pl.pallas_call(
        functools.partial(sum_kernel, sides, slots, z_count, x_count),
        out_shape=jax.ShapeDtypeStruct((3, tile_rows, tile_cols), jnp.bfloat16),
        in_specs=[vmem()] * (3 + sides),
        out_specs=vmem(),
        compiler_params=pltpu.CompilerParams(vmem_limit_bytes=small_bytes),
        name="sums",
    )(weight, leveled, rows, *corners)
    return pl.pallas_call(
        update_kernel,
        out_shape=jax.ShapeDtypeStruct(object_field.shape, jnp.float32),
        in_specs=[vmem()] * 3,
        out_specs=vmem(),
        compiler_params=pltpu.CompilerParams(vmem_limit_bytes=small_bytes),
        name="update",
    )(object_field, summed, exchange(summed, 1))


def solution(mesh):
    return jax.shard_map(
        on_device,
        mesh=mesh,
        in_specs=(
            P(None, "tx", "ty"),
            P(None, "mode", None, None),
            P("tx", "ty", None, None, None),
            P("tx", "ty", None, None),
            P("tx", "ty"),
        ),
        out_specs=P(None, "tx", "ty"),
        check_vma=False,
    )
```

```python
import functools
import math

import jax
import jax.numpy as jnp
import numpy as np
from jax import lax
from jax.experimental import pallas as pl
from jax.experimental.pallas import tpu as pltpu
from jax.sharding import PartitionSpec as P

power_floor = 0.01
regularizer = 0.1
nowhere = -(1 << 20)
record_rows = 16
wave_bytes = 32 * 1024 * 1024
small_bytes = 8 * 1024 * 1024


def dft_table(side):
    line = np.arange(side, dtype=np.int32)
    angle = (line[:, None] * line[None, :] % side).astype(np.float32) * np.float32(
        2.0 * math.pi / side
    )
    scaling = np.float32(1.0 / math.sqrt(side))
    real = (np.cos(angle) * scaling).astype(jnp.bfloat16)
    imag = (-np.sin(angle) * scaling).astype(jnp.bfloat16)
    return np.stack([real, imag])


def dot(left, right):
    return jnp.dot(left, right, preferred_element_type=jnp.float32)


def iota(shape, dim):
    return lax.broadcasted_iota(jnp.int32, shape, dim)


def sent_order(sides):
    corners = [at for index in range(sides) for at in (4 + 3 * index, 5 + 3 * index)]
    return [0] + corners + [1, 2] + [3 + 3 * index for index in range(sides)]


def in_sent_order(pieces):
    return [pieces[at] for at in sent_order(len(pieces) // 3 - 1)]


def from_sent_order(pieces):
    order = sent_order(len(pieces) // 3 - 1)
    return [pieces[order.index(at)] for at in range(len(pieces))]


def wide(tall):
    side = tall.shape[0] // 2
    return jnp.concatenate([tall[:side], tall[side:]], axis=1)


def tall(wide):
    side = wide.shape[1] // 2
    return jnp.concatenate([wide[:, :side], wide[:, side:]], axis=0)


def here():
    return (lax.axis_index("tx"), lax.axis_index("ty"), lax.axis_index("mode") % 2)


def start_kernel(
    sides,
    slots,
    object_hbm,
    probe_hbm,
    centers_hbm,
    table_hbm,
    low_ref,
    shared_ref,
    rest_ref,
    record_ref,
    spot_ref,
    direct_ref,
    swapped_ref,
    packed_ref,
    *refs,
):
    edges = refs[:sides]
    object_ref, probe_ref, centers_ref, table_ref, sems = refs[sides:]
    copies = [
        pltpu.make_async_copy(source, target, sems.at[index])
        for index, (source, target) in enumerate(
            (
                (probe_hbm, probe_ref),
                (object_hbm, object_ref),
                (centers_hbm, centers_ref),
                (table_hbm, table_ref),
            )
        )
    ]
    for copy in copies:
        copy.start()
    tile_cols = object_ref.shape[2]
    half = edges[0].shape[2]
    z_index, x_index, parity = here()
    copies[0].wait()
    low_ref[...] = probe_ref[...].astype(jnp.bfloat16)
    shared_ref[...] = jnp.where(z_index % 2 == 0, low_ref[0, 0], low_ref[1, 0])
    rest_ref[...] = low_ref[:, 1:]
    copies[1].wait()
    first, last = slice(0, half), slice(tile_cols - half, tile_cols)
    for channel in range(2):
        values = object_ref[channel].astype(jnp.bfloat16)
        packed_ref[channel] = values
        if sides == 1:
            edges[0][channel] = jnp.where(x_index == 0, values[:, last], values[:, first])
        else:
            edges[0][channel] = values[:, last]
            edges[1][channel] = values[:, first]
    copies[2].wait()
    spot_ref[...] = jnp.where(
        iota(spot_ref.shape, 0) == 0, centers_ref[0, 0, parity, 0], centers_ref[0, 0, parity, 1]
    )
    record = jnp.zeros(record_ref.shape, jnp.float32)
    line = iota(record_ref.shape, 0)
    for slot in range(slots):
        for axis in range(2):
            value = centers_ref[0, 0, slot, axis].astype(jnp.float32)
            record = jnp.where(line == 2 * slot + axis, value, record)
    record_ref[...] = record.astype(jnp.bfloat16)
    copies[3].wait()
    real, imag = table_ref[0], table_ref[1]
    side = real.shape[0]
    first, last = slice(0, side), slice(side, 2 * side)
    for matrix_ref, upper, lower in ((direct_ref, -imag, imag), (swapped_ref, imag, -imag)):
        matrix_ref[first, first] = real
        matrix_ref[first, last] = upper
        matrix_ref[last, first] = lower
        matrix_ref[last, last] = real


def live_kernel(slots, record_ref, live_ref, out_ref):
    line = iota(record_ref.shape, 0)
    record = record_ref[...].astype(jnp.float32)
    record = jnp.where(line == 2 * slots, live_ref[0, 0].astype(jnp.float32), record)
    out_ref[...] = record.astype(jnp.bfloat16)


def position_of(record, slots, wanted):
    record = record[:, :128].astype(jnp.float32).astype(jnp.int32)[:, :1]

    def of_slot(axis):
        value = record[axis : axis + 1]
        for slot in range(1, slots):
            value = jnp.where(wanted == slot, record[2 * slot + axis : 2 * slot + axis + 1], value)
        return value

    return of_slot(0), of_slot(1), record[2 * slots : 2 * slots + 1] > wanted


def turned_back(value, side):
    return jnp.where(value == 0, 0, side - value)


def patch_of(sides, z_count, x_count, side, spot_ref, pieces):
    z_index, x_index, parity = here()
    row_at, col_at = spot_ref[0, 0], spot_ref[1, 0]
    half = side // 2
    even = parity == 0
    low_shown = z_index > 0
    high_shown = z_index < z_count - 1

    def joined(piece, a, b, channel):
        level = piece[channel].astype(jnp.float32)
        turn_a = a[channel].astype(jnp.float32)
        turn_b = b[channel].astype(jnp.float32)
        low = jnp.where(even & low_shown, turn_a, jnp.where(low_shown, turn_b, 0.0))
        high = jnp.where(even & high_shown, turn_b, jnp.where(high_shown, turn_a, 0.0))
        first = jnp.where(iota(low.shape, 0) >= row_at, low, high)
        return jnp.concatenate([first, level], axis=0)

    out = []
    for channel in range(2):
        own = joined(*pieces[:3], channel)
        sides_joined = [
            joined(*pieces[3 + 3 * index : 6 + 3 * index], channel) for index in range(sides)
        ]
        if sides == 1:
            left = jnp.where(x_index == 1, sides_joined[0], 0.0)
            right = jnp.where(x_index == 0, sides_joined[0], 0.0)
        else:
            left = jnp.where(x_index > 0, sides_joined[0], 0.0)
            right = jnp.where(x_index < x_count - 1, sides_joined[1], 0.0)
        at = iota(left.shape, 1)
        window = jnp.concatenate(
            [
                jnp.where(at >= col_at, left, own[:, half:]),
                jnp.where(at + half >= col_at, own[:, :half], right),
            ],
            axis=1,
        )
        window = pltpu.roll(window, turned_back(row_at, side), 0)
        out.append(pltpu.roll(window, turned_back(col_at, side), 1))
    return out


def modes_of(group):
    def reader(k):
        return lambda: (group[0, k].astype(jnp.float32), group[1, k].astype(jnp.float32))

    return [reader(k) for k in range(group.shape[1])]


def shared_mode(over_y, over_z):
    def read():
        z_index, _, _ = here()
        even = z_index % 2 == 0
        over_y_values = over_y[...].astype(jnp.float32)
        over_z_values = over_z[...].astype(jnp.float32)
        return (
            jnp.where(even, over_y_values, over_z_values),
            jnp.where(even, over_z_values, over_y_values),
        )

    return read


def forward(modes, patch, direct, swapped, far_ref, exit_ref, at):
    patch_real, patch_imag = patch
    side = patch_real.shape[0]
    power = jnp.zeros((side, side), jnp.float32)
    weight = jnp.zeros((side, side), jnp.float32)
    halves = []
    for k, mode in enumerate(modes):
        real, imag = mode()
        exit_wave = jnp.concatenate(
            [
                (real * patch_real - imag * patch_imag).astype(jnp.bfloat16),
                (real * patch_imag + imag * patch_real).astype(jnp.bfloat16),
            ],
            axis=0,
        )
        exit_ref[at + k] = exit_wave
        halves.append(wide(dot(direct, exit_wave).astype(jnp.bfloat16)))
        weight = weight + (real * real + imag * imag)
    far_all = dot(jnp.concatenate(halves, axis=0), swapped)
    for k in range(len(modes)):
        far = far_all[k * side : (k + 1) * side]
        far_ref[at + k] = far
        power = power + (far[:, :side] * far[:, :side] + far[:, side:] * far[:, side:])
    return power, weight


def backward(modes, factor, direct, swapped, far_ref, exit_ref, at):
    side = factor.shape[0]
    grad_real = jnp.zeros((side, side), jnp.float32)
    grad_imag = jnp.zeros((side, side), jnp.float32)
    halves = []
    for k in range(len(modes)):
        fixed = (far_ref[at + k] * factor).astype(jnp.bfloat16)
        halves.append(wide(dot(swapped, tall(fixed)).astype(jnp.bfloat16)))
    back_all = dot(jnp.concatenate(halves, axis=0), direct)
    for k, mode in enumerate(modes):
        back = back_all[k * side : (k + 1) * side]
        exit_wave = exit_ref[at + k].astype(jnp.float32)
        real, imag = mode()
        diff_real = back[:, :side] - exit_wave[:side]
        diff_imag = back[:, side:] - exit_wave[side:]
        grad_real = grad_real + (real * diff_real + imag * diff_imag)
        grad_imag = grad_imag + (real * diff_imag - imag * diff_real)
    return grad_real, grad_imag


def near_kernel(sides, z_count, x_count, spot_ref, *refs):
    n_pieces = 3 + 3 * sides
    pieces = from_sent_order(refs[:n_pieces])
    own, direct, swapped = refs[n_pieces : n_pieces + 3]
    patch_ref, far_ref, exit_ref, sum_ref = refs[n_pieces + 3 :]
    side = own.shape[2]
    patch = patch_of(sides, z_count, x_count, side, spot_ref, pieces)
    patch_ref[0], patch_ref[1] = patch
    sum_ref[0], sum_ref[1] = forward(
        modes_of(own), patch, direct[...], swapped[...], far_ref, exit_ref, 0
    )


def core_kernel(patch_ref, core, direct, swapped, far_ref, exit_ref, sum_ref):
    patch = (patch_ref[0], patch_ref[1])
    sum_ref[0], sum_ref[1] = forward(
        modes_of(core), patch, direct[...], swapped[...], far_ref, exit_ref, 0
    )


def over_kernel(patch_ref, over_y, over_z, rest, direct, swapped, far_ref, exit_ref, sum_ref):
    patch = (patch_ref[0], patch_ref[1])
    modes = [shared_mode(over_y, over_z)] + modes_of(rest)
    sum_ref[0], sum_ref[1] = forward(modes, patch, direct[...], swapped[...], far_ref, exit_ref, 0)


def back_kernel(sides, slots, tile_cols, record_ref, spot_ref, *refs):
    amplitude_ref, patch_ref, own, core = refs[:4]
    over_modes = [shared_mode(*refs[4:6])] + modes_of(refs[6])
    last_modes = [shared_mode(*refs[7:9])] + modes_of(refs[9])
    direct_ref, swapped_ref = refs[10:12]
    near_far, near_exit, near_sum, core_far, core_exit, core_sum = refs[12:18]
    over_far, over_exit, over_sum = refs[18:21]
    weight_out, own_out, keep_out, swap_out = refs[21:25]
    side_outs = refs[25 : 25 + sides]
    last_far, last_exit = refs[25 + sides :]
    side = own.shape[2]
    half = side // 2
    _, x_index, parity = here()
    row_at, col_at = spot_ref[0, 0], spot_ref[1, 0]
    _, _, is_live = position_of(record_ref, slots, parity)
    direct = direct_ref[...]
    swapped = swapped_ref[...]
    patch = (patch_ref[0], patch_ref[1])
    power, weight = forward(last_modes, patch, direct, swapped, last_far, last_exit, 0)
    power = (near_sum[0] + core_sum[0]) + (over_sum[0] + power)
    weight = (near_sum[1] + core_sum[1]) + (over_sum[1] + weight)
    weight_out[...] = weight.astype(jnp.bfloat16)
    amplitude = amplitude_ref[0, 0, parity].astype(jnp.float32)
    factor = amplitude / jnp.sqrt(power + power_floor)
    factor = jnp.concatenate([factor, factor], axis=1)
    tables = (factor, direct, swapped)
    grads = [
        backward(modes_of(own), *tables, near_far, near_exit, 0),
        backward(modes_of(core), *tables, core_far, core_exit, 0),
        backward(over_modes, *tables, over_far, over_exit, 0),
        backward(last_modes, *tables, last_far, last_exit, 0),
    ]
    even = parity == 0
    for channel in range(2):
        gradient = (grads[0][channel] + grads[1][channel]) + (grads[2][channel] + grads[3][channel])
        gradient = jnp.where(is_live, gradient, 0.0)
        gradient = pltpu.roll(pltpu.roll(gradient, col_at, 1), row_at, 0)
        first, second = gradient[:, :half], gradient[:, half:]
        at = iota(first.shape, 1)
        left = jnp.where(at >= col_at, first, 0.0)
        own = [
            jnp.where(at + half >= col_at, second, 0.0),
            jnp.where(at < col_at, first, 0.0),
        ]
        right = jnp.where(at + half < col_at, second, 0.0)
        if sides == 1:
            beside = [jnp.where(x_index == 0, right, left)]
        else:
            beside = [left, right]
        placed = jnp.concatenate(own + beside, axis=1)
        row = iota((half, placed.shape[1]), 0)
        low = jnp.where(row >= row_at, placed[:half], 0.0).astype(jnp.bfloat16)
        high = jnp.where(row < row_at, placed[:half], 0.0).astype(jnp.bfloat16)
        inner = placed[half:].astype(jnp.bfloat16)
        rows = slice(channel * half, (channel + 1) * half)
        own_out[rows] = inner[:, :tile_cols]
        keep_out[rows] = jnp.where(even, high, low)
        swap_out[rows] = jnp.where(even, low, high)
        for index, out in enumerate(side_outs):
            out[rows] = inner[:, tile_cols + index * half : tile_cols + (index + 1) * half]
    for out in side_outs:
        out[2 * half :] = record_ref[:, :half]


def meet_kernel(first_column, record_ref, keep_ref, swap_ref, *outs):
    at = first_column
    for out in outs:
        height, width = keep_ref.shape[0], out.shape[1]
        columns = slice(at, at + width)
        total = keep_ref[:, columns].astype(jnp.float32) + swap_ref[:, columns].astype(jnp.float32)
        out[:height] = total.astype(jnp.bfloat16)
        out[height:] = record_ref[:, :width]
        at += width


def placed_weight(weight, position, z_step, x_step, shown, shape):
    tile_rows, tile_cols = shape
    side = weight.shape[0]
    half = side // 2
    row, col, is_live = position
    row = jnp.where(is_live & shown, row + (z_step * tile_rows - half), nowhere)
    col = col + (x_step * tile_cols - half)
    put_rows = (iota((tile_rows, side), 0) == iota((tile_rows, side), 1) + row).astype(jnp.bfloat16)
    put_cols = (iota((side, tile_cols), 1) == iota((side, tile_cols), 0) + col).astype(jnp.bfloat16)
    return dot(dot(put_rows, weight).astype(jnp.bfloat16), put_cols)


def beside(sides, x_count):
    z_index, x_index, _ = here()
    if sides == 1:
        return [jnp.where(x_index == 0, 1, -1)], [z_index >= 0]
    return [1, -1], [x_index < x_count - 1, x_index > 0]


def edges_added(inner, edges, sides, shown):
    _, x_index, _ = here()
    half = edges[0].shape[1]
    first = jnp.zeros(edges[0].shape, jnp.float32)
    last = first
    for index, edge in enumerate(edges):
        if sides == 1:
            first = jnp.where(x_index == 1, edge, 0.0)
            last = jnp.where(x_index == 0, edge, 0.0)
        elif index == 0:
            last = jnp.where(shown[0], edge, 0.0)
        else:
            first = jnp.where(shown[1], edge, 0.0)
    middle = inner.shape[1] - 2 * half
    parts = [inner[:, :half] + first]
    if middle:
        parts.append(inner[:, half : half + middle])
    parts.append(inner[:, half + middle :] + last)
    return jnp.concatenate(parts, axis=1)


def level_kernel(sides, slots, x_count, weight_ref, record_ref, own_ref, *refs):
    levels, out_ref = refs[:sides], refs[-1]
    shape = out_ref.shape[1:]
    half = levels[0].shape[1]
    z_index, _, parity = here()
    x_steps, shown = beside(sides, x_count)
    weight = weight_ref[...]
    position = position_of(record_ref, slots, parity)
    total = placed_weight(weight, position, 0, 0, z_index >= 0, shape)
    for level, x_step, is_shown in zip(levels, x_steps, shown):
        position = position_of(level[2 * half :], slots, parity)
        total = total + placed_weight(weight, position, 0, x_step, is_shown, shape)
    out_ref[2] = total
    for channel in range(2):
        rows = slice(channel * half, (channel + 1) * half)
        edges = [level[rows].astype(jnp.float32) for level in levels]
        out_ref[channel] = edges_added(own_ref[rows].astype(jnp.float32), edges, sides, shown)


def sum_kernel(sides, slots, z_count, x_count, weight_ref, level_ref, rows_ref, *refs):
    corners, out_ref = refs[:sides], refs[-1]
    shape = out_ref.shape[1:]
    half = corners[0].shape[1]
    z_index, _, parity = here()
    z_step = jnp.where(parity == 0, -1, 1)
    z_shown = jnp.where(parity == 0, z_index > 0, z_index < z_count - 1)
    x_steps, shown = beside(sides, x_count)
    weight = weight_ref[...]
    total = level_ref[2]
    for piece, x_step, is_shown in zip(
        (rows_ref,) + corners, [0] + x_steps, [z_index >= 0] + shown
    ):
        for slot in range(slots):
            position = position_of(piece[2 * half :], slots, slot)
            total = total + placed_weight(
                weight, position, z_step, x_step, is_shown & z_shown, shape
            )
    out_ref[2] = total.astype(jnp.bfloat16)
    for channel in range(2):
        rows = slice(channel * half, (channel + 1) * half)
        edges = [corner[rows].astype(jnp.float32) for corner in corners]
        above = edges_added(rows_ref[rows].astype(jnp.float32), edges, sides, shown)
        total = level_ref[channel] + jnp.where(z_shown, above, 0.0)
        out_ref[channel] = total.astype(jnp.bfloat16)


def update_kernel(object_ref, own_ref, other_ref, out_ref):
    weight = own_ref[2].astype(jnp.float32) + other_ref[2].astype(jnp.float32) + regularizer
    for channel in range(2):
        gradient = own_ref[channel].astype(jnp.float32) + other_ref[channel].astype(jnp.float32)
        out_ref[channel] = object_ref[channel] + gradient / weight


def cost(products):
    return pl.CostEstimate(flops=products * 2 * 256**3, bytes_accessed=0, transcendentals=0)


def in_hbm(array):
    return pltpu.with_memory_space_constraint(array, pltpu.HBM)


def smem():
    return pl.BlockSpec(memory_space=pltpu.SMEM)


def hbm():
    return pl.BlockSpec(memory_space=pltpu.HBM)


def vmem():
    return pl.BlockSpec(memory_space=pltpu.VMEM)


def on_device(object_field, probe, amplitudes, centers, live):
    side = probe.shape[2]
    half = side // 2
    _, tile_rows, tile_cols = object_field.shape
    slots = centers.shape[2]
    z_count = lax.axis_size("tx")
    x_count = lax.axis_size("ty")
    m_count = lax.axis_size("mode")
    modes = probe.shape[1]
    if tile_rows != half or slots != 2 or m_count != 4 or z_count % 2 or x_count < 2 or modes < 2:
        raise ValueError("unsupported sizes")
    sides = 1 if x_count == 2 else 2
    axes = ("tx", "ty", "mode")

    def zigzag(x_step):
        def moved(z, m):
            if m % 2 == 0:
                return (z + 1, m) if z < z_count - 1 else (z, m ^ 1)
            return (z - 1, m) if z > 0 else (z, m ^ 1)

        pairs = []
        for z in range(z_count):
            for x in range(x_count):
                for m in range(m_count):
                    z_to, m_to = moved(z, m)
                    x_to = (x + x_step) % x_count
                    pairs.append(
                        (
                            (z * x_count + x) * m_count + m,
                            (z_to * x_count + x_to) * m_count + m_to,
                        )
                    )
        return pairs

    def level(step):
        return [(x, (x + step) % x_count) for x in range(x_count)]

    def exchange(array, flip):
        return lax.ppermute(array, "mode", [(m, m ^ flip) for m in range(m_count)])

    table = jnp.asarray(dft_table(side))
    probe_low, shared, rest, record, spot, direct, swapped, *packed = pl.pallas_call(
        functools.partial(start_kernel, sides, slots),
        out_shape=[
            jax.ShapeDtypeStruct(probe.shape, jnp.bfloat16),
            jax.ShapeDtypeStruct((side, side), jnp.bfloat16),
            jax.ShapeDtypeStruct((2, modes - 1, side, side), jnp.bfloat16),
            jax.ShapeDtypeStruct((record_rows, tile_cols), jnp.bfloat16),
            jax.ShapeDtypeStruct((8, 128), jnp.int32),
            jax.ShapeDtypeStruct((2 * side, 2 * side), jnp.bfloat16),
            jax.ShapeDtypeStruct((2 * side, 2 * side), jnp.bfloat16),
            jax.ShapeDtypeStruct(object_field.shape, jnp.bfloat16),
        ]
        + [jax.ShapeDtypeStruct((2, tile_rows, half), jnp.bfloat16)] * sides,
        in_specs=[hbm()] * 4,
        out_specs=[vmem()] * (8 + sides),
        scratch_shapes=[
            pltpu.VMEM(object_field.shape, jnp.float32),
            pltpu.VMEM(probe.shape, jnp.float32),
            pltpu.SMEM(centers.shape, jnp.int32),
            pltpu.VMEM((2, side, side), jnp.bfloat16),
            pltpu.SemaphoreType.DMA((4,)),
        ],
        compiler_params=pltpu.CompilerParams(vmem_limit_bytes=small_bytes),
        name="start",
    )(*(in_hbm(array) for array in (object_field, probe, centers, table)))
    over_y = exchange(shared, 2)
    probe_core = exchange(probe_low, 1)
    rest = exchange(rest, 2)
    over_z = lax.ppermute(over_y, "tx", [(z, z ^ 1) for z in range(z_count)])
    x_steps = [1] if sides == 1 else [1, -1]
    rows = lax.ppermute(packed[0], axes, zigzag(0))
    probe_core, *corner_edges = lax.optimization_barrier((probe_core, *packed[1:]))
    corners = [lax.ppermute(edge, axes, zigzag(step)) for step, edge in zip(x_steps, corner_edges)]
    levels = [lax.ppermute(edge, "ty", level(step)) for step, edge in zip(x_steps, packed[1:])]
    corners, record = lax.optimization_barrier((corners, record))
    record = pl.pallas_call(
        functools.partial(live_kernel, slots),
        out_shape=jax.ShapeDtypeStruct(record.shape, jnp.bfloat16),
        in_specs=[vmem(), smem()],
        out_specs=vmem(),
        compiler_params=pltpu.CompilerParams(vmem_limit_bytes=small_bytes),
        cost_estimate=cost(50),
        name="live",
    )(record, live)
    corners, record = lax.optimization_barrier((corners, record))
    pieces = [packed[0], rows, exchange(rows, 1)]
    for at_level, corner in zip(levels, corners):
        pieces += [at_level, corner, exchange(corner, 1)]
    n_pieces = len(pieces)
    ext_cols = tile_cols + sides * half

    waves = [
        jax.ShapeDtypeStruct((modes, side, 2 * side), jnp.float32),
        jax.ShapeDtypeStruct((modes, 2 * side, side), jnp.bfloat16),
        jax.ShapeDtypeStruct((2, side, side), jnp.float32),
    ]
    patch, *near = pl.pallas_call(
        functools.partial(near_kernel, sides, z_count, x_count),
        out_shape=[jax.ShapeDtypeStruct((2, side, side), jnp.float32)] + waves,
        in_specs=[vmem()] * (n_pieces + 4),
        out_specs=[vmem()] * 4,
        compiler_params=pltpu.CompilerParams(vmem_limit_bytes=wave_bytes),
        cost_estimate=cost(1),
        name="near",
    )(spot, *in_sent_order(pieces), probe_low, direct, swapped)
    rest, patch = lax.optimization_barrier((rest, patch))
    other = pl.pallas_call(
        core_kernel,
        out_shape=waves,
        in_specs=[vmem()] * 4,
        out_specs=[vmem()] * 3,
        compiler_params=pltpu.CompilerParams(vmem_limit_bytes=wave_bytes),
        cost_estimate=cost(1),
        name="core",
    )(patch, probe_core, direct, swapped)
    last_y = exchange(over_y, 1)
    over_z, other = lax.optimization_barrier((over_z, other))
    over_group = (over_y, over_z, rest)
    last_group = [last_y, exchange(over_z, 1), exchange(rest, 1)]
    over = pl.pallas_call(
        over_kernel,
        out_shape=waves,
        in_specs=[vmem()] * 6,
        out_specs=[vmem()] * 3,
        compiler_params=pltpu.CompilerParams(vmem_limit_bytes=wave_bytes),
        cost_estimate=cost(100),
        name="over",
    )(patch, *over_group, direct, swapped)
    piece_rows = 2 * half + record_rows
    shapes = [(side, side), (2 * half, tile_cols)] + [(2 * half, ext_cols)] * 2
    shapes += [(piece_rows, half)] * sides
    weight, own, keep, swap, *levels = pl.pallas_call(
        functools.partial(back_kernel, sides, slots, tile_cols),
        out_shape=[jax.ShapeDtypeStruct(shape, jnp.bfloat16) for shape in shapes],
        in_specs=[vmem()] * 23,
        out_specs=[vmem()] * (4 + sides),
        scratch_shapes=[
            pltpu.VMEM((modes, side, 2 * side), jnp.float32),
            pltpu.VMEM((modes, 2 * side, side), jnp.bfloat16),
        ],
        compiler_params=pltpu.CompilerParams(vmem_limit_bytes=wave_bytes),
        cost_estimate=cost(80),
        name="back",
    )(
        record,
        spot,
        amplitudes,
        patch,
        probe_low,
        probe_core,
        *over_group,
        *last_group,
        direct,
        swapped,
        *near,
        *other,
        *over,
    )
    levels = [lax.ppermute(piece, "ty", level(-step)) for piece, step in zip(levels, x_steps)]
    rows, *corners = pl.pallas_call(
        functools.partial(meet_kernel, 0),
        out_shape=[
            jax.ShapeDtypeStruct((piece_rows, width), jnp.bfloat16)
            for width in [tile_cols] + [half] * sides
        ],
        in_specs=[vmem()] * 3,
        out_specs=[vmem()] * (1 + sides),
        compiler_params=pltpu.CompilerParams(vmem_limit_bytes=small_bytes),
        name="meet",
    )(record, keep, exchange(swap, 1))
    rows = lax.ppermute(rows, axes, zigzag(0))
    corners = [
        lax.ppermute(piece, axes, zigzag(-step)) for piece, step in zip(corners, x_steps)
    ]
    leveled = pl.pallas_call(
        functools.partial(level_kernel, sides, slots, x_count),
        out_shape=jax.ShapeDtypeStruct((3, tile_rows, tile_cols), jnp.float32),
        in_specs=[vmem()] * (3 + sides),
        out_specs=vmem(),
        compiler_params=pltpu.CompilerParams(vmem_limit_bytes=small_bytes),
        cost_estimate=cost(40),
        name="levels",
    )(weight, record, own, *levels)
    summed = pl.pallas_call(
        functools.partial(sum_kernel, sides, slots, z_count, x_count),
        out_shape=jax.ShapeDtypeStruct((3, tile_rows, tile_cols), jnp.bfloat16),
        in_specs=[vmem()] * (3 + sides),
        out_specs=vmem(),
        compiler_params=pltpu.CompilerParams(vmem_limit_bytes=small_bytes),
        name="sums",
    )(weight, leveled, rows, *corners)
    return pl.pallas_call(
        update_kernel,
        out_shape=jax.ShapeDtypeStruct(object_field.shape, jnp.float32),
        in_specs=[vmem()] * 3,
        out_specs=vmem(),
        compiler_params=pltpu.CompilerParams(vmem_limit_bytes=small_bytes),
        name="update",
    )(object_field, summed, exchange(summed, 1))


def solution(mesh):
    return jax.shard_map(
        on_device,
        mesh=mesh,
        in_specs=(
            P(None, "tx", "ty"),
            P(None, "mode", None, None),
            P("tx", "ty", None, None, None),
            P("tx", "ty", None, None),
            P("tx", "ty"),
        ),
        out_specs=P(None, "tx", "ty"),
        check_vma=False,
    )
```

```python
import functools
import math

import jax
import jax.numpy as jnp
import numpy as np
from jax import lax
from jax.experimental import pallas as pl
from jax.experimental.pallas import tpu as pltpu
from jax.sharding import PartitionSpec as P

power_floor = 0.01
regularizer = 0.1
nowhere = -(1 << 20)
record_rows = 16
wave_bytes = 32 * 1024 * 1024
small_bytes = 8 * 1024 * 1024


def dft_table(side):
    line = np.arange(side, dtype=np.int32)
    angle = (line[:, None] * line[None, :] % side).astype(np.float32) * np.float32(
        2.0 * math.pi / side
    )
    scaling = np.float32(1.0 / math.sqrt(side))
    real = (np.cos(angle) * scaling).astype(jnp.bfloat16)
    imag = (-np.sin(angle) * scaling).astype(jnp.bfloat16)
    return np.stack([real, imag])


def dot(left, right):
    return jnp.dot(left, right, preferred_element_type=jnp.float32)


def iota(shape, dim):
    return lax.broadcasted_iota(jnp.int32, shape, dim)


def sent_order(sides):
    corners = [at for index in range(sides) for at in (4 + 3 * index, 5 + 3 * index)]
    return [0] + corners + [1, 2] + [3 + 3 * index for index in range(sides)]


def in_sent_order(pieces):
    return [pieces[at] for at in sent_order(len(pieces) // 3 - 1)]


def from_sent_order(pieces):
    order = sent_order(len(pieces) // 3 - 1)
    return [pieces[order.index(at)] for at in range(len(pieces))]


def wide(tall):
    side = tall.shape[0] // 2
    return jnp.concatenate([tall[:side], tall[side:]], axis=1)


def tall(wide):
    side = wide.shape[1] // 2
    return jnp.concatenate([wide[:, :side], wide[:, side:]], axis=0)


def here():
    return (lax.axis_index("tx"), lax.axis_index("ty"), lax.axis_index("mode") % 2)


def start_kernel(
    sides,
    slots,
    object_hbm,
    probe_hbm,
    centers_hbm,
    table_hbm,
    low_ref,
    shared_ref,
    rest_ref,
    record_ref,
    spot_ref,
    direct_ref,
    swapped_ref,
    packed_ref,
    *refs,
):
    edges = refs[:sides]
    object_ref, probe_ref, centers_ref, table_ref, sems = refs[sides:]
    copies = [
        pltpu.make_async_copy(source, target, sems.at[index])
        for index, (source, target) in enumerate(
            (
                (probe_hbm, probe_ref),
                (object_hbm, object_ref),
                (centers_hbm, centers_ref),
                (table_hbm, table_ref),
            )
        )
    ]
    for copy in copies:
        copy.start()
    tile_cols = object_ref.shape[2]
    half = edges[0].shape[2]
    z_index, x_index, parity = here()
    copies[0].wait()
    low_ref[...] = probe_ref[...].astype(jnp.bfloat16)
    shared_ref[...] = jnp.where(z_index % 2 == 0, low_ref[0, 0], low_ref[1, 0])
    rest_ref[...] = low_ref[:, 1:]
    copies[1].wait()
    first, last = slice(0, half), slice(tile_cols - half, tile_cols)
    for channel in range(2):
        values = object_ref[channel].astype(jnp.bfloat16)
        packed_ref[channel] = values
        if sides == 1:
            edges[0][channel] = jnp.where(x_index == 0, values[:, last], values[:, first])
        else:
            edges[0][channel] = values[:, last]
            edges[1][channel] = values[:, first]
    copies[2].wait()
    spot_ref[...] = jnp.where(
        iota(spot_ref.shape, 0) == 0, centers_ref[0, 0, parity, 0], centers_ref[0, 0, parity, 1]
    )
    record = jnp.zeros(record_ref.shape, jnp.float32)
    line = iota(record_ref.shape, 0)
    for slot in range(slots):
        for axis in range(2):
            value = centers_ref[0, 0, slot, axis].astype(jnp.float32)
            record = jnp.where(line == 2 * slot + axis, value, record)
    record_ref[...] = record.astype(jnp.bfloat16)
    copies[3].wait()
    real, imag = table_ref[0], table_ref[1]
    side = real.shape[0]
    first, last = slice(0, side), slice(side, 2 * side)
    for matrix_ref, upper, lower in ((direct_ref, -imag, imag), (swapped_ref, imag, -imag)):
        matrix_ref[first, first] = real
        matrix_ref[first, last] = upper
        matrix_ref[last, first] = lower
        matrix_ref[last, last] = real


def live_kernel(slots, record_ref, live_ref, out_ref):
    line = iota(record_ref.shape, 0)
    record = record_ref[...].astype(jnp.float32)
    record = jnp.where(line == 2 * slots, live_ref[0, 0].astype(jnp.float32), record)
    out_ref[...] = record.astype(jnp.bfloat16)


def position_of(record, slots, wanted):
    record = record[:, :128].astype(jnp.float32).astype(jnp.int32)[:, :1]

    def of_slot(axis):
        value = record[axis : axis + 1]
        for slot in range(1, slots):
            value = jnp.where(wanted == slot, record[2 * slot + axis : 2 * slot + axis + 1], value)
        return value

    return of_slot(0), of_slot(1), record[2 * slots : 2 * slots + 1] > wanted


def turned_back(value, side):
    return jnp.where(value == 0, 0, side - value)


def patch_of(sides, z_count, x_count, side, spot_ref, pieces):
    z_index, x_index, parity = here()
    row_at, col_at = spot_ref[0, 0], spot_ref[1, 0]
    half = side // 2
    even = parity == 0
    low_shown = z_index > 0
    high_shown = z_index < z_count - 1

    def joined(piece, a, b, channel):
        level = piece[channel].astype(jnp.float32)
        turn_a = a[channel].astype(jnp.float32)
        turn_b = b[channel].astype(jnp.float32)
        low = jnp.where(even & low_shown, turn_a, jnp.where(low_shown, turn_b, 0.0))
        high = jnp.where(even & high_shown, turn_b, jnp.where(high_shown, turn_a, 0.0))
        first = jnp.where(iota(low.shape, 0) >= row_at, low, high)
        return jnp.concatenate([first, level], axis=0)

    out = []
    for channel in range(2):
        own = joined(*pieces[:3], channel)
        sides_joined = [
            joined(*pieces[3 + 3 * index : 6 + 3 * index], channel) for index in range(sides)
        ]
        if sides == 1:
            left = jnp.where(x_index == 1, sides_joined[0], 0.0)
            right = jnp.where(x_index == 0, sides_joined[0], 0.0)
        else:
            left = jnp.where(x_index > 0, sides_joined[0], 0.0)
            right = jnp.where(x_index < x_count - 1, sides_joined[1], 0.0)
        at = iota(left.shape, 1)
        window = jnp.concatenate(
            [
                jnp.where(at >= col_at, left, own[:, half:]),
                jnp.where(at + half >= col_at, own[:, :half], right),
            ],
            axis=1,
        )
        window = pltpu.roll(window, turned_back(row_at, side), 0)
        out.append(pltpu.roll(window, turned_back(col_at, side), 1))
    return out


def modes_of(group):
    def reader(k):
        return lambda: (group[0, k].astype(jnp.float32), group[1, k].astype(jnp.float32))

    return [reader(k) for k in range(group.shape[1])]


def shared_mode(over_y, over_z):
    def read():
        z_index, _, _ = here()
        even = z_index % 2 == 0
        over_y_values = over_y[...].astype(jnp.float32)
        over_z_values = over_z[...].astype(jnp.float32)
        return (
            jnp.where(even, over_y_values, over_z_values),
            jnp.where(even, over_z_values, over_y_values),
        )

    return read


def forward(modes, patch, direct, swapped, far_ref, exit_ref, at):
    patch_real, patch_imag = patch
    side = patch_real.shape[0]
    power = jnp.zeros((side, side), jnp.float32)
    weight = jnp.zeros((side, side), jnp.float32)
    halves = []
    for k, mode in enumerate(modes):
        real, imag = mode()
        exit_wave = jnp.concatenate(
            [
                (real * patch_real - imag * patch_imag).astype(jnp.bfloat16),
                (real * patch_imag + imag * patch_real).astype(jnp.bfloat16),
            ],
            axis=0,
        )
        exit_ref[at + k] = exit_wave
        halves.append(wide(dot(direct, exit_wave).astype(jnp.bfloat16)))
        weight = weight + (real * real + imag * imag)
    far_all = dot(jnp.concatenate(halves, axis=0), swapped)
    for k in range(len(modes)):
        far = far_all[k * side : (k + 1) * side]
        far_ref[at + k] = far
        power = power + (far[:, :side] * far[:, :side] + far[:, side:] * far[:, side:])
    return power, weight


def backward(modes, factor, direct, swapped, far_ref, exit_ref, at):
    side = factor.shape[0]
    grad_real = jnp.zeros((side, side), jnp.float32)
    grad_imag = jnp.zeros((side, side), jnp.float32)
    halves = []
    for k in range(len(modes)):
        fixed = (far_ref[at + k] * factor).astype(jnp.bfloat16)
        halves.append(wide(dot(swapped, tall(fixed)).astype(jnp.bfloat16)))
    back_all = dot(jnp.concatenate(halves, axis=0), direct)
    for k, mode in enumerate(modes):
        back = back_all[k * side : (k + 1) * side]
        exit_wave = exit_ref[at + k].astype(jnp.float32)
        real, imag = mode()
        diff_real = back[:, :side] - exit_wave[:side]
        diff_imag = back[:, side:] - exit_wave[side:]
        grad_real = grad_real + (real * diff_real + imag * diff_imag)
        grad_imag = grad_imag + (real * diff_imag - imag * diff_real)
    return grad_real, grad_imag


def near_kernel(sides, z_count, x_count, spot_ref, *refs):
    n_pieces = 3 + 3 * sides
    pieces = from_sent_order(refs[:n_pieces])
    own, direct, swapped = refs[n_pieces : n_pieces + 3]
    patch_ref, far_ref, exit_ref, sum_ref = refs[n_pieces + 3 :]
    side = own.shape[2]
    patch = patch_of(sides, z_count, x_count, side, spot_ref, pieces)
    patch_ref[0], patch_ref[1] = patch
    sum_ref[0], sum_ref[1] = forward(
        modes_of(own), patch, direct[...], swapped[...], far_ref, exit_ref, 0
    )


def core_kernel(patch_ref, core, direct, swapped, far_ref, exit_ref, sum_ref):
    patch = (patch_ref[0], patch_ref[1])
    sum_ref[0], sum_ref[1] = forward(
        modes_of(core), patch, direct[...], swapped[...], far_ref, exit_ref, 0
    )


def over_kernel(patch_ref, over_y, over_z, rest, direct, swapped, far_ref, exit_ref, sum_ref):
    patch = (patch_ref[0], patch_ref[1])
    modes = [shared_mode(over_y, over_z)] + modes_of(rest)
    sum_ref[0], sum_ref[1] = forward(modes, patch, direct[...], swapped[...], far_ref, exit_ref, 0)


def back_kernel(sides, slots, tile_cols, record_ref, spot_ref, *refs):
    amplitude_ref, patch_ref, own, core = refs[:4]
    over_modes = [shared_mode(*refs[4:6])] + modes_of(refs[6])
    last_modes = [shared_mode(*refs[7:9])] + modes_of(refs[9])
    direct_ref, swapped_ref = refs[10:12]
    near_far, near_exit, near_sum, core_far, core_exit, core_sum = refs[12:18]
    over_far, over_exit, over_sum = refs[18:21]
    weight_out, own_out, keep_out, swap_out = refs[21:25]
    side_outs = refs[25 : 25 + sides]
    last_far, last_exit = refs[25 + sides :]
    side = own.shape[2]
    half = side // 2
    _, x_index, parity = here()
    row_at, col_at = spot_ref[0, 0], spot_ref[1, 0]
    _, _, is_live = position_of(record_ref, slots, parity)
    direct = direct_ref[...]
    swapped = swapped_ref[...]
    patch = (patch_ref[0], patch_ref[1])
    power, weight = forward(last_modes, patch, direct, swapped, last_far, last_exit, 0)
    power = (near_sum[0] + core_sum[0]) + (over_sum[0] + power)
    weight = (near_sum[1] + core_sum[1]) + (over_sum[1] + weight)
    weight_out[...] = weight.astype(jnp.bfloat16)
    amplitude = amplitude_ref[0, 0, parity].astype(jnp.float32)
    factor = amplitude / jnp.sqrt(power + power_floor)
    factor = jnp.concatenate([factor, factor], axis=1)
    tables = (factor, direct, swapped)
    grads = [
        backward(modes_of(own), *tables, near_far, near_exit, 0),
        backward(modes_of(core), *tables, core_far, core_exit, 0),
        backward(over_modes, *tables, over_far, over_exit, 0),
        backward(last_modes, *tables, last_far, last_exit, 0),
    ]
    even = parity == 0
    for channel in range(2):
        gradient = (grads[0][channel] + grads[1][channel]) + (grads[2][channel] + grads[3][channel])
        gradient = jnp.where(is_live, gradient, 0.0)
        gradient = pltpu.roll(pltpu.roll(gradient, col_at, 1), row_at, 0)
        first, second = gradient[:, :half], gradient[:, half:]
        at = iota(first.shape, 1)
        left = jnp.where(at >= col_at, first, 0.0)
        own = [
            jnp.where(at + half >= col_at, second, 0.0),
            jnp.where(at < col_at, first, 0.0),
        ]
        right = jnp.where(at + half < col_at, second, 0.0)
        if sides == 1:
            beside = [jnp.where(x_index == 0, right, left)]
        else:
            beside = [left, right]
        placed = jnp.concatenate(own + beside, axis=1)
        row = iota((half, placed.shape[1]), 0)
        low = jnp.where(row >= row_at, placed[:half], 0.0).astype(jnp.bfloat16)
        high = jnp.where(row < row_at, placed[:half], 0.0).astype(jnp.bfloat16)
        inner = placed[half:].astype(jnp.bfloat16)
        rows = slice(channel * half, (channel + 1) * half)
        own_out[rows] = inner[:, :tile_cols]
        keep_out[rows] = jnp.where(even, high, low)
        swap_out[rows] = jnp.where(even, low, high)
        for index, out in enumerate(side_outs):
            out[rows] = inner[:, tile_cols + index * half : tile_cols + (index + 1) * half]
    for out in side_outs:
        out[2 * half :] = record_ref[:, :half]


def meet_kernel(first_column, record_ref, keep_ref, swap_ref, *outs):
    at = first_column
    for out in outs:
        height, width = keep_ref.shape[0], out.shape[1]
        columns = slice(at, at + width)
        total = keep_ref[:, columns].astype(jnp.float32) + swap_ref[:, columns].astype(jnp.float32)
        out[:height] = total.astype(jnp.bfloat16)
        out[height:] = record_ref[:, :width]
        at += width


def placed_weight(weight, position, z_step, x_step, shown, shape):
    tile_rows, tile_cols = shape
    side = weight.shape[0]
    half = side // 2
    row, col, is_live = position
    row = jnp.where(is_live & shown, row + (z_step * tile_rows - half), nowhere)
    col = col + (x_step * tile_cols - half)
    put_rows = (iota((tile_rows, side), 0) == iota((tile_rows, side), 1) + row).astype(jnp.bfloat16)
    put_cols = (iota((side, tile_cols), 1) == iota((side, tile_cols), 0) + col).astype(jnp.bfloat16)
    return dot(dot(put_rows, weight).astype(jnp.bfloat16), put_cols)


def beside(sides, x_count):
    z_index, x_index, _ = here()
    if sides == 1:
        return [jnp.where(x_index == 0, 1, -1)], [z_index >= 0]
    return [1, -1], [x_index < x_count - 1, x_index > 0]


def edges_added(inner, edges, sides, shown):
    _, x_index, _ = here()
    half = edges[0].shape[1]
    first = jnp.zeros(edges[0].shape, jnp.float32)
    last = first
    for index, edge in enumerate(edges):
        if sides == 1:
            first = jnp.where(x_index == 1, edge, 0.0)
            last = jnp.where(x_index == 0, edge, 0.0)
        elif index == 0:
            last = jnp.where(shown[0], edge, 0.0)
        else:
            first = jnp.where(shown[1], edge, 0.0)
    middle = inner.shape[1] - 2 * half
    parts = [inner[:, :half] + first]
    if middle:
        parts.append(inner[:, half : half + middle])
    parts.append(inner[:, half + middle :] + last)
    return jnp.concatenate(parts, axis=1)


def level_kernel(sides, slots, x_count, weight_ref, record_ref, own_ref, *refs):
    levels, out_ref = refs[:sides], refs[-1]
    shape = out_ref.shape[1:]
    half = levels[0].shape[1]
    z_index, _, parity = here()
    x_steps, shown = beside(sides, x_count)
    weight = weight_ref[...]
    position = position_of(record_ref, slots, parity)
    total = placed_weight(weight, position, 0, 0, z_index >= 0, shape)
    for level, x_step, is_shown in zip(levels, x_steps, shown):
        position = position_of(level[2 * half :], slots, parity)
        total = total + placed_weight(weight, position, 0, x_step, is_shown, shape)
    out_ref[2] = total
    for channel in range(2):
        rows = slice(channel * half, (channel + 1) * half)
        edges = [level[rows].astype(jnp.float32) for level in levels]
        out_ref[channel] = edges_added(own_ref[rows].astype(jnp.float32), edges, sides, shown)


def sum_kernel(sides, slots, z_count, x_count, weight_ref, level_ref, rows_ref, *refs):
    corners, out_ref = refs[:sides], refs[-1]
    shape = out_ref.shape[1:]
    half = corners[0].shape[1]
    z_index, _, parity = here()
    z_step = jnp.where(parity == 0, -1, 1)
    z_shown = jnp.where(parity == 0, z_index > 0, z_index < z_count - 1)
    x_steps, shown = beside(sides, x_count)
    weight = weight_ref[...]
    total = level_ref[2]
    for piece, x_step, is_shown in zip(
        (rows_ref,) + corners, [0] + x_steps, [z_index >= 0] + shown
    ):
        for slot in range(slots):
            position = position_of(piece[2 * half :], slots, slot)
            total = total + placed_weight(
                weight, position, z_step, x_step, is_shown & z_shown, shape
            )
    out_ref[2] = total.astype(jnp.bfloat16)
    for channel in range(2):
        rows = slice(channel * half, (channel + 1) * half)
        edges = [corner[rows].astype(jnp.float32) for corner in corners]
        above = edges_added(rows_ref[rows].astype(jnp.float32), edges, sides, shown)
        total = level_ref[channel] + jnp.where(z_shown, above, 0.0)
        out_ref[channel] = total.astype(jnp.bfloat16)


def update_kernel(object_ref, own_ref, other_ref, out_ref):
    weight = own_ref[2].astype(jnp.float32) + other_ref[2].astype(jnp.float32) + regularizer
    for channel in range(2):
        gradient = own_ref[channel].astype(jnp.float32) + other_ref[channel].astype(jnp.float32)
        out_ref[channel] = object_ref[channel] + gradient / weight


def cost(products):
    return pl.CostEstimate(flops=products * 2 * 256**3, bytes_accessed=0, transcendentals=0)


def in_hbm(array):
    return pltpu.with_memory_space_constraint(array, pltpu.HBM)


def smem():
    return pl.BlockSpec(memory_space=pltpu.SMEM)


def hbm():
    return pl.BlockSpec(memory_space=pltpu.HBM)


def vmem():
    return pl.BlockSpec(memory_space=pltpu.VMEM)


def on_device(object_field, probe, amplitudes, centers, live):
    side = probe.shape[2]
    half = side // 2
    _, tile_rows, tile_cols = object_field.shape
    slots = centers.shape[2]
    z_count = lax.axis_size("tx")
    x_count = lax.axis_size("ty")
    m_count = lax.axis_size("mode")
    modes = probe.shape[1]
    if tile_rows != half or slots != 2 or m_count != 4 or z_count % 2 or x_count < 2 or modes < 2:
        raise ValueError("unsupported sizes")
    sides = 1 if x_count == 2 else 2
    axes = ("tx", "ty", "mode")

    def zigzag(x_step):
        def moved(z, m):
            if m % 2 == 0:
                return (z + 1, m) if z < z_count - 1 else (z, m ^ 1)
            return (z - 1, m) if z > 0 else (z, m ^ 1)

        pairs = []
        for z in range(z_count):
            for x in range(x_count):
                for m in range(m_count):
                    z_to, m_to = moved(z, m)
                    x_to = (x + x_step) % x_count
                    pairs.append(
                        (
                            (z * x_count + x) * m_count + m,
                            (z_to * x_count + x_to) * m_count + m_to,
                        )
                    )
        return pairs

    def level(step):
        return [(x, (x + step) % x_count) for x in range(x_count)]

    def exchange(array, flip):
        return lax.ppermute(array, "mode", [(m, m ^ flip) for m in range(m_count)])

    table = jnp.asarray(dft_table(side))
    probe_low, shared, rest, record, spot, direct, swapped, *packed = pl.pallas_call(
        functools.partial(start_kernel, sides, slots),
        out_shape=[
            jax.ShapeDtypeStruct(probe.shape, jnp.bfloat16),
            jax.ShapeDtypeStruct((side, side), jnp.bfloat16),
            jax.ShapeDtypeStruct((2, modes - 1, side, side), jnp.bfloat16),
            jax.ShapeDtypeStruct((record_rows, tile_cols), jnp.bfloat16),
            jax.ShapeDtypeStruct((8, 128), jnp.int32),
            jax.ShapeDtypeStruct((2 * side, 2 * side), jnp.bfloat16),
            jax.ShapeDtypeStruct((2 * side, 2 * side), jnp.bfloat16),
            jax.ShapeDtypeStruct(object_field.shape, jnp.bfloat16),
        ]
        + [jax.ShapeDtypeStruct((2, tile_rows, half), jnp.bfloat16)] * sides,
        in_specs=[hbm()] * 4,
        out_specs=[vmem()] * (8 + sides),
        scratch_shapes=[
            pltpu.VMEM(object_field.shape, jnp.float32),
            pltpu.VMEM(probe.shape, jnp.float32),
            pltpu.SMEM(centers.shape, jnp.int32),
            pltpu.VMEM((2, side, side), jnp.bfloat16),
            pltpu.SemaphoreType.DMA((4,)),
        ],
        compiler_params=pltpu.CompilerParams(vmem_limit_bytes=small_bytes),
        name="start",
    )(*(in_hbm(array) for array in (object_field, probe, centers, table)))
    over_y = exchange(shared, 2)
    probe_core = exchange(probe_low, 1)
    rest = exchange(rest, 2)
    over_z = lax.ppermute(over_y, "tx", [(z, z ^ 1) for z in range(z_count)])
    x_steps = [1] if sides == 1 else [1, -1]
    rows = lax.ppermute(packed[0], axes, zigzag(0))
    probe_core, *corner_edges = lax.optimization_barrier((probe_core, *packed[1:]))
    corners = [lax.ppermute(edge, axes, zigzag(step)) for step, edge in zip(x_steps, corner_edges)]
    levels = [lax.ppermute(edge, "ty", level(step)) for step, edge in zip(x_steps, packed[1:])]
    corners, record = lax.optimization_barrier((corners, record))
    record = pl.pallas_call(
        functools.partial(live_kernel, slots),
        out_shape=jax.ShapeDtypeStruct(record.shape, jnp.bfloat16),
        in_specs=[vmem(), smem()],
        out_specs=vmem(),
        compiler_params=pltpu.CompilerParams(vmem_limit_bytes=small_bytes),
        cost_estimate=cost(20),
        name="live",
    )(record, live)
    corners, record = lax.optimization_barrier((corners, record))
    pieces = [packed[0], rows, exchange(rows, 1)]
    for at_level, corner in zip(levels, corners):
        pieces += [at_level, corner, exchange(corner, 1)]
    n_pieces = len(pieces)
    ext_cols = tile_cols + sides * half

    waves = [
        jax.ShapeDtypeStruct((modes, side, 2 * side), jnp.float32),
        jax.ShapeDtypeStruct((modes, 2 * side, side), jnp.bfloat16),
        jax.ShapeDtypeStruct((2, side, side), jnp.float32),
    ]
    patch, *near = pl.pallas_call(
        functools.partial(near_kernel, sides, z_count, x_count),
        out_shape=[jax.ShapeDtypeStruct((2, side, side), jnp.float32)] + waves,
        in_specs=[vmem()] * (n_pieces + 4),
        out_specs=[vmem()] * 4,
        compiler_params=pltpu.CompilerParams(vmem_limit_bytes=wave_bytes),
        cost_estimate=cost(1),
        name="near",
    )(spot, *in_sent_order(pieces), probe_low, direct, swapped)
    rest, patch = lax.optimization_barrier((rest, patch))
    other = pl.pallas_call(
        core_kernel,
        out_shape=waves,
        in_specs=[vmem()] * 4,
        out_specs=[vmem()] * 3,
        compiler_params=pltpu.CompilerParams(vmem_limit_bytes=wave_bytes),
        cost_estimate=cost(1),
        name="core",
    )(patch, probe_core, direct, swapped)
    last_y = exchange(over_y, 1)
    over_z, other = lax.optimization_barrier((over_z, other))
    over_group = (over_y, over_z, rest)
    last_group = [last_y, exchange(over_z, 1), exchange(rest, 1)]
    over = pl.pallas_call(
        over_kernel,
        out_shape=waves,
        in_specs=[vmem()] * 6,
        out_specs=[vmem()] * 3,
        compiler_params=pltpu.CompilerParams(vmem_limit_bytes=wave_bytes),
        cost_estimate=cost(100),
        name="over",
    )(patch, *over_group, direct, swapped)
    piece_rows = 2 * half + record_rows
    shapes = [(side, side), (2 * half, tile_cols)] + [(2 * half, ext_cols)] * 2
    shapes += [(piece_rows, half)] * sides
    weight, own, keep, swap, *levels = pl.pallas_call(
        functools.partial(back_kernel, sides, slots, tile_cols),
        out_shape=[jax.ShapeDtypeStruct(shape, jnp.bfloat16) for shape in shapes],
        in_specs=[vmem()] * 23,
        out_specs=[vmem()] * (4 + sides),
        scratch_shapes=[
            pltpu.VMEM((modes, side, 2 * side), jnp.float32),
            pltpu.VMEM((modes, 2 * side, side), jnp.bfloat16),
        ],
        compiler_params=pltpu.CompilerParams(vmem_limit_bytes=wave_bytes),
        cost_estimate=cost(80),
        name="back",
    )(
        record,
        spot,
        amplitudes,
        patch,
        probe_low,
        probe_core,
        *over_group,
        *last_group,
        direct,
        swapped,
        *near,
        *other,
        *over,
    )
    levels = [lax.ppermute(piece, "ty", level(-step)) for piece, step in zip(levels, x_steps)]
    rows, *corners = pl.pallas_call(
        functools.partial(meet_kernel, 0),
        out_shape=[
            jax.ShapeDtypeStruct((piece_rows, width), jnp.bfloat16)
            for width in [tile_cols] + [half] * sides
        ],
        in_specs=[vmem()] * 3,
        out_specs=[vmem()] * (1 + sides),
        compiler_params=pltpu.CompilerParams(vmem_limit_bytes=small_bytes),
        name="meet",
    )(record, keep, exchange(swap, 1))
    rows = lax.ppermute(rows, axes, zigzag(0))
    corners = [
        lax.ppermute(piece, axes, zigzag(-step)) for piece, step in zip(corners, x_steps)
    ]
    leveled = pl.pallas_call(
        functools.partial(level_kernel, sides, slots, x_count),
        out_shape=jax.ShapeDtypeStruct((3, tile_rows, tile_cols), jnp.float32),
        in_specs=[vmem()] * (3 + sides),
        out_specs=vmem(),
        compiler_params=pltpu.CompilerParams(vmem_limit_bytes=small_bytes),
        cost_estimate=cost(40),
        name="levels",
    )(weight, record, own, *levels)
    summed = pl.pallas_call(
        functools.partial(sum_kernel, sides, slots, z_count, x_count),
        out_shape=jax.ShapeDtypeStruct((3, tile_rows, tile_cols), jnp.bfloat16),
        in_specs=[vmem()] * (3 + sides),
        out_specs=vmem(),
        compiler_params=pltpu.CompilerParams(vmem_limit_bytes=small_bytes),
        name="sums",
    )(weight, leveled, rows, *corners)
    return pl.pallas_call(
        update_kernel,
        out_shape=jax.ShapeDtypeStruct(object_field.shape, jnp.float32),
        in_specs=[vmem()] * 3,
        out_specs=vmem(),
        compiler_params=pltpu.CompilerParams(vmem_limit_bytes=small_bytes),
        name="update",
    )(object_field, summed, exchange(summed, 1))


def solution(mesh):
    return jax.shard_map(
        on_device,
        mesh=mesh,
        in_specs=(
            P(None, "tx", "ty"),
            P(None, "mode", None, None),
            P("tx", "ty", None, None, None),
            P("tx", "ty", None, None),
            P("tx", "ty"),
        ),
        out_specs=P(None, "tx", "ty"),
        check_vma=False,
    )
```

```python
import functools
import math

import jax
import jax.numpy as jnp
import numpy as np
from jax import lax
from jax.experimental import pallas as pl
from jax.experimental.pallas import tpu as pltpu
from jax.sharding import PartitionSpec as P

power_floor = 0.01
regularizer = 0.1
nowhere = -(1 << 20)
record_rows = 16
wave_bytes = 32 * 1024 * 1024
small_bytes = 8 * 1024 * 1024


def dft_table(side):
    line = np.arange(side, dtype=np.int32)
    angle = (line[:, None] * line[None, :] % side).astype(np.float32) * np.float32(
        2.0 * math.pi / side
    )
    scaling = np.float32(1.0 / math.sqrt(side))
    real = (np.cos(angle) * scaling).astype(jnp.bfloat16)
    imag = (-np.sin(angle) * scaling).astype(jnp.bfloat16)
    return np.stack([real, imag])


def dot(left, right):
    return jnp.dot(left, right, preferred_element_type=jnp.float32)


def iota(shape, dim):
    return lax.broadcasted_iota(jnp.int32, shape, dim)


def sent_order(sides):
    corners = [at for index in range(sides) for at in (4 + 3 * index, 5 + 3 * index)]
    return [0] + corners + [1, 2] + [3 + 3 * index for index in range(sides)]


def in_sent_order(pieces):
    return [pieces[at] for at in sent_order(len(pieces) // 3 - 1)]


def from_sent_order(pieces):
    order = sent_order(len(pieces) // 3 - 1)
    return [pieces[order.index(at)] for at in range(len(pieces))]


def wide(tall):
    side = tall.shape[0] // 2
    return jnp.concatenate([tall[:side], tall[side:]], axis=1)


def tall(wide):
    side = wide.shape[1] // 2
    return jnp.concatenate([wide[:, :side], wide[:, side:]], axis=0)


def here():
    return (lax.axis_index("tx"), lax.axis_index("ty"), lax.axis_index("mode") % 2)


def start_kernel(
    sides,
    slots,
    object_hbm,
    probe_hbm,
    centers_hbm,
    table_hbm,
    low_ref,
    shared_ref,
    rest_ref,
    record_ref,
    spot_ref,
    direct_ref,
    swapped_ref,
    packed_ref,
    *refs,
):
    edges = refs[:sides]
    object_ref, probe_ref, centers_ref, table_ref, sems = refs[sides:]
    copies = [
        pltpu.make_async_copy(source, target, sems.at[index])
        for index, (source, target) in enumerate(
            (
                (probe_hbm, probe_ref),
                (object_hbm, object_ref),
                (centers_hbm, centers_ref),
                (table_hbm, table_ref),
            )
        )
    ]
    for copy in copies:
        copy.start()
    tile_cols = object_ref.shape[2]
    half = edges[0].shape[2]
    z_index, x_index, parity = here()
    copies[0].wait()
    low_ref[...] = probe_ref[...].astype(jnp.bfloat16)
    shared_ref[...] = jnp.where(z_index % 2 == 0, low_ref[0, 0], low_ref[1, 0])
    rest_ref[...] = low_ref[:, 1:]
    copies[1].wait()
    first, last = slice(0, half), slice(tile_cols - half, tile_cols)
    for channel in range(2):
        values = object_ref[channel].astype(jnp.bfloat16)
        packed_ref[channel] = values
        if sides == 1:
            edges[0][channel] = jnp.where(x_index == 0, values[:, last], values[:, first])
        else:
            edges[0][channel] = values[:, last]
            edges[1][channel] = values[:, first]
    copies[2].wait()
    spot_ref[...] = jnp.where(
        iota(spot_ref.shape, 0) == 0, centers_ref[0, 0, parity, 0], centers_ref[0, 0, parity, 1]
    )
    record = jnp.zeros(record_ref.shape, jnp.float32)
    line = iota(record_ref.shape, 0)
    for slot in range(slots):
        for axis in range(2):
            value = centers_ref[0, 0, slot, axis].astype(jnp.float32)
            record = jnp.where(line == 2 * slot + axis, value, record)
    record_ref[...] = record.astype(jnp.bfloat16)
    copies[3].wait()
    real, imag = table_ref[0], table_ref[1]
    side = real.shape[0]
    first, last = slice(0, side), slice(side, 2 * side)
    for matrix_ref, upper, lower in ((direct_ref, -imag, imag), (swapped_ref, imag, -imag)):
        matrix_ref[first, first] = real
        matrix_ref[first, last] = upper
        matrix_ref[last, first] = lower
        matrix_ref[last, last] = real


def live_kernel(slots, record_ref, live_ref, out_ref):
    line = iota(record_ref.shape, 0)
    record = record_ref[...].astype(jnp.float32)
    record = jnp.where(line == 2 * slots, live_ref[0, 0].astype(jnp.float32), record)
    out_ref[...] = record.astype(jnp.bfloat16)


def position_of(record, slots, wanted):
    record = record[:, :128].astype(jnp.float32).astype(jnp.int32)[:, :1]

    def of_slot(axis):
        value = record[axis : axis + 1]
        for slot in range(1, slots):
            value = jnp.where(wanted == slot, record[2 * slot + axis : 2 * slot + axis + 1], value)
        return value

    return of_slot(0), of_slot(1), record[2 * slots : 2 * slots + 1] > wanted


def turned_back(value, side):
    return jnp.where(value == 0, 0, side - value)


def patch_of(sides, z_count, x_count, side, spot_ref, pieces):
    z_index, x_index, parity = here()
    row_at, col_at = spot_ref[0, 0], spot_ref[1, 0]
    half = side // 2
    even = parity == 0
    low_shown = z_index > 0
    high_shown = z_index < z_count - 1

    def joined(piece, a, b, channel):
        level = piece[channel].astype(jnp.float32)
        turn_a = a[channel].astype(jnp.float32)
        turn_b = b[channel].astype(jnp.float32)
        low = jnp.where(even & low_shown, turn_a, jnp.where(low_shown, turn_b, 0.0))
        high = jnp.where(even & high_shown, turn_b, jnp.where(high_shown, turn_a, 0.0))
        first = jnp.where(iota(low.shape, 0) >= row_at, low, high)
        return jnp.concatenate([first, level], axis=0)

    out = []
    for channel in range(2):
        own = joined(*pieces[:3], channel)
        sides_joined = [
            joined(*pieces[3 + 3 * index : 6 + 3 * index], channel) for index in range(sides)
        ]
        if sides == 1:
            left = jnp.where(x_index == 1, sides_joined[0], 0.0)
            right = jnp.where(x_index == 0, sides_joined[0], 0.0)
        else:
            left = jnp.where(x_index > 0, sides_joined[0], 0.0)
            right = jnp.where(x_index < x_count - 1, sides_joined[1], 0.0)
        at = iota(left.shape, 1)
        window = jnp.concatenate(
            [
                jnp.where(at >= col_at, left, own[:, half:]),
                jnp.where(at + half >= col_at, own[:, :half], right),
            ],
            axis=1,
        )
        window = pltpu.roll(window, turned_back(row_at, side), 0)
        out.append(pltpu.roll(window, turned_back(col_at, side), 1))
    return out


def modes_of(group):
    def reader(k):
        return lambda: (group[0, k].astype(jnp.float32), group[1, k].astype(jnp.float32))

    return [reader(k) for k in range(group.shape[1])]


def shared_mode(over_y, over_z):
    def read():
        z_index, _, _ = here()
        even = z_index % 2 == 0
        over_y_values = over_y[...].astype(jnp.float32)
        over_z_values = over_z[...].astype(jnp.float32)
        return (
            jnp.where(even, over_y_values, over_z_values),
            jnp.where(even, over_z_values, over_y_values),
        )

    return read


def forward(modes, patch, direct, swapped, far_ref, exit_ref, at):
    patch_real, patch_imag = patch
    side = patch_real.shape[0]
    power = jnp.zeros((side, side), jnp.float32)
    weight = jnp.zeros((side, side), jnp.float32)
    halves = []
    for k, mode in enumerate(modes):
        real, imag = mode()
        exit_wave = jnp.concatenate(
            [
                (real * patch_real - imag * patch_imag).astype(jnp.bfloat16),
                (real * patch_imag + imag * patch_real).astype(jnp.bfloat16),
            ],
            axis=0,
        )
        exit_ref[at + k] = exit_wave
        halves.append(wide(dot(direct, exit_wave).astype(jnp.bfloat16)))
        weight = weight + (real * real + imag * imag)
    far_all = dot(jnp.concatenate(halves, axis=0), swapped)
    for k in range(len(modes)):
        far = far_all[k * side : (k + 1) * side]
        far_ref[at + k] = far
        power = power + (far[:, :side] * far[:, :side] + far[:, side:] * far[:, side:])
    return power, weight


def backward(modes, factor, direct, swapped, far_ref, exit_ref, at):
    side = factor.shape[0]
    grad_real = jnp.zeros((side, side), jnp.float32)
    grad_imag = jnp.zeros((side, side), jnp.float32)
    halves = []
    for k in range(len(modes)):
        fixed = (far_ref[at + k] * factor).astype(jnp.bfloat16)
        halves.append(wide(dot(swapped, tall(fixed)).astype(jnp.bfloat16)))
    back_all = dot(jnp.concatenate(halves, axis=0), direct)
    for k, mode in enumerate(modes):
        back = back_all[k * side : (k + 1) * side]
        exit_wave = exit_ref[at + k].astype(jnp.float32)
        real, imag = mode()
        diff_real = back[:, :side] - exit_wave[:side]
        diff_imag = back[:, side:] - exit_wave[side:]
        grad_real = grad_real + (real * diff_real + imag * diff_imag)
        grad_imag = grad_imag + (real * diff_imag - imag * diff_real)
    return grad_real, grad_imag


def near_kernel(sides, z_count, x_count, spot_ref, *refs):
    n_pieces = 3 + 3 * sides
    pieces = from_sent_order(refs[:n_pieces])
    own, direct, swapped = refs[n_pieces : n_pieces + 3]
    patch_ref, far_ref, exit_ref, sum_ref = refs[n_pieces + 3 :]
    side = own.shape[2]
    patch = patch_of(sides, z_count, x_count, side, spot_ref, pieces)
    patch_ref[0], patch_ref[1] = patch
    sum_ref[0], sum_ref[1] = forward(
        modes_of(own), patch, direct[...], swapped[...], far_ref, exit_ref, 0
    )


def core_kernel(patch_ref, core, direct, swapped, far_ref, exit_ref, sum_ref):
    patch = (patch_ref[0], patch_ref[1])
    sum_ref[0], sum_ref[1] = forward(
        modes_of(core), patch, direct[...], swapped[...], far_ref, exit_ref, 0
    )


def over_kernel(patch_ref, over_y, over_z, rest, direct, swapped, far_ref, exit_ref, sum_ref):
    patch = (patch_ref[0], patch_ref[1])
    modes = [shared_mode(over_y, over_z)] + modes_of(rest)
    sum_ref[0], sum_ref[1] = forward(modes, patch, direct[...], swapped[...], far_ref, exit_ref, 0)


def back_kernel(sides, slots, tile_cols, record_ref, spot_ref, *refs):
    amplitude_ref, patch_ref, own, core = refs[:4]
    over_modes = [shared_mode(*refs[4:6])] + modes_of(refs[6])
    last_modes = [shared_mode(*refs[7:9])] + modes_of(refs[9])
    direct_ref, swapped_ref = refs[10:12]
    near_far, near_exit, near_sum, core_far, core_exit, core_sum = refs[12:18]
    over_far, over_exit, over_sum = refs[18:21]
    weight_out, own_out, keep_out, swap_out = refs[21:25]
    side_outs = refs[25 : 25 + sides]
    last_far, last_exit = refs[25 + sides :]
    side = own.shape[2]
    half = side // 2
    _, x_index, parity = here()
    row_at, col_at = spot_ref[0, 0], spot_ref[1, 0]
    _, _, is_live = position_of(record_ref, slots, parity)
    direct = direct_ref[...]
    swapped = swapped_ref[...]
    patch = (patch_ref[0], patch_ref[1])
    power, weight = forward(last_modes, patch, direct, swapped, last_far, last_exit, 0)
    power = (near_sum[0] + core_sum[0]) + (over_sum[0] + power)
    weight = (near_sum[1] + core_sum[1]) + (over_sum[1] + weight)
    weight_out[...] = weight.astype(jnp.bfloat16)
    amplitude = amplitude_ref[0, 0, parity].astype(jnp.float32)
    factor = amplitude / jnp.sqrt(power + power_floor)
    factor = jnp.concatenate([factor, factor], axis=1)
    tables = (factor, direct, swapped)
    grads = [
        backward(modes_of(own), *tables, near_far, near_exit, 0),
        backward(modes_of(core), *tables, core_far, core_exit, 0),
        backward(over_modes, *tables, over_far, over_exit, 0),
        backward(last_modes, *tables, last_far, last_exit, 0),
    ]
    even = parity == 0
    for channel in range(2):
        gradient = (grads[0][channel] + grads[1][channel]) + (grads[2][channel] + grads[3][channel])
        gradient = jnp.where(is_live, gradient, 0.0)
        gradient = pltpu.roll(pltpu.roll(gradient, col_at, 1), row_at, 0)
        first, second = gradient[:, :half], gradient[:, half:]
        at = iota(first.shape, 1)
        left = jnp.where(at >= col_at, first, 0.0)
        own = [
            jnp.where(at + half >= col_at, second, 0.0),
            jnp.where(at < col_at, first, 0.0),
        ]
        right = jnp.where(at + half < col_at, second, 0.0)
        if sides == 1:
            beside = [jnp.where(x_index == 0, right, left)]
        else:
            beside = [left, right]
        placed = jnp.concatenate(own + beside, axis=1)
        row = iota((half, placed.shape[1]), 0)
        low = jnp.where(row >= row_at, placed[:half], 0.0).astype(jnp.bfloat16)
        high = jnp.where(row < row_at, placed[:half], 0.0).astype(jnp.bfloat16)
        inner = placed[half:].astype(jnp.bfloat16)
        rows = slice(channel * half, (channel + 1) * half)
        own_out[rows] = inner[:, :tile_cols]
        keep_out[rows] = jnp.where(even, high, low)
        swap_out[rows] = jnp.where(even, low, high)
        for index, out in enumerate(side_outs):
            out[rows] = inner[:, tile_cols + index * half : tile_cols + (index + 1) * half]
    for out in side_outs:
        out[2 * half :] = record_ref[:, :half]


def meet_kernel(first_column, record_ref, keep_ref, swap_ref, *outs):
    at = first_column
    for out in outs:
        height, width = keep_ref.shape[0], out.shape[1]
        columns = slice(at, at + width)
        total = keep_ref[:, columns].astype(jnp.float32) + swap_ref[:, columns].astype(jnp.float32)
        out[:height] = total.astype(jnp.bfloat16)
        out[height:] = record_ref[:, :width]
        at += width


def placed_weight(weight, position, z_step, x_step, shown, shape):
    tile_rows, tile_cols = shape
    side = weight.shape[0]
    half = side // 2
    row, col, is_live = position
    row = jnp.where(is_live & shown, row + (z_step * tile_rows - half), nowhere)
    col = col + (x_step * tile_cols - half)
    put_rows = (iota((tile_rows, side), 0) == iota((tile_rows, side), 1) + row).astype(jnp.bfloat16)
    put_cols = (iota((side, tile_cols), 1) == iota((side, tile_cols), 0) + col).astype(jnp.bfloat16)
    return dot(dot(put_rows, weight).astype(jnp.bfloat16), put_cols)


def beside(sides, x_count):
    z_index, x_index, _ = here()
    if sides == 1:
        return [jnp.where(x_index == 0, 1, -1)], [z_index >= 0]
    return [1, -1], [x_index < x_count - 1, x_index > 0]


def edges_added(inner, edges, sides, shown):
    _, x_index, _ = here()
    half = edges[0].shape[1]
    first = jnp.zeros(edges[0].shape, jnp.float32)
    last = first
    for index, edge in enumerate(edges):
        if sides == 1:
            first = jnp.where(x_index == 1, edge, 0.0)
            last = jnp.where(x_index == 0, edge, 0.0)
        elif index == 0:
            last = jnp.where(shown[0], edge, 0.0)
        else:
            first = jnp.where(shown[1], edge, 0.0)
    middle = inner.shape[1] - 2 * half
    parts = [inner[:, :half] + first]
    if middle:
        parts.append(inner[:, half : half + middle])
    parts.append(inner[:, half + middle :] + last)
    return jnp.concatenate(parts, axis=1)


def level_kernel(sides, slots, x_count, weight_ref, record_ref, own_ref, *refs):
    levels, out_ref = refs[:sides], refs[-1]
    shape = out_ref.shape[1:]
    half = levels[0].shape[1]
    z_index, _, parity = here()
    x_steps, shown = beside(sides, x_count)
    weight = weight_ref[...]
    position = position_of(record_ref, slots, parity)
    total = placed_weight(weight, position, 0, 0, z_index >= 0, shape)
    for level, x_step, is_shown in zip(levels, x_steps, shown):
        position = position_of(level[2 * half :], slots, parity)
        total = total + placed_weight(weight, position, 0, x_step, is_shown, shape)
    out_ref[2] = total
    for channel in range(2):
        rows = slice(channel * half, (channel + 1) * half)
        edges = [level[rows].astype(jnp.float32) for level in levels]
        out_ref[channel] = edges_added(own_ref[rows].astype(jnp.float32), edges, sides, shown)


def sum_kernel(sides, slots, z_count, x_count, weight_ref, level_ref, rows_ref, *refs):
    corners, out_ref = refs[:sides], refs[-1]
    shape = out_ref.shape[1:]
    half = corners[0].shape[1]
    z_index, _, parity = here()
    z_step = jnp.where(parity == 0, -1, 1)
    z_shown = jnp.where(parity == 0, z_index > 0, z_index < z_count - 1)
    x_steps, shown = beside(sides, x_count)
    weight = weight_ref[...]
    total = level_ref[2]
    for piece, x_step, is_shown in zip(
        (rows_ref,) + corners, [0] + x_steps, [z_index >= 0] + shown
    ):
        for slot in range(slots):
            position = position_of(piece[2 * half :], slots, slot)
            total = total + placed_weight(
                weight, position, z_step, x_step, is_shown & z_shown, shape
            )
    out_ref[2] = total.astype(jnp.bfloat16)
    for channel in range(2):
        rows = slice(channel * half, (channel + 1) * half)
        edges = [corner[rows].astype(jnp.float32) for corner in corners]
        above = edges_added(rows_ref[rows].astype(jnp.float32), edges, sides, shown)
        total = level_ref[channel] + jnp.where(z_shown, above, 0.0)
        out_ref[channel] = total.astype(jnp.bfloat16)


def update_kernel(object_ref, own_ref, other_ref, out_ref):
    weight = own_ref[2].astype(jnp.float32) + other_ref[2].astype(jnp.float32) + regularizer
    for channel in range(2):
        gradient = own_ref[channel].astype(jnp.float32) + other_ref[channel].astype(jnp.float32)
        out_ref[channel] = object_ref[channel] + gradient / weight


def cost(products):
    return pl.CostEstimate(flops=products * 2 * 256**3, bytes_accessed=0, transcendentals=0)


def in_hbm(array):
    return pltpu.with_memory_space_constraint(array, pltpu.HBM)


def smem():
    return pl.BlockSpec(memory_space=pltpu.SMEM)


def hbm():
    return pl.BlockSpec(memory_space=pltpu.HBM)


def vmem():
    return pl.BlockSpec(memory_space=pltpu.VMEM)


def on_device(object_field, probe, amplitudes, centers, live):
    side = probe.shape[2]
    half = side // 2
    _, tile_rows, tile_cols = object_field.shape
    slots = centers.shape[2]
    z_count = lax.axis_size("tx")
    x_count = lax.axis_size("ty")
    m_count = lax.axis_size("mode")
    modes = probe.shape[1]
    if tile_rows != half or slots != 2 or m_count != 4 or z_count % 2 or x_count < 2 or modes < 2:
        raise ValueError("unsupported sizes")
    sides = 1 if x_count == 2 else 2
    axes = ("tx", "ty", "mode")

    def zigzag(x_step):
        def moved(z, m):
            if m % 2 == 0:
                return (z + 1, m) if z < z_count - 1 else (z, m ^ 1)
            return (z - 1, m) if z > 0 else (z, m ^ 1)

        pairs = []
        for z in range(z_count):
            for x in range(x_count):
                for m in range(m_count):
                    z_to, m_to = moved(z, m)
                    x_to = (x + x_step) % x_count
                    pairs.append(
                        (
                            (z * x_count + x) * m_count + m,
                            (z_to * x_count + x_to) * m_count + m_to,
                        )
                    )
        return pairs

    def level(step):
        return [(x, (x + step) % x_count) for x in range(x_count)]

    def exchange(array, flip):
        return lax.ppermute(array, "mode", [(m, m ^ flip) for m in range(m_count)])

    table = jnp.asarray(dft_table(side))
    probe_low, shared, rest, record, spot, direct, swapped, *packed = pl.pallas_call(
        functools.partial(start_kernel, sides, slots),
        out_shape=[
            jax.ShapeDtypeStruct(probe.shape, jnp.bfloat16),
            jax.ShapeDtypeStruct((side, side), jnp.bfloat16),
            jax.ShapeDtypeStruct((2, modes - 1, side, side), jnp.bfloat16),
            jax.ShapeDtypeStruct((record_rows, tile_cols), jnp.bfloat16),
            jax.ShapeDtypeStruct((8, 128), jnp.int32),
            jax.ShapeDtypeStruct((2 * side, 2 * side), jnp.bfloat16),
            jax.ShapeDtypeStruct((2 * side, 2 * side), jnp.bfloat16),
            jax.ShapeDtypeStruct(object_field.shape, jnp.bfloat16),
        ]
        + [jax.ShapeDtypeStruct((2, tile_rows, half), jnp.bfloat16)] * sides,
        in_specs=[hbm()] * 4,
        out_specs=[vmem()] * (8 + sides),
        scratch_shapes=[
            pltpu.VMEM(object_field.shape, jnp.float32),
            pltpu.VMEM(probe.shape, jnp.float32),
            pltpu.SMEM(centers.shape, jnp.int32),
            pltpu.VMEM((2, side, side), jnp.bfloat16),
            pltpu.SemaphoreType.DMA((4,)),
        ],
        compiler_params=pltpu.CompilerParams(vmem_limit_bytes=small_bytes),
        name="start",
    )(*(in_hbm(array) for array in (object_field, probe, centers, table)))
    over_y = exchange(shared, 2)
    probe_core = exchange(probe_low, 1)
    rest = exchange(rest, 2)
    over_z = lax.ppermute(over_y, "tx", [(z, z ^ 1) for z in range(z_count)])
    x_steps = [1] if sides == 1 else [1, -1]
    rows = lax.ppermute(packed[0], axes, zigzag(0))
    probe_core, *corner_edges = lax.optimization_barrier((probe_core, *packed[1:]))
    corners = [lax.ppermute(edge, axes, zigzag(step)) for step, edge in zip(x_steps, corner_edges)]
    levels = [lax.ppermute(edge, "ty", level(step)) for step, edge in zip(x_steps, packed[1:])]
    rows, levels = lax.optimization_barrier((rows, levels))
    corners, record = lax.optimization_barrier((corners, record))
    record = pl.pallas_call(
        functools.partial(live_kernel, slots),
        out_shape=jax.ShapeDtypeStruct(record.shape, jnp.bfloat16),
        in_specs=[vmem(), smem()],
        out_specs=vmem(),
        compiler_params=pltpu.CompilerParams(vmem_limit_bytes=small_bytes),
        cost_estimate=cost(20),
        name="live",
    )(record, live)
    corners, record = lax.optimization_barrier((corners, record))
    pieces = [packed[0], rows, exchange(rows, 1)]
    for at_level, corner in zip(levels, corners):
        pieces += [at_level, corner, exchange(corner, 1)]
    n_pieces = len(pieces)
    ext_cols = tile_cols + sides * half

    waves = [
        jax.ShapeDtypeStruct((modes, side, 2 * side), jnp.float32),
        jax.ShapeDtypeStruct((modes, 2 * side, side), jnp.bfloat16),
        jax.ShapeDtypeStruct((2, side, side), jnp.float32),
    ]
    patch, *near = pl.pallas_call(
        functools.partial(near_kernel, sides, z_count, x_count),
        out_shape=[jax.ShapeDtypeStruct((2, side, side), jnp.float32)] + waves,
        in_specs=[vmem()] * (n_pieces + 4),
        out_specs=[vmem()] * 4,
        compiler_params=pltpu.CompilerParams(vmem_limit_bytes=wave_bytes),
        cost_estimate=cost(1),
        name="near",
    )(spot, *in_sent_order(pieces), probe_low, direct, swapped)
    rest, patch = lax.optimization_barrier((rest, patch))
    other = pl.pallas_call(
        core_kernel,
        out_shape=waves,
        in_specs=[vmem()] * 4,
        out_specs=[vmem()] * 3,
        compiler_params=pltpu.CompilerParams(vmem_limit_bytes=wave_bytes),
        cost_estimate=cost(1),
        name="core",
    )(patch, probe_core, direct, swapped)
    last_y = exchange(over_y, 1)
    over_z, other = lax.optimization_barrier((over_z, other))
    over_group = (over_y, over_z, rest)
    last_group = [last_y, exchange(over_z, 1), exchange(rest, 1)]
    over = pl.pallas_call(
        over_kernel,
        out_shape=waves,
        in_specs=[vmem()] * 6,
        out_specs=[vmem()] * 3,
        compiler_params=pltpu.CompilerParams(vmem_limit_bytes=wave_bytes),
        cost_estimate=cost(100),
        name="over",
    )(patch, *over_group, direct, swapped)
    piece_rows = 2 * half + record_rows
    shapes = [(side, side), (2 * half, tile_cols)] + [(2 * half, ext_cols)] * 2
    shapes += [(piece_rows, half)] * sides
    weight, own, keep, swap, *levels = pl.pallas_call(
        functools.partial(back_kernel, sides, slots, tile_cols),
        out_shape=[jax.ShapeDtypeStruct(shape, jnp.bfloat16) for shape in shapes],
        in_specs=[vmem()] * 23,
        out_specs=[vmem()] * (4 + sides),
        scratch_shapes=[
            pltpu.VMEM((modes, side, 2 * side), jnp.float32),
            pltpu.VMEM((modes, 2 * side, side), jnp.bfloat16),
        ],
        compiler_params=pltpu.CompilerParams(vmem_limit_bytes=wave_bytes),
        cost_estimate=cost(80),
        name="back",
    )(
        record,
        spot,
        amplitudes,
        patch,
        probe_low,
        probe_core,
        *over_group,
        *last_group,
        direct,
        swapped,
        *near,
        *other,
        *over,
    )
    levels = [lax.ppermute(piece, "ty", level(-step)) for piece, step in zip(levels, x_steps)]
    rows, *corners = pl.pallas_call(
        functools.partial(meet_kernel, 0),
        out_shape=[
            jax.ShapeDtypeStruct((piece_rows, width), jnp.bfloat16)
            for width in [tile_cols] + [half] * sides
        ],
        in_specs=[vmem()] * 3,
        out_specs=[vmem()] * (1 + sides),
        compiler_params=pltpu.CompilerParams(vmem_limit_bytes=small_bytes),
        name="meet",
    )(record, keep, exchange(swap, 1))
    rows = lax.ppermute(rows, axes, zigzag(0))
    corners = [
        lax.ppermute(piece, axes, zigzag(-step)) for piece, step in zip(corners, x_steps)
    ]
    leveled = pl.pallas_call(
        functools.partial(level_kernel, sides, slots, x_count),
        out_shape=jax.ShapeDtypeStruct((3, tile_rows, tile_cols), jnp.float32),
        in_specs=[vmem()] * (3 + sides),
        out_specs=vmem(),
        compiler_params=pltpu.CompilerParams(vmem_limit_bytes=small_bytes),
        cost_estimate=cost(40),
        name="levels",
    )(weight, record, own, *levels)
    summed = pl.pallas_call(
        functools.partial(sum_kernel, sides, slots, z_count, x_count),
        out_shape=jax.ShapeDtypeStruct((3, tile_rows, tile_cols), jnp.bfloat16),
        in_specs=[vmem()] * (3 + sides),
        out_specs=vmem(),
        compiler_params=pltpu.CompilerParams(vmem_limit_bytes=small_bytes),
        name="sums",
    )(weight, leveled, rows, *corners)
    return pl.pallas_call(
        update_kernel,
        out_shape=jax.ShapeDtypeStruct(object_field.shape, jnp.float32),
        in_specs=[vmem()] * 3,
        out_specs=vmem(),
        compiler_params=pltpu.CompilerParams(vmem_limit_bytes=small_bytes),
        name="update",
    )(object_field, summed, exchange(summed, 1))


def solution(mesh):
    return jax.shard_map(
        on_device,
        mesh=mesh,
        in_specs=(
            P(None, "tx", "ty"),
            P(None, "mode", None, None),
            P("tx", "ty", None, None, None),
            P("tx", "ty", None, None),
            P("tx", "ty"),
        ),
        out_specs=P(None, "tx", "ty"),
        check_vma=False,
    )
```
